32 devices in a mesh: dp: 8 (over z, x), tensor: 4 (over y, core).
Axes of the slice: x: 2, y: 2, z: 4, core: 2. Of those that a mesh axis runs over, the one named last changes fastest.
Arguments:
- resid: bfloat16 [8192, 1536], P(('dp', 'tensor')), may hold values from -6 to 6
- segment_ids: int32 [8192], P('dp'), may hold values from 0 to 127, as said below
- cotangent: float32 [8192, 1536], P(('dp', 'tensor')), may hold values from -6 to 6
- w_z: bfloat16 [2, 1536, 3072], P(None, 'dp', 'tensor'), may hold values from -0.15625 to 0.15625
- w_x: bfloat16 [2, 1536, 3072], P(None, 'dp', 'tensor'), may hold values from -0.15625 to 0.15625
- w_bc: bfloat16 [2, 1536, 256], P(None, ('dp', 'tensor')), may hold values from -0.15625 to 0.15625
- w_dt: bfloat16 [2, 1536, 48], P(None, 'dp', 'tensor'), may hold values from -0.15625 to 0.15625
- w_out: bfloat16 [2, 3072, 1536], P(None, 'tensor', 'dp'), may hold values from -0.109375 to 0.109375
- norm_gain: float32 [2, 1536], replicated, may hold values from 0.5 to 1.5
- conv_x: float32 [2, 4, 3072], P(None, None, 'tensor'), may hold values from -3 to 3
- conv_bc: float32 [2, 4, 256], replicated, may hold values from -3 to 3
- a_log: float32 [2, 48], P(None, 'tensor'), may hold values from -4 to 1.5
- dt_bias: float32 [2, 48], P(None, 'tensor'), may hold values from -4.5 to -2.5
- d_skip: float32 [2, 48], P(None, 'tensor'), may hold values from 0.5 to 1.5
- gated_gain: float32 [2, 3072], P(None, 'tensor'), may hold values from 0.5 to 1.5
Outputs:
- hidden_out: float32 [8192, 1536], P(('dp', 'tensor'))
- grad_resid: float32 [8192, 1536], P(('dp', 'tensor'))
- grad_w_z: float32 [2, 1536, 3072], P(None, 'dp', 'tensor')
- grad_w_x: float32 [2, 1536, 3072], P(None, 'dp', 'tensor')
- grad_w_bc: float32 [2, 1536, 256], P(None, ('dp', 'tensor'))
- grad_w_dt: float32 [2, 1536, 48], P(None, 'dp', 'tensor')
- grad_w_out: float32 [2, 3072, 1536], P(None, 'tensor', 'dp')
- grad_norm_gain: float32 [2, 1536], replicated
- grad_conv_x: float32 [2, 4, 3072], P(None, None, 'tensor')
- grad_conv_bc: float32 [2, 4, 256], replicated
- grad_a_log: float32 [2, 48], P(None, 'tensor')
- grad_dt_bias: float32 [2, 48], P(None, 'tensor')
- grad_d_skip: float32 [2, 48], P(None, 'tensor')
- grad_gated_gain: float32 [2, 3072], P(None, 'tensor')
The draws below stay inside these ranges and needn't reach their ends.
Inputs may be any that keep to these rules, and one draw needn't show every extreme that they name: `segment_ids`: within each sequence (aligned run of 1024 tokens) the ids never fall; each document (run of equal ids) has 102 to 999 tokens except the last of a sequence, which may be shorter; the ids of sequence i lie in 16 i to 16 i + 15, and its last document has id 16 i + 15.
All inputs are finite; a program needn't handle non-finite values.
Results may differ from the reference program's by a relative error of at most 0.019.
Values may be sent and summed in bfloat16 or wider, within the bound.
A program may use at most 192 MiB of HBM per device.

```python
import jax
import jax.numpy as jnp
from jax import lax

D = 1536
H = 48
P_SIZE = 64
N = 128
K = 4
LEN = 1024
LAYERS = 2
GROUP_ROWS = 1024
TOKENS = 8192


def draw_segment_ids(key, part):
    key = jax.random.fold_in(key, 7)
    sequences = TOKENS // LEN
    shortest = LEN // 10
    longest = LEN - LEN // 40
    lengths = jax.random.randint(key, (sequences, 12), shortest, longest + 1)
    ends = jnp.cumsum(lengths, axis=1)
    place = jnp.arange(LEN)
    local = jnp.sum((place[None, :, None] >= ends[:, None, :]).astype(jnp.int32), axis=2)
    final = local[:, LEN - 1:LEN]
    numbered = jnp.where(local == final, 15, local)
    labels = numbered + 16 * jnp.arange(sequences)[:, None]
    return labels.reshape(-1).astype(jnp.int32)


def block_levels(own_key, shape, split, low, top_value):
    loudness = 1.0
    for position, blocks in split:
        steps = jax.random.uniform(jax.random.fold_in(jax.random.fold_in(own_key, 6), position), (blocks,), jnp.float32, low / len(split), top_value / len(split))
        loudness = loudness * jnp.repeat(jnp.exp(steps), shape[position] // blocks).reshape((-1,) + (1,) * (len(shape) - 1 - position))
    return loudness


def gaussian(own_key, shape, spread, bound, shards=(), kind=jnp.bfloat16):
    factor_of = block_levels(own_key, shape, shards, -0.22, 0.18) if shards else 1.0
    array = jax.random.normal(own_key, shape, jnp.float32) * spread * factor_of
    return jnp.minimum(jnp.maximum(array, -bound), bound).astype(kind)


def setup_inputs(seed: int = 0) -> dict:
    key_list = jax.random.split(jax.random.key(seed), 16)
    resid = gaussian(key_list[0], (TOKENS, D), 1.0, 6.0, ((0, 32),))
    segment_ids = draw_segment_ids(jax.random.fold_in(key_list[15], 71), 0)
    cotangent = gaussian(key_list[2], (TOKENS, D), 1.0, 6.0, ((0, 32),), jnp.float32)
    w_z = gaussian(key_list[3], (LAYERS, D, H * P_SIZE), D ** -0.5, 0.15625, ((1, 8), (2, 4)))
    w_x = gaussian(key_list[4], (LAYERS, D, H * P_SIZE), D ** -0.5, 0.15625, ((1, 8), (2, 4)))
    w_bc = gaussian(key_list[5], (LAYERS, D, 2 * N), D ** -0.5, 0.15625, ((1, 32),))
    w_dt = gaussian(key_list[6], (LAYERS, D, H), D ** -0.5, 0.15625, ((1, 8), (2, 4)))
    w_out = gaussian(key_list[7], (LAYERS, H * P_SIZE, D), (H * P_SIZE) ** -0.5, 0.109375, ((1, 4), (2, 8)))
    norm_gain = jnp.clip(1.0 + 0.1 * jax.random.normal(key_list[8], (LAYERS, D), jnp.float32), 0.5, 1.5)
    conv_x = gaussian(key_list[9], (LAYERS, K, H * P_SIZE), K ** -0.5, 3.0, ((2, 4),), jnp.float32)
    conv_bc = gaussian(key_list[10], (LAYERS, K, 2 * N), K ** -0.5, 3.0, (), jnp.float32)
    a_log = jnp.clip(-4.0 + 5.5 * jax.random.uniform(key_list[11], (LAYERS, H), jnp.float32) ** block_levels(key_list[11], (LAYERS, H), ((1, 4),), -0.2, 0.2), -4.0, 1.5)
    dt_bias = jnp.clip(-4.5 + 2.0 * jax.random.uniform(key_list[12], (LAYERS, H), jnp.float32) ** block_levels(key_list[12], (LAYERS, H), ((1, 4),), -0.2, 0.2), -4.5, -2.5)
    d_skip = jnp.clip(0.5 + 1.0 * jax.random.uniform(key_list[13], (LAYERS, H), jnp.float32) ** block_levels(key_list[13], (LAYERS, H), ((1, 4),), -0.2, 0.2), 0.5, 1.5)
    gated_gain = jnp.clip(1.0 + 0.1 * jax.random.normal(key_list[14], (LAYERS, H * P_SIZE), jnp.float32), 0.5, 1.5)
    return {"resid": resid, "segment_ids": segment_ids, "cotangent": cotangent, "w_z": w_z, "w_x": w_x, "w_bc": w_bc, "w_dt": w_dt, "w_out": w_out, "norm_gain": norm_gain, "conv_x": conv_x, "conv_bc": conv_bc, "a_log": a_log, "dt_bias": dt_bias, "d_skip": d_skip, "gated_gain": gated_gain}


highest = lax.Precision.HIGHEST
epsilon = 1e-05

@jax.custom_vjp
def low(v):
    return lax.optimization_barrier(v.astype(jnp.bfloat16)).astype(jnp.float32)

@jax.custom_vjp
def low_back(v):
    return v

def low_keep(v):
    return (low(v), None)

def low_pass(kept, grad):
    return (grad,)

def back_keep(v):
    return (v, None)

def back_low(kept, grad):
    return (low(grad),)
low.defvjp(low_keep, low_pass)
low_back.defvjp(back_keep, back_low)

def product(left, right):
    return jnp.dot(left, right, precision=highest)

def document_filter(values, kernel, labels):
    width = kernel.shape[0]
    length = values.shape[0]
    total = kernel[width - 1] * values
    for steps in range(1, width):
        moved = jnp.pad(values, ((steps, 0), (0, 0)))[:length]
        earlier = jnp.pad(labels, (steps, 0), constant_values=-1)[:length]
        keep_rows = (earlier == labels).astype(values.dtype)
        total = total + kernel[width - 1 - steps] * moved * keep_rows[:, None]
    return total

def mix_heads(inner_low, keys_low, query_low, step_size, rate, labels):
    rows = inner_low.shape[0]
    sequences = rows // LEN
    heads = step_size.shape[1]
    coupling = jnp.einsum('sqn,skn->sqk', query_low.reshape(sequences, LEN, N), keys_low.reshape(sequences, LEN, N), precision=highest)
    grouped = labels.reshape(sequences, LEN)
    place = jnp.arange(LEN)
    visible = (grouped[:, :, None] == grouped[:, None, :]) & (place[:, None] >= place[None, :])[None]
    cumulative = jnp.cumsum((step_size * rate).reshape(sequences, LEN, heads), axis=1)

    def one_head(item):
        decay_one, step_one, inner_one = item
        shared = low_back(coupling)
        gap = jnp.where(visible, decay_one[:, :, None] - decay_one[:, None, :], 0.0)
        decay = jnp.where(visible, jnp.exp(gap), 0.0)
        weights = low(shared * decay * step_one[:, None, :])
        return jnp.einsum('sqk,skp->sqp', weights, inner_one, precision=highest)
    items = (jnp.moveaxis(cumulative, 2, 0), jnp.moveaxis(step_size.reshape(sequences, LEN, heads), 2, 0), jnp.moveaxis(inner_low.reshape(sequences, LEN, heads, P_SIZE), 2, 0))
    mixed = lax.map(jax.checkpoint(one_head), items)
    return jnp.moveaxis(mixed, 0, 2).reshape(rows, heads * P_SIZE)

def block(params, state, labels, layer):
    w_z, w_x, w_bc, w_dt, w_out, norm_gain, conv_x, conv_bc, a_log, dt_bias, d_skip, gated_gain = params
    scale_in = lax.rsqrt(lax.optimization_barrier(jnp.mean(state * state, axis=1, keepdims=True)) + epsilon)
    normed = low(state * scale_in * norm_gain[layer])
    gate_raw = low_back(product(normed, w_z[layer]))
    inner_raw = low_back(product(normed, w_x[layer]))
    step_raw = low_back(product(normed, w_dt[layer]))
    shared_raw = product(normed, w_bc[layer])
    inner_act = jax.nn.silu(document_filter(inner_raw, conv_x[layer], labels))
    shared_act = jax.nn.silu(document_filter(shared_raw, conv_bc[layer], labels))
    step_size = jax.nn.softplus(step_raw + dt_bias[layer])
    rate = -jnp.exp(a_log[layer])
    mixed = mix_heads(low(inner_act), low(shared_act[:, :N]), low(shared_act[:, N:]), step_size, rate, labels)
    output_full = low_back(mixed + inner_act * jnp.repeat(d_skip[layer], P_SIZE))
    gated = output_full * jax.nn.silu(gate_raw)
    scale_out = lax.rsqrt(lax.optimization_barrier(jnp.mean(gated * gated, axis=1, keepdims=True)) + epsilon)
    out_low = low(gated * scale_out * gated_gain[layer])
    return state + low_back(product(out_low, w_out[layer]))

def forward(params, state, labels):
    for layer in range(LAYERS):
        state = block(params, state, labels, layer)
    return state

def reference(resid, segment_ids, cotangent, w_z, w_x, w_bc, w_dt, w_out, norm_gain, conv_x, conv_bc, a_log, dt_bias, d_skip, gated_gain):
    params = tuple((value.astype(jnp.float32) for value in (w_z, w_x, w_bc, w_dt, w_out, norm_gain, conv_x, conv_bc, a_log, dt_bias, d_skip, gated_gain)))
    groups = TOKENS // GROUP_ROWS
    states = resid.astype(jnp.float32).reshape(groups, GROUP_ROWS, D)
    labels_all = segment_ids.reshape(groups, GROUP_ROWS)
    cotangents = cotangent.astype(jnp.float32).reshape(groups, GROUP_ROWS, D)

    def one_group(totals, item):
        state, labels, grad_top = item
        result, pull = jax.vjp(lambda weights, start: forward(weights, start, labels), params, state)
        grad_params, grad_state = pull(grad_top)
        return (tuple((left + right for left, right in zip(totals, grad_params))), (result, grad_state))
    zeros = tuple((jnp.zeros_like(value) for value in params))
    totals, (results, grad_states) = lax.scan(one_group, zeros, (states, labels_all, cotangents))
    return (results.reshape(TOKENS, D), grad_states.reshape(TOKENS, D), totals[0], totals[1], totals[2], totals[3], totals[4], totals[5], totals[6], totals[7], totals[8], totals[9], totals[10], totals[11])
```

```python
import functools

import jax
import jax.numpy as jnp
from jax import lax
from jax.experimental import pallas as pl
from jax.experimental.pallas import tpu as pltpu
from jax.sharding import PartitionSpec as P

P_SIZE = 64
N = 128
LEN = 1024
CHUNK = 256
LANES = 128
TAPS = 4

highest = lax.Precision.HIGHEST
epsilon = 1e-05
F32 = jnp.float32
BF16 = jnp.bfloat16


def mm(left, right):
    return jnp.dot(left, right, preferred_element_type=F32)


def mm_nt(left, right):
    return lax.dot_general(left, right, (((1,), (1,)), ((), ())), preferred_element_type=F32)


def sigmoid(values):
    return 1.0 / (1.0 + jnp.exp(-values))


def softplus(values):
    return jnp.maximum(values, 0.0) + jnp.log1p(jnp.exp(-jnp.abs(values)))


def iota2(shape, dim):
    return lax.broadcasted_iota(jnp.int32, shape, dim)


def pair_of(columns, head):
    shape = (columns.shape[0], LANES)
    first = jnp.broadcast_to(columns[:, head : head + 1], shape)
    second = jnp.broadcast_to(columns[:, head + 1 : head + 2], shape)
    return jnp.where(iota2(shape, 1) < P_SIZE, first, second)


def head_sums(values, spread):
    high = values.astype(BF16)
    low = (values - high.astype(F32)).astype(BF16)
    return mm(high, spread) + mm(low, spread)


def decays(step_pre, rate, aux):
    step = softplus(step_pre)
    order = (iota2((CHUNK, CHUNK), 0) >= iota2((CHUNK, CHUNK), 1)).astype(F32)
    cum = jnp.dot(order, step * rate, precision=highest, preferred_element_type=F32)
    last = cum[CHUNK - 1 : CHUNK, :]
    decay_in = jnp.exp(cum) * aux[:, 4:5]
    decay_out = jnp.exp(last - cum) * aux[:, 5:6]
    decay_pass = jnp.exp(last) * aux[0:1, 6:7]
    return step, cum, decay_in, decay_out, decay_pass


def forward_kernel(
    rows_ref,
    wz_ref,
    wx_ref,
    wbc_ref,
    wdt_ref,
    wout_ref,
    convx_ref,
    convbc_ref,
    heads_ref,
    wide_ref,
    aux_ref,
    segrow_ref,
    part_ref,
    sq_ref,
    gate_ref,
    iraw_ref,
    iconv_ref,
    sraw_ref,
    sconv_ref,
    step_ref,
    mixed_ref,
    sin_ref,
    ext_x,
    ext_bc,
    state,
    gg_ref,
):
    inner = wx_ref.shape[1]

    @pl.when(pl.program_id(0) == 0)
    def _():
        state[...] = jnp.zeros_like(state)
        ext_x[0:8, :] = jnp.zeros((8, inner), F32)
        ext_bc[0:8, :] = jnp.zeros((8, 2 * N), F32)

    rows = rows_ref[...]
    aux = aux_ref[...]
    rate = heads_ref[1:2, :]
    shared = mm(rows, wbc_ref[...])
    sraw_ref[...] = shared
    ext_bc[8 : 8 + CHUNK, :] = shared
    shared_conv = convbc_ref[TAPS - 1 : TAPS, :] * shared
    for j in range(1, TAPS):
        shared_conv = shared_conv + convbc_ref[TAPS - 1 - j : TAPS - j, :] * (
            ext_bc[8 - j : 8 - j + CHUNK, :] * aux[:, j : j + 1]
        )
    sconv_ref[...] = shared_conv
    ext_bc[0:8, :] = ext_bc[CHUNK : CHUNK + 8, :]
    shared_act = shared_conv * sigmoid(shared_conv)
    keys = shared_act[:, :N].astype(BF16)
    keys_t = jnp.transpose(shared_act[:, :N]).astype(BF16)
    query = shared_act[:, N:].astype(BF16)
    visible = (aux[:, 15:16] == segrow_ref[0:1, :]) & (
        iota2((CHUNK, CHUNK), 0) >= iota2((CHUNK, CHUNK), 1)
    )
    coupling = jnp.where(visible, mm_nt(query, keys), 0.0)
    step_raw = mm(rows, wdt_ref[...])
    step_ref[...] = step_raw
    step, cum, decay_in, decay_out, decay_pass = decays(
        step_raw + heads_ref[0:1, :], rate, aux
    )
    cum_t = jnp.transpose(cum)
    ext_x[8 : 8 + CHUNK, :] = mm(rows, wx_ref[...])
    gate_ref[...] = mm(rows, wz_ref[...])
    squares = jnp.zeros((CHUNK, LANES), F32)
    half = iota2((CHUNK, LANES), 1) < P_SIZE
    for pair in range(inner // LANES):
        cols = slice(pair * LANES, (pair + 1) * LANES)
        head = 2 * pair
        raw = ext_x[8 : 8 + CHUNK, cols]
        iraw_ref[:, cols] = raw
        conv = convx_ref[TAPS - 1 : TAPS, cols] * raw
        for j in range(1, TAPS):
            conv = conv + convx_ref[TAPS - 1 - j : TAPS - j, cols] * (
                ext_x[8 - j : 8 - j + CHUNK, cols] * aux[:, j : j + 1]
            )
        iconv_ref[:, cols] = conv
        ext_x[0:8, cols] = ext_x[CHUNK : CHUNK + 8, cols]
        act = conv * sigmoid(conv)
        scaled = (act * pair_of(step, head)).astype(BF16)
        parts = []
        for one in (head, head + 1):
            gap = cum[:, one : one + 1] - cum_t[one : one + 1, :]
            weights = (coupling * jnp.exp(jnp.minimum(gap, 0.0))).astype(BF16)
            parts.append(mm(weights, scaled))
        before = state[:, cols]
        sin_ref[0, :, cols] = before
        mixed = jnp.where(half, parts[0], parts[1])
        mixed = mixed + pair_of(decay_in, head) * mm(query, before.astype(BF16))
        mixed_ref[:, cols] = mixed
        leaving = (scaled.astype(F32) * pair_of(decay_out, head)).astype(BF16)
        state[:, cols] = pair_of(decay_pass, head) * before + mm(keys_t, leaving)
        gate = gate_ref[:, cols]
        gated = (mixed + wide_ref[0:1, cols] * act) * (gate * sigmoid(gate))
        squares = squares + gated * gated
        gg_ref[:, cols] = (gated * wide_ref[1:2, cols]).astype(BF16)
    total = jnp.sum(squares, axis=1, keepdims=True)
    sq_ref[...] = jnp.transpose(jnp.broadcast_to(total, (CHUNK, LANES)))[0:8, :]
    part_ref[...] = mm_nt(gg_ref[...], wout_ref[...]).astype(BF16)


def backward_kernel(
    top_ref,
    sc_ref,
    gate_ref,
    iraw_ref,
    iconv_ref,
    sraw_ref,
    sconv_ref,
    step_ref,
    mixed_ref,
    sin_ref,
    sout_ref,
    wz_ref,
    wx_ref,
    wbc_ref,
    wdt_ref,
    wout_ref,
    convx_ref,
    convbc_ref,
    heads_ref,
    wide_ref,
    spread_ref,
    aux_ref,
    segrow_ref,
    part_ref,
    ggate_ref,
    ginner_ref,
    gstep_ref,
    gshared_ref,
    outlow_ref,
    small_ref,
    smallbc_ref,
    gext_x,
    gext_bc,
    dstate,
    gno_ref,
    balance,
    direct,
    edge,
    dcoup,
):
    inner = wx_ref.shape[1]

    @pl.when(pl.program_id(0) == 0)
    def _():
        dstate[...] = jnp.zeros_like(dstate)
        gext_x[CHUNK : CHUNK + 8, :] = jnp.zeros((8, inner), F32)
        gext_bc[CHUNK : CHUNK + 8, :] = jnp.zeros((8, 2 * N), F32)
        small_ref[...] = jnp.zeros_like(small_ref)
        smallbc_ref[...] = jnp.zeros_like(smallbc_ref)
        edge[...] = jnp.zeros_like(edge)

    aux = aux_ref[...]
    rate = heads_ref[1:2, :]
    gno_ref[...] = mm(top_ref[...], wout_ref[...])
    per_row = jnp.transpose(sc_ref[...])
    scale = per_row[:, 0:1]
    coef = per_row[:, 1:2]
    step_pre = step_ref[...] + heads_ref[0:1, :]
    step, cum, decay_in, decay_out, decay_pass = decays(step_pre, rate, aux)
    cum_t = jnp.transpose(cum)
    shared_conv = sconv_ref[...]
    shared_sig = sigmoid(shared_conv)
    shared_act = shared_conv * shared_sig
    keys = shared_act[:, :N].astype(BF16)
    query = shared_act[:, N:].astype(BF16)
    query_t = jnp.transpose(shared_act[:, N:]).astype(BF16)
    visible = (aux[:, 15:16] == segrow_ref[0:1, :]) & (
        iota2((CHUNK, CHUNK), 0) <= iota2((CHUNK, CHUNK), 1)
    )
    coupling = jnp.where(visible, mm_nt(keys, query), 0.0)
    half = iota2((CHUNK, LANES), 1) < P_SIZE
    dcoup[...] = jnp.zeros_like(dcoup)
    dkeys = jnp.zeros((CHUNK, N), F32)
    dquery = jnp.zeros((CHUNK, N), F32)
    for pair in range(inner // LANES):
        cols = slice(pair * LANES, (pair + 1) * LANES)
        head = 2 * pair
        skip = wide_ref[0:1, cols]
        gain = wide_ref[1:2, cols]
        conv = iconv_ref[:, cols]
        conv_sig = sigmoid(conv)
        act = conv * conv_sig
        step_pair = pair_of(step, head)
        scaled = (act * step_pair).astype(BF16)
        gate = gate_ref[:, cols]
        gate_sig = sigmoid(gate)
        gate_act = gate * gate_sig
        mixed = mixed_ref[:, cols]
        full = mixed + skip * act
        gated = full * gate_act
        gno = gno_ref[:, cols]
        gated_scaled = gated * scale
        small_ref[4:5, cols] += jnp.sum(gno * gated_scaled, axis=0, keepdims=True)
        outlow_ref[:, cols] = (gated_scaled * gain).astype(BF16)
        ggated = scale * (gno * gain) - gated * coef
        gout_low = (ggated * gate_act).astype(BF16)
        ggate_ref[:, cols] = (
            ggated * full * (gate_sig * (1.0 + gate * (1.0 - gate_sig)))
        ).astype(BF16)
        gout = gout_low.astype(F32)
        small_ref[5:6, cols] += jnp.sum(gout * act, axis=0, keepdims=True)
        zero = jnp.zeros_like(gout)
        parts = []
        for one, own in (
            (head, jnp.where(half, gout, zero).astype(BF16)),
            (head + 1, jnp.where(half, zero, gout).astype(BF16)),
        ):
            gap = cum_t[one : one + 1, :] - cum[:, one : one + 1]
            decay = jnp.exp(jnp.minimum(gap, 0.0))
            weights = (coupling * decay).astype(BF16)
            parts.append(mm(weights, gout_low))
            dcoup[...] += mm_nt(scaled, own) * decay
        after = dstate[:, cols]
        after_low = after.astype(BF16)
        out_pair = pair_of(decay_out, head)
        gscaled = jnp.where(half, parts[0], parts[1]) + out_pair * mm(keys, after_low)
        scaled_wide = scaled.astype(F32)
        dkeys = dkeys + mm_nt((scaled_wide * out_pair).astype(BF16), after_low)
        entering = (gout * pair_of(decay_in, head)).astype(BF16)
        dquery = dquery + mm_nt(entering, sin_ref[0, :, cols].astype(BF16))
        edge[0:1, cols] = jnp.sum(sout_ref[0, :, cols] * after, axis=0, keepdims=True)
        dstate[:, cols] = pair_of(decay_pass, head) * after + mm(query_t, entering)
        balance[:, cols] = gout * mixed - scaled_wide * gscaled
        direct[:, cols] = act * gscaled
        gact = step_pair * gscaled + skip * gout
        gext_x[0:CHUNK, cols] = gact * (conv_sig * (1.0 + conv * (1.0 - conv_sig)))
        raw = iraw_ref[:, cols]
        gconv = gext_x[0:CHUNK, cols]
        graw = convx_ref[TAPS - 1 : TAPS, cols] * gconv
        small_ref[TAPS - 1 : TAPS, cols] += jnp.sum(raw * gconv, axis=0, keepdims=True)
        for j in range(1, TAPS):
            moved = gext_x[j : j + CHUNK, cols] * aux[:, 8 + j : 9 + j]
            graw = graw + convx_ref[TAPS - 1 - j : TAPS - j, cols] * moved
            small_ref[TAPS - 1 - j : TAPS - j, cols] += jnp.sum(
                raw * moved, axis=0, keepdims=True
            )
        ginner_ref[:, cols] = graw.astype(BF16)
        gext_x[CHUNK : CHUNK + 8, cols] = gext_x[0:8, cols]
    spread = spread_ref[...]
    order = (iota2((CHUNK, CHUNK), 0) <= iota2((CHUNK, CHUNK), 1)).astype(F32)
    running = jnp.dot(
        order, head_sums(balance[...], spread), precision=highest, preferred_element_type=F32
    )
    running = running + head_sums(edge[...], spread)[0:1, :]
    gstep = (head_sums(direct[...], spread) + running * rate) * sigmoid(step_pre)
    small_ref[6:7, 0:LANES] += rate * jnp.sum(running * step, axis=0, keepdims=True)
    small_ref[7:8, 0:LANES] += jnp.sum(gstep, axis=0, keepdims=True)
    gstep_ref[...] = gstep.astype(BF16)
    dcoupling = jnp.where(visible, dcoup[...], 0.0)
    dkeys = dkeys + mm(dcoupling.astype(BF16), query)
    dquery = dquery + mm(jnp.transpose(dcoupling).astype(BF16), keys)
    slope = shared_sig * (1.0 + shared_conv * (1.0 - shared_sig))
    gext_bc[0:CHUNK, 0:N] = dkeys * slope[:, :N]
    gext_bc[0:CHUNK, N : 2 * N] = dquery * slope[:, N:]
    raw = sraw_ref[...]
    gconv = gext_bc[0:CHUNK, :]
    graw = convbc_ref[TAPS - 1 : TAPS, :] * gconv
    smallbc_ref[TAPS - 1 : TAPS, :] += jnp.sum(raw * gconv, axis=0, keepdims=True)
    for j in range(1, TAPS):
        moved = gext_bc[j : j + CHUNK, :] * aux[:, 8 + j : 9 + j]
        graw = graw + convbc_ref[TAPS - 1 - j : TAPS - j, :] * moved
        smallbc_ref[TAPS - 1 - j : TAPS - j, :] += jnp.sum(raw * moved, axis=0, keepdims=True)
    gshared_ref[...] = graw.astype(BF16)
    gext_bc[CHUNK : CHUNK + 8, :] = gext_bc[0:8, :]
    total = mm_nt(ggate_ref[...], wz_ref[...]) + mm_nt(ginner_ref[...], wx_ref[...])
    total = total + mm_nt(gstep_ref[...], wdt_ref[...])
    part_ref[...] = (total + mm_nt(gshared_ref[...], wbc_ref[...])).astype(BF16)


def whole_spec(shape):
    zeros = (0,) * len(shape)
    return pl.BlockSpec(shape, lambda i: zeros, pipeline_mode=pl.Buffered(1))


VMEM_LIMIT = 60 * 1024 * 1024


def forward_layer(rows_all, weights, layer_args, aux, segrow):
    length, width = rows_all.shape
    chunks = length // CHUNK
    inner = weights[1].shape[1]
    by_rows = lambda cols: pl.BlockSpec((CHUNK, cols), lambda i: (i, 0))
    by_lanes = pl.BlockSpec((8, CHUNK), lambda i: (0, i))
    shape = jax.ShapeDtypeStruct
    return pl.pallas_call(
        forward_kernel,
        grid=(chunks,),
        in_specs=[by_rows(width)]
        + [whole_spec(w.shape) for w in weights]
        + [whole_spec(w.shape) for w in layer_args]
        + [by_rows(LANES), by_lanes],
        out_specs=[
            by_rows(width),
            by_lanes,
            by_rows(inner),
            by_rows(inner),
            by_rows(inner),
            by_rows(2 * N),
            by_rows(2 * N),
            by_rows(LANES),
            by_rows(inner),
            pl.BlockSpec((1, N, inner), lambda i: (i, 0, 0)),
        ],
        out_shape=[
            shape((length, width), BF16),
            shape((8, length), F32),
            shape((length, inner), F32),
            shape((length, inner), F32),
            shape((length, inner), F32),
            shape((length, 2 * N), F32),
            shape((length, 2 * N), F32),
            shape((length, LANES), F32),
            shape((length, inner), F32),
            shape((chunks, N, inner), F32),
        ],
        scratch_shapes=[
            pltpu.VMEM((CHUNK + 8, inner), F32),
            pltpu.VMEM((CHUNK + 8, 2 * N), F32),
            pltpu.VMEM((N, inner), F32),
            pltpu.VMEM((CHUNK, inner), BF16),
        ],
        compiler_params=pltpu.CompilerParams(
            dimension_semantics=("arbitrary",), vmem_limit_bytes=VMEM_LIMIT
        ),
        cost_estimate=pl.CostEstimate(
            flops=length * width * inner * 7, bytes_accessed=40_000_000, transcendentals=8_000_000
        ),
    )(rows_all, *weights, *layer_args, aux, segrow)


def backward_layer(top_all, per_row, saved, weights, layer_args, spread, aux, segrow):
    length, width = top_all.shape
    chunks = length // CHUNK
    inner = weights[1].shape[1]
    last = chunks - 1
    by_rows = lambda cols: pl.BlockSpec((CHUNK, cols), lambda i: (last - i, 0))
    by_lanes = pl.BlockSpec((8, CHUNK), lambda i: (0, last - i))
    shape = jax.ShapeDtypeStruct
    gate, iraw, iconv, sraw, sconv, step, mixed, sin = saved
    return pl.pallas_call(
        backward_kernel,
        grid=(chunks,),
        in_specs=[
            by_rows(width),
            by_lanes,
            by_rows(inner),
            by_rows(inner),
            by_rows(inner),
            by_rows(2 * N),
            by_rows(2 * N),
            by_rows(LANES),
            by_rows(inner),
            pl.BlockSpec((1, N, inner), lambda i: (last - i, 0, 0)),
            pl.BlockSpec((1, N, inner), lambda i: (jnp.minimum(chunks - i, last), 0, 0)),
        ]
        + [whole_spec(w.shape) for w in weights]
        + [whole_spec(w.shape) for w in layer_args]
        + [whole_spec(spread.shape), by_rows(LANES), by_lanes],
        out_specs=[
            by_rows(width),
            by_rows(inner),
            by_rows(inner),
            by_rows(LANES),
            by_rows(2 * N),
            by_rows(inner),
            pl.BlockSpec((8, inner), lambda i: (0, 0)),
            pl.BlockSpec((8, 2 * N), lambda i: (0, 0)),
        ],
        out_shape=[
            shape((length, width), BF16),
            shape((length, inner), BF16),
            shape((length, inner), BF16),
            shape((length, LANES), BF16),
            shape((length, 2 * N), BF16),
            shape((length, inner), BF16),
            shape((8, inner), F32),
            shape((8, 2 * N), F32),
        ],
        scratch_shapes=[
            pltpu.VMEM((CHUNK + 8, inner), F32),
            pltpu.VMEM((CHUNK + 8, 2 * N), F32),
            pltpu.VMEM((N, inner), F32),
            pltpu.VMEM((CHUNK, inner), F32),
            pltpu.VMEM((CHUNK, inner), F32),
            pltpu.VMEM((CHUNK, inner), F32),
            pltpu.VMEM((8, inner), F32),
            pltpu.VMEM((CHUNK, CHUNK), F32),
        ],
        compiler_params=pltpu.CompilerParams(
            dimension_semantics=("arbitrary",), vmem_limit_bytes=VMEM_LIMIT
        ),
        cost_estimate=pl.CostEstimate(
            flops=length * width * inner * 7, bytes_accessed=40_000_000, transcendentals=8_000_000
        ),
    )(
        top_all,
        per_row,
        gate,
        iraw,
        iconv,
        sraw,
        sconv,
        step,
        mixed,
        sin,
        sin,
        *weights,
        *layer_args,
        spread,
        aux,
        segrow,
    )


def row_masks(segment_ids):
    length = segment_ids.shape[0]
    seg = segment_ids.astype(F32)

    def shifted(j):
        return jnp.concatenate([jnp.full((j,), -1.0, F32), seg[: length - j]])

    def ahead(j):
        return jnp.concatenate([seg[j:], jnp.full((j,), -1.0, F32)])

    ends = seg[CHUNK - 1 :: CHUNK]
    own_end = jnp.repeat(ends, CHUNK)
    old_end = jnp.repeat(jnp.concatenate([jnp.full((1,), -1.0, F32), ends[:-1]]), CHUNK)
    lanes = [jnp.zeros_like(seg)] * 16
    for j in range(1, TAPS):
        lanes[j] = (shifted(j) == seg).astype(F32)
        lanes[8 + j] = (ahead(j) == seg).astype(F32)
    lanes[4] = (old_end == seg).astype(F32)
    lanes[5] = (own_end == seg).astype(F32)
    lanes[6] = (own_end == old_end).astype(F32)
    lanes[15] = seg
    aux = jnp.pad(jnp.stack(lanes, axis=1), ((0, 0), (0, LANES - 16)))
    return aux, jnp.broadcast_to(seg[None, :], (8, length))


def layer_parameters(layer, conv_x, conv_bc, a_log, dt_bias, d_skip, gated_gain):
    heads = a_log.shape[1]
    pad = ((0, 0), (0, LANES - heads))
    head_rows = jnp.pad(jnp.stack([dt_bias[layer], -jnp.exp(a_log[layer])]), pad)
    wide = jnp.stack([jnp.repeat(d_skip[layer], P_SIZE), gated_gain[layer]])
    return (conv_x[layer], conv_bc[layer], head_rows, wide)


def head_spread(inner):
    return (
        jnp.arange(inner)[:, None] // P_SIZE == jnp.arange(LANES)[None, :]
    ).astype(BF16)


def on_device(
    resid,
    segment_ids,
    cotangent,
    w_z,
    w_x,
    w_bc,
    w_dt,
    w_out,
    norm_gain,
    conv_x,
    conv_bc,
    a_log,
    dt_bias,
    d_skip,
    gated_gain,
):
    tensor_size = lax.axis_size("tensor")
    heads = a_log.shape[1]
    inner = heads * P_SIZE
    inner_all = inner * tensor_size
    layers = a_log.shape[0]
    aux, segrow = row_masks(segment_ids)
    spread = head_spread(inner)
    args = [
        layer_parameters(layer, conv_x, conv_bc, a_log, dt_bias, d_skip, gated_gain)
        for layer in range(layers)
    ]
    weights = []
    for layer in range(layers):
        weights.append(
            (
                lax.all_gather(w_z[layer], "dp", axis=0, tiled=True),
                lax.all_gather(w_x[layer], "dp", axis=0, tiled=True),
                lax.all_gather(w_bc[layer], ("dp", "tensor"), axis=0, tiled=True),
                lax.all_gather(
                    jnp.pad(w_dt[layer], ((0, 0), (0, LANES - heads))), "dp", axis=0, tiled=True
                ),
                lax.all_gather(jnp.transpose(w_out[layer]), "dp", axis=0, tiled=True),
            )
        )
    state = resid.astype(F32)
    states, kept, scales, branches, rows_list = [], [], [], [], []
    for layer in range(layers):
        scale_in = lax.rsqrt(jnp.mean(state * state, axis=1, keepdims=True) + epsilon)
        normed = (state * scale_in * norm_gain[layer]).astype(BF16)
        rows_all = lax.all_gather(normed, "tensor", axis=0, tiled=True)
        part, sq, *saved = forward_layer(rows_all, weights[layer], args[layer], aux, segrow)
        squares = lax.psum_scatter(sq[0], "tensor", scatter_dimension=0, tiled=True)
        scale_out = lax.rsqrt(squares / inner_all + epsilon)
        raw = lax.psum_scatter(part, "tensor", scatter_dimension=0, tiled=True).astype(F32)
        states.append((state, scale_in))
        kept.append(saved)
        rows_list.append(rows_all)
        scales.append(scale_out)
        branches.append(raw)
        state = state + raw * scale_out[:, None]
    grad_state = cotangent
    grads = [None] * layers
    for layer in reversed(range(layers)):
        low = grad_state.astype(BF16)
        cross = jnp.sum(low.astype(F32) * branches[layer], axis=1)
        coef = scales[layer] ** 3 * cross / inner_all
        per_row = jnp.pad(jnp.stack([scales[layer], coef]), ((0, 6), (0, 0)))
        per_row = lax.all_gather(per_row, "tensor", axis=1, tiled=True)
        top_all = lax.all_gather(low, "tensor", axis=0, tiled=True)
        part, ggate, ginner, gstep, gshared, outlow, small, small_bc = backward_layer(
            top_all, per_row, kept[layer], weights[layer], args[layer], spread, aux, segrow
        )

        def contract(left, right):
            return lax.dot_general(
                left, right, (((0,), (0,)), ((), ())), preferred_element_type=F32
            ).astype(BF16)

        def scatter(values, axes="dp"):
            return lax.psum_scatter(values, axes, scatter_dimension=0, tiled=True).astype(F32)

        rows_all = rows_list[layer]
        gz = scatter(contract(rows_all, ggate))
        gx = scatter(contract(rows_all, ginner))
        gdt = scatter(contract(rows_all, gstep))[:, :heads]
        gbc = scatter(contract(rows_all, gshared), ("dp", "tensor"))
        gout = jnp.transpose(scatter(contract(top_all, outlow)))
        grad_normed = lax.psum_scatter(
            part, "tensor", scatter_dimension=0, tiled=True
        ).astype(F32)
        state_in, scale_in = states[layer]
        gained = grad_normed * norm_gain[layer]
        gnorm = jnp.sum(grad_normed * state_in * scale_in, axis=0)
        grad_state = (
            grad_state
            + scale_in * gained
            - state_in * scale_in**3 * jnp.mean(gained * state_in, axis=1, keepdims=True)
        )
        grads[layer] = (gz, gx, gbc, gdt, gout, gnorm, small, small_bc)
    stacked = [jnp.stack(values) for values in zip(*grads)]
    small = lax.psum(stacked[6], "dp")
    gnorm, small_bc = lax.psum((stacked[5], stacked[7]), ("dp", "tensor"))
    return (
        state,
        grad_state,
        stacked[0],
        stacked[1],
        stacked[2],
        stacked[3],
        stacked[4],
        gnorm,
        small[:, :TAPS],
        small_bc[:, :TAPS],
        small[:, 6, :heads],
        small[:, 7, :heads],
        jnp.sum(small[:, 5].reshape(layers, heads, P_SIZE), axis=2),
        small[:, 4],
    )


def solution(mesh):
    rows = P(("dp", "tensor"), None)
    matrix = P(None, "dp", "tensor")
    shared = P(None, ("dp", "tensor"), None)
    wide = P(None, None, "tensor")
    head = P(None, "tensor")
    out = P(None, "tensor", "dp")
    return jax.shard_map(
        on_device,
        mesh=mesh,
        in_specs=(
            rows, P("dp"), rows, matrix, matrix, shared, matrix, out, P(), wide, P(), head, head, head, head,
        ),
        out_specs=(
            rows, rows, matrix, matrix, shared, matrix, out, P(), wide, P(), head, head, head, head,
        ),
        check_vma=False,
    )
```

```python
import functools

import jax
import jax.numpy as jnp
from jax import lax
from jax.experimental import pallas as pl
from jax.experimental.pallas import tpu as pltpu
from jax.sharding import PartitionSpec as P

P_SIZE = 64
N = 128
LEN = 1024
CHUNK = 256
LANES = 128
TAPS = 4

highest = lax.Precision.HIGHEST
epsilon = 1e-05
F32 = jnp.float32
BF16 = jnp.bfloat16


def mm(left, right):
    return jnp.dot(left, right, preferred_element_type=F32)


def mm_nt(left, right):
    return lax.dot_general(left, right, (((1,), (1,)), ((), ())), preferred_element_type=F32)


def sigmoid(values):
    return 1.0 / (1.0 + jnp.exp(-values))


def softplus(values):
    return jnp.maximum(values, 0.0) + jnp.log1p(jnp.exp(-jnp.abs(values)))


def iota2(shape, dim):
    return lax.broadcasted_iota(jnp.int32, shape, dim)


def pair_of(columns, head):
    shape = (columns.shape[0], LANES)
    first = jnp.broadcast_to(columns[:, head : head + 1], shape)
    second = jnp.broadcast_to(columns[:, head + 1 : head + 2], shape)
    return jnp.where(iota2(shape, 1) < P_SIZE, first, second)


def head_sums(values, spread):
    high = values.astype(BF16)
    low = (values - high.astype(F32)).astype(BF16)
    return mm(high, spread) + mm(low, spread)


def decays(step_pre, rate, aux):
    step = softplus(step_pre)
    order = (iota2((CHUNK, CHUNK), 0) >= iota2((CHUNK, CHUNK), 1)).astype(F32)
    cum = jnp.dot(order, step * rate, precision=highest, preferred_element_type=F32)
    last = cum[CHUNK - 1 : CHUNK, :]
    decay_in = jnp.exp(cum) * aux[:, 4:5]
    decay_out = jnp.exp(last - cum) * aux[:, 5:6]
    decay_pass = jnp.exp(last) * aux[0:1, 6:7]
    return step, cum, decay_in, decay_out, decay_pass


def forward_kernel(
    rows_ref,
    wz_ref,
    wx_ref,
    wbc_ref,
    wdt_ref,
    wout_ref,
    convx_ref,
    convbc_ref,
    heads_ref,
    wide_ref,
    aux_ref,
    segrow_ref,
    part_ref,
    sq_ref,
    gate_ref,
    iraw_ref,
    iconv_ref,
    sraw_ref,
    sconv_ref,
    step_ref,
    mixed_ref,
    sin_ref,
    ext_x,
    ext_bc,
    state,
    gg_ref,
):
    inner = wx_ref.shape[1]

    @pl.when(pl.program_id(0) == 0)
    def _():
        state[...] = jnp.zeros_like(state)
        ext_x[0:8, :] = jnp.zeros((8, inner), F32)
        ext_bc[0:8, :] = jnp.zeros((8, 2 * N), F32)

    rows = rows_ref[...]
    aux = aux_ref[...]
    rate = heads_ref[1:2, :]
    shared = mm(rows, wbc_ref[...])
    sraw_ref[...] = shared
    ext_bc[8 : 8 + CHUNK, :] = shared
    shared_conv = convbc_ref[TAPS - 1 : TAPS, :] * shared
    for j in range(1, TAPS):
        shared_conv = shared_conv + convbc_ref[TAPS - 1 - j : TAPS - j, :] * (
            ext_bc[8 - j : 8 - j + CHUNK, :] * aux[:, j : j + 1]
        )
    sconv_ref[...] = shared_conv
    ext_bc[0:8, :] = ext_bc[CHUNK : CHUNK + 8, :]
    shared_act = shared_conv * sigmoid(shared_conv)
    keys = shared_act[:, :N].astype(BF16)
    keys_t = jnp.transpose(shared_act[:, :N]).astype(BF16)
    query = shared_act[:, N:].astype(BF16)
    visible = (aux[:, 15:16] == segrow_ref[0:1, :]) & (
        iota2((CHUNK, CHUNK), 0) >= iota2((CHUNK, CHUNK), 1)
    )
    coupling = jnp.where(visible, mm_nt(query, keys), 0.0)
    step_raw = mm(rows, wdt_ref[...])
    step_ref[...] = step_raw
    step, cum, decay_in, decay_out, decay_pass = decays(
        step_raw + heads_ref[0:1, :], rate, aux
    )
    cum_t = jnp.transpose(cum)
    ext_x[8 : 8 + CHUNK, :] = mm(rows, wx_ref[...])
    gate_ref[...] = mm(rows, wz_ref[...])
    squares = jnp.zeros((CHUNK, LANES), F32)
    half = iota2((CHUNK, LANES), 1) < P_SIZE
    for pair in range(inner // LANES):
        cols = slice(pair * LANES, (pair + 1) * LANES)
        head = 2 * pair
        raw = ext_x[8 : 8 + CHUNK, cols]
        iraw_ref[:, cols] = raw
        conv = convx_ref[TAPS - 1 : TAPS, cols] * raw
        for j in range(1, TAPS):
            conv = conv + convx_ref[TAPS - 1 - j : TAPS - j, cols] * (
                ext_x[8 - j : 8 - j + CHUNK, cols] * aux[:, j : j + 1]
            )
        iconv_ref[:, cols] = conv
        ext_x[0:8, cols] = ext_x[CHUNK : CHUNK + 8, cols]
        act = conv * sigmoid(conv)
        scaled = (act * pair_of(step, head)).astype(BF16)
        parts = []
        for one in (head, head + 1):
            gap = cum[:, one : one + 1] - cum_t[one : one + 1, :]
            weights = (coupling * jnp.exp(jnp.minimum(gap, 0.0))).astype(BF16)
            parts.append(mm(weights, scaled))
        before = state[:, cols]
        sin_ref[0, :, cols] = before
        mixed = jnp.where(half, parts[0], parts[1])
        mixed = mixed + pair_of(decay_in, head) * mm(query, before.astype(BF16))
        mixed_ref[:, cols] = mixed
        leaving = (scaled.astype(F32) * pair_of(decay_out, head)).astype(BF16)
        state[:, cols] = pair_of(decay_pass, head) * before + mm(keys_t, leaving)
        gate = gate_ref[:, cols]
        gated = (mixed + wide_ref[0:1, cols] * act) * (gate * sigmoid(gate))
        squares = squares + gated * gated
        gg_ref[:, cols] = (gated * wide_ref[1:2, cols]).astype(BF16)
    total = jnp.sum(squares, axis=1, keepdims=True)
    sq_ref[...] = jnp.transpose(jnp.broadcast_to(total, (CHUNK, LANES)))[0:8, :]
    part_ref[...] = mm_nt(gg_ref[...], wout_ref[...]).astype(BF16)


def backward_kernel(
    top_ref,
    sc_ref,
    gate_ref,
    iraw_ref,
    iconv_ref,
    sraw_ref,
    sconv_ref,
    step_ref,
    mixed_ref,
    sin_ref,
    sout_ref,
    wz_ref,
    wx_ref,
    wbc_ref,
    wdt_ref,
    wout_ref,
    convx_ref,
    convbc_ref,
    heads_ref,
    wide_ref,
    spread_ref,
    aux_ref,
    segrow_ref,
    part_ref,
    ggate_ref,
    ginner_ref,
    gstep_ref,
    gshared_ref,
    outlow_ref,
    small_ref,
    smallbc_ref,
    gext_x,
    gext_bc,
    dstate,
    gno_ref,
    balance,
    direct,
    edge,
    dcoup,
):
    inner = wx_ref.shape[1]

    @pl.when(pl.program_id(0) == 0)
    def _():
        dstate[...] = jnp.zeros_like(dstate)
        gext_x[CHUNK : CHUNK + 8, :] = jnp.zeros((8, inner), F32)
        gext_bc[CHUNK : CHUNK + 8, :] = jnp.zeros((8, 2 * N), F32)
        small_ref[...] = jnp.zeros_like(small_ref)
        smallbc_ref[...] = jnp.zeros_like(smallbc_ref)
        edge[...] = jnp.zeros_like(edge)

    aux = aux_ref[...]
    rate = heads_ref[1:2, :]
    gno_ref[...] = mm(top_ref[...], wout_ref[...])
    per_row = jnp.transpose(sc_ref[...])
    scale = per_row[:, 0:1]
    coef = per_row[:, 1:2]
    step_pre = step_ref[...] + heads_ref[0:1, :]
    step, cum, decay_in, decay_out, decay_pass = decays(step_pre, rate, aux)
    cum_t = jnp.transpose(cum)
    shared_conv = sconv_ref[...]
    shared_sig = sigmoid(shared_conv)
    shared_act = shared_conv * shared_sig
    keys = shared_act[:, :N].astype(BF16)
    query = shared_act[:, N:].astype(BF16)
    query_t = jnp.transpose(shared_act[:, N:]).astype(BF16)
    visible = (aux[:, 15:16] == segrow_ref[0:1, :]) & (
        iota2((CHUNK, CHUNK), 0) <= iota2((CHUNK, CHUNK), 1)
    )
    coupling = jnp.where(visible, mm_nt(keys, query), 0.0)
    half = iota2((CHUNK, LANES), 1) < P_SIZE
    dcoup[...] = jnp.zeros_like(dcoup)
    dkeys = jnp.zeros((CHUNK, N), F32)
    dquery = jnp.zeros((CHUNK, N), F32)
    for pair in range(inner // LANES):
        cols = slice(pair * LANES, (pair + 1) * LANES)
        head = 2 * pair
        skip = wide_ref[0:1, cols]
        gain = wide_ref[1:2, cols]
        conv = iconv_ref[:, cols]
        conv_sig = sigmoid(conv)
        act = conv * conv_sig
        step_pair = pair_of(step, head)
        scaled = (act * step_pair).astype(BF16)
        gate = gate_ref[:, cols]
        gate_sig = sigmoid(gate)
        gate_act = gate * gate_sig
        mixed = mixed_ref[:, cols]
        full = mixed + skip * act
        gated = full * gate_act
        gno = gno_ref[:, cols]
        gated_scaled = gated * scale
        small_ref[4:5, cols] += jnp.sum(gno * gated_scaled, axis=0, keepdims=True)
        outlow_ref[:, cols] = (gated_scaled * gain).astype(BF16)
        ggated = scale * (gno * gain) - gated * coef
        gout_low = (ggated * gate_act).astype(BF16)
        ggate_ref[:, cols] = (
            ggated * full * (gate_sig * (1.0 + gate * (1.0 - gate_sig)))
        ).astype(BF16)
        gout = gout_low.astype(F32)
        small_ref[5:6, cols] += jnp.sum(gout * act, axis=0, keepdims=True)
        zero = jnp.zeros_like(gout)
        parts = []
        for one, own in (
            (head, jnp.where(half, gout, zero).astype(BF16)),
            (head + 1, jnp.where(half, zero, gout).astype(BF16)),
        ):
            gap = cum_t[one : one + 1, :] - cum[:, one : one + 1]
            decay = jnp.exp(jnp.minimum(gap, 0.0))
            weights = (coupling * decay).astype(BF16)
            parts.append(mm(weights, gout_low))
            dcoup[...] += mm_nt(scaled, own) * decay
        after = dstate[:, cols]
        after_low = after.astype(BF16)
        out_pair = pair_of(decay_out, head)
        gscaled = jnp.where(half, parts[0], parts[1]) + out_pair * mm(keys, after_low)
        scaled_wide = scaled.astype(F32)
        dkeys = dkeys + mm_nt((scaled_wide * out_pair).astype(BF16), after_low)
        entering = (gout * pair_of(decay_in, head)).astype(BF16)
        dquery = dquery + mm_nt(entering, sin_ref[0, :, cols].astype(BF16))
        edge[0:1, cols] = jnp.sum(sout_ref[0, :, cols] * after, axis=0, keepdims=True)
        dstate[:, cols] = pair_of(decay_pass, head) * after + mm(query_t, entering)
        balance[:, cols] = gout * mixed - scaled_wide * gscaled
        direct[:, cols] = act * gscaled
        gact = step_pair * gscaled + skip * gout
        gext_x[0:CHUNK, cols] = gact * (conv_sig * (1.0 + conv * (1.0 - conv_sig)))
        raw = iraw_ref[:, cols]
        gconv = gext_x[0:CHUNK, cols]
        graw = convx_ref[TAPS - 1 : TAPS, cols] * gconv
        small_ref[TAPS - 1 : TAPS, cols] += jnp.sum(raw * gconv, axis=0, keepdims=True)
        for j in range(1, TAPS):
            moved = gext_x[j : j + CHUNK, cols] * aux[:, 8 + j : 9 + j]
            graw = graw + convx_ref[TAPS - 1 - j : TAPS - j, cols] * moved
            small_ref[TAPS - 1 - j : TAPS - j, cols] += jnp.sum(
                raw * moved, axis=0, keepdims=True
            )
        ginner_ref[:, cols] = graw.astype(BF16)
        gext_x[CHUNK : CHUNK + 8, cols] = gext_x[0:8, cols]
    spread = spread_ref[...]
    order = (iota2((CHUNK, CHUNK), 0) <= iota2((CHUNK, CHUNK), 1)).astype(F32)
    running = jnp.dot(
        order, head_sums(balance[...], spread), precision=highest, preferred_element_type=F32
    )
    running = running + head_sums(edge[...], spread)[0:1, :]
    gstep = (head_sums(direct[...], spread) + running * rate) * sigmoid(step_pre)
    small_ref[6:7, 0:LANES] += rate * jnp.sum(running * step, axis=0, keepdims=True)
    small_ref[7:8, 0:LANES] += jnp.sum(gstep, axis=0, keepdims=True)
    gstep_ref[...] = gstep.astype(BF16)
    dcoupling = jnp.where(visible, dcoup[...], 0.0)
    dkeys = dkeys + mm(dcoupling.astype(BF16), query)
    dquery = dquery + mm(jnp.transpose(dcoupling).astype(BF16), keys)
    slope = shared_sig * (1.0 + shared_conv * (1.0 - shared_sig))
    gext_bc[0:CHUNK, 0:N] = dkeys * slope[:, :N]
    gext_bc[0:CHUNK, N : 2 * N] = dquery * slope[:, N:]
    raw = sraw_ref[...]
    gconv = gext_bc[0:CHUNK, :]
    graw = convbc_ref[TAPS - 1 : TAPS, :] * gconv
    smallbc_ref[TAPS - 1 : TAPS, :] += jnp.sum(raw * gconv, axis=0, keepdims=True)
    for j in range(1, TAPS):
        moved = gext_bc[j : j + CHUNK, :] * aux[:, 8 + j : 9 + j]
        graw = graw + convbc_ref[TAPS - 1 - j : TAPS - j, :] * moved
        smallbc_ref[TAPS - 1 - j : TAPS - j, :] += jnp.sum(raw * moved, axis=0, keepdims=True)
    gshared_ref[...] = graw.astype(BF16)
    gext_bc[CHUNK : CHUNK + 8, :] = gext_bc[0:8, :]
    total = mm_nt(ggate_ref[...], wz_ref[...]) + mm_nt(ginner_ref[...], wx_ref[...])
    total = total + mm_nt(gstep_ref[...], wdt_ref[...])
    part_ref[...] = (total + mm_nt(gshared_ref[...], wbc_ref[...])).astype(BF16)


def whole_spec(shape):
    zeros = (0,) * len(shape)
    return pl.BlockSpec(shape, lambda i: zeros, pipeline_mode=pl.Buffered(1))


VMEM_LIMIT = 60 * 1024 * 1024


def forward_layer(rows_all, weights, layer_args, aux, segrow):
    length, width = rows_all.shape
    chunks = length // CHUNK
    inner = weights[1].shape[1]
    by_rows = lambda cols: pl.BlockSpec((CHUNK, cols), lambda i: (i, 0))
    by_lanes = pl.BlockSpec((8, CHUNK), lambda i: (0, i))
    shape = jax.ShapeDtypeStruct
    return pl.pallas_call(
        forward_kernel,
        grid=(chunks,),
        in_specs=[by_rows(width)]
        + [whole_spec(w.shape) for w in weights]
        + [whole_spec(w.shape) for w in layer_args]
        + [by_rows(LANES), by_lanes],
        out_specs=[
            by_rows(width),
            by_lanes,
            by_rows(inner),
            by_rows(inner),
            by_rows(inner),
            by_rows(2 * N),
            by_rows(2 * N),
            by_rows(LANES),
            by_rows(inner),
            pl.BlockSpec((1, N, inner), lambda i: (i, 0, 0)),
        ],
        out_shape=[
            shape((length, width), BF16),
            shape((8, length), F32),
            shape((length, inner), F32),
            shape((length, inner), F32),
            shape((length, inner), F32),
            shape((length, 2 * N), F32),
            shape((length, 2 * N), F32),
            shape((length, LANES), F32),
            shape((length, inner), F32),
            shape((chunks, N, inner), F32),
        ],
        scratch_shapes=[
            pltpu.VMEM((CHUNK + 8, inner), F32),
            pltpu.VMEM((CHUNK + 8, 2 * N), F32),
            pltpu.VMEM((N, inner), F32),
            pltpu.VMEM((CHUNK, inner), BF16),
        ],
        compiler_params=pltpu.CompilerParams(
            dimension_semantics=("arbitrary",), vmem_limit_bytes=VMEM_LIMIT
        ),
        cost_estimate=pl.CostEstimate(
            flops=length * width * inner * 7, bytes_accessed=40_000_000, transcendentals=8_000_000
        ),
    )(rows_all, *weights, *layer_args, aux, segrow)


def backward_layer(top_all, per_row, saved, weights, layer_args, spread, aux, segrow):
    length, width = top_all.shape
    chunks = length // CHUNK
    inner = weights[1].shape[1]
    last = chunks - 1
    by_rows = lambda cols: pl.BlockSpec((CHUNK, cols), lambda i: (last - i, 0))
    by_lanes = pl.BlockSpec((8, CHUNK), lambda i: (0, last - i))
    shape = jax.ShapeDtypeStruct
    gate, iraw, iconv, sraw, sconv, step, mixed, sin = saved
    return pl.pallas_call(
        backward_kernel,
        grid=(chunks,),
        in_specs=[
            by_rows(width),
            by_lanes,
            by_rows(inner),
            by_rows(inner),
            by_rows(inner),
            by_rows(2 * N),
            by_rows(2 * N),
            by_rows(LANES),
            by_rows(inner),
            pl.BlockSpec((1, N, inner), lambda i: (last - i, 0, 0)),
            pl.BlockSpec((1, N, inner), lambda i: (jnp.minimum(chunks - i, last), 0, 0)),
        ]
        + [whole_spec(w.shape) for w in weights]
        + [whole_spec(w.shape) for w in layer_args]
        + [whole_spec(spread.shape), by_rows(LANES), by_lanes],
        out_specs=[
            by_rows(width),
            by_rows(inner),
            by_rows(inner),
            by_rows(LANES),
            by_rows(2 * N),
            by_rows(inner),
            pl.BlockSpec((8, inner), lambda i: (0, 0)),
            pl.BlockSpec((8, 2 * N), lambda i: (0, 0)),
        ],
        out_shape=[
            shape((length, width), BF16),
            shape((length, inner), BF16),
            shape((length, inner), BF16),
            shape((length, LANES), BF16),
            shape((length, 2 * N), BF16),
            shape((length, inner), BF16),
            shape((8, inner), F32),
            shape((8, 2 * N), F32),
        ],
        scratch_shapes=[
            pltpu.VMEM((CHUNK + 8, inner), F32),
            pltpu.VMEM((CHUNK + 8, 2 * N), F32),
            pltpu.VMEM((N, inner), F32),
            pltpu.VMEM((CHUNK, inner), F32),
            pltpu.VMEM((CHUNK, inner), F32),
            pltpu.VMEM((CHUNK, inner), F32),
            pltpu.VMEM((8, inner), F32),
            pltpu.VMEM((CHUNK, CHUNK), F32),
        ],
        compiler_params=pltpu.CompilerParams(
            dimension_semantics=("arbitrary",), vmem_limit_bytes=VMEM_LIMIT
        ),
        cost_estimate=pl.CostEstimate(
            flops=length * width * inner * 7, bytes_accessed=40_000_000, transcendentals=8_000_000
        ),
    )(
        top_all,
        per_row,
        gate,
        iraw,
        iconv,
        sraw,
        sconv,
        step,
        mixed,
        sin,
        sin,
        *weights,
        *layer_args,
        spread,
        aux,
        segrow,
    )


def row_masks(segment_ids):
    length = segment_ids.shape[0]
    seg = segment_ids.astype(F32)

    def shifted(j):
        return jnp.concatenate([jnp.full((j,), -1.0, F32), seg[: length - j]])

    def ahead(j):
        return jnp.concatenate([seg[j:], jnp.full((j,), -1.0, F32)])

    ends = seg[CHUNK - 1 :: CHUNK]
    own_end = jnp.repeat(ends, CHUNK)
    old_end = jnp.repeat(jnp.concatenate([jnp.full((1,), -1.0, F32), ends[:-1]]), CHUNK)
    lanes = [jnp.zeros_like(seg)] * 16
    for j in range(1, TAPS):
        lanes[j] = (shifted(j) == seg).astype(F32)
        lanes[8 + j] = (ahead(j) == seg).astype(F32)
    lanes[4] = (old_end == seg).astype(F32)
    lanes[5] = (own_end == seg).astype(F32)
    lanes[6] = (own_end == old_end).astype(F32)
    lanes[15] = seg
    aux = jnp.pad(jnp.stack(lanes, axis=1), ((0, 0), (0, LANES - 16)))
    return aux, jnp.broadcast_to(seg[None, :], (8, length))


def layer_parameters(layer, conv_x, conv_bc, a_log, dt_bias, d_skip, gated_gain):
    heads = a_log.shape[1]
    pad = ((0, 0), (0, LANES - heads))
    head_rows = jnp.pad(jnp.stack([dt_bias[layer], -jnp.exp(a_log[layer])]), pad)
    wide = jnp.stack([jnp.repeat(d_skip[layer], P_SIZE), gated_gain[layer]])
    return (conv_x[layer], conv_bc[layer], head_rows, wide)


def head_spread(inner):
    return (
        jnp.arange(inner)[:, None] // P_SIZE == jnp.arange(LANES)[None, :]
    ).astype(BF16)


MESH = pl.DeviceIdType.MESH
ANY = pl.BlockSpec(memory_space=pl.ANY)
IN_VMEM = pl.BlockSpec(memory_space=pltpu.VMEM)
PIECES = 4
TENSOR = 4
LATE = 1e9


class Place:
    def __init__(self, line):
        self.line = line
        dp, t = lax.axis_index("dp"), lax.axis_index("tensor")
        self.dp, self.t = dp, t
        self.z, self.x = lax.div(dp, 2), lax.rem(dp, 2)
        self.other = 1 - self.x
        self.sibling = t + 1 - 2 * lax.rem(t, 2)
        self.mate = lax.rem(t + 2, TENSOR)
        self.diagonal = TENSOR - 1 - t
        self.right = (lax.rem(self.z + 1, line) * 2 + self.x, t)
        self.left = (lax.rem(self.z + line - 1, line) * 2 + self.x, t)
        self.across = (self.z * 2 + self.other, t)

    def tensor_peers(self):
        return [(self.dp, self.sibling), (self.dp, self.mate), (self.dp, self.diagonal)]

    def partner(self, bit):
        return (self.dp + bit - 2 * bit * lax.rem(lax.div(self.dp, bit), 2), self.t)

    def greet(self, across=True, far_bits=()):
        barrier = pltpu.get_barrier_semaphore()
        peers = self.tensor_peers()
        if across:
            peers = peers + [self.across]
        peers = peers + [self.partner(bit) for bit in far_bits]
        for peer in peers:
            pl.semaphore_signal(barrier, inc=1, device_id=peer, device_id_type=MESH)
        count = len(peers)
        if across and self.line > 1:
            has_right = self.z < self.line - 1
            has_left = self.z > 0

            @pl.when(has_right)
            def _():
                pl.semaphore_signal(barrier, inc=1, device_id=self.right, device_id_type=MESH)

            @pl.when(has_left)
            def _():
                pl.semaphore_signal(barrier, inc=1, device_id=self.left, device_id_type=MESH)

            count = count + has_right.astype(jnp.int32) + has_left.astype(jnp.int32)
        pl.semaphore_wait(barrier, count)


class Timeline:
    def __init__(self):
        self.steps = []

    def add(self, when, step):
        self.steps.append((when, len(self.steps), step))

    def run(self):
        for _, _, step in sorted(self.steps, key=lambda entry: entry[:2]):
            step()


def remote(src, dst, send, recv, device):
    return pltpu.make_async_remote_copy(
        src_ref=src, dst_ref=dst, send_sem=send, recv_sem=recv, device_id=device, device_id_type=MESH
    )


def gather_semaphores(count, line):
    return [pltpu.SemaphoreType.DMA((count, 2, line))] * 5


def gather_weights(place, timeline, items, sems, start=0.0):
    send_r, send_l, send_x, recv_z, recv_x = sems
    line = place.line
    z = place.z

    def copy(i, way, zz, xs, src=None):
        dst = items[i][1](zz, xs)
        return remote(
            dst if src is None else src,
            dst,
            (send_r, send_l, send_x)[way].at[i, xs, zz],
            (recv_x if way == 2 else recv_z).at[i, xs, zz],
            (place.right, place.left, place.across)[way],
        )

    def begin(i):
        own = items[i][0]

        def step():
            @pl.when(z < line - 1)
            def _():
                copy(i, 0, z, place.x, own).start()

            @pl.when(z > 0)
            def _():
                copy(i, 1, z, place.x, own).start()

            copy(i, 2, z, place.x, own).start()

        return step

    def hop(i, way, k, xs, to_x):
        source = z - k if way == 0 else z + k
        here = source >= 0 if way == 0 else source < line
        more = z < line - 1 if way == 0 else z > 0

        def arrive():
            @pl.when(here)
            def _():
                copy(i, way, source, xs).wait_recv()
                if to_x:
                    copy(i, 2, source, xs).start()

            @pl.when(here & more)
            def _():
                copy(i, way, source, xs).start()

        def finish():
            @pl.when(here & more)
            def _():
                copy(i, way, source, xs).wait_send()

            if to_x:

                @pl.when(here)
                def _():
                    copy(i, 2, source, xs).wait_send()

        return arrive, finish

    def side(i):
        def step():
            copy(i, 2, z, place.other).wait_recv()

            @pl.when(z < line - 1)
            def _():
                copy(i, 0, z, place.other).start()

            @pl.when(z > 0)
            def _():
                copy(i, 1, z, place.other).start()

        return step

    def end(i):
        route = items[i][2]

        def step():
            for xs in (place.x,) if route == "zx" else (place.x, place.other):

                @pl.when(z < line - 1)
                def _(xs=xs):
                    copy(i, 0, z, xs).wait_send()

                @pl.when(z > 0)
                def _(xs=xs):
                    copy(i, 1, z, xs).wait_send()

            copy(i, 2, z, place.x).wait_send()

        return step

    def settle(i):
        def step():
            for zz in range(line):
                copy(i, 2, zz, place.other).wait_recv()

        return step

    period = sum(item[3] for item in items)
    passed = 0.0
    for i, (_, _, route, cost, due) in enumerate(items):
        passed += cost
        timeline.add(start, begin(i))
        if route == "xz":
            timeline.add(start + passed, side(i))
        for k in range(1, line):
            for way in (0, 1):
                for xs in (place.x,) if route == "zx" else (place.x, place.other):
                    late = 0.0 if xs is place.x else period / 2
                    arrive, finish = hop(i, way, k, xs, route == "zx")
                    timeline.add(start + period * (k - 1) + passed + late, arrive)
                    timeline.add(LATE, finish)
        if route == "zx":
            timeline.add(due, settle(i))
        timeline.add(LATE, end(i))


def scatter_semaphores(count, line):
    return [pltpu.SemaphoreType.DMA((count, line))] * 6


def add_into(target, other, rows):
    step = 48

    def body(n, carry):
        part = pl.ds(pl.multiple_of(n * step, step), step)
        target[part, :] = (target[part, :].astype(F32) + other[part, :].astype(F32)).astype(BF16)
        return carry

    lax.fori_loop(0, rows // step, body, 0)


def scatter_order(line):
    order = []
    for n in range((line + 1) // 2):
        order += [n] if n == line - 1 - n else [n, line - 1 - n]
    return order


def scatter_weights(place, timeline, items, sems):
    send_x, recv_x, send_r, recv_r, send_l, recv_l = sems
    line = place.line
    z = place.z

    def side(i, zz):
        piece, (land_x, _, _), *_ = items[i]
        return remote(
            piece(zz, place.other), land_x.at[zz], send_x.at[i, zz], recv_x.at[i, zz], place.across
        )

    def along(i, zz, way, source=None):
        land = items[i][1][1 + way]
        return remote(
            land.at[zz] if source is None else source,
            land.at[zz],
            (send_r, send_l)[way].at[i, zz],
            (recv_r, recv_l)[way].at[i, zz],
            (place.right, place.left)[way],
        )

    def begin(i, zz):
        return lambda: side(i, zz).start()

    def join(i, zz):
        def step():
            side(i, zz).wait_recv()
            land = items[i][1][0]
            add_into(land.at[zz], items[i][0](zz, place.x), land.shape[1])

        return step

    def send(i, zz, way, h):
        land = items[i][1]
        if way == 0:
            mine, first = (z == h) & (z < zz), h == 0
        else:
            mine, first = (z == line - 1 - h) & (z > zz), h == 0

        def step():
            @pl.when(mine)
            def _():
                if first:
                    along(i, zz, way, land[0].at[zz]).start()
                else:
                    along(i, zz, way).wait_recv()
                    add_into(land[1 + way].at[zz], land[0].at[zz], land[0].shape[1])
                    along(i, zz, way).start()

        return step

    def last(i):
        _, (land_x, land_r, land_l), out, *_ = items[i]

        def step():
            out[...] = land_x[z].astype(F32)

            @pl.when(z > 0)
            def _():
                along(i, z, 0).wait_recv()
                out[...] += land_r[z].astype(F32)

            @pl.when(z < line - 1)
            def _():
                along(i, z, 1).wait_recv()
                out[...] += land_l[z].astype(F32)

        return step

    def end(i, zz):
        def step():
            side(i, zz).wait_send()

            @pl.when(z < zz)
            def _():
                along(i, zz, 0).wait_send()

            @pl.when(z > zz)
            def _():
                along(i, zz, 1).wait_send()

        return step

    now = 0.0
    for i, (_, _, _, cost, ready) in enumerate(items):
        now = max(now, ready)
        for zz in scatter_order(line):
            now += cost
            timeline.add(ready, begin(i, zz))
            timeline.add(now, join(i, zz))
            for way in (0, 1):
                hops = zz if way == 0 else line - 1 - zz
                for h in range(hops):
                    timeline.add(now + 0.01 + h * cost, send(i, zz, way, h))
            timeline.add(LATE, end(i, zz))
        timeline.add(now + line * cost, last(i))


def spread_semaphores():
    return [pltpu.SemaphoreType.DMA((PIECES,))] * 6


def spread_rows(place, own, whole, sems):
    send_y, recv_y, send_s, recv_s, send_f, recv_f = sems
    rows = own.shape[0]
    step = rows // PIECES

    def at(owner, p):
        return whole.at[pl.ds(pl.multiple_of(owner * rows, rows) + p * step, step), :]

    def source(p):
        return own.at[pl.ds(p * step, step), :]

    def to_mate(p):
        return remote(
            source(p), at(place.t, p), send_y.at[p], recv_y.at[p], (place.dp, place.mate)
        )

    def to_sibling(p):
        return remote(
            source(p), at(place.t, p), send_s.at[p], recv_s.at[p], (place.dp, place.sibling)
        )

    def passed_on(p):
        return remote(
            at(place.mate, p), at(place.mate, p), send_f.at[p], recv_f.at[p], (place.dp, place.sibling)
        )

    def begin(p):
        to_mate(p).start()
        to_sibling(p).start()

    def forward(p):
        to_mate(p).wait_recv()
        passed_on(p).start()

    def finish():
        for p in range(PIECES):
            to_mate(p).wait_send()
            to_sibling(p).wait()
            passed_on(p).wait()

    return begin, forward, finish


def reduce_semaphores():
    return [pltpu.SemaphoreType.DMA((PIECES,))] * 6


def reduce_rows(place, timeline, part, lands, sems, owner, rate, start=0.0):
    land_far, land_near, land_mate = lands
    send_a, recv_a, send_b, recv_b, send_z, recv_z = sems
    rows = land_far.shape[0]
    step = rows // PIECES

    def at(block, p):
        return part.at[pl.ds(pl.multiple_of(block * rows, rows) + p * step, step), :]

    def own(ref, p):
        return ref.at[pl.ds(p * step, step), :]

    def far(p):
        return remote(
            at(place.diagonal, p), own(land_far, p), send_a.at[p], recv_a.at[p], (place.dp, place.sibling)
        )

    def near(p):
        return remote(
            at(place.sibling, p), own(land_near, p), send_b.at[p], recv_b.at[p], (place.dp, place.sibling)
        )

    def over(p):
        return remote(
            own(land_far, p), own(land_mate, p), send_z.at[p], recv_z.at[p], (place.dp, place.mate)
        )

    def begin():
        for p in range(PIECES):
            far(p).start()
        for p in range(PIECES):
            near(p).start()

    def middle(p):
        def run():
            far(p).wait_recv()
            mine = own(land_far, p)
            mine[...] = (mine[...].astype(F32) + at(place.mate, p)[...].astype(F32)).astype(BF16)
            over(p).start()

        return run

    def final(p):
        def run():
            near(p).wait_recv()
            over(p).wait_recv()
            sums = at(place.t, p)[...].astype(F32) + own(land_near, p)[...].astype(F32)
            owner(p, sums + own(land_mate, p)[...].astype(F32))

        return run

    def finish():
        for p in range(PIECES):
            far(p).wait_send()
            near(p).wait_send()
            over(p).wait_send()

    timeline.add(start, begin)
    for p in range(PIECES):
        timeline.add(start + 1.0 * (p + 1), middle(p))
        timeline.add(start + 2.0 + rate * (p + 1), final(p))
    timeline.add(LATE, finish)


def share_semaphores():
    return [pltpu.SemaphoreType.DMA((3,))] * 2


def share_blocks(place, source_of, target_of, sems):
    send, recv = sems
    peers = (place.sibling, place.mate, place.diagonal)
    return [
        remote(source_of(peer), target_of(n), send.at[n], recv.at[n], (place.dp, peer))
        for n, peer in enumerate(peers)
    ]


BIG = 6.5
SMALL = 1.1


def row_norm(state):
    return lax.rsqrt(jnp.mean(state * state, axis=1, keepdims=True) + epsilon)


def by_rows_piece(whole, rows):
    def piece(zz, xs):
        return whole.at[pl.ds(pl.multiple_of((zz * 2 + xs) * rows, rows), rows), :]

    return piece


def own_copies(place, blocks, sems):
    return [
        pltpu.make_async_copy(own, piece(place.z, place.x), sems.at[n])
        for n, (own, piece) in enumerate(blocks)
    ]


def weight_gather(place, timeline, refs, wholes, sems, share_sems, own_sems):
    bc_own, bc_all = refs[4], wholes[4]
    pieces = [by_rows_piece(whole, ref.shape[0]) for ref, whole in zip(refs[:4], wholes[:4])]

    def bc_piece(zz, xs):
        return bc_all.at[zz * 2 + xs, place.t]

    due = (3 * BIG + 2 * SMALL) * (place.line - 1) + 3.0
    items = [
        (bc_own, bc_piece, "zx", SMALL / 2, due),
        (refs[3], pieces[3], "zx", SMALL, LATE),
        (refs[1], pieces[1], "zx", BIG, LATE),
        (refs[0], pieces[0], "zx", BIG, LATE),
        (refs[2], pieces[2], "zx", BIG, LATE),
    ]
    copies = own_copies(place, [(item[0], item[1]) for item in items], own_sems)
    shares = share_blocks(
        place, lambda peer: bc_all.at[:, place.t], lambda n: bc_all.at[:, place.t], share_sems
    )
    timeline.add(-1.0, lambda: [copy.start() for copy in copies] and None)
    timeline.add(1.0, lambda: copies[0].wait())
    gather_weights(place, timeline, items, sems)
    timeline.add(due + 0.1, lambda: [copy.start() for copy in shares] and None)
    timeline.add(LATE + 1, lambda: [copy.wait() for copy in shares] and None)
    timeline.add(LATE + 1, lambda: [copy.wait() for copy in copies[1:]] and None)


def gather_outputs(line, width, inner, dp):
    shape = jax.ShapeDtypeStruct
    return [
        shape((width, inner), BF16),
        shape((width, inner), BF16),
        shape((width, inner), BF16),
        shape((width, LANES), BF16),
        shape((dp, TENSOR, width // (dp * TENSOR), 2 * N), BF16),
    ]


def gather_scratch(line):
    return gather_semaphores(5, line) + share_semaphores() + [pltpu.SemaphoreType.DMA((5,))]


def start_kernel(line, resid, cotangent, gain, *refs):
    own, wholes, refs = refs[:5], refs[5:10], refs[10:]
    rows_all, top_all, normed, low = refs[:4]
    sems, share_sems, own_sems = refs[4:9], refs[9:11], refs[11]
    rows_sems, top_sems, local = refs[12:18], refs[18:24], refs[24]
    place = Place(line)
    place.greet()
    timeline = Timeline()
    weight_gather(place, timeline, own, wholes, sems, share_sems, own_sems)
    rows = normed.shape[0]
    block = pl.ds(pl.multiple_of(place.t * rows, rows), rows)
    local_copies = [
        pltpu.make_async_copy(normed, rows_all.at[block, :], local.at[0]),
        pltpu.make_async_copy(low, top_all.at[block, :], local.at[1]),
    ]

    def prepare():
        state = resid[...].astype(F32)
        normed[...] = (state * row_norm(state) * gain[...]).astype(BF16)
        low[...] = cotangent[...].astype(BF16)
        for copy in local_copies:
            copy.start()

    timeline.add(0.5, prepare)
    for n, (source, whole, group) in enumerate(((normed, rows_all, rows_sems), (low, top_all, top_sems))):
        begin, forward, finish = spread_rows(place, source, whole, group)
        for p in range(PIECES):
            timeline.add(0.6, functools.partial(begin, p))
            timeline.add(1.0 + (4 * n + p + 1) * 4.4, functools.partial(forward, p))
        timeline.add(LATE, finish)
    timeline.add(LATE, lambda: [copy.wait() for copy in local_copies] and None)
    timeline.run()


def call_kernel(kernel, outs, in_specs, out_specs, scratch, number, args):
    return pl.pallas_call(
        kernel,
        out_shape=outs,
        in_specs=in_specs,
        out_specs=out_specs,
        scratch_shapes=scratch,
        compiler_params=pltpu.CompilerParams(
            collective_id=number, has_side_effects=True, vmem_limit_bytes=VMEM_LIMIT
        ),
    )(*args)


def start_layer(line, resid, cotangent, gain, own):
    rows, width = resid.shape
    inner = own[0].shape[1]
    shape = jax.ShapeDtypeStruct
    outs = gather_outputs(line, width, inner, 2 * line) + [
        shape((rows * TENSOR, width), BF16),
        shape((rows * TENSOR, width), BF16),
    ]
    scratch = [pltpu.VMEM((rows, width), BF16)] * 2 + gather_scratch(line)
    scratch += spread_semaphores() * 2 + [pltpu.SemaphoreType.DMA((2,))]
    return call_kernel(
        functools.partial(start_kernel, line),
        outs,
        [IN_VMEM] * 3 + [ANY] * 5,
        [ANY] * 7,
        scratch,
        0,
        (resid, cotangent, gain, *own),
    )


def scale_steps(place, timeline, sq, land, scale_row, scale_col, sems, inner_all):
    rows = scale_col.shape[0]

    def at(owner):
        return sq.at[:, pl.ds(pl.multiple_of(owner * rows, rows), rows)]

    copies = share_blocks(place, at, lambda n: land.at[n], sems)

    def arrive():
        for copy in copies:
            copy.wait()
        squares = at(place.t)[...] + land[0] + land[1] + land[2]
        scale = lax.rsqrt(squares / inner_all + epsilon)
        scale_row[...] = scale
        scale_col[...] = jnp.transpose(scale)

    timeline.add(-0.5, lambda: [copy.start() for copy in copies] and None)
    timeline.add(1.5, arrive)


RATE_SHARED = 8.8
RATE = 4.4


def middle_kernel(line, inner_all, part, sq, resid, gain, *refs):
    own, refs = refs[:5], refs[5:]
    state_out, raw_out, scale_row, rows_all, refs = *refs[:4], refs[4:]
    wholes, refs = refs[:5], refs[5:]
    far, near, mate, land, scale_col, normed = refs[:6]
    refs = refs[6:]
    sems, share_sems, own_sems = refs[:5], refs[5:7], refs[7]
    reduce_sems, sq_sems, rows_sems, local = refs[8:14], refs[14:16], refs[16:22], refs[22]
    place = Place(line)
    place.greet()
    timeline = Timeline()
    scale_steps(place, timeline, sq, land, scale_row, scale_col, sq_sems, inner_all)
    rows = normed.shape[0]
    step = rows // PIECES
    begin, forward, finish = spread_rows(place, normed, rows_all, rows_sems)

    def owner(p, sums):
        part_rows = slice(p * step, (p + 1) * step)
        raw_out[part_rows, :] = sums
        state = resid[part_rows, :].astype(F32) + sums * scale_col[part_rows, 0:1]
        state_out[part_rows, :] = state
        normed[part_rows, :] = (state * row_norm(state) * gain[...]).astype(BF16)
        begin(p)

    reduce_rows(place, timeline, part, (far, near, mate), reduce_sems, owner, RATE)
    weight_gather(place, timeline, own, wholes, sems, share_sems, own_sems)
    for p in range(PIECES):
        timeline.add(3.0 + RATE * (PIECES + 1 + p), functools.partial(forward, p))
    block = pl.ds(pl.multiple_of(place.t * rows, rows), rows)
    keep = pltpu.make_async_copy(normed, rows_all.at[block, :], local.at[0])
    timeline.add(3.0 + RATE * PIECES, keep.start)
    timeline.add(LATE, keep.wait)
    timeline.add(LATE, finish)
    timeline.run()


def middle_layer(line, inner_all, part, sq, resid, gain, own):
    rows, width = resid.shape
    inner = own[0].shape[1]
    shape = jax.ShapeDtypeStruct
    outs = [
        shape((rows, width), F32),
        shape((rows, width), F32),
        shape((8, rows), F32),
        shape((rows * TENSOR, width), BF16),
    ] + gather_outputs(line, width, inner, 2 * line)
    scratch = [pltpu.VMEM((rows, width), BF16)] * 3
    scratch += [pltpu.VMEM((3, 8, rows), F32), pltpu.VMEM((rows, 8), F32), pltpu.VMEM((rows, width), BF16)]
    scratch += gather_scratch(line) + reduce_semaphores() + share_semaphores() + spread_semaphores()
    scratch += [pltpu.SemaphoreType.DMA((1,))]
    return call_kernel(
        functools.partial(middle_kernel, line, inner_all),
        outs,
        [IN_VMEM] * 4 + [ANY] * 5,
        [IN_VMEM] * 3 + [ANY] * 6,
        scratch,
        1,
        (part, sq, resid, gain, *own),
    )


def per_row_steps(place, timeline, scale_row, cross_col, stage, land, out, sems, inner_all, when):
    rows = cross_col.shape[0]
    copies = share_blocks(place, lambda peer: stage, lambda n: land.at[n], sems)
    peers = (place.sibling, place.mate, place.diagonal)

    def send():
        cross = jnp.transpose(jnp.broadcast_to(cross_col[:, 0:1], (rows, LANES)))[0:8, :]
        scale = scale_row[...]
        coef = scale * scale * scale * cross / inner_all
        stage[...] = jnp.where(iota2((8, rows), 0) == 0, scale, coef)
        for copy in copies:
            copy.start()
        out[:, pl.ds(pl.multiple_of(place.t * rows, rows), rows)] = stage[...]

    def arrive():
        for n, (copy, peer) in enumerate(zip(copies, peers)):
            copy.wait()
            out[:, pl.ds(pl.multiple_of(peer * rows, rows), rows)] = land[n]

    timeline.add(when, send)
    timeline.add(LATE, arrive)


def top_kernel(
    line, inner_all, part, sq, state, cotangent, hidden, per_row,
    far, near, mate, sq_land, row_land, scale_col, scale_row, cross_col, stage, *refs
):
    reduce_sems, sq_sems, row_sems = refs[:6], refs[6:8], refs[8:10]
    place = Place(line)
    place.greet(across=False)
    timeline = Timeline()
    scale_steps(place, timeline, sq, sq_land, scale_row, scale_col, sq_sems, inner_all)
    step = cross_col.shape[0] // PIECES

    def owner(p, sums):
        part_rows = slice(p * step, (p + 1) * step)
        hidden[part_rows, :] = state[part_rows, :] + sums * scale_col[part_rows, 0:1]
        low = cotangent[part_rows, :].astype(BF16).astype(F32)
        cross = jnp.sum(low * sums, axis=1, keepdims=True)
        cross_col[part_rows, :] = jnp.broadcast_to(cross, (step, LANES))

    reduce_rows(place, timeline, part, (far, near, mate), reduce_sems, owner, RATE)
    per_row_steps(
        place, timeline, scale_row, cross_col, stage, row_land, per_row, row_sems, inner_all, 1e3
    )
    timeline.run()


def top_layer(line, inner_all, part, sq, state, cotangent):
    rows, width = state.shape
    shape = jax.ShapeDtypeStruct
    scratch = [pltpu.VMEM((rows, width), BF16)] * 3 + [pltpu.VMEM((3, 8, rows), F32)] * 2
    scratch += [
        pltpu.VMEM((rows, 8), F32),
        pltpu.VMEM((8, rows), F32),
        pltpu.VMEM((rows, LANES), F32),
        pltpu.VMEM((8, rows), F32),
    ]
    scratch += reduce_semaphores() + share_semaphores() * 2
    return call_kernel(
        functools.partial(top_kernel, line, inner_all),
        [shape((rows, width), F32), shape((8, rows * TENSOR), F32)],
        [IN_VMEM] * 4,
        [IN_VMEM] * 2,
        scratch,
        2,
        (part, sq, state, cotangent),
    )


def weight_scatter(place, timeline, grads, outs, lands, sems, bc_land, bc_sum, share_sems):
    bc = grads[4]
    shares = share_blocks(
        place, lambda peer: bc.at[:, peer], lambda n: bc_land.at[n], share_sems
    )
    bc_ready = 12.0

    def bc_add():
        for copy in shares:
            copy.wait()

        def body(n, carry):
            total = bc[n, place.t].astype(F32) + bc_land[0, n].astype(F32)
            total = total + bc_land[1, n].astype(F32) + bc_land[2, n].astype(F32)
            bc_sum[n] = total.astype(BF16)
            return carry

        lax.fori_loop(0, bc.shape[0], body, 0)

    timeline.add(-1.0, lambda: [copy.start() for copy in shares] and None)
    timeline.add(bc_ready, bc_add)
    items = []
    for n in range(4):
        rows = lands[3 * n].shape[1]
        cost = BIG if n < 3 else SMALL
        items.append((by_rows_piece(grads[n], rows), lands[3 * n : 3 * n + 3], outs[n], cost, 0.0))
    items.append((lambda zz, xs: bc_sum.at[zz * 2 + xs], lands[12:15], outs[4], SMALL / 2, bc_ready + 0.1))
    scatter_weights(place, timeline, items, sems)


def scatter_outputs(width, inner, dp):
    shape = jax.ShapeDtypeStruct
    rows = width // dp
    return [shape((rows, inner), F32)] * 3 + [
        shape((rows, LANES), F32),
        shape((rows // TENSOR, 2 * N), F32),
    ]


def scatter_scratch(line, width, inner):
    dp = 2 * line
    rows = width // dp
    scratch = [pltpu.VMEM((line, rows, inner), BF16)] * 9
    scratch += [pltpu.VMEM((line, rows, LANES), BF16)] * 3
    scratch += [pltpu.VMEM((line, rows // TENSOR, 2 * N), BF16)] * 3
    scratch += [
        pltpu.VMEM((3, dp, rows // TENSOR, 2 * N), BF16),
        pltpu.VMEM((dp, rows // TENSOR, 2 * N), BF16),
    ]
    return scratch + scatter_semaphores(5, line) + share_semaphores()


def input_gradient(state, gain, before, sums):
    scale = row_norm(state)
    gained = sums * gain
    mean = jnp.mean(gained * state, axis=1, keepdims=True)
    grad = before + scale * gained - state * (scale * scale * scale * mean)
    return grad, jnp.sum(sums * state * scale, axis=0, keepdims=True)


def turn_kernel(line, inner_all, part, before, state, gain, raw, scale_row, *refs):
    grads, refs = refs[:5], refs[5:]
    grad_out, gnorm, per_row, top_all, refs = *refs[:4], refs[4:]
    outs, refs = refs[:5], refs[5:]
    far, near, mate, row_land, cross_col, stage, low = refs[:7]
    refs = refs[7:]
    lands, bc_land, bc_sum, sems, share_sems = refs[:15], refs[15], refs[16], refs[17:23], refs[23:25]
    refs = refs[25:]
    reduce_sems, row_sems, top_sems, local = refs[:6], refs[6:8], refs[8:14], refs[14]
    place = Place(line)
    place.greet()
    timeline = Timeline()
    rows = low.shape[0]
    step = rows // PIECES
    begin, forward, finish = spread_rows(place, low, top_all, top_sems)
    gnorm[...] = jnp.zeros_like(gnorm)

    def owner(p, sums):
        part_rows = slice(p * step, (p + 1) * step)
        grad, column = input_gradient(
            state[part_rows, :], gain[...], before[part_rows, :], sums
        )
        grad_out[part_rows, :] = grad
        gnorm[0:1, :] += column
        low[part_rows, :] = grad.astype(BF16)
        cross = jnp.sum(low[part_rows, :].astype(F32) * raw[part_rows, :], axis=1, keepdims=True)
        cross_col[part_rows, :] = jnp.broadcast_to(cross, (step, LANES))
        begin(p)

    reduce_rows(place, timeline, part, (far, near, mate), reduce_sems, owner, RATE)
    for p in range(PIECES):
        timeline.add(3.0 + RATE * (PIECES + 1 + p), functools.partial(forward, p))
    block = pl.ds(pl.multiple_of(place.t * rows, rows), rows)
    keep = pltpu.make_async_copy(low, top_all.at[block, :], local.at[0])
    timeline.add(3.0 + RATE * PIECES, keep.start)
    timeline.add(LATE, keep.wait)
    timeline.add(LATE, finish)
    per_row_steps(
        place, timeline, scale_row, cross_col, stage, row_land, per_row, row_sems, inner_all,
        3.0 + RATE * PIECES,
    )
    weight_scatter(place, timeline, grads, outs, lands, sems, bc_land, bc_sum, share_sems)
    timeline.run()


def turn_layer(line, inner_all, part, before, state, gain, raw, scale_row, grads):
    rows, width = state.shape
    inner = grads[0].shape[1]
    shape = jax.ShapeDtypeStruct
    outs = [
        shape((rows, width), F32),
        shape((8, width), F32),
        shape((8, rows * TENSOR), F32),
        shape((rows * TENSOR, width), BF16),
    ] + scatter_outputs(width, inner, 2 * line)
    scratch = [pltpu.VMEM((rows, width), BF16)] * 3
    scratch += [
        pltpu.VMEM((3, 8, rows), F32),
        pltpu.VMEM((rows, LANES), F32),
        pltpu.VMEM((8, rows), F32),
        pltpu.VMEM((rows, width), BF16),
    ]
    scratch += scatter_scratch(line, width, inner)
    scratch += reduce_semaphores() + share_semaphores() + spread_semaphores()
    scratch += [pltpu.SemaphoreType.DMA((1,))]
    return call_kernel(
        functools.partial(turn_kernel, line, inner_all),
        outs,
        [IN_VMEM] * 11,
        [IN_VMEM] * 3 + [ANY] + [IN_VMEM] * 5,
        scratch,
        3,
        (part, before, state, gain, raw, scale_row, *grads),
    )


def end_kernel(line, part, before, state, gain, gnorm_top, small_a, small_b, bc_a, bc_b, *refs):
    grads, refs = refs[:5], refs[5:]
    grad_out, norm_sum, small_sum, bc_sums, refs = *refs[:4], refs[4:]
    outs, refs = refs[:5], refs[5:]
    far, near, mate = refs[:3]
    lands, bc_land, bc_sum, sems, share_sems = refs[3:18], refs[18], refs[19], refs[20:26], refs[26:28]
    refs = refs[28:]
    reduce_sems, refs = refs[:6], refs[6:]
    small_land, bc_land_sums, norm_land, small_send, small_recv = refs
    dp = 2 * line
    bits = [1 << n for n in range(dp.bit_length() - 1)]
    place = Place(line)
    place.greet(far_bits=[bit for bit in bits if bit >= 4])
    timeline = Timeline()
    step = state.shape[0] // PIECES
    norm_sum[...] = jnp.zeros_like(norm_sum)
    norm_sum[1:2, :] = gnorm_top[0:1, :]
    small_sum[0:8, :] = small_a[...]
    small_sum[8:16, :] = small_b[...]
    bc_sums[0:8, :] = bc_a[...]
    bc_sums[8:16, :] = bc_b[...]

    def owner(p, sums):
        part_rows = slice(p * step, (p + 1) * step)
        grad, column = input_gradient(
            state[part_rows, :], gain[...], before[part_rows, :], sums
        )
        grad_out[part_rows, :] = grad
        norm_sum[0:1, :] += column

    reduce_rows(place, timeline, part, (far, near, mate), reduce_sems, owner, RATE)
    weight_scatter(place, timeline, grads, outs, lands, sems, bc_land, bc_sum, share_sems)
    partners = [place.partner(bit) for bit in bits]
    partners += [(place.dp, place.sibling), (place.dp, place.mate)]
    for n, partner in enumerate(partners):
        trio = [(bc_sums, bc_land_sums), (norm_sum, norm_land)]
        if n < len(bits):
            trio.append((small_sum, small_land))
        copies = [
            remote(own, land.at[n], small_send.at[n, m], small_recv.at[n, m], partner)
            for m, (own, land) in enumerate(trio)
        ]

        def send(copies=copies):
            for copy in copies:
                copy.start()

        def take(copies=copies, trio=trio, n=n):
            for copy, (own, land) in zip(copies, trio):
                copy.wait()
                own[...] += land[n]

        timeline.add(25.0 + 10.0 * n, send)
        timeline.add(34.9 + 10.0 * n, take)
    timeline.run()


def end_layer(line, part, before, state, gain, gnorm_top, smalls, grads):
    rows, width = state.shape
    inner = grads[0].shape[1]
    shape = jax.ShapeDtypeStruct
    dp = 2 * line
    steps = dp.bit_length() - 1
    outs = [
        shape((rows, width), F32),
        shape((8, width), F32),
        shape((16, inner), F32),
        shape((16, 2 * N), F32),
    ] + scatter_outputs(width, inner, dp)
    scratch = [pltpu.VMEM((rows, width), BF16)] * 3 + scatter_scratch(line, width, inner)
    scratch += reduce_semaphores()
    scratch += [
        pltpu.VMEM((steps, 16, inner), F32),
        pltpu.VMEM((steps + 2, 16, 2 * N), F32),
        pltpu.VMEM((steps + 2, 8, width), F32),
        pltpu.SemaphoreType.DMA((steps + 2, 3)),
        pltpu.SemaphoreType.DMA((steps + 2, 3)),
    ]
    return call_kernel(
        functools.partial(end_kernel, line),
        outs,
        [IN_VMEM] * 14,
        [IN_VMEM] * 9,
        scratch,
        4,
        (part, before, state, gain, gnorm_top, *smalls, *grads),
    )


def contract(left, right):
    return lax.dot_general(
        left, right, (((0,), (0,)), ((), ())), preferred_element_type=F32
    ).astype(BF16)


def on_device(
    resid,
    segment_ids,
    cotangent,
    w_z,
    w_x,
    w_bc,
    w_dt,
    w_out,
    norm_gain,
    conv_x,
    conv_bc,
    a_log,
    dt_bias,
    d_skip,
    gated_gain,
):
    dp = lax.axis_size("dp")
    assert lax.axis_size("tensor") == TENSOR and segment_ids.shape[0] == LEN and a_log.shape[0] == 2
    line = dp // 2
    heads = a_log.shape[1]
    inner = heads * P_SIZE
    inner_all = inner * TENSOR
    width = resid.shape[1]
    aux, segrow = row_masks(segment_ids)
    spread = head_spread(inner)
    args = [
        layer_parameters(layer, conv_x, conv_bc, a_log, dt_bias, d_skip, gated_gain)
        for layer in range(2)
    ]
    own = [
        (
            w_z[layer],
            w_x[layer],
            jnp.transpose(w_out[layer]),
            jnp.pad(w_dt[layer], ((0, 0), (0, LANES - heads))),
            w_bc[layer],
        )
        for layer in range(2)
    ]
    gains = [norm_gain[layer : layer + 1] for layer in range(2)]

    def arranged(gathered):
        gate, inner_w, out_w, step_w, shared_w = gathered
        return gate, inner_w, shared_w.reshape(width, 2 * N), step_w, out_w

    *gathered, rows_low, top_high = start_layer(line, resid, cotangent, gains[0], own[0])
    weights_low = arranged(gathered)
    part, sq, *saved_low = forward_layer(rows_low, weights_low, args[0], aux, segrow)
    state, raw, scale_row, rows_high, *gathered = middle_layer(
        line, inner_all, part, sq, resid, gains[1], own[1]
    )
    weights_high = arranged(gathered)
    part, sq, *saved_high = forward_layer(rows_high, weights_high, args[1], aux, segrow)
    hidden, per_row = top_layer(line, inner_all, part, sq, state, cotangent)

    def weight_grads(rows_all, top_all, pulled):
        ggate, ginner, gstep, gshared, outlow = pulled
        return (
            contract(top_all, outlow),
            contract(rows_all, ggate),
            contract(rows_all, ginner),
            contract(rows_all, gstep),
            contract(rows_all, gshared).reshape(dp, TENSOR, width // (dp * TENSOR), 2 * N),
        )

    part, *pulled, small_high, bc_high = backward_layer(
        top_high, per_row, saved_high, weights_high, args[1], spread, aux, segrow
    )
    grads = weight_grads(rows_high, top_high, pulled)
    grad_state, gnorm_high, per_row, top_low, *grads_high = turn_layer(
        line, inner_all, part, cotangent, state, gains[1], raw, scale_row, grads
    )
    part, *pulled, small_low, bc_low = backward_layer(
        top_low, per_row, saved_low, weights_low, args[0], spread, aux, segrow
    )
    grads = weight_grads(rows_low, top_low, pulled)
    grad_resid, norm_sum, small, small_bc, *grads_low = end_layer(
        line,
        part,
        grad_state,
        resid.astype(F32),
        gains[0],
        gnorm_high,
        (small_low, small_high, bc_low, bc_high),
        grads,
    )
    gout, gz, gx, gdt, gbc = [
        jnp.stack([low, high]) for low, high in zip(grads_low, grads_high)
    ]
    small = small.reshape(2, 8, inner)
    return (
        hidden,
        grad_resid,
        gz,
        gx,
        gbc,
        gdt[:, :, :heads],
        jnp.swapaxes(gout, 1, 2),
        norm_sum[:2],
        small[:, :TAPS],
        small_bc.reshape(2, 8, 2 * N)[:, :TAPS],
        small[:, 6, :heads],
        small[:, 7, :heads],
        jnp.sum(small[:, 5].reshape(2, heads, P_SIZE), axis=2),
        small[:, 4],
    )


def solution(mesh):
    rows = P(("dp", "tensor"), None)
    matrix = P(None, "dp", "tensor")
    shared = P(None, ("dp", "tensor"), None)
    wide = P(None, None, "tensor")
    head = P(None, "tensor")
    out = P(None, "tensor", "dp")
    return jax.shard_map(
        on_device,
        mesh=mesh,
        in_specs=(
            rows, P("dp"), rows, matrix, matrix, shared, matrix, out, P(), wide, P(), head, head, head, head,
        ),
        out_specs=(
            rows, rows, matrix, matrix, shared, matrix, out, P(), wide, P(), head, head, head, head,
        ),
        check_vma=False,
    )
```

```python
import functools

import jax
import jax.numpy as jnp
from jax import lax
from jax.experimental import pallas as pl
from jax.experimental.pallas import tpu as pltpu
from jax.sharding import PartitionSpec as P

P_SIZE = 64
N = 128
LEN = 1024
CHUNK = 256
LANES = 128
TAPS = 4

highest = lax.Precision.HIGHEST
epsilon = 1e-05
F32 = jnp.float32
BF16 = jnp.bfloat16


def mm(left, right):
    return jnp.dot(left, right, preferred_element_type=F32)


def mm_nt(left, right):
    return lax.dot_general(left, right, (((1,), (1,)), ((), ())), preferred_element_type=F32)


def sigmoid(values):
    return 1.0 / (1.0 + jnp.exp(-values))


def softplus(values):
    return jnp.maximum(values, 0.0) + jnp.log1p(jnp.exp(-jnp.abs(values)))


def iota2(shape, dim):
    return lax.broadcasted_iota(jnp.int32, shape, dim)


def pair_of(columns, head):
    shape = (columns.shape[0], LANES)
    first = jnp.broadcast_to(columns[:, head : head + 1], shape)
    second = jnp.broadcast_to(columns[:, head + 1 : head + 2], shape)
    return jnp.where(iota2(shape, 1) < P_SIZE, first, second)


def head_sums(values, spread):
    high = values.astype(BF16)
    low = (values - high.astype(F32)).astype(BF16)
    return mm(high, spread) + mm(low, spread)


def decays(step_pre, rate, aux):
    step = softplus(step_pre)
    order = (iota2((CHUNK, CHUNK), 0) >= iota2((CHUNK, CHUNK), 1)).astype(F32)
    cum = jnp.dot(order, step * rate, precision=highest, preferred_element_type=F32)
    last = cum[CHUNK - 1 : CHUNK, :]
    decay_in = jnp.exp(cum) * aux[:, 4:5]
    decay_out = jnp.exp(last - cum) * aux[:, 5:6]
    decay_pass = jnp.exp(last) * aux[0:1, 6:7]
    return step, cum, decay_in, decay_out, decay_pass


def forward_kernel(
    rows_ref,
    wz_ref,
    wx_ref,
    wbc_ref,
    wdt_ref,
    wout_ref,
    convx_ref,
    convbc_ref,
    heads_ref,
    wide_ref,
    aux_ref,
    segrow_ref,
    part_ref,
    sq_ref,
    gate_ref,
    iraw_ref,
    iconv_ref,
    sraw_ref,
    sconv_ref,
    step_ref,
    mixed_ref,
    sin_ref,
    ext_x,
    ext_bc,
    state,
    gg_ref,
    hook=None,
):
    inner = wx_ref.shape[1]
    hook = hook or (lambda slot: None)

    @pl.when(pl.program_id(0) == 0)
    def _():
        state[...] = jnp.zeros_like(state)
        ext_x[0:8, :] = jnp.zeros((8, inner), F32)
        ext_bc[0:8, :] = jnp.zeros((8, 2 * N), F32)

    hook(0)
    rows = rows_ref[...]
    aux = aux_ref[...]
    rate = heads_ref[1:2, :]
    shared = mm(rows, wbc_ref[...])
    sraw_ref[...] = shared
    ext_bc[8 : 8 + CHUNK, :] = shared
    shared_conv = convbc_ref[TAPS - 1 : TAPS, :] * shared
    for j in range(1, TAPS):
        shared_conv = shared_conv + convbc_ref[TAPS - 1 - j : TAPS - j, :] * (
            ext_bc[8 - j : 8 - j + CHUNK, :] * aux[:, j : j + 1]
        )
    sconv_ref[...] = shared_conv
    ext_bc[0:8, :] = ext_bc[CHUNK : CHUNK + 8, :]
    shared_act = shared_conv * sigmoid(shared_conv)
    keys = shared_act[:, :N].astype(BF16)
    keys_t = jnp.transpose(shared_act[:, :N]).astype(BF16)
    query = shared_act[:, N:].astype(BF16)
    visible = (aux[:, 15:16] == segrow_ref[0:1, :]) & (
        iota2((CHUNK, CHUNK), 0) >= iota2((CHUNK, CHUNK), 1)
    )
    coupling = jnp.where(visible, mm_nt(query, keys), 0.0)
    step_raw = mm(rows, wdt_ref[...])
    step_ref[...] = step_raw
    step, cum, decay_in, decay_out, decay_pass = decays(
        step_raw + heads_ref[0:1, :], rate, aux
    )
    cum_t = jnp.transpose(cum)
    ext_x[8 : 8 + CHUNK, :] = mm(rows, wx_ref[...])
    gate_ref[...] = mm(rows, wz_ref[...])
    hook(1)
    squares = jnp.zeros((CHUNK, LANES), F32)
    half = iota2((CHUNK, LANES), 1) < P_SIZE
    for pair in range(inner // LANES):
        cols = slice(pair * LANES, (pair + 1) * LANES)
        head = 2 * pair
        raw = ext_x[8 : 8 + CHUNK, cols]
        iraw_ref[:, cols] = raw
        conv = convx_ref[TAPS - 1 : TAPS, cols] * raw
        for j in range(1, TAPS):
            conv = conv + convx_ref[TAPS - 1 - j : TAPS - j, cols] * (
                ext_x[8 - j : 8 - j + CHUNK, cols] * aux[:, j : j + 1]
            )
        iconv_ref[:, cols] = conv
        ext_x[0:8, cols] = ext_x[CHUNK : CHUNK + 8, cols]
        act = conv * sigmoid(conv)
        scaled = (act * pair_of(step, head)).astype(BF16)
        parts = []
        for one in (head, head + 1):
            gap = cum[:, one : one + 1] - cum_t[one : one + 1, :]
            weights = (coupling * jnp.exp(jnp.minimum(gap, 0.0))).astype(BF16)
            parts.append(mm(weights, scaled))
        before = state[:, cols]
        sin_ref[0, :, cols] = before
        mixed = jnp.where(half, parts[0], parts[1])
        mixed = mixed + pair_of(decay_in, head) * mm(query, before.astype(BF16))
        mixed_ref[:, cols] = mixed
        leaving = (scaled.astype(F32) * pair_of(decay_out, head)).astype(BF16)
        state[:, cols] = pair_of(decay_pass, head) * before + mm(keys_t, leaving)
        gate = gate_ref[:, cols]
        gated = (mixed + wide_ref[0:1, cols] * act) * (gate * sigmoid(gate))
        squares = squares + gated * gated
        gg_ref[:, cols] = (gated * wide_ref[1:2, cols]).astype(BF16)
        hook(2 + pair)
    total = jnp.sum(squares, axis=1, keepdims=True)
    sq_ref[...] = jnp.transpose(jnp.broadcast_to(total, (CHUNK, LANES)))[0:8, :]
    part_ref[...] = mm_nt(gg_ref[...], wout_ref[...]).astype(BF16)


def backward_kernel(
    top_ref,
    sc_ref,
    gate_ref,
    iraw_ref,
    iconv_ref,
    sraw_ref,
    sconv_ref,
    step_ref,
    mixed_ref,
    sin_ref,
    sout_ref,
    wz_ref,
    wx_ref,
    wbc_ref,
    wdt_ref,
    wout_ref,
    convx_ref,
    convbc_ref,
    heads_ref,
    wide_ref,
    spread_ref,
    aux_ref,
    segrow_ref,
    part_ref,
    ggate_ref,
    ginner_ref,
    gstep_ref,
    gshared_ref,
    outlow_ref,
    small_ref,
    smallbc_ref,
    gext_x,
    gext_bc,
    dstate,
    gno_ref,
    balance,
    direct,
    edge,
    dcoup,
):
    inner = wx_ref.shape[1]

    @pl.when(pl.program_id(0) == 0)
    def _():
        dstate[...] = jnp.zeros_like(dstate)
        gext_x[CHUNK : CHUNK + 8, :] = jnp.zeros((8, inner), F32)
        gext_bc[CHUNK : CHUNK + 8, :] = jnp.zeros((8, 2 * N), F32)
        small_ref[...] = jnp.zeros_like(small_ref)
        smallbc_ref[...] = jnp.zeros_like(smallbc_ref)
        edge[...] = jnp.zeros_like(edge)

    aux = aux_ref[...]
    rate = heads_ref[1:2, :]
    gno_ref[...] = mm(top_ref[...], wout_ref[...])
    per_row = jnp.transpose(sc_ref[...])
    scale = per_row[:, 0:1]
    coef = per_row[:, 1:2]
    step_pre = step_ref[...] + heads_ref[0:1, :]
    step, cum, decay_in, decay_out, decay_pass = decays(step_pre, rate, aux)
    cum_t = jnp.transpose(cum)
    shared_conv = sconv_ref[...]
    shared_sig = sigmoid(shared_conv)
    shared_act = shared_conv * shared_sig
    keys = shared_act[:, :N].astype(BF16)
    query = shared_act[:, N:].astype(BF16)
    query_t = jnp.transpose(shared_act[:, N:]).astype(BF16)
    visible = (aux[:, 15:16] == segrow_ref[0:1, :]) & (
        iota2((CHUNK, CHUNK), 0) <= iota2((CHUNK, CHUNK), 1)
    )
    coupling = jnp.where(visible, mm_nt(keys, query), 0.0)
    half = iota2((CHUNK, LANES), 1) < P_SIZE
    dcoup[...] = jnp.zeros_like(dcoup)
    dkeys = jnp.zeros((CHUNK, N), F32)
    dquery = jnp.zeros((CHUNK, N), F32)
    for pair in range(inner // LANES):
        cols = slice(pair * LANES, (pair + 1) * LANES)
        head = 2 * pair
        skip = wide_ref[0:1, cols]
        gain = wide_ref[1:2, cols]
        conv = iconv_ref[:, cols]
        conv_sig = sigmoid(conv)
        act = conv * conv_sig
        step_pair = pair_of(step, head)
        scaled = (act * step_pair).astype(BF16)
        gate = gate_ref[:, cols]
        gate_sig = sigmoid(gate)
        gate_act = gate * gate_sig
        mixed = mixed_ref[:, cols]
        full = mixed + skip * act
        gated = full * gate_act
        gno = gno_ref[:, cols]
        gated_scaled = gated * scale
        small_ref[4:5, cols] += jnp.sum(gno * gated_scaled, axis=0, keepdims=True)
        outlow_ref[:, cols] = (gated_scaled * gain).astype(BF16)
        ggated = scale * (gno * gain) - gated * coef
        gout_low = (ggated * gate_act).astype(BF16)
        ggate_ref[:, cols] = (
            ggated * full * (gate_sig * (1.0 + gate * (1.0 - gate_sig)))
        ).astype(BF16)
        gout = gout_low.astype(F32)
        small_ref[5:6, cols] += jnp.sum(gout * act, axis=0, keepdims=True)
        zero = jnp.zeros_like(gout)
        parts = []
        for one, own in (
            (head, jnp.where(half, gout, zero).astype(BF16)),
            (head + 1, jnp.where(half, zero, gout).astype(BF16)),
        ):
            gap = cum_t[one : one + 1, :] - cum[:, one : one + 1]
            decay = jnp.exp(jnp.minimum(gap, 0.0))
            weights = (coupling * decay).astype(BF16)
            parts.append(mm(weights, gout_low))
            dcoup[...] += mm_nt(scaled, own) * decay
        after = dstate[:, cols]
        after_low = after.astype(BF16)
        out_pair = pair_of(decay_out, head)
        gscaled = jnp.where(half, parts[0], parts[1]) + out_pair * mm(keys, after_low)
        scaled_wide = scaled.astype(F32)
        dkeys = dkeys + mm_nt((scaled_wide * out_pair).astype(BF16), after_low)
        entering = (gout * pair_of(decay_in, head)).astype(BF16)
        dquery = dquery + mm_nt(entering, sin_ref[0, :, cols].astype(BF16))
        edge[0:1, cols] = jnp.sum(sout_ref[0, :, cols] * after, axis=0, keepdims=True)
        dstate[:, cols] = pair_of(decay_pass, head) * after + mm(query_t, entering)
        balance[:, cols] = gout * mixed - scaled_wide * gscaled
        direct[:, cols] = act * gscaled
        gact = step_pair * gscaled + skip * gout
        gext_x[0:CHUNK, cols] = gact * (conv_sig * (1.0 + conv * (1.0 - conv_sig)))
        raw = iraw_ref[:, cols]
        gconv = gext_x[0:CHUNK, cols]
        graw = convx_ref[TAPS - 1 : TAPS, cols] * gconv
        small_ref[TAPS - 1 : TAPS, cols] += jnp.sum(raw * gconv, axis=0, keepdims=True)
        for j in range(1, TAPS):
            moved = gext_x[j : j + CHUNK, cols] * aux[:, 8 + j : 9 + j]
            graw = graw + convx_ref[TAPS - 1 - j : TAPS - j, cols] * moved
            small_ref[TAPS - 1 - j : TAPS - j, cols] += jnp.sum(
                raw * moved, axis=0, keepdims=True
            )
        ginner_ref[:, cols] = graw.astype(BF16)
        gext_x[CHUNK : CHUNK + 8, cols] = gext_x[0:8, cols]
    spread = spread_ref[...]
    order = (iota2((CHUNK, CHUNK), 0) <= iota2((CHUNK, CHUNK), 1)).astype(F32)
    running = jnp.dot(
        order, head_sums(balance[...], spread), precision=highest, preferred_element_type=F32
    )
    running = running + head_sums(edge[...], spread)[0:1, :]
    gstep = (head_sums(direct[...], spread) + running * rate) * sigmoid(step_pre)
    small_ref[6:7, 0:LANES] += rate * jnp.sum(running * step, axis=0, keepdims=True)
    small_ref[7:8, 0:LANES] += jnp.sum(gstep, axis=0, keepdims=True)
    gstep_ref[...] = gstep.astype(BF16)
    dcoupling = jnp.where(visible, dcoup[...], 0.0)
    dkeys = dkeys + mm(dcoupling.astype(BF16), query)
    dquery = dquery + mm(jnp.transpose(dcoupling).astype(BF16), keys)
    slope = shared_sig * (1.0 + shared_conv * (1.0 - shared_sig))
    gext_bc[0:CHUNK, 0:N] = dkeys * slope[:, :N]
    gext_bc[0:CHUNK, N : 2 * N] = dquery * slope[:, N:]
    raw = sraw_ref[...]
    gconv = gext_bc[0:CHUNK, :]
    graw = convbc_ref[TAPS - 1 : TAPS, :] * gconv
    smallbc_ref[TAPS - 1 : TAPS, :] += jnp.sum(raw * gconv, axis=0, keepdims=True)
    for j in range(1, TAPS):
        moved = gext_bc[j : j + CHUNK, :] * aux[:, 8 + j : 9 + j]
        graw = graw + convbc_ref[TAPS - 1 - j : TAPS - j, :] * moved
        smallbc_ref[TAPS - 1 - j : TAPS - j, :] += jnp.sum(raw * moved, axis=0, keepdims=True)
    gshared_ref[...] = graw.astype(BF16)
    gext_bc[CHUNK : CHUNK + 8, :] = gext_bc[0:8, :]
    total = mm_nt(ggate_ref[...], wz_ref[...]) + mm_nt(ginner_ref[...], wx_ref[...])
    total = total + mm_nt(gstep_ref[...], wdt_ref[...])
    part_ref[...] = (total + mm_nt(gshared_ref[...], wbc_ref[...])).astype(BF16)


def whole_spec(shape):
    zeros = (0,) * len(shape)
    return pl.BlockSpec(shape, lambda i: zeros, pipeline_mode=pl.Buffered(1))


VMEM_LIMIT = 60 * 1024 * 1024


def block_rows(cols):
    return pl.BlockSpec((CHUNK, cols), lambda i: (i, 0))


def forward_in_specs(rows_all, weights, layer_args):
    return (
        [block_rows(rows_all.shape[1])]
        + [whole_spec(w.shape) for w in weights]
        + [whole_spec(w.shape) for w in layer_args]
        + [block_rows(LANES), pl.BlockSpec((8, CHUNK), lambda i: (0, i))]
    )


def saved_specs(inner):
    return [
        block_rows(inner),
        block_rows(inner),
        block_rows(inner),
        block_rows(2 * N),
        block_rows(2 * N),
        block_rows(LANES),
        block_rows(inner),
        pl.BlockSpec((1, N, inner), lambda i: (i, 0, 0)),
    ]


def saved_shapes(length, inner):
    shape = jax.ShapeDtypeStruct
    return [
        shape((length, inner), F32),
        shape((length, inner), F32),
        shape((length, inner), F32),
        shape((length, 2 * N), F32),
        shape((length, 2 * N), F32),
        shape((length, LANES), F32),
        shape((length, inner), F32),
        shape((length // CHUNK, N, inner), F32),
    ]


def forward_scratch(inner):
    return [
        pltpu.VMEM((CHUNK + 8, inner), F32),
        pltpu.VMEM((CHUNK + 8, 2 * N), F32),
        pltpu.VMEM((N, inner), F32),
        pltpu.VMEM((CHUNK, inner), BF16),
    ]


def forward_layer(rows_all, weights, layer_args, aux, segrow):
    length, width = rows_all.shape
    inner = weights[1].shape[1]
    shape = jax.ShapeDtypeStruct
    return pl.pallas_call(
        forward_kernel,
        grid=(length // CHUNK,),
        in_specs=forward_in_specs(rows_all, weights, layer_args),
        out_specs=[block_rows(width), pl.BlockSpec((8, CHUNK), lambda i: (0, i))]
        + saved_specs(inner),
        out_shape=[shape((length, width), BF16), shape((8, length), F32)]
        + saved_shapes(length, inner),
        scratch_shapes=forward_scratch(inner),
        compiler_params=pltpu.CompilerParams(
            dimension_semantics=("arbitrary",), vmem_limit_bytes=VMEM_LIMIT
        ),
        cost_estimate=pl.CostEstimate(
            flops=length * width * inner * 7, bytes_accessed=40_000_000, transcendentals=8_000_000
        ),
    )(rows_all, *weights, *layer_args, aux, segrow)


def backward_layer(top_all, per_row, saved, weights, layer_args, spread, aux, segrow):
    length, width = top_all.shape
    chunks = length // CHUNK
    inner = weights[1].shape[1]
    last = chunks - 1
    by_rows = lambda cols: pl.BlockSpec((CHUNK, cols), lambda i: (last - i, 0))
    by_lanes = pl.BlockSpec((8, CHUNK), lambda i: (0, last - i))
    shape = jax.ShapeDtypeStruct
    gate, iraw, iconv, sraw, sconv, step, mixed, sin = saved
    return pl.pallas_call(
        backward_kernel,
        grid=(chunks,),
        in_specs=[
            by_rows(width),
            by_lanes,
            by_rows(inner),
            by_rows(inner),
            by_rows(inner),
            by_rows(2 * N),
            by_rows(2 * N),
            by_rows(LANES),
            by_rows(inner),
            pl.BlockSpec((1, N, inner), lambda i: (last - i, 0, 0)),
            pl.BlockSpec((1, N, inner), lambda i: (jnp.minimum(chunks - i, last), 0, 0)),
        ]
        + [whole_spec(w.shape) for w in weights]
        + [whole_spec(w.shape) for w in layer_args]
        + [whole_spec(spread.shape), by_rows(LANES), by_lanes],
        out_specs=[
            by_rows(width),
            by_rows(inner),
            by_rows(inner),
            by_rows(LANES),
            by_rows(2 * N),
            by_rows(inner),
            pl.BlockSpec((8, inner), lambda i: (0, 0)),
            pl.BlockSpec((8, 2 * N), lambda i: (0, 0)),
        ],
        out_shape=[
            shape((length, width), BF16),
            shape((length, inner), BF16),
            shape((length, inner), BF16),
            shape((length, LANES), BF16),
            shape((length, 2 * N), BF16),
            shape((length, inner), BF16),
            shape((8, inner), F32),
            shape((8, 2 * N), F32),
        ],
        scratch_shapes=[
            pltpu.VMEM((CHUNK + 8, inner), F32),
            pltpu.VMEM((CHUNK + 8, 2 * N), F32),
            pltpu.VMEM((N, inner), F32),
            pltpu.VMEM((CHUNK, inner), F32),
            pltpu.VMEM((CHUNK, inner), F32),
            pltpu.VMEM((CHUNK, inner), F32),
            pltpu.VMEM((8, inner), F32),
            pltpu.VMEM((CHUNK, CHUNK), F32),
        ],
        compiler_params=pltpu.CompilerParams(
            dimension_semantics=("arbitrary",), vmem_limit_bytes=VMEM_LIMIT
        ),
        cost_estimate=pl.CostEstimate(
            flops=length * width * inner * 7, bytes_accessed=40_000_000, transcendentals=8_000_000
        ),
    )(
        top_all,
        per_row,
        gate,
        iraw,
        iconv,
        sraw,
        sconv,
        step,
        mixed,
        sin,
        sin,
        *weights,
        *layer_args,
        spread,
        aux,
        segrow,
    )


def row_masks(segment_ids):
    length = segment_ids.shape[0]
    seg = segment_ids.astype(F32)

    def shifted(j):
        return jnp.concatenate([jnp.full((j,), -1.0, F32), seg[: length - j]])

    def ahead(j):
        return jnp.concatenate([seg[j:], jnp.full((j,), -1.0, F32)])

    ends = seg[CHUNK - 1 :: CHUNK]
    own_end = jnp.repeat(ends, CHUNK)
    old_end = jnp.repeat(jnp.concatenate([jnp.full((1,), -1.0, F32), ends[:-1]]), CHUNK)
    lanes = [jnp.zeros_like(seg)] * 16
    for j in range(1, TAPS):
        lanes[j] = (shifted(j) == seg).astype(F32)
        lanes[8 + j] = (ahead(j) == seg).astype(F32)
    lanes[4] = (old_end == seg).astype(F32)
    lanes[5] = (own_end == seg).astype(F32)
    lanes[6] = (own_end == old_end).astype(F32)
    lanes[15] = seg
    aux = jnp.pad(jnp.stack(lanes, axis=1), ((0, 0), (0, LANES - 16)))
    return aux, jnp.broadcast_to(seg[None, :], (8, length))


def layer_parameters(layer, conv_x, conv_bc, a_log, dt_bias, d_skip, gated_gain):
    heads = a_log.shape[1]
    pad = ((0, 0), (0, LANES - heads))
    head_rows = jnp.pad(jnp.stack([dt_bias[layer], -jnp.exp(a_log[layer])]), pad)
    wide = jnp.stack([jnp.repeat(d_skip[layer], P_SIZE), gated_gain[layer]])
    return (conv_x[layer], conv_bc[layer], head_rows, wide)


def head_spread(inner):
    return (
        jnp.arange(inner)[:, None] // P_SIZE == jnp.arange(LANES)[None, :]
    ).astype(BF16)


MESH = pl.DeviceIdType.MESH
ANY = pl.BlockSpec(memory_space=pl.ANY)
IN_VMEM = pl.BlockSpec(memory_space=pltpu.VMEM)
PIECES = 4
TENSOR = 4
LATE = 1e9
BIG = 6.5
SMALL = 1.1


class Place:
    def __init__(self, line):
        self.line = line
        dp, t = lax.axis_index("dp"), lax.axis_index("tensor")
        self.dp, self.t = dp, t
        self.z, self.x = lax.div(dp, 2), lax.rem(dp, 2)
        self.other = 1 - self.x
        self.sibling = t + 1 - 2 * lax.rem(t, 2)
        self.mate = lax.rem(t + 2, TENSOR)
        self.diagonal = TENSOR - 1 - t
        self.right = (lax.rem(self.z + 1, line) * 2 + self.x, t)
        self.left = (lax.rem(self.z + line - 1, line) * 2 + self.x, t)
        self.across = (self.z * 2 + self.other, t)

    def tensor_peers(self):
        return [(self.dp, self.sibling), (self.dp, self.mate), (self.dp, self.diagonal)]

    def partner(self, bit):
        return (self.dp + bit - 2 * bit * lax.rem(lax.div(self.dp, bit), 2), self.t)

    def greet(self, across=True, far_bits=()):
        barrier = pltpu.get_barrier_semaphore()
        peers = self.tensor_peers()
        if across:
            peers = peers + [self.across]
        peers = peers + [self.partner(bit) for bit in far_bits]
        for peer in peers:
            pl.semaphore_signal(barrier, inc=1, device_id=peer, device_id_type=MESH)
        count = len(peers)
        if across and self.line > 1:
            has_right = self.z < self.line - 1
            has_left = self.z > 0

            @pl.when(has_right)
            def _():
                pl.semaphore_signal(barrier, inc=1, device_id=self.right, device_id_type=MESH)

            @pl.when(has_left)
            def _():
                pl.semaphore_signal(barrier, inc=1, device_id=self.left, device_id_type=MESH)

            count = count + has_right.astype(jnp.int32) + has_left.astype(jnp.int32)
        pl.semaphore_wait(barrier, count)


class Timeline:
    def __init__(self):
        self.steps = []

    def add(self, when, step):
        self.steps.append((when, len(self.steps), step))

    def ordered(self):
        return sorted(self.steps, key=lambda entry: entry[:2])

    def run(self):
        for _, _, step in self.ordered():
            step()

    def spread(self, chunks, slots, chunk_us):
        places = {}
        after = []
        for when, _, step in self.ordered():
            spot = max(0, int(when / chunk_us * slots))
            if spot < chunks * slots:
                places.setdefault((spot % slots, spot // slots), []).append(step)
            else:
                after.append(step)

        def hook(slot):
            for chunk in range(chunks):
                steps = places.get((slot, chunk))
                if steps:

                    @pl.when(pl.program_id(0) == chunk)
                    def _(steps=steps):
                        for step in steps:
                            step()

        def end():
            @pl.when(pl.program_id(0) == chunks - 1)
            def _():
                for step in after:
                    step()

        return hook, end


def remote(src, dst, send, recv, device):
    return pltpu.make_async_remote_copy(
        src_ref=src, dst_ref=dst, send_sem=send, recv_sem=recv, device_id=device, device_id_type=MESH
    )


def gather_semaphores(count, line):
    return [pltpu.SemaphoreType.DMA((count, 2, line))] * 5


def gather_weights(place, timeline, items, sems, start=0.0):
    send_r, send_l, send_x, recv_z, recv_x = sems
    line = place.line
    z = place.z

    def copy(i, way, zz, xs, src=None):
        dst = items[i][1](zz, xs)
        return remote(
            dst if src is None else src,
            dst,
            (send_r, send_l, send_x)[way].at[i, xs, zz],
            (recv_x if way == 2 else recv_z).at[i, xs, zz],
            (place.right, place.left, place.across)[way],
        )

    def begin(i):
        own = items[i][0]

        def step():
            @pl.when(z < line - 1)
            def _():
                copy(i, 0, z, place.x, own).start()

            @pl.when(z > 0)
            def _():
                copy(i, 1, z, place.x, own).start()

            copy(i, 2, z, place.x, own).start()

        return step

    def hop(i, way, k, xs, to_x):
        source = z - k if way == 0 else z + k
        here = source >= 0 if way == 0 else source < line
        more = z < line - 1 if way == 0 else z > 0

        def arrive():
            @pl.when(here)
            def _():
                copy(i, way, source, xs).wait_recv()
                if to_x:
                    copy(i, 2, source, xs).start()

            @pl.when(here & more)
            def _():
                copy(i, way, source, xs).start()

        def finish():
            @pl.when(here & more)
            def _():
                copy(i, way, source, xs).wait_send()

            if to_x:

                @pl.when(here)
                def _():
                    copy(i, 2, source, xs).wait_send()

        return arrive, finish

    def side(i):
        def step():
            copy(i, 2, z, place.other).wait_recv()

            @pl.when(z < line - 1)
            def _():
                copy(i, 0, z, place.other).start()

            @pl.when(z > 0)
            def _():
                copy(i, 1, z, place.other).start()

        return step

    def end(i):
        route = items[i][2]

        def step():
            for xs in (place.x,) if route == "zx" else (place.x, place.other):

                @pl.when(z < line - 1)
                def _(xs=xs):
                    copy(i, 0, z, xs).wait_send()

                @pl.when(z > 0)
                def _(xs=xs):
                    copy(i, 1, z, xs).wait_send()

            copy(i, 2, z, place.x).wait_send()

        return step

    def settle(i):
        def step():
            for zz in range(line):
                copy(i, 2, zz, place.other).wait_recv()

        return step

    period = sum(item[3] for item in items)
    passed = 0.0
    for i, (_, _, route, cost, due) in enumerate(items):
        passed += cost
        timeline.add(start, begin(i))
        if route == "xz":
            timeline.add(start + passed, side(i))
        for k in range(1, line):
            for way in (0, 1):
                for xs in (place.x,) if route == "zx" else (place.x, place.other):
                    late = 0.0 if xs is place.x else period / 2
                    arrive, finish = hop(i, way, k, xs, route == "zx")
                    timeline.add(start + period * (k - 1) + passed + late, arrive)
                    timeline.add(LATE, finish)
        if route == "zx":
            timeline.add(due, settle(i))
        timeline.add(LATE, end(i))


def scatter_semaphores(count, line):
    return [pltpu.SemaphoreType.DMA((count, 2, line))] * 6


def add_into(target, other, rows):
    step = 48

    def body(n, carry):
        part = pl.ds(pl.multiple_of(n * step, step), step)
        target[part, :] = (target[part, :].astype(F32) + other[part, :].astype(F32)).astype(BF16)
        return carry

    lax.fori_loop(0, rows // step, body, 0)


def scatter_order(line):
    order = []
    for n in range((line + 1) // 2):
        order += [n] if n == line - 1 - n else [n, line - 1 - n]
    return order


def scatter_weights(place, timeline, items, sems):
    send_x, recv_x, send_r, recv_r, send_l, recv_l = sems
    line = place.line
    z = place.z

    def rows_of(i):
        return items[i][1][0].shape[1]

    def side(i, zz):
        piece, (land_x, _, _), *_ = items[i]
        return remote(
            piece(zz, place.other), land_x.at[zz], send_x.at[i, 0, zz], recv_x.at[i, 0, zz], place.across
        )

    def land_along(i, zz, way, xs):
        land = items[i][1][1 + way]
        return land.at[zz, xs] if items[i][3] == "zx" else land.at[zz]

    def along(i, zz, way, xs, source=None):
        land = land_along(i, zz, way, xs)
        return remote(
            land if source is None else source,
            land,
            (send_r, send_l)[way].at[i, xs, zz],
            (recv_r, recv_l)[way].at[i, xs, zz],
            (place.right, place.left)[way],
        )

    def own(i, zz, xs):
        return items[i][0](zz, xs) if items[i][3] == "zx" else items[i][1][0].at[zz]

    def join(i, zz):
        def step():
            side(i, zz).wait_recv()
            add_into(items[i][1][0].at[zz], items[i][0](zz, place.x), rows_of(i))

        return step

    def send(i, zz, way, xs, h):
        if way == 0:
            mine = (z == h) & (z < zz)
        else:
            mine = (z == line - 1 - h) & (z > zz)

        def step():
            @pl.when(mine)
            def _():
                if h == 0:
                    along(i, zz, way, xs, own(i, zz, xs)).start()
                else:
                    along(i, zz, way, xs).wait_recv()
                    add_into(land_along(i, zz, way, xs), own(i, zz, xs), rows_of(i))
                    along(i, zz, way, xs).start()

        return step

    def last(i):
        out = items[i][2]

        def step():
            out[...] = items[i][1][0][z].astype(F32)
            for way, there in ((0, z > 0), (1, z < line - 1)):

                @pl.when(there)
                def _(way=way):
                    along(i, z, way, 0).wait_recv()
                    out[...] += items[i][1][1 + way][z].astype(F32)

        return step

    def swap(i):
        piece, (land_x, land_r, _), *_ = items[i]
        stage = land_r.at[z, place.other]
        return remote(stage, land_x.at[0], send_x.at[i, 0, 0], recv_x.at[i, 0, 0], place.across)

    def gather_line(i, xs):
        piece = items[i][0]

        def step():
            right, left = land_along(i, z, 0, xs), land_along(i, z, 1, xs)

            @pl.when(z > 0)
            def _():
                along(i, z, 0, xs).wait_recv()
                add_into(right, piece(z, xs), rows_of(i))

            @pl.when(z == 0)
            def _():
                right[...] = piece(z, xs)[...]

            @pl.when(z < line - 1)
            def _():
                along(i, z, 1, xs).wait_recv()
                add_into(right, left, rows_of(i))

        return step

    def swap_end(i):
        piece, (land_x, land_r, _), out, *_ = items[i]

        def step():
            swap(i).wait()
            out[...] = land_r[z, place.x].astype(F32) + land_x[0].astype(F32)

        return step

    def end(i, zz, xs):
        def step():
            if items[i][3] == "xz":
                side(i, zz).wait_send()
            for way, there in ((0, z < zz), (1, z > zz)):

                @pl.when(there)
                def _(way=way):
                    along(i, zz, way, xs).wait_send()

        return step

    now = 0.0
    for i, (_, _, _, route, cost, ready) in enumerate(items):
        if route == "zx":
            then = ready
            for zz in scatter_order(line):
                for xs in (0, 1):
                    for way in (0, 1):
                        for h in range(zz if way == 0 else line - 1 - zz):
                            timeline.add(then + h * cost + 0.2, send(i, zz, way, xs, h))
                    timeline.add(LATE, end(i, zz, xs))
                    then += cost
            then += line * cost / 2
            for xs in (0, 1):
                timeline.add(then, gather_line(i, xs))
            timeline.add(then + 0.1, lambda i=i: swap(i).start())
            timeline.add(LATE - 1, swap_end(i))
            continue
        now = max(now, ready)
        for zz in scatter_order(line):
            timeline.add(max(ready, now - 2 * BIG), lambda i=i, zz=zz: side(i, zz).start())
            now += cost
            timeline.add(now, join(i, zz))
            for way in (0, 1):
                hops = zz if way == 0 else line - 1 - zz
                for h in range(hops):
                    timeline.add(now + 0.01 + h * cost, send(i, zz, way, 0, h))
            timeline.add(LATE, end(i, zz, 0))
        timeline.add(now + line * cost, last(i))


def spread_semaphores():
    return [pltpu.SemaphoreType.DMA((PIECES,))] * 6


def spread_rows(place, own, whole, sems):
    send_y, recv_y, send_s, recv_s, send_f, recv_f = sems
    rows = own.shape[0]
    step = rows // PIECES

    def at(owner, p):
        return whole.at[pl.ds(pl.multiple_of(owner * rows, rows) + p * step, step), :]

    def source(p):
        return own.at[pl.ds(p * step, step), :]

    def to_mate(p):
        return remote(
            source(p), at(place.t, p), send_y.at[p], recv_y.at[p], (place.dp, place.mate)
        )

    def to_sibling(p):
        return remote(
            source(p), at(place.t, p), send_s.at[p], recv_s.at[p], (place.dp, place.sibling)
        )

    def passed_on(p):
        return remote(
            at(place.mate, p), at(place.mate, p), send_f.at[p], recv_f.at[p], (place.dp, place.sibling)
        )

    def begin(p):
        to_mate(p).start()
        to_sibling(p).start()

    def forward(p):
        to_mate(p).wait_recv()
        passed_on(p).start()

    def finish():
        for p in range(PIECES):
            to_mate(p).wait_send()
            to_sibling(p).wait()
            passed_on(p).wait()

    return begin, forward, finish


def reduce_semaphores():
    return [pltpu.SemaphoreType.DMA((PIECES,))] * 6


def reduce_rows(place, timeline, part, lands, sems, owner, rate, start=0.0):
    land_far, land_near, land_mate = lands
    send_a, recv_a, send_b, recv_b, send_z, recv_z = sems
    rows = land_far.shape[0]
    step = rows // PIECES

    def at(block, p):
        return part.at[pl.ds(pl.multiple_of(block * rows, rows) + p * step, step), :]

    def own(ref, p):
        return ref.at[pl.ds(p * step, step), :]

    def far(p):
        return remote(
            at(place.diagonal, p), own(land_far, p), send_a.at[p], recv_a.at[p], (place.dp, place.sibling)
        )

    def near(p):
        return remote(
            at(place.sibling, p), own(land_near, p), send_b.at[p], recv_b.at[p], (place.dp, place.sibling)
        )

    def over(p):
        return remote(
            own(land_far, p), own(land_mate, p), send_z.at[p], recv_z.at[p], (place.dp, place.mate)
        )

    def begin():
        for p in range(PIECES):
            far(p).start()
        for p in range(PIECES):
            near(p).start()

    def middle(p):
        def run():
            far(p).wait_recv()
            mine = own(land_far, p)
            mine[...] = (mine[...].astype(F32) + at(place.mate, p)[...].astype(F32)).astype(BF16)
            over(p).start()

        return run

    def final(p):
        def run():
            near(p).wait_recv()
            over(p).wait_recv()
            sums = at(place.t, p)[...].astype(F32) + own(land_near, p)[...].astype(F32)
            owner(p, sums + own(land_mate, p)[...].astype(F32))

        return run

    def finish():
        for p in range(PIECES):
            far(p).wait_send()
            near(p).wait_send()
            over(p).wait_send()

    timeline.add(start, begin)
    for p in range(PIECES):
        timeline.add(start + 1.0 * (p + 1), middle(p))
        timeline.add(start + 2.0 + rate * (p + 1), final(p))
    timeline.add(LATE, finish)


def share_semaphores():
    return [pltpu.SemaphoreType.DMA((3,))] * 2


def share_blocks(place, source_of, target_of, sems):
    send, recv = sems
    peers = (place.sibling, place.mate, place.diagonal)
    return [
        remote(source_of(peer), target_of(n), send.at[n], recv.at[n], (place.dp, peer))
        for n, peer in enumerate(peers)
    ]


def row_norm(state):
    return lax.rsqrt(jnp.mean(state * state, axis=1, keepdims=True) + epsilon)


def by_rows_piece(whole, rows, start=0, count=None):
    count = rows if count is None else count

    def piece(zz, xs):
        return whole.at[pl.ds(pl.multiple_of((zz * 2 + xs) * rows, rows) + start, count), :]

    return piece


def own_copies(place, blocks, sems):
    return [
        pltpu.make_async_copy(own, piece(place.z, place.x), sems.at[n])
        for n, (own, piece) in enumerate(blocks)
    ]


def weight_gather(place, timeline, refs, wholes, sems, share_sems, own_sems):
    bc_own, bc_all = refs[4], wholes[4]
    rows = refs[0].shape[0]
    half = rows // 2
    pieces = [by_rows_piece(whole, rows) for whole in wholes[:4]]

    def bc_piece(zz, xs):
        return bc_all.at[zz * 2 + xs, place.t]

    due = (3 * BIG + 2 * SMALL) * (place.line - 1) + 3.0
    items = [
        (bc_own, bc_piece, "zx", SMALL / 2, due),
        (refs[3], pieces[3], "zx", SMALL, LATE),
        (refs[1], pieces[1], "zx", BIG, LATE),
        (refs[0], pieces[0], "zx", BIG, LATE),
        (refs[2].at[pl.ds(0, half), :], by_rows_piece(wholes[2], rows, 0, half), "xz", BIG / 2, LATE),
        (refs[2].at[pl.ds(half, half), :], by_rows_piece(wholes[2], rows, half, half), "zx", BIG / 2, LATE),
    ]
    copies = own_copies(place, [(item[0], item[1]) for item in items], own_sems)
    shares = share_blocks(
        place, lambda peer: bc_all.at[:, place.t], lambda n: bc_all.at[:, place.t], share_sems
    )
    timeline.add(-1.0, lambda: [copy.start() for copy in copies] and None)
    timeline.add(1.0, lambda: copies[0].wait())
    gather_weights(place, timeline, items, sems)
    timeline.add(due + 0.1, lambda: [copy.start() for copy in shares] and None)
    timeline.add(LATE + 1, lambda: [copy.wait() for copy in shares] and None)
    timeline.add(LATE + 1, lambda: [copy.wait() for copy in copies[1:]] and None)


def gather_outputs(line, width, inner, dp):
    shape = jax.ShapeDtypeStruct
    return [
        shape((width, inner), BF16),
        shape((width, inner), BF16),
        shape((width, inner), BF16),
        shape((width, LANES), BF16),
        shape((dp, TENSOR, width // (dp * TENSOR), 2 * N), BF16),
    ]


def gather_scratch(line):
    return gather_semaphores(6, line) + share_semaphores() + [pltpu.SemaphoreType.DMA((6,))]


def start_kernel(line, resid, cotangent, gain, *refs):
    own, wholes, refs = refs[:5], refs[5:10], refs[10:]
    rows_all, top_all, normed, low = refs[:4]
    sems, share_sems, own_sems = refs[4:9], refs[9:11], refs[11]
    rows_sems, top_sems, local = refs[12:18], refs[18:24], refs[24]
    place = Place(line)
    place.greet()
    timeline = Timeline()
    weight_gather(place, timeline, own, wholes, sems, share_sems, own_sems)
    rows = normed.shape[0]
    block = pl.ds(pl.multiple_of(place.t * rows, rows), rows)
    local_copies = [
        pltpu.make_async_copy(normed, rows_all.at[block, :], local.at[0]),
        pltpu.make_async_copy(low, top_all.at[block, :], local.at[1]),
    ]

    def prepare():
        state = resid[...].astype(F32)
        normed[...] = (state * row_norm(state) * gain[...]).astype(BF16)
        low[...] = cotangent[...].astype(BF16)
        for copy in local_copies:
            copy.start()

    timeline.add(0.5, prepare)
    for n, (source, whole, group) in enumerate(((normed, rows_all, rows_sems), (low, top_all, top_sems))):
        begin, forward, finish = spread_rows(place, source, whole, group)
        for p in range(PIECES):
            timeline.add(0.6, functools.partial(begin, p))
            timeline.add(1.0 + (4 * n + p + 1) * 4.4, functools.partial(forward, p))
        timeline.add(LATE, finish)
    timeline.add(LATE, lambda: [copy.wait() for copy in local_copies] and None)
    timeline.run()


def call_kernel(kernel, outs, in_specs, out_specs, scratch, number, args, grid=()):
    return pl.pallas_call(
        kernel,
        grid=grid,
        out_shape=outs,
        in_specs=in_specs,
        out_specs=out_specs,
        scratch_shapes=scratch,
        compiler_params=pltpu.CompilerParams(
            collective_id=number, has_side_effects=True, vmem_limit_bytes=VMEM_LIMIT
        ),
    )(*args)


def start_layer(line, resid, cotangent, gain, own):
    rows, width = resid.shape
    inner = own[0].shape[1]
    shape = jax.ShapeDtypeStruct
    outs = gather_outputs(line, width, inner, 2 * line) + [
        shape((rows * TENSOR, width), BF16),
        shape((rows * TENSOR, width), BF16),
    ]
    scratch = [pltpu.VMEM((rows, width), BF16)] * 2 + gather_scratch(line)
    scratch += spread_semaphores() * 2 + [pltpu.SemaphoreType.DMA((2,))]
    return call_kernel(
        functools.partial(start_kernel, line),
        outs,
        [IN_VMEM] * 3 + [ANY] * 5,
        [ANY] * 7,
        scratch,
        0,
        (resid, cotangent, gain, *own),
    )


def scale_steps(place, timeline, sq, land, scale_row, scale_col, sems, inner_all, start=0.0):
    rows = scale_col.shape[0]

    def at(owner):
        return sq.at[:, pl.ds(pl.multiple_of(owner * rows, rows), rows)]

    copies = share_blocks(place, at, lambda n: land.at[n], sems)

    def arrive():
        for copy in copies:
            copy.wait()
        squares = at(place.t)[...] + land[0] + land[1] + land[2]
        scale = lax.rsqrt(squares / inner_all + epsilon)
        scale_row[...] = scale
        scale_col[...] = jnp.transpose(scale)

    timeline.add(start - 0.5, lambda: [copy.start() for copy in copies] and None)
    timeline.add(start + 1.5, arrive)


RATE_SHARED = 8.8
RATE = 4.4


SLOTS = 8
FORWARD_US = 6.7


def middle_kernel(line, inner_all, *refs):
    work, refs = refs[:12], refs[12:]
    (resid, gain), own, refs = refs[:2], refs[2:7], refs[7:]
    saved, refs = refs[:8], refs[8:]
    state_out, raw_out, scale_row, rows_all, refs = *refs[:4], refs[4:]
    wholes, refs = refs[:5], refs[5:]
    scratch, refs = refs[:4], refs[4:]
    part, sq, far, near, mate, land, scale_col, normed = refs[:8]
    refs = refs[8:]
    sems, share_sems, own_sems = refs[:5], refs[5:7], refs[7]
    reduce_sems, sq_sems, rows_sems, local = refs[8:14], refs[14:16], refs[16:22], refs[22]
    chunk = pl.program_id(0)
    chunks = part.shape[0] // CHUNK
    place = Place(line)
    pl.when(chunk == 0)(place.greet)
    timeline = Timeline()
    done = FORWARD_US * chunks + 1.0
    scale_steps(place, timeline, sq, land, scale_row, scale_col, sq_sems, inner_all, done)
    rows = normed.shape[0]
    step = rows // PIECES
    begin, forward, finish = spread_rows(place, normed, rows_all, rows_sems)

    def owner(p, sums):
        part_rows = slice(p * step, (p + 1) * step)
        raw_out[part_rows, :] = sums
        state = resid[part_rows, :].astype(F32) + sums * scale_col[part_rows, 0:1]
        state_out[part_rows, :] = state
        normed[part_rows, :] = (state * row_norm(state) * gain[...]).astype(BF16)
        begin(p)

    reduce_rows(place, timeline, part, (far, near, mate), reduce_sems, owner, RATE, done)
    weight_gather(place, timeline, own, wholes, sems, share_sems, own_sems)
    for p in range(PIECES):
        timeline.add(done + 3.0 + RATE * (PIECES + 1 + p), functools.partial(forward, p))
    block = pl.ds(pl.multiple_of(place.t * rows, rows), rows)
    keep = pltpu.make_async_copy(normed, rows_all.at[block, :], local.at[0])
    timeline.add(done + 3.0 + RATE * PIECES, keep.start)
    timeline.add(LATE, keep.wait)
    timeline.add(LATE, finish)
    hook, end = timeline.spread(chunks, SLOTS, FORWARD_US)
    at = pl.multiple_of(chunk * CHUNK, CHUNK)
    forward_kernel(
        *work, part.at[pl.ds(at, CHUNK), :], sq.at[:, pl.ds(at, CHUNK)], *saved, *scratch, hook=hook
    )
    end()


def middle_layer(line, inner_all, rows_all, weights, layer_args, aux, segrow, resid, gain, own):
    rows, width = resid.shape
    length = rows_all.shape[0]
    inner = own[0].shape[1]
    shape = jax.ShapeDtypeStruct
    outs = (
        saved_shapes(length, inner)
        + [
            shape((rows, width), F32),
            shape((rows, width), F32),
            shape((8, rows), F32),
            shape((length, width), BF16),
        ]
        + gather_outputs(line, width, inner, 2 * line)
    )
    scratch = forward_scratch(inner)
    scratch += [pltpu.VMEM((length, width), BF16), pltpu.VMEM((8, length), F32)]
    scratch += [pltpu.VMEM((rows, width), BF16)] * 3
    scratch += [pltpu.VMEM((3, 8, rows), F32), pltpu.VMEM((rows, 8), F32), pltpu.VMEM((rows, width), BF16)]
    scratch += gather_scratch(line) + reduce_semaphores() + share_semaphores() + spread_semaphores()
    scratch += [pltpu.SemaphoreType.DMA((1,))]
    return call_kernel(
        functools.partial(middle_kernel, line, inner_all),
        outs,
        forward_in_specs(rows_all, weights, layer_args)
        + [whole_spec(resid.shape), whole_spec(gain.shape)]
        + [ANY] * 5,
        saved_specs(inner)
        + [whole_spec((rows, width)), whole_spec((rows, width)), whole_spec((8, rows))]
        + [ANY] * 6,
        scratch,
        1,
        (rows_all, *weights, *layer_args, aux, segrow, resid, gain, *own),
        (length // CHUNK,),
    )


def per_row_steps(place, timeline, scale_row, cross_col, stage, land, out, sems, inner_all, when):
    rows = cross_col.shape[0]
    copies = share_blocks(place, lambda peer: stage, lambda n: land.at[n], sems)
    peers = (place.sibling, place.mate, place.diagonal)

    def send():
        cross = jnp.transpose(jnp.broadcast_to(cross_col[:, 0:1], (rows, LANES)))[0:8, :]
        scale = scale_row[...]
        coef = scale * scale * scale * cross / inner_all
        stage[...] = jnp.where(iota2((8, rows), 0) == 0, scale, coef)
        for copy in copies:
            copy.start()
        out[:, pl.ds(pl.multiple_of(place.t * rows, rows), rows)] = stage[...]

    def arrive():
        for n, (copy, peer) in enumerate(zip(copies, peers)):
            copy.wait()
            out[:, pl.ds(pl.multiple_of(peer * rows, rows), rows)] = land[n]

    timeline.add(when, send)
    timeline.add(LATE, arrive)


def top_kernel(
    line, inner_all, part, sq, state, cotangent, hidden, per_row,
    far, near, mate, sq_land, row_land, scale_col, scale_row, cross_col, stage, *refs
):
    reduce_sems, sq_sems, row_sems = refs[:6], refs[6:8], refs[8:10]
    place = Place(line)
    place.greet(across=False)
    timeline = Timeline()
    scale_steps(place, timeline, sq, sq_land, scale_row, scale_col, sq_sems, inner_all)
    step = cross_col.shape[0] // PIECES

    def owner(p, sums):
        part_rows = slice(p * step, (p + 1) * step)
        hidden[part_rows, :] = state[part_rows, :] + sums * scale_col[part_rows, 0:1]
        low = cotangent[part_rows, :].astype(BF16).astype(F32)
        cross = jnp.sum(low * sums, axis=1, keepdims=True)
        cross_col[part_rows, :] = jnp.broadcast_to(cross, (step, LANES))

    reduce_rows(place, timeline, part, (far, near, mate), reduce_sems, owner, RATE)
    per_row_steps(
        place, timeline, scale_row, cross_col, stage, row_land, per_row, row_sems, inner_all, 1e3
    )
    timeline.run()


def top_layer(line, inner_all, part, sq, state, cotangent):
    rows, width = state.shape
    shape = jax.ShapeDtypeStruct
    scratch = [pltpu.VMEM((rows, width), BF16)] * 3 + [pltpu.VMEM((3, 8, rows), F32)] * 2
    scratch += [
        pltpu.VMEM((rows, 8), F32),
        pltpu.VMEM((8, rows), F32),
        pltpu.VMEM((rows, LANES), F32),
        pltpu.VMEM((8, rows), F32),
    ]
    scratch += reduce_semaphores() + share_semaphores() * 2
    return call_kernel(
        functools.partial(top_kernel, line, inner_all),
        [shape((rows, width), F32), shape((8, rows * TENSOR), F32)],
        [IN_VMEM] * 4,
        [IN_VMEM] * 2,
        scratch,
        2,
        (part, sq, state, cotangent),
    )


def weight_scatter(place, timeline, grads, outs, lands, sems, bc_land, bc_sum, share_sems):
    bc = grads[4]
    shares = share_blocks(
        place, lambda peer: bc.at[:, peer], lambda n: bc_land.at[n], share_sems
    )
    bc_ready = 12.0

    def bc_add():
        for copy in shares:
            copy.wait()

        def body(n, carry):
            total = bc[n, place.t].astype(F32) + bc_land[0, n].astype(F32)
            total = total + bc_land[1, n].astype(F32) + bc_land[2, n].astype(F32)
            bc_sum[n] = total.astype(BF16)
            return carry

        lax.fori_loop(0, bc.shape[0], body, 0)

    timeline.add(-1.0, lambda: [copy.start() for copy in shares] and None)
    timeline.add(bc_ready, bc_add)
    rows = outs[0].shape[0]
    half = rows // 2
    first, second = pl.ds(0, half), pl.ds(half, half)
    items = [
        (by_rows_piece(grads[0], rows, 0, half), lands[15:18], outs[0].at[first, :], "zx", BIG / 2, 0.0),
        (by_rows_piece(grads[0], rows, half, half), lands[0:3], outs[0].at[second, :], "xz", BIG / 2, 0.0),
        (by_rows_piece(grads[1], rows), lands[3:6], outs[1], "xz", BIG, 0.0),
        (by_rows_piece(grads[2], rows), lands[6:9], outs[2], "xz", BIG, 0.0),
        (by_rows_piece(grads[3], rows), lands[9:12], outs[3], "xz", SMALL, 0.0),
        (lambda zz, xs: bc_sum.at[zz * 2 + xs], lands[12:15], outs[4], "xz", SMALL / 2, bc_ready + 0.1),
    ]
    scatter_weights(place, timeline, items, sems)


def scatter_outputs(width, inner, dp):
    shape = jax.ShapeDtypeStruct
    rows = width // dp
    return [shape((rows, inner), F32)] * 3 + [
        shape((rows, LANES), F32),
        shape((rows // TENSOR, 2 * N), F32),
    ]


def scatter_scratch(line, width, inner):
    dp = 2 * line
    rows = width // dp
    scratch = [pltpu.VMEM((line, rows // 2, inner), BF16)] * 3
    scratch += [pltpu.VMEM((line, rows, inner), BF16)] * 6
    scratch += [pltpu.VMEM((line, rows, LANES), BF16)] * 3
    scratch += [pltpu.VMEM((line, rows // TENSOR, 2 * N), BF16)] * 3
    scratch += [pltpu.VMEM((1, rows // 2, inner), BF16)]
    scratch += [pltpu.VMEM((line, 2, rows // 2, inner), BF16)] * 2
    scratch += [
        pltpu.VMEM((3, dp, rows // TENSOR, 2 * N), BF16),
        pltpu.VMEM((dp, rows // TENSOR, 2 * N), BF16),
    ]
    return scratch + scatter_semaphores(6, line) + share_semaphores()


def input_gradient(state, gain, before, sums):
    scale = row_norm(state)
    gained = sums * gain
    mean = jnp.mean(gained * state, axis=1, keepdims=True)
    grad = before + scale * gained - state * (scale * scale * scale * mean)
    return grad, jnp.sum(sums * state * scale, axis=0, keepdims=True)


def turn_kernel(line, inner_all, part, before, state, gain, raw, scale_row, *refs):
    grads, refs = refs[:5], refs[5:]
    grad_out, gnorm, per_row, top_all, refs = *refs[:4], refs[4:]
    outs, refs = refs[:5], refs[5:]
    far, near, mate, row_land, cross_col, stage, low = refs[:7]
    refs = refs[7:]
    lands, bc_land, bc_sum, sems, share_sems = refs[:18], refs[18], refs[19], refs[20:26], refs[26:28]
    refs = refs[28:]
    reduce_sems, row_sems, top_sems, local = refs[:6], refs[6:8], refs[8:14], refs[14]
    place = Place(line)
    place.greet()
    timeline = Timeline()
    rows = low.shape[0]
    step = rows // PIECES
    begin, forward, finish = spread_rows(place, low, top_all, top_sems)
    gnorm[...] = jnp.zeros_like(gnorm)

    def owner(p, sums):
        part_rows = slice(p * step, (p + 1) * step)
        grad, column = input_gradient(
            state[part_rows, :], gain[...], before[part_rows, :], sums
        )
        grad_out[part_rows, :] = grad
        gnorm[0:1, :] += column
        low[part_rows, :] = grad.astype(BF16)
        cross = jnp.sum(low[part_rows, :].astype(F32) * raw[part_rows, :], axis=1, keepdims=True)
        cross_col[part_rows, :] = jnp.broadcast_to(cross, (step, LANES))
        begin(p)

    reduce_rows(place, timeline, part, (far, near, mate), reduce_sems, owner, RATE)
    for p in range(PIECES):
        timeline.add(3.0 + RATE * (PIECES + 1 + p), functools.partial(forward, p))
    block = pl.ds(pl.multiple_of(place.t * rows, rows), rows)
    keep = pltpu.make_async_copy(low, top_all.at[block, :], local.at[0])
    timeline.add(3.0 + RATE * PIECES, keep.start)
    timeline.add(LATE, keep.wait)
    timeline.add(LATE, finish)
    per_row_steps(
        place, timeline, scale_row, cross_col, stage, row_land, per_row, row_sems, inner_all,
        3.0 + RATE * PIECES,
    )
    weight_scatter(place, timeline, grads, outs, lands, sems, bc_land, bc_sum, share_sems)
    timeline.run()


def turn_layer(line, inner_all, part, before, state, gain, raw, scale_row, grads):
    rows, width = state.shape
    inner = grads[0].shape[1]
    shape = jax.ShapeDtypeStruct
    outs = [
        shape((rows, width), F32),
        shape((8, width), F32),
        shape((8, rows * TENSOR), F32),
        shape((rows * TENSOR, width), BF16),
    ] + scatter_outputs(width, inner, 2 * line)
    scratch = [pltpu.VMEM((rows, width), BF16)] * 3
    scratch += [
        pltpu.VMEM((3, 8, rows), F32),
        pltpu.VMEM((rows, LANES), F32),
        pltpu.VMEM((8, rows), F32),
        pltpu.VMEM((rows, width), BF16),
    ]
    scratch += scatter_scratch(line, width, inner)
    scratch += reduce_semaphores() + share_semaphores() + spread_semaphores()
    scratch += [pltpu.SemaphoreType.DMA((1,))]
    return call_kernel(
        functools.partial(turn_kernel, line, inner_all),
        outs,
        [IN_VMEM] * 11,
        [IN_VMEM] * 3 + [ANY] + [IN_VMEM] * 5,
        scratch,
        3,
        (part, before, state, gain, raw, scale_row, *grads),
    )


def end_kernel(line, part, before, state, gain, gnorm_top, small_a, small_b, bc_a, bc_b, *refs):
    grads, refs = refs[:5], refs[5:]
    grad_out, norm_sum, small_sum, bc_sums, refs = *refs[:4], refs[4:]
    outs, refs = refs[:5], refs[5:]
    far, near, mate = refs[:3]
    lands, bc_land, bc_sum, sems, share_sems = refs[3:21], refs[21], refs[22], refs[23:29], refs[29:31]
    refs = refs[31:]
    reduce_sems, refs = refs[:6], refs[6:]
    small_land, bc_land_sums, top_land, norm_land, norm_top, small_send, small_recv = refs
    dp = 2 * line
    bits = [1 << n for n in range(dp.bit_length() - 1)]
    place = Place(line)
    place.greet(far_bits=[bit for bit in bits if bit >= 4])
    timeline = Timeline()
    step = state.shape[0] // PIECES
    norm_sum[...] = jnp.zeros_like(norm_sum)
    norm_top[...] = gnorm_top[...]
    small_sum[0:8, :] = small_a[...]
    small_sum[8:16, :] = small_b[...]
    bc_sums[0:8, :] = bc_a[...]
    bc_sums[8:16, :] = bc_b[...]

    def owner(p, sums):
        part_rows = slice(p * step, (p + 1) * step)
        grad, column = input_gradient(
            state[part_rows, :], gain[...], before[part_rows, :], sums
        )
        grad_out[part_rows, :] = grad
        norm_sum[0:1, :] += column

    reduce_rows(place, timeline, part, (far, near, mate), reduce_sems, owner, RATE)
    weight_scatter(place, timeline, grads, outs, lands, sems, bc_land, bc_sum, share_sems)
    along = [place.partner(bit) for bit in bits]
    across = [(place.dp, place.sibling), (place.dp, place.mate)]

    def exchange(n, partner, group, start, end):
        copies = [
            remote(own, land.at[n], small_send.at[n, m], small_recv.at[n, m], partner)
            for m, own, land in group
        ]

        def send():
            for copy in copies:
                copy.start()

        def take():
            for copy, (_, own, land) in zip(copies, group):
                copy.wait()
                own[...] += land[n]

        timeline.add(start, send)
        timeline.add(end, take)

    early = -1.5
    for n, partner in enumerate(along + across):
        group = [(0, bc_sums, bc_land_sums), (1, norm_top, top_land)]
        if n < len(bits):
            group.append((2, small_sum, small_land))
        later = 3.0 if n == 0 else early + 5.0
        exchange(n, partner, group, early, later)
        early = later + 0.01
    late = 4.0 + RATE * PIECES
    for n, partner in list(enumerate(along + across))[::-1]:
        later = late + (3.5 if n >= len(bits) else 16.0)
        exchange(n, partner, [(3, norm_sum, norm_land)], late, later)
        late = later + 0.01
    timeline.add(LATE + 1, lambda: norm_sum.__setitem__((slice(1, 2), slice(None)), norm_top[0:1, :]))
    timeline.run()


def end_layer(line, part, before, state, gain, gnorm_top, smalls, grads):
    rows, width = state.shape
    inner = grads[0].shape[1]
    shape = jax.ShapeDtypeStruct
    dp = 2 * line
    steps = dp.bit_length() - 1
    outs = [
        shape((rows, width), F32),
        shape((8, width), F32),
        shape((16, inner), F32),
        shape((16, 2 * N), F32),
    ] + scatter_outputs(width, inner, dp)
    scratch = [pltpu.VMEM((rows, width), BF16)] * 3 + scatter_scratch(line, width, inner)
    scratch += reduce_semaphores()
    scratch += [
        pltpu.VMEM((steps, 16, inner), F32),
        pltpu.VMEM((steps + 2, 16, 2 * N), F32),
        pltpu.VMEM((steps + 2, 8, width), F32),
        pltpu.VMEM((steps + 2, 8, width), F32),
        pltpu.VMEM((8, width), F32),
        pltpu.SemaphoreType.DMA((steps + 2, 4)),
        pltpu.SemaphoreType.DMA((steps + 2, 4)),
    ]
    return call_kernel(
        functools.partial(end_kernel, line),
        outs,
        [IN_VMEM] * 14,
        [IN_VMEM] * 9,
        scratch,
        4,
        (part, before, state, gain, gnorm_top, *smalls, *grads),
    )


def contract(left, right):
    return lax.dot_general(
        left, right, (((0,), (0,)), ((), ())), preferred_element_type=F32
    ).astype(BF16)


def on_device(
    resid,
    segment_ids,
    cotangent,
    w_z,
    w_x,
    w_bc,
    w_dt,
    w_out,
    norm_gain,
    conv_x,
    conv_bc,
    a_log,
    dt_bias,
    d_skip,
    gated_gain,
):
    dp = lax.axis_size("dp")
    assert lax.axis_size("tensor") == TENSOR and segment_ids.shape[0] == LEN and a_log.shape[0] == 2
    line = dp // 2
    heads = a_log.shape[1]
    inner = heads * P_SIZE
    inner_all = inner * TENSOR
    width = resid.shape[1]
    aux, segrow = row_masks(segment_ids)
    spread = head_spread(inner)
    args = [
        layer_parameters(layer, conv_x, conv_bc, a_log, dt_bias, d_skip, gated_gain)
        for layer in range(2)
    ]
    own = [
        (
            w_z[layer],
            w_x[layer],
            jnp.transpose(w_out[layer]),
            jnp.pad(w_dt[layer], ((0, 0), (0, LANES - heads))),
            w_bc[layer],
        )
        for layer in range(2)
    ]
    gains = [norm_gain[layer : layer + 1] for layer in range(2)]

    def arranged(gathered):
        gate, inner_w, out_w, step_w, shared_w = gathered
        return gate, inner_w, shared_w.reshape(width, 2 * N), step_w, out_w

    *gathered, rows_low, top_high = start_layer(line, resid, cotangent, gains[0], own[0])
    weights_low = arranged(gathered)
    results = middle_layer(
        line, inner_all, rows_low, weights_low, args[0], aux, segrow, resid, gains[1], own[1]
    )
    saved_low = results[:8]
    state, raw, scale_row, rows_high, *gathered = results[8:]
    weights_high = arranged(gathered)
    part, sq, *saved_high = forward_layer(rows_high, weights_high, args[1], aux, segrow)
    hidden, per_row = top_layer(line, inner_all, part, sq, state, cotangent)

    def weight_grads(rows_all, top_all, pulled):
        ggate, ginner, gstep, gshared, outlow = pulled
        return (
            contract(top_all, outlow),
            contract(rows_all, ggate),
            contract(rows_all, ginner),
            contract(rows_all, gstep),
            contract(rows_all, gshared).reshape(dp, TENSOR, width // (dp * TENSOR), 2 * N),
        )

    part, *pulled, small_high, bc_high = backward_layer(
        top_high, per_row, saved_high, weights_high, args[1], spread, aux, segrow
    )
    grads = weight_grads(rows_high, top_high, pulled)
    grad_state, gnorm_high, per_row, top_low, *grads_high = turn_layer(
        line, inner_all, part, cotangent, state, gains[1], raw, scale_row, grads
    )
    part, *pulled, small_low, bc_low = backward_layer(
        top_low, per_row, saved_low, weights_low, args[0], spread, aux, segrow
    )
    grads = weight_grads(rows_low, top_low, pulled)
    grad_resid, norm_sum, small, small_bc, *grads_low = end_layer(
        line,
        part,
        grad_state,
        resid.astype(F32),
        gains[0],
        gnorm_high,
        (small_low, small_high, bc_low, bc_high),
        grads,
    )
    gout, gz, gx, gdt, gbc = [
        jnp.stack([low, high]) for low, high in zip(grads_low, grads_high)
    ]
    small = small.reshape(2, 8, inner)
    return (
        hidden,
        grad_resid,
        gz,
        gx,
        gbc,
        gdt[:, :, :heads],
        jnp.swapaxes(gout, 1, 2),
        norm_sum[:2],
        small[:, :TAPS],
        small_bc.reshape(2, 8, 2 * N)[:, :TAPS],
        small[:, 6, :heads],
        small[:, 7, :heads],
        jnp.sum(small[:, 5].reshape(2, heads, P_SIZE), axis=2),
        small[:, 4],
    )


def solution(mesh):
    rows = P(("dp", "tensor"), None)
    matrix = P(None, "dp", "tensor")
    shared = P(None, ("dp", "tensor"), None)
    wide = P(None, None, "tensor")
    head = P(None, "tensor")
    out = P(None, "tensor", "dp")
    return jax.shard_map(
        on_device,
        mesh=mesh,
        in_specs=(
            rows, P("dp"), rows, matrix, matrix, shared, matrix, out, P(), wide, P(), head, head, head, head,
        ),
        out_specs=(
            rows, rows, matrix, matrix, shared, matrix, out, P(), wide, P(), head, head, head, head,
        ),
        check_vma=False,
    )
```

```python
import functools
import heapq
import itertools

import jax
import jax.numpy as jnp
from jax import lax
from jax.experimental import pallas as pl
from jax.experimental.pallas import tpu as pltpu
from jax.sharding import PartitionSpec as P

P_SIZE = 64
N = 128
LEN = 1024
CHUNK = 256
LANES = 128
TAPS = 4

highest = lax.Precision.HIGHEST
epsilon = 1e-05
F32 = jnp.float32
BF16 = jnp.bfloat16


def mm(left, right):
    return jnp.dot(left, right, preferred_element_type=F32)


def mm_nt(left, right):
    return lax.dot_general(left, right, (((1,), (1,)), ((), ())), preferred_element_type=F32)


def sigmoid(values):
    return 1.0 / (1.0 + jnp.exp(-values))


def softplus(values):
    return jnp.maximum(values, 0.0) + jnp.log1p(jnp.exp(-jnp.abs(values)))


def iota2(shape, dim):
    return lax.broadcasted_iota(jnp.int32, shape, dim)


def pair_of(columns, head):
    shape = (columns.shape[0], LANES)
    first = jnp.broadcast_to(columns[:, head : head + 1], shape)
    second = jnp.broadcast_to(columns[:, head + 1 : head + 2], shape)
    return jnp.where(iota2(shape, 1) < P_SIZE, first, second)


def head_sums(values, spread):
    high = values.astype(BF16)
    low = (values - high.astype(F32)).astype(BF16)
    return mm(high, spread) + mm(low, spread)


def decays(step_pre, rate, aux):
    step = softplus(step_pre)
    order = (iota2((CHUNK, CHUNK), 0) >= iota2((CHUNK, CHUNK), 1)).astype(F32)
    cum = jnp.dot(order, step * rate, precision=highest, preferred_element_type=F32)
    last = cum[CHUNK - 1 : CHUNK, :]
    decay_in = jnp.exp(cum) * aux[:, 4:5]
    decay_out = jnp.exp(last - cum) * aux[:, 5:6]
    decay_pass = jnp.exp(last) * aux[0:1, 6:7]
    return step, cum, decay_in, decay_out, decay_pass


def forward_kernel(
    rows_ref,
    wz_ref,
    wx_ref,
    wbc_ref,
    wdt_ref,
    wout_ref,
    convx_ref,
    convbc_ref,
    heads_ref,
    wide_ref,
    aux_ref,
    segrow_ref,
    part_ref,
    sq_ref,
    gate_ref,
    iraw_ref,
    iconv_ref,
    sraw_ref,
    sconv_ref,
    step_ref,
    mixed_ref,
    sin_ref,
    ext_x,
    ext_bc,
    state,
    gg_ref,
    hook=None,
):
    inner = wx_ref.shape[1]
    hook = hook or (lambda slot: None)

    @pl.when(pl.program_id(0) == 0)
    def _():
        state[...] = jnp.zeros_like(state)
        ext_x[0:8, :] = jnp.zeros((8, inner), F32)
        ext_bc[0:8, :] = jnp.zeros((8, 2 * N), F32)

    hook(0)
    rows = rows_ref[...]
    aux = aux_ref[...]
    rate = heads_ref[1:2, :]
    shared = mm(rows, wbc_ref[...])
    sraw_ref[...] = shared
    ext_bc[8 : 8 + CHUNK, :] = shared
    shared_conv = convbc_ref[TAPS - 1 : TAPS, :] * shared
    for j in range(1, TAPS):
        shared_conv = shared_conv + convbc_ref[TAPS - 1 - j : TAPS - j, :] * (
            ext_bc[8 - j : 8 - j + CHUNK, :] * aux[:, j : j + 1]
        )
    sconv_ref[...] = shared_conv
    ext_bc[0:8, :] = ext_bc[CHUNK : CHUNK + 8, :]
    shared_act = shared_conv * sigmoid(shared_conv)
    keys = shared_act[:, :N].astype(BF16)
    keys_t = jnp.transpose(shared_act[:, :N]).astype(BF16)
    query = shared_act[:, N:].astype(BF16)
    visible = (aux[:, 15:16] == segrow_ref[0:1, :]) & (
        iota2((CHUNK, CHUNK), 0) >= iota2((CHUNK, CHUNK), 1)
    )
    coupling = jnp.where(visible, mm_nt(query, keys), 0.0)
    step_raw = mm(rows, wdt_ref[...])
    step_ref[...] = step_raw
    step, cum, decay_in, decay_out, decay_pass = decays(
        step_raw + heads_ref[0:1, :], rate, aux
    )
    cum_t = jnp.transpose(cum)
    ext_x[8 : 8 + CHUNK, :] = mm(rows, wx_ref[...])
    gate_ref[...] = mm(rows, wz_ref[...])
    hook(1)
    squares = jnp.zeros((CHUNK, LANES), F32)
    half = iota2((CHUNK, LANES), 1) < P_SIZE
    for pair in range(inner // LANES):
        cols = slice(pair * LANES, (pair + 1) * LANES)
        head = 2 * pair
        raw = ext_x[8 : 8 + CHUNK, cols]
        iraw_ref[:, cols] = raw.astype(BF16)
        conv = convx_ref[TAPS - 1 : TAPS, cols] * raw
        for j in range(1, TAPS):
            conv = conv + convx_ref[TAPS - 1 - j : TAPS - j, cols] * (
                ext_x[8 - j : 8 - j + CHUNK, cols] * aux[:, j : j + 1]
            )
        iconv_ref[:, cols] = conv
        ext_x[0:8, cols] = ext_x[CHUNK : CHUNK + 8, cols]
        act = conv * sigmoid(conv)
        scaled = (act * pair_of(step, head)).astype(BF16)
        parts = []
        for one in (head, head + 1):
            gap = cum[:, one : one + 1] - cum_t[one : one + 1, :]
            weights = (coupling * jnp.exp(jnp.minimum(gap, 0.0))).astype(BF16)
            parts.append(mm(weights, scaled))
        before = state[:, cols]
        sin_ref[0, :, cols] = before
        mixed = jnp.where(half, parts[0], parts[1])
        mixed = mixed + pair_of(decay_in, head) * mm(query, before.astype(BF16))
        mixed_ref[:, cols] = mixed
        leaving = (scaled.astype(F32) * pair_of(decay_out, head)).astype(BF16)
        state[:, cols] = pair_of(decay_pass, head) * before + mm(keys_t, leaving)
        gate = gate_ref[:, cols]
        gated = (mixed + wide_ref[0:1, cols] * act) * (gate * sigmoid(gate))
        squares = squares + gated * gated
        gg_ref[:, cols] = (gated * wide_ref[1:2, cols]).astype(BF16)
        hook(2 + pair)
    total = jnp.sum(squares, axis=1, keepdims=True)
    sq_ref[...] = jnp.transpose(jnp.broadcast_to(total, (CHUNK, LANES)))[0:8, :]
    part_ref[...] = mm_nt(gg_ref[...], wout_ref[...]).astype(BF16)


def gate_back_kernel(
    top_ref,
    sc_ref,
    gate_ref,
    iconv_ref,
    mixed_ref,
    wout_ref,
    wide_ref,
    ggate_ref,
    gout_ref,
    outlow_ref,
    small_ref,
    gno_ref,
):
    inner = wout_ref.shape[1]

    @pl.when(pl.program_id(0) == 0)
    def _():
        small_ref[...] = jnp.zeros_like(small_ref)

    gno_ref[...] = mm(top_ref[...], wout_ref[...])
    per_row = jnp.transpose(sc_ref[...])
    scale = per_row[:, 0:1]
    coef = per_row[:, 1:2]
    for pair in range(inner // LANES):
        cols = slice(pair * LANES, (pair + 1) * LANES)
        gain = wide_ref[1:2, cols]
        conv = iconv_ref[:, cols]
        act = conv * sigmoid(conv)
        gate = gate_ref[:, cols]
        gate_sig = sigmoid(gate)
        gate_act = gate * gate_sig
        full = mixed_ref[:, cols] + wide_ref[0:1, cols] * act
        gated = full * gate_act
        gno = gno_ref[:, cols]
        gated_scaled = gated * scale
        small_ref[4:5, cols] += jnp.sum(gno * gated_scaled, axis=0, keepdims=True)
        outlow_ref[:, cols] = (gated_scaled * gain).astype(BF16)
        ggated = scale * (gno * gain) - gated * coef
        gout_low = (ggated * gate_act).astype(BF16)
        gout_ref[:, cols] = gout_low
        ggate_ref[:, cols] = (
            ggated * full * (gate_sig * (1.0 + gate * (1.0 - gate_sig)))
        ).astype(BF16)
        small_ref[5:6, cols] += jnp.sum(gout_low.astype(F32) * act, axis=0, keepdims=True)


def gate_back(top_all, per_row, saved, weight_out, wide):
    length, width = top_all.shape
    inner = weight_out.shape[1]
    gate, iconv, mixed = saved[0], saved[2], saved[6]
    shape = jax.ShapeDtypeStruct
    return pl.pallas_call(
        gate_back_kernel,
        grid=(length // CHUNK,),
        in_specs=[block_rows(width), pl.BlockSpec((8, CHUNK), lambda i: (0, i))]
        + [block_rows(inner)] * 3
        + [whole_spec(weight_out.shape), whole_spec(wide.shape)],
        out_specs=[block_rows(inner)] * 3 + [pl.BlockSpec((8, inner), lambda i: (0, 0))],
        out_shape=[shape((length, inner), BF16)] * 3 + [shape((8, inner), F32)],
        scratch_shapes=[pltpu.VMEM((CHUNK, inner), F32)],
        compiler_params=pltpu.CompilerParams(
            dimension_semantics=("arbitrary",), vmem_limit_bytes=VMEM_LIMIT
        ),
    )(top_all, per_row, gate, iconv, mixed, weight_out, wide)


def mix_back_kernel(
    iraw_ref,
    iconv_ref,
    sraw_ref,
    sconv_ref,
    step_ref,
    mixed_ref,
    sin_ref,
    sout_ref,
    ggate_ref,
    gout_ref,
    wz_ref,
    wx_ref,
    wbc_ref,
    wdt_ref,
    convx_ref,
    convbc_ref,
    heads_ref,
    wide_ref,
    spread_ref,
    aux_ref,
    segrow_ref,
    part_ref,
    ginner_ref,
    gstep_ref,
    gshared_ref,
    small_ref,
    smallbc_ref,
    gext_x,
    gext_bc,
    dstate,
    balance,
    direct,
    edge,
    dcoup,
    hook,
):
    inner = wx_ref.shape[1]

    @pl.when(pl.program_id(0) == 0)
    def _():
        dstate[...] = jnp.zeros_like(dstate)
        gext_x[CHUNK : CHUNK + 8, :] = jnp.zeros((8, inner), F32)
        gext_bc[CHUNK : CHUNK + 8, :] = jnp.zeros((8, 2 * N), F32)
        small_ref[...] = jnp.zeros_like(small_ref)
        smallbc_ref[...] = jnp.zeros_like(smallbc_ref)
        edge[...] = jnp.zeros_like(edge)

    hook(0)
    aux = aux_ref[...]
    rate = heads_ref[1:2, :]
    step_pre = step_ref[...] + heads_ref[0:1, :]
    step, cum, decay_in, decay_out, decay_pass = decays(step_pre, rate, aux)
    cum_t = jnp.transpose(cum)
    shared_conv = sconv_ref[...]
    shared_sig = sigmoid(shared_conv)
    shared_act = shared_conv * shared_sig
    keys = shared_act[:, :N].astype(BF16)
    query = shared_act[:, N:].astype(BF16)
    query_t = jnp.transpose(shared_act[:, N:]).astype(BF16)
    visible = (aux[:, 15:16] == segrow_ref[0:1, :]) & (
        iota2((CHUNK, CHUNK), 0) <= iota2((CHUNK, CHUNK), 1)
    )
    coupling = jnp.where(visible, mm_nt(keys, query), 0.0)
    half = iota2((CHUNK, LANES), 1) < P_SIZE
    dcoup[...] = jnp.zeros_like(dcoup)
    dkeys = jnp.zeros((CHUNK, N), F32)
    dquery = jnp.zeros((CHUNK, N), F32)
    for pair in range(inner // LANES):
        cols = slice(pair * LANES, (pair + 1) * LANES)
        head = 2 * pair
        skip = wide_ref[0:1, cols]
        conv = iconv_ref[:, cols]
        conv_sig = sigmoid(conv)
        act = conv * conv_sig
        step_pair = pair_of(step, head)
        scaled = (act * step_pair).astype(BF16)
        gout_low = gout_ref[:, cols]
        gout = gout_low.astype(F32)
        zero = jnp.zeros_like(gout)
        parts = []
        for one, own in (
            (head, jnp.where(half, gout, zero).astype(BF16)),
            (head + 1, jnp.where(half, zero, gout).astype(BF16)),
        ):
            gap = cum_t[one : one + 1, :] - cum[:, one : one + 1]
            decay = jnp.exp(jnp.minimum(gap, 0.0))
            weights = (coupling * decay).astype(BF16)
            parts.append(mm(weights, gout_low))
            dcoup[...] += mm_nt(scaled, own) * decay
        after = dstate[:, cols]
        after_low = after.astype(BF16)
        out_pair = pair_of(decay_out, head)
        gscaled = jnp.where(half, parts[0], parts[1]) + out_pair * mm(keys, after_low)
        scaled_wide = scaled.astype(F32)
        dkeys = dkeys + mm_nt((scaled_wide * out_pair).astype(BF16), after_low)
        entering = (gout * pair_of(decay_in, head)).astype(BF16)
        dquery = dquery + mm_nt(entering, sin_ref[0, :, cols].astype(BF16))
        edge[0:1, cols] = jnp.sum(sout_ref[0, :, cols] * after, axis=0, keepdims=True)
        dstate[:, cols] = pair_of(decay_pass, head) * after + mm(query_t, entering)
        balance[:, cols] = gout * mixed_ref[:, cols] - scaled_wide * gscaled
        direct[:, cols] = act * gscaled
        gact = step_pair * gscaled + skip * gout
        gext_x[0:CHUNK, cols] = gact * (conv_sig * (1.0 + conv * (1.0 - conv_sig)))
        raw = iraw_ref[:, cols].astype(F32)
        gconv = gext_x[0:CHUNK, cols]
        graw = convx_ref[TAPS - 1 : TAPS, cols] * gconv
        small_ref[TAPS - 1 : TAPS, cols] += jnp.sum(raw * gconv, axis=0, keepdims=True)
        for j in range(1, TAPS):
            moved = gext_x[j : j + CHUNK, cols] * aux[:, 8 + j : 9 + j]
            graw = graw + convx_ref[TAPS - 1 - j : TAPS - j, cols] * moved
            small_ref[TAPS - 1 - j : TAPS - j, cols] += jnp.sum(
                raw * moved, axis=0, keepdims=True
            )
        ginner_ref[:, cols] = graw.astype(BF16)
        gext_x[CHUNK : CHUNK + 8, cols] = gext_x[0:8, cols]
        hook(1 + pair)
    spread = spread_ref[...]
    order = (iota2((CHUNK, CHUNK), 0) <= iota2((CHUNK, CHUNK), 1)).astype(F32)
    running = jnp.dot(
        order, head_sums(balance[...], spread), precision=highest, preferred_element_type=F32
    )
    running = running + head_sums(edge[...], spread)[0:1, :]
    gstep = (head_sums(direct[...], spread) + running * rate) * sigmoid(step_pre)
    small_ref[6:7, 0:LANES] += rate * jnp.sum(running * step, axis=0, keepdims=True)
    small_ref[7:8, 0:LANES] += jnp.sum(gstep, axis=0, keepdims=True)
    gstep_ref[...] = gstep.astype(BF16)
    dcoupling = jnp.where(visible, dcoup[...], 0.0)
    dkeys = dkeys + mm(dcoupling.astype(BF16), query)
    dquery = dquery + mm(jnp.transpose(dcoupling).astype(BF16), keys)
    slope = shared_sig * (1.0 + shared_conv * (1.0 - shared_sig))
    gext_bc[0:CHUNK, 0:N] = dkeys * slope[:, :N]
    gext_bc[0:CHUNK, N : 2 * N] = dquery * slope[:, N:]
    raw = sraw_ref[...]
    gconv = gext_bc[0:CHUNK, :]
    graw = convbc_ref[TAPS - 1 : TAPS, :] * gconv
    smallbc_ref[TAPS - 1 : TAPS, :] += jnp.sum(raw * gconv, axis=0, keepdims=True)
    for j in range(1, TAPS):
        moved = gext_bc[j : j + CHUNK, :] * aux[:, 8 + j : 9 + j]
        graw = graw + convbc_ref[TAPS - 1 - j : TAPS - j, :] * moved
        smallbc_ref[TAPS - 1 - j : TAPS - j, :] += jnp.sum(raw * moved, axis=0, keepdims=True)
    gshared_ref[...] = graw.astype(BF16)
    gext_bc[CHUNK : CHUNK + 8, :] = gext_bc[0:8, :]
    hook(7)
    total = mm_nt(ggate_ref[...], wz_ref[...]) + mm_nt(ginner_ref[...], wx_ref[...])
    total = total + mm_nt(gstep_ref[...], wdt_ref[...])
    part_ref[...] = (total + mm_nt(gshared_ref[...], wbc_ref[...])).astype(BF16)


def whole_spec(shape):
    zeros = (0,) * len(shape)
    return pl.BlockSpec(shape, lambda i: zeros, pipeline_mode=pl.Buffered(1))


VMEM_LIMIT = 62 * 1024 * 1024


def block_rows(cols):
    return pl.BlockSpec((CHUNK, cols), lambda i: (i, 0))


def forward_in_specs(rows_all, weights, layer_args):
    return (
        [block_rows(rows_all.shape[1])]
        + [whole_spec(w.shape) for w in weights]
        + [whole_spec(w.shape) for w in layer_args]
        + [block_rows(LANES), pl.BlockSpec((8, CHUNK), lambda i: (0, i))]
    )


def saved_specs(inner):
    return [
        block_rows(inner),
        block_rows(inner),
        block_rows(inner),
        block_rows(2 * N),
        block_rows(2 * N),
        block_rows(LANES),
        block_rows(inner),
        pl.BlockSpec((1, N, inner), lambda i: (i, 0, 0)),
    ]


def saved_shapes(length, inner):
    shape = jax.ShapeDtypeStruct
    return [
        shape((length, inner), F32),
        shape((length, inner), BF16),
        shape((length, inner), F32),
        shape((length, 2 * N), F32),
        shape((length, 2 * N), F32),
        shape((length, LANES), F32),
        shape((length, inner), F32),
        shape((length // CHUNK, N, inner), F32),
    ]


def forward_scratch(inner):
    return [
        pltpu.VMEM((CHUNK + 8, inner), F32),
        pltpu.VMEM((CHUNK + 8, 2 * N), F32),
        pltpu.VMEM((N, inner), F32),
        pltpu.VMEM((CHUNK, inner), BF16),
    ]


def forward_layer(rows_all, weights, layer_args, aux, segrow):
    length, width = rows_all.shape
    inner = weights[1].shape[1]
    shape = jax.ShapeDtypeStruct
    return pl.pallas_call(
        forward_kernel,
        grid=(length // CHUNK,),
        in_specs=forward_in_specs(rows_all, weights, layer_args),
        out_specs=[block_rows(width), pl.BlockSpec((8, CHUNK), lambda i: (0, i))]
        + saved_specs(inner),
        out_shape=[shape((length, width), BF16), shape((8, length), F32)]
        + saved_shapes(length, inner),
        scratch_shapes=forward_scratch(inner),
        compiler_params=pltpu.CompilerParams(
            dimension_semantics=("arbitrary",), vmem_limit_bytes=VMEM_LIMIT
        ),
        cost_estimate=pl.CostEstimate(
            flops=length * width * inner * 7, bytes_accessed=40_000_000, transcendentals=8_000_000
        ),
    )(rows_all, *weights, *layer_args, aux, segrow)


def mix_back_specs(chunks, inner, weights, layer_args, spread):
    last = chunks - 1

    def turned(cols):
        return pl.BlockSpec((CHUNK, cols), lambda i: (last - i, 0))

    return (
        [
            turned(inner),
            turned(inner),
            turned(2 * N),
            turned(2 * N),
            turned(LANES),
            turned(inner),
            pl.BlockSpec((1, N, inner), lambda i: (last - i, 0, 0)),
            pl.BlockSpec((1, N, inner), lambda i: (jnp.minimum(chunks - i, last), 0, 0)),
            turned(inner),
            turned(inner),
        ]
        + [whole_spec(w.shape) for w in weights]
        + [whole_spec(w.shape) for w in layer_args]
        + [
            whole_spec(spread.shape),
            turned(LANES),
            pl.BlockSpec((8, CHUNK), lambda i: (0, last - i)),
        ]
    )


def mix_back_scratch(inner):
    return [
        pltpu.VMEM((CHUNK + 8, inner), F32),
        pltpu.VMEM((CHUNK + 8, 2 * N), F32),
        pltpu.VMEM((N, inner), F32),
        pltpu.VMEM((CHUNK, inner), F32),
        pltpu.VMEM((CHUNK, inner), F32),
        pltpu.VMEM((8, inner), F32),
        pltpu.VMEM((CHUNK, CHUNK), F32),
    ]


def row_masks(segment_ids):
    length = segment_ids.shape[0]
    seg = segment_ids.astype(F32)

    def shifted(j):
        return jnp.concatenate([jnp.full((j,), -1.0, F32), seg[: length - j]])

    def ahead(j):
        return jnp.concatenate([seg[j:], jnp.full((j,), -1.0, F32)])

    ends = seg[CHUNK - 1 :: CHUNK]
    own_end = jnp.repeat(ends, CHUNK)
    old_end = jnp.repeat(jnp.concatenate([jnp.full((1,), -1.0, F32), ends[:-1]]), CHUNK)
    lanes = [jnp.zeros_like(seg)] * 16
    for j in range(1, TAPS):
        lanes[j] = (shifted(j) == seg).astype(F32)
        lanes[8 + j] = (ahead(j) == seg).astype(F32)
    lanes[4] = (old_end == seg).astype(F32)
    lanes[5] = (own_end == seg).astype(F32)
    lanes[6] = (own_end == old_end).astype(F32)
    lanes[15] = seg
    aux = jnp.pad(jnp.stack(lanes, axis=1), ((0, 0), (0, LANES - 16)))
    return aux, jnp.broadcast_to(seg[None, :], (8, length))


def layer_parameters(layer, conv_x, conv_bc, a_log, dt_bias, d_skip, gated_gain):
    heads = a_log.shape[1]
    pad = ((0, 0), (0, LANES - heads))
    head_rows = jnp.pad(jnp.stack([dt_bias[layer], -jnp.exp(a_log[layer])]), pad)
    wide = jnp.stack([jnp.repeat(d_skip[layer], P_SIZE), gated_gain[layer]])
    return (conv_x[layer], conv_bc[layer], head_rows, wide)


def head_spread(inner):
    return (
        jnp.arange(inner)[:, None] // P_SIZE == jnp.arange(LANES)[None, :]
    ).astype(BF16)


MESH = pl.DeviceIdType.MESH
ANY = pl.BlockSpec(memory_space=pl.ANY)
IN_VMEM = pl.BlockSpec(memory_space=pltpu.VMEM)
PIECES = 4
TENSOR = 4
LATE = 1e9
LAG = 8.0
BIG = 6.5
SMALL = 1.1


class Place:
    def __init__(self, line):
        self.line = line
        dp, t = lax.axis_index("dp"), lax.axis_index("tensor")
        self.dp, self.t = dp, t
        self.z, self.x = lax.div(dp, 2), lax.rem(dp, 2)
        self.other = 1 - self.x
        self.sibling = t + 1 - 2 * lax.rem(t, 2)
        self.mate = lax.rem(t + 2, TENSOR)
        self.diagonal = TENSOR - 1 - t
        self.right = (lax.rem(self.z + 1, line) * 2 + self.x, t)
        self.left = (lax.rem(self.z + line - 1, line) * 2 + self.x, t)
        self.across = (self.z * 2 + self.other, t)

    def tensor_peers(self):
        return [(self.dp, self.sibling), (self.dp, self.mate), (self.dp, self.diagonal)]

    def partner(self, bit):
        return (self.dp + bit - 2 * bit * lax.rem(lax.div(self.dp, bit), 2), self.t)

    def greet(self, across=True, far_bits=()):
        barrier = pltpu.get_barrier_semaphore()
        peers = self.tensor_peers()
        if across:
            peers = peers + [self.across]
        peers = peers + [self.partner(bit) for bit in far_bits]
        for peer in peers:
            pl.semaphore_signal(barrier, inc=1, device_id=peer, device_id_type=MESH)
        count = len(peers)
        if across and self.line > 1:
            has_right = self.z < self.line - 1
            has_left = self.z > 0

            @pl.when(has_right)
            def _():
                pl.semaphore_signal(barrier, inc=1, device_id=self.right, device_id_type=MESH)

            @pl.when(has_left)
            def _():
                pl.semaphore_signal(barrier, inc=1, device_id=self.left, device_id_type=MESH)

            count = count + has_right.astype(jnp.int32) + has_left.astype(jnp.int32)
        pl.semaphore_wait(barrier, count)


class Timeline:
    def __init__(self):
        self.steps = []
        self.rolling = []

    def follow(self, slot, step):
        self.rolling.append((slot, step))

    def add(self, when, step):
        self.steps.append((when, len(self.steps), step))

    def ordered(self):
        return sorted(self.steps, key=lambda entry: entry[:2])

    def run(self):
        for _, _, step in self.ordered():
            step()

    def spread(self, chunks, slots, chunk_us, order=lambda k: k):
        places = {}
        for slot, step in self.rolling:
            for k in range(chunks):
                if (k + 1) * slots + slot >= chunks * slots:
                    when = ((k + 1) * slots + slot) * chunk_us / slots + (LAG if slot > 3 else 0.0)
                    self.add(when, functools.partial(step, order(k)))
        after = []
        for when, _, step in self.ordered():
            spot = max(0, int(when / chunk_us * slots))
            if spot < chunks * slots:
                places.setdefault((spot % slots, spot // slots), []).append(step)
            else:
                after.append(step)
        now = pl.program_id(0)

        def hook(slot):
            for chunk in range(chunks):
                steps = places.get((slot, chunk))
                if steps:

                    @pl.when(now == chunk)
                    def _(steps=steps):
                        for step in steps:
                            step()

            for offset, step in self.rolling:
                if offset % slots == slot:
                    lag = 1 + offset // slots
                    step(jnp.where(now >= lag, order(now - lag), -1))

        def end():
            @pl.when(now == chunks - 1)
            def _():
                for step in after:
                    step()

        return hook, end


def remote(src, dst, send, recv, device):
    return pltpu.make_async_remote_copy(
        src_ref=src, dst_ref=dst, send_sem=send, recv_sem=recv, device_id=device, device_id_type=MESH
    )


def gather_semaphores(count, line):
    return [pltpu.SemaphoreType.DMA((count, 2, line))] * 5


HOP_US = 0.8
ADD_US = 0.5


def plan_gather(items, line):
    free, plan = {}, {}
    queue, count = [], itertools.count()

    def push(when, *action):
        heapq.heappush(queue, (when, next(count), action))

    def transfer(link, when, cost):
        begin = max(when, free.get(link, 0.0))
        free[link] = begin + cost
        return begin + cost + HOP_US

    def note(step, when):
        plan[step] = max(plan.get(step, 0.0), when)

    def along(when, way, z, i, source, xs):
        stop = z + 1 if way == 0 else z - 1
        if 0 <= stop < line:
            push(transfer((way, z), when, items[i][1]), "hop", way, stop, i, source, xs)

    def cross(when, z, i, source):
        push(transfer(("x", z), when, items[i][1]), "side", z, i, source)

    for i, (_, _, ready) in enumerate(items):
        push(ready, "own", i)
    while queue:
        when, _, (kind, *rest) = heapq.heappop(queue)
        if kind == "own":
            (i,) = rest
            for z in range(line):
                along(when, 0, z, i, z, 0)
                along(when, 1, z, i, z, 0)
                cross(when, z, i, z)
        elif kind == "hop":
            way, z, i, source, xs = rest
            note(("hop", i, way, abs(z - source), xs), when)
            along(when, way, z, i, source, xs)
            if items[i][0] == "zx":
                cross(when, z, i, source)
        else:
            z, i, source = rest
            note(("side", i), when)
            if items[i][0] == "xz":
                along(when, 0, z, i, source, 1)
                along(when, 1, z, i, source, 1)
    return plan


def gather_weights(place, timeline, items, sems):
    send_r, send_l, send_x, recv_z, recv_x = sems
    line = place.line
    z = place.z

    def copy(i, way, zz, xs, src=None):
        dst = items[i][1](zz, xs)
        return remote(
            dst if src is None else src,
            dst,
            (send_r, send_l, send_x)[way].at[i, xs, zz],
            (recv_x if way == 2 else recv_z).at[i, xs, zz],
            (place.right, place.left, place.across)[way],
        )

    def begin(i):
        own = items[i][0]

        def step():
            @pl.when(z < line - 1)
            def _():
                copy(i, 0, z, place.x, own).start()

            @pl.when(z > 0)
            def _():
                copy(i, 1, z, place.x, own).start()

            copy(i, 2, z, place.x, own).start()

        return step

    def hop(i, way, k, xs, to_x):
        source = z - k if way == 0 else z + k
        here = source >= 0 if way == 0 else source < line
        more = z < line - 1 if way == 0 else z > 0

        def arrive():
            @pl.when(here)
            def _():
                copy(i, way, source, xs).wait_recv()
                if to_x:
                    copy(i, 2, source, xs).start()

            @pl.when(here & more)
            def _():
                copy(i, way, source, xs).start()

        def finish():
            @pl.when(here & more)
            def _():
                copy(i, way, source, xs).wait_send()

            if to_x:

                @pl.when(here)
                def _():
                    copy(i, 2, source, xs).wait_send()

        return arrive, finish

    def side(i):
        def step():
            copy(i, 2, z, place.other).wait_recv()

            @pl.when(z < line - 1)
            def _():
                copy(i, 0, z, place.other).start()

            @pl.when(z > 0)
            def _():
                copy(i, 1, z, place.other).start()

        return step

    def end(i):
        route = items[i][2]

        def step():
            for xs in (place.x,) if route == "zx" else (place.x, place.other):

                @pl.when(z < line - 1)
                def _(xs=xs):
                    copy(i, 0, z, xs).wait_send()

                @pl.when(z > 0)
                def _(xs=xs):
                    copy(i, 1, z, xs).wait_send()

            copy(i, 2, z, place.x).wait_send()

        return step

    def settle(i):
        def step():
            for zz in range(line):
                copy(i, 2, zz, place.other).wait_recv()

        return step

    plan = plan_gather([(item[2], item[3], 0.0) for item in items], line)
    for i, (_, _, route, _, early) in enumerate(items):
        timeline.add(0.0, begin(i))
        if route == "xz":
            timeline.add(plan["side", i], side(i))
        for k in range(1, line):
            for way in (0, 1):
                for column, xs in enumerate((place.x,) if route == "zx" else (place.x, place.other)):
                    arrive, finish = hop(i, way, k, xs, route == "zx")
                    timeline.add(plan["hop", i, way, k, column], arrive)
                    timeline.add(LATE, finish)
        if route == "zx":
            timeline.add(plan["side", i] + 1.0 if early else LATE, settle(i))
        timeline.add(LATE, end(i))
    return plan


def scatter_semaphores(count, line):
    return [pltpu.SemaphoreType.DMA((count, 2, line))] * 6


def add_into(target, other, rows):
    step = 48 if rows % 48 == 0 else rows

    def body(n, carry):
        part = pl.ds(pl.multiple_of(n * step, step), step)
        target[part, :] = (target[part, :].astype(F32) + other[part, :].astype(F32)).astype(BF16)
        return carry

    lax.fori_loop(0, rows // step, body, 0)


def scatter_order(line):
    order = []
    for n in range((line + 1) // 2):
        order += [n] if n == line - 1 - n else [n, line - 1 - n]
    return order


def plan_scatter(items, line):
    free, arrived, joined, plan = {}, {}, {}, {}
    queue, count = [], itertools.count()

    def push(when, *action):
        heapq.heappush(queue, (when, next(count), action))

    def transfer(link, when, cost):
        begin = max(when, free.get(link, 0.0))
        free[link] = begin + cost
        return begin + cost + HOP_US

    def note(step, when):
        plan[step] = max(plan.get(step, 0.0), when)

    def go(when, z, i, zz, xs):
        first = {"r": z == 0, "l": z == line - 1}
        if z == zz:
            need = [way for way, there in (("r", z > 0), ("l", z < line - 1)) if there]
            times = [arrived.get((way, z, i, zz, xs)) for way in need] + [joined.get((z, i, zz, xs))]
            if None in times:
                return
            when = max(times)
            if items[i][0] == "xz":
                note(("last", i), when)
                return
            note(("line", i, xs), when)
            done = joined.setdefault(("line", z, i), [])
            done.append(when)
            if len(done) == 2:
                note(("swap", i), max(done))
                note(("last", i), transfer(("x", z), max(done) + 2 * ADD_US, items[i][1]))
            return
        way = "r" if z < zz else "l"
        times = [joined.get((z, i, zz, xs))]
        if not first[way]:
            times.append(arrived.get((way, z, i, zz, xs)))
        if None in times:
            return
        when = max(times)
        h = z if way == "r" else line - 1 - z
        note(("send", i, zz, way, xs, h), when)
        stop = z + 1 if way == "r" else z - 1
        push(transfer((way, z), when + ADD_US, items[i][1]), "arrive", way, stop, i, zz, xs)

    for i, (route, cost, ready) in enumerate(items):
        for zz in scatter_order(line):
            for xs in (0,) if route == "xz" else (0, 1):
                push(ready, "start", i, zz, xs)
    while queue:
        when, _, (kind, *rest) = heapq.heappop(queue)
        if kind == "start":
            i, zz, xs = rest
            for z in range(line):
                if items[i][0] == "xz":
                    push(transfer(("x", z), when, items[i][1]), "join", z, i, zz, xs)
                else:
                    push(when, "join", z, i, zz, xs)
        elif kind == "join":
            z, i, zz, xs = rest
            if items[i][0] == "xz":
                note(("join", i, zz), when)
                when += ADD_US
            joined[z, i, zz, xs] = when
            go(when, z, i, zz, xs)
        else:
            way, z, i, zz, xs = rest
            arrived[way, z, i, zz, xs] = when
            go(when, z, i, zz, xs)
    return plan


def scatter_weights(place, timeline, items, sems):
    send_x, recv_x, send_r, recv_r, send_l, recv_l = sems
    line = place.line
    z = place.z

    def rows_of(i):
        return items[i][2][0].shape[1]

    def side(i, zz):
        _, source, (land_x, _), *_ = items[i]
        return remote(
            source(zz, place.other), land_x.at[zz], send_x.at[i, 0, zz], recv_x.at[i, 0, zz], place.across
        )

    def land_along(i, zz, way, xs, stop):
        slot = zz if way == 0 else jnp.where(stop == zz, line, zz)
        land = items[i][2][1]
        return land.at[slot, xs] if items[i][4] == "zx" else land.at[slot]

    def along(i, zz, way, xs, source=None):
        here = land_along(i, zz, way, xs, z)
        return remote(
            here if source is None else source,
            land_along(i, zz, way, xs, z + 1 if way == 0 else z - 1),
            (send_r, send_l)[way].at[i, xs, zz],
            (recv_r, recv_l)[way].at[i, xs, zz],
            (place.right, place.left)[way],
        )

    def own(i, zz, xs):
        return items[i][0](zz, xs) if items[i][4] == "zx" else items[i][2][0].at[zz]

    def outgoing(i, zz, xs):
        return items[i][1](zz, xs) if items[i][4] == "zx" else items[i][2][0].at[zz]

    def join(i, zz):
        def step():
            side(i, zz).wait_recv()
            add_into(items[i][2][0].at[zz], items[i][0](zz, place.x), rows_of(i))

        return step

    def send(i, zz, way, xs, h):
        if way == 0:
            mine = (z == h) & (z < zz)
        else:
            mine = (z == line - 1 - h) & (z > zz)

        def step():
            @pl.when(mine)
            def _():
                if h == 0:
                    along(i, zz, way, xs, outgoing(i, zz, xs)).start()
                else:
                    along(i, zz, way, xs).wait_recv()
                    add_into(land_along(i, zz, way, xs, z), own(i, zz, xs), rows_of(i))
                    along(i, zz, way, xs).start()

        return step

    def last(i):
        out = items[i][3]

        def step():
            out[...] = items[i][2][0][z].astype(F32)
            for way, there in ((0, z > 0), (1, z < line - 1)):

                @pl.when(there)
                def _(way=way):
                    along(i, z, way, 0).wait_recv()
                    out[...] += items[i][2][1][z if way == 0 else line].astype(F32)

        return step

    def swap(i):
        land_x, land = items[i][2]
        stage = land.at[z, place.other]
        return remote(stage, land_x.at[0], send_x.at[i, 0, 0], recv_x.at[i, 0, 0], place.across)

    def gather_line(i, xs):
        piece = items[i][0]

        def step():
            right, left = land_along(i, z, 0, xs, z), land_along(i, z, 1, xs, z)

            @pl.when(z > 0)
            def _():
                along(i, z, 0, xs).wait_recv()
                add_into(right, piece(z, xs), rows_of(i))

            @pl.when(z == 0)
            def _():
                right[...] = piece(z, xs)[...]

            @pl.when(z < line - 1)
            def _():
                along(i, z, 1, xs).wait_recv()
                add_into(right, left, rows_of(i))

        return step

    def swap_end(i):
        (land_x, land), out = items[i][2:4]

        def step():
            swap(i).wait()
            out[...] = land[z, place.x].astype(F32) + land_x[0].astype(F32)

        return step

    def end(i, zz, xs):
        def step():
            if items[i][4] == "xz":
                side(i, zz).wait_send()
            for way, there in ((0, z < zz), (1, z > zz)):

                @pl.when(there)
                def _(way=way):
                    along(i, zz, way, xs).wait_send()

        return step

    plan = plan_scatter([item[4:] for item in items], line)
    for i, (_, _, _, _, route, _, ready) in enumerate(items):
        columns = (0,) if route == "xz" else (0, 1)
        for zz in scatter_order(line):
            if route == "xz":
                timeline.add(ready, lambda i=i, zz=zz: side(i, zz).start())
                timeline.add(plan["join", i, zz], join(i, zz))
            for xs in columns:
                for way, name in enumerate("rl"):
                    for h in range(zz if way == 0 else line - 1 - zz):
                        timeline.add(plan["send", i, zz, name, xs, h], send(i, zz, way, xs, h))
                timeline.add(LATE, end(i, zz, xs))
        if route == "xz":
            timeline.add(plan["last", i], last(i))
            continue
        for xs in columns:
            timeline.add(plan["line", i, xs], gather_line(i, xs))
        timeline.add(plan["swap", i] + ADD_US, lambda i=i: swap(i).start())
        timeline.add(plan["last", i], swap_end(i))


def spread_semaphores():
    return [pltpu.SemaphoreType.DMA((PIECES,))] * 6


def spread_rows(place, own, whole, sems):
    send_y, recv_y, send_s, recv_s, send_f, recv_f = sems
    rows = own.shape[0]
    step = rows // PIECES

    def at(owner, p):
        return whole.at[pl.ds(pl.multiple_of(owner * rows, rows) + p * step, step), :]

    def source(p):
        return own.at[pl.ds(p * step, step), :]

    def to_mate(p):
        return remote(
            source(p), at(place.t, p), send_y.at[p], recv_y.at[p], (place.dp, place.mate)
        )

    def to_sibling(p):
        return remote(
            source(p), at(place.t, p), send_s.at[p], recv_s.at[p], (place.dp, place.sibling)
        )

    def passed_on(p):
        return remote(
            at(place.mate, p), at(place.mate, p), send_f.at[p], recv_f.at[p], (place.dp, place.sibling)
        )

    def begin(p):
        to_mate(p).start()
        to_sibling(p).start()

    def forward(p):
        to_mate(p).wait_recv()
        passed_on(p).start()

    def finish():
        for p in range(PIECES):
            to_mate(p).wait_send()
            to_sibling(p).wait()
            passed_on(p).wait()

    return begin, forward, finish


def reduce_semaphores():
    return [pltpu.SemaphoreType.DMA((PIECES,))] * 6


def reduce_rows(place, timeline, part, lands, sems, owner, rate, start=0.0):
    land_far, land_near, land_mate = lands
    send_a, recv_a, send_b, recv_b, send_z, recv_z = sems
    rows = land_far.shape[0]
    step = rows // PIECES

    def at(block, p):
        return part.at[pl.ds(pl.multiple_of(block * rows, rows) + p * step, step), :]

    def own(ref, p):
        return ref.at[pl.ds(p * step, step), :]

    def far(p):
        return remote(
            at(place.diagonal, p), own(land_far, p), send_a.at[p], recv_a.at[p], (place.dp, place.sibling)
        )

    def near(p):
        return remote(
            at(place.sibling, p), own(land_near, p), send_b.at[p], recv_b.at[p], (place.dp, place.sibling)
        )

    def over(p):
        return remote(
            own(land_far, p), own(land_mate, p), send_z.at[p], recv_z.at[p], (place.dp, place.mate)
        )

    def begin():
        for p in range(PIECES):
            far(p).start()
        for p in range(PIECES):
            near(p).start()

    def middle(p):
        def run():
            far(p).wait_recv()
            mine = own(land_far, p)
            mine[...] = (mine[...].astype(F32) + at(place.mate, p)[...].astype(F32)).astype(BF16)
            over(p).start()

        return run

    def final(p):
        def run():
            near(p).wait_recv()
            over(p).wait_recv()
            sums = at(place.t, p)[...].astype(F32) + own(land_near, p)[...].astype(F32)
            owner(p, sums + own(land_mate, p)[...].astype(F32))

        return run

    def finish():
        for p in range(PIECES):
            far(p).wait_send()
            near(p).wait_send()
            over(p).wait_send()

    timeline.add(start, begin)
    for p in range(PIECES):
        timeline.add(start + 1.0 * (p + 1), middle(p))
        timeline.add(start + 2.0 + rate * (p + 1), final(p))
    timeline.add(LATE, finish)


def roll_rows(place, timeline, part, lands, sems, owner, forward):
    land_far, land_near, land_mate = lands
    send_a, recv_a, send_b, recv_b, send_z, recv_z = sems
    rows = land_far.shape[0]
    step = rows // PIECES

    def at(block, p):
        return part.at[pl.ds(pl.multiple_of(block * rows, rows) + p * step, step), :]

    def own(ref, p):
        return ref.at[pl.ds(p * step, step), :]

    def far(p):
        return remote(
            at(place.diagonal, p), own(land_far, p), send_a.at[p], recv_a.at[p], (place.dp, place.sibling)
        )

    def near(p):
        return remote(
            at(place.sibling, p), own(land_near, p), send_b.at[p], recv_b.at[p], (place.dp, place.sibling)
        )

    def over(p):
        return remote(
            own(land_far, p), own(land_mate, p), send_z.at[p], recv_z.at[p], (place.dp, place.mate)
        )

    def begin(chunk):
        @pl.when(place.diagonal == chunk)
        def _():
            for p in range(PIECES):
                far(p).start()

        @pl.when(place.sibling == chunk)
        def _():
            for p in range(PIECES):
                near(p).start()

    def middle(p, chunk):
        @pl.when(place.mate == chunk)
        def _():
            far(p).wait_recv()
            mine = own(land_far, p)
            mine[...] = (mine[...].astype(F32) + at(place.mate, p)[...].astype(F32)).astype(BF16)
            over(p).start()

    def final(p, chunk):
        @pl.when(place.t == chunk)
        def _():
            near(p).wait_recv()
            over(p).wait_recv()
            sums = at(place.t, p)[...].astype(F32) + own(land_near, p)[...].astype(F32)
            owner(p, sums + own(land_mate, p)[...].astype(F32))

    def pass_on(p, chunk):
        @pl.when(place.mate == chunk)
        def _():
            forward(p)

    def finish():
        for p in range(PIECES):
            far(p).wait_send()
            near(p).wait_send()
            over(p).wait_send()

    timeline.follow(0, begin)
    for p in range(PIECES):
        timeline.follow(1 + p // 2, functools.partial(middle, p))
        timeline.follow(4 + 3 * p, functools.partial(final, p))
        if forward:
            timeline.follow(8 + 3 * p, functools.partial(pass_on, p))
    timeline.add(LATE, finish)


def share_semaphores():
    return [pltpu.SemaphoreType.DMA((3,))] * 2


def share_blocks(place, source_of, target_of, sems):
    send, recv = sems
    peers = (place.sibling, place.mate, place.diagonal)
    return [
        remote(source_of(peer), target_of(n), send.at[n], recv.at[n], (place.dp, peer))
        for n, peer in enumerate(peers)
    ]


def row_norm(state):
    return lax.rsqrt(jnp.mean(state * state, axis=1, keepdims=True) + epsilon)


def by_rows_piece(whole, rows, start=0, count=None):
    count = rows if count is None else count

    def piece(zz, xs):
        return whole.at[pl.ds(pl.multiple_of((zz * 2 + xs) * rows, rows) + start, count), :]

    return piece


def own_copies(place, blocks, sems):
    return [
        pltpu.make_async_copy(own, piece(place.z, place.x), sems.at[n])
        for n, (own, piece) in enumerate(blocks)
    ]


def weight_gather(place, timeline, refs, wholes, sems, share_sems, own_sems):
    bc_own, bc_all = refs[4], wholes[4]
    rows = refs[0].shape[0]
    head, tail = halves(rows)
    pieces = [by_rows_piece(whole, rows) for whole in wholes[:4]]

    def bc_piece(zz, xs):
        return bc_all.at[zz * 2 + xs, place.t]

    items = [
        (bc_own, bc_piece, "zx", SMALL / 2, True),
        (refs[3], pieces[3], "zx", SMALL, False),
        (refs[1], pieces[1], "zx", BIG, False),
        (refs[0], pieces[0], "zx", BIG, False),
        (refs[2].at[pl.ds(0, head), :], by_rows_piece(wholes[2], rows, 0, head), "xz", BIG / 2, False),
        (refs[2].at[pl.ds(head, tail), :], by_rows_piece(wholes[2], rows, head, tail), "zx", BIG / 2, False),
    ]
    copies = own_copies(place, [(item[0], item[1]) for item in items], own_sems)
    shares = share_blocks(
        place, lambda peer: bc_all.at[:, place.t], lambda n: bc_all.at[:, place.t], share_sems
    )
    timeline.add(-1.0, lambda: [copy.start() for copy in copies] and None)
    timeline.add(1.0, lambda: copies[0].wait())
    plan = gather_weights(place, timeline, items, sems)
    timeline.add(plan["side", 0] + 1.1, lambda: [copy.start() for copy in shares] and None)
    timeline.add(LATE + 1, lambda: [copy.wait() for copy in shares] and None)
    timeline.add(LATE + 1, lambda: [copy.wait() for copy in copies[1:]] and None)


def gather_outputs(line, width, inner, dp):
    shape = jax.ShapeDtypeStruct
    return [
        shape((width, inner), BF16),
        shape((width, inner), BF16),
        shape((width, inner), BF16),
        shape((width, LANES), BF16),
        shape((dp, TENSOR, width // (dp * TENSOR), 2 * N), BF16),
    ]


def gather_scratch(line):
    return gather_semaphores(6, line) + share_semaphores() + [pltpu.SemaphoreType.DMA((6,))]


def start_kernel(line, resid, cotangent, gain, *refs):
    own, wholes, refs = refs[:5], refs[5:10], refs[10:]
    rows_all, top_all, normed, low = refs[:4]
    sems, share_sems, own_sems = refs[4:9], refs[9:11], refs[11]
    rows_sems, top_sems, local = refs[12:18], refs[18:24], refs[24]
    place = Place(line)
    place.greet()
    timeline = Timeline()
    weight_gather(place, timeline, own, wholes, sems, share_sems, own_sems)
    rows = normed.shape[0]
    block = pl.ds(pl.multiple_of(place.t * rows, rows), rows)
    local_copies = [
        pltpu.make_async_copy(normed, rows_all.at[block, :], local.at[0]),
        pltpu.make_async_copy(low, top_all.at[block, :], local.at[1]),
    ]

    def prepare():
        state = resid[...].astype(F32)
        normed[...] = (state * row_norm(state) * gain[...]).astype(BF16)
        low[...] = cotangent[...].astype(BF16)
        for copy in local_copies:
            copy.start()

    timeline.add(0.5, prepare)
    for n, (source, whole, group) in enumerate(((normed, rows_all, rows_sems), (low, top_all, top_sems))):
        begin, forward, finish = spread_rows(place, source, whole, group)
        for p in range(PIECES):
            timeline.add(0.6, functools.partial(begin, p))
            timeline.add(1.0 + (4 * n + p + 1) * 4.4, functools.partial(forward, p))
        timeline.add(LATE, finish)
    timeline.add(LATE, lambda: [copy.wait() for copy in local_copies] and None)
    timeline.run()


def call_kernel(kernel, outs, in_specs, out_specs, scratch, number, args, grid=()):
    return pl.pallas_call(
        kernel,
        grid=grid,
        out_shape=outs,
        in_specs=in_specs,
        out_specs=out_specs,
        scratch_shapes=scratch,
        compiler_params=pltpu.CompilerParams(
            collective_id=number, has_side_effects=True, vmem_limit_bytes=VMEM_LIMIT
        ),
    )(*args)


def start_layer(line, resid, cotangent, gain, own):
    rows, width = resid.shape
    inner = own[0].shape[1]
    shape = jax.ShapeDtypeStruct
    outs = gather_outputs(line, width, inner, 2 * line) + [
        shape((rows * TENSOR, width), BF16),
        shape((rows * TENSOR, width), BF16),
    ]
    scratch = [pltpu.VMEM((rows, width), BF16)] * 2 + gather_scratch(line)
    scratch += spread_semaphores() * 2 + [pltpu.SemaphoreType.DMA((2,))]
    return call_kernel(
        functools.partial(start_kernel, line),
        outs,
        [IN_VMEM] * 3 + [ANY] * 5,
        [ANY] * 7,
        scratch,
        0,
        (resid, cotangent, gain, *own),
    )


def scale_steps(place, timeline, sq, land, scale_row, scale_col, sems, inner_all, start=0.0):
    rows = scale_col.shape[0]

    def at(owner):
        return sq.at[:, pl.ds(pl.multiple_of(owner * rows, rows), rows)]

    copies = share_blocks(place, at, lambda n: land.at[n], sems)

    def arrive():
        for copy in copies:
            copy.wait()
        squares = at(place.t)[...] + land[0] + land[1] + land[2]
        scale = lax.rsqrt(squares / inner_all + epsilon)
        scale_row[...] = scale
        scale_col[...] = jnp.transpose(scale)

    timeline.add(start - 0.5, lambda: [copy.start() for copy in copies] and None)
    timeline.add(start + 1.5, arrive)


RATE_SHARED = 8.8
RATE = 4.4


SLOTS = 8
FORWARD_US = 6.7


def middle_kernel(line, inner_all, *refs):
    work, refs = refs[:12], refs[12:]
    (resid, gain), own, refs = refs[:2], refs[2:7], refs[7:]
    saved, refs = refs[:8], refs[8:]
    state_out, raw_out, scale_row, rows_all, refs = *refs[:4], refs[4:]
    wholes, refs = refs[:5], refs[5:]
    scratch, refs = refs[:4], refs[4:]
    part, sq, far, near, mate, land, scale_col, normed = refs[:8]
    refs = refs[8:]
    sems, share_sems, own_sems = refs[:5], refs[5:7], refs[7]
    reduce_sems, sq_sems, rows_sems, local = refs[8:14], refs[14:16], refs[16:22], refs[22]
    chunk = pl.program_id(0)
    chunks = part.shape[0] // CHUNK
    place = Place(line)
    pl.when(chunk == 0)(place.greet)
    timeline = Timeline()
    done = FORWARD_US * chunks + 1.0
    scale_steps(place, timeline, sq, land, scale_row, scale_col, sq_sems, inner_all, done)
    rows = normed.shape[0]
    step = rows // PIECES
    begin, forward, finish = spread_rows(place, normed, rows_all, rows_sems)

    def owner(p, sums):
        part_rows = slice(p * step, (p + 1) * step)
        raw_out[part_rows, :] = sums
        state = resid[part_rows, :].astype(F32) + sums * scale_col[part_rows, 0:1]
        state_out[part_rows, :] = state
        normed[part_rows, :] = (state * row_norm(state) * gain[...]).astype(BF16)
        begin(p)

    reduce_rows(place, timeline, part, (far, near, mate), reduce_sems, owner, RATE, done)
    weight_gather(place, timeline, own, wholes, sems, share_sems, own_sems)
    for p in range(PIECES):
        timeline.add(done + 3.0 + RATE * (PIECES + 1 + p), functools.partial(forward, p))
    block = pl.ds(pl.multiple_of(place.t * rows, rows), rows)
    keep = pltpu.make_async_copy(normed, rows_all.at[block, :], local.at[0])
    timeline.add(done + 3.0 + RATE * PIECES, keep.start)
    timeline.add(LATE, keep.wait)
    timeline.add(LATE, finish)
    hook, end = timeline.spread(chunks, SLOTS, FORWARD_US)
    at = pl.multiple_of(chunk * CHUNK, CHUNK)
    forward_kernel(
        *work, part.at[pl.ds(at, CHUNK), :], sq.at[:, pl.ds(at, CHUNK)], *saved, *scratch, hook=hook
    )
    end()


def middle_layer(line, inner_all, rows_all, weights, layer_args, aux, segrow, resid, gain, own):
    rows, width = resid.shape
    length = rows_all.shape[0]
    inner = own[0].shape[1]
    shape = jax.ShapeDtypeStruct
    outs = (
        saved_shapes(length, inner)
        + [
            shape((rows, width), F32),
            shape((rows, width), F32),
            shape((8, rows), F32),
            shape((length, width), BF16),
        ]
        + gather_outputs(line, width, inner, 2 * line)
    )
    scratch = forward_scratch(inner)
    scratch += [pltpu.VMEM((length, width), BF16), pltpu.VMEM((8, length), F32)]
    scratch += [pltpu.VMEM((rows, width), BF16)] * 3
    scratch += [pltpu.VMEM((3, 8, rows), F32), pltpu.VMEM((rows, 8), F32), pltpu.VMEM((rows, width), BF16)]
    scratch += gather_scratch(line) + reduce_semaphores() + share_semaphores() + spread_semaphores()
    scratch += [pltpu.SemaphoreType.DMA((1,))]
    return call_kernel(
        functools.partial(middle_kernel, line, inner_all),
        outs,
        forward_in_specs(rows_all, weights, layer_args)
        + [whole_spec(resid.shape), whole_spec(gain.shape)]
        + [ANY] * 5,
        saved_specs(inner)
        + [whole_spec((rows, width)), whole_spec((rows, width)), whole_spec((8, rows))]
        + [ANY] * 6,
        scratch,
        1,
        (rows_all, *weights, *layer_args, aux, segrow, resid, gain, *own),
        (length // CHUNK,),
    )


def per_row_steps(place, timeline, scale_row, cross_col, stage, land, out, sems, inner_all, when):
    rows = cross_col.shape[0]
    copies = share_blocks(place, lambda peer: stage, lambda n: land.at[n], sems)
    peers = (place.sibling, place.mate, place.diagonal)

    def send():
        cross = jnp.transpose(jnp.broadcast_to(cross_col[:, 0:1], (rows, LANES)))[0:8, :]
        scale = scale_row[...]
        coef = scale * scale * scale * cross / inner_all
        stage[...] = jnp.where(iota2((8, rows), 0) == 0, scale, coef)
        for copy in copies:
            copy.start()
        out[:, pl.ds(pl.multiple_of(place.t * rows, rows), rows)] = stage[...]

    def follow(chunk):
        pl.when(place.t == chunk)(send)

    def arrive():
        for n, (copy, peer) in enumerate(zip(copies, peers)):
            copy.wait()
            out[:, pl.ds(pl.multiple_of(peer * rows, rows), rows)] = land[n]

    if when is None:
        timeline.follow(5 + 3 * (PIECES - 1), follow)
    else:
        timeline.add(when, send)
    timeline.add(LATE, arrive)


def top_kernel(
    line, inner_all, part, sq, state, cotangent, hidden, per_row,
    far, near, mate, sq_land, row_land, scale_col, scale_row, cross_col, stage, *refs
):
    reduce_sems, sq_sems, row_sems = refs[:6], refs[6:8], refs[8:10]
    place = Place(line)
    place.greet(across=False)
    timeline = Timeline()
    scale_steps(place, timeline, sq, sq_land, scale_row, scale_col, sq_sems, inner_all)
    step = cross_col.shape[0] // PIECES

    def owner(p, sums):
        part_rows = slice(p * step, (p + 1) * step)
        hidden[part_rows, :] = state[part_rows, :] + sums * scale_col[part_rows, 0:1]
        low = cotangent[part_rows, :].astype(BF16).astype(F32)
        cross = jnp.sum(low * sums, axis=1, keepdims=True)
        cross_col[part_rows, :] = jnp.broadcast_to(cross, (step, LANES))

    reduce_rows(place, timeline, part, (far, near, mate), reduce_sems, owner, RATE)
    per_row_steps(
        place, timeline, scale_row, cross_col, stage, row_land, per_row, row_sems, inner_all, 1e3
    )
    timeline.run()


def top_layer(line, inner_all, part, sq, state, cotangent):
    rows, width = state.shape
    shape = jax.ShapeDtypeStruct
    scratch = [pltpu.VMEM((rows, width), BF16)] * 3 + [pltpu.VMEM((3, 8, rows), F32)] * 2
    scratch += [
        pltpu.VMEM((rows, 8), F32),
        pltpu.VMEM((8, rows), F32),
        pltpu.VMEM((rows, LANES), F32),
        pltpu.VMEM((8, rows), F32),
    ]
    scratch += reduce_semaphores() + share_semaphores() * 2
    return call_kernel(
        functools.partial(top_kernel, line, inner_all),
        [shape((rows, width), F32), shape((8, rows * TENSOR), F32)],
        [IN_VMEM] * 4,
        [IN_VMEM] * 2,
        scratch,
        2,
        (part, sq, state, cotangent),
    )


def halves(rows):
    first = max(rows // 32 * 16, 16)
    return first, rows - first


BACKWARD_US = 10.0
DOTS_US = 6.0


def weight_scatter(
    place, timeline, grads, early, outs, lands, sems, bc_land, bc_sum, share_sems, late
):
    bc = grads[4]
    shares = share_blocks(
        place, lambda peer: bc.at[:, peer], lambda n: bc_land.at[n], share_sems
    )
    bc_ready = late + 12.0

    def bc_add():
        for copy in shares:
            copy.wait()

        def body(n, carry):
            total = bc[n, place.t].astype(F32) + bc_land[0, n].astype(F32)
            total = total + bc_land[1, n].astype(F32) + bc_land[2, n].astype(F32)
            bc_sum[n] = total.astype(BF16)
            return carry

        lax.fori_loop(0, bc.shape[0], body, 0)

    timeline.add(late, lambda: [copy.start() for copy in shares] and None)
    timeline.add(bc_ready, bc_add)
    rows = outs[0].shape[0]
    head, tail = halves(rows)
    first, second = pl.ds(0, head), pl.ds(head, tail)

    def low(ref):
        return by_rows_piece(ref, rows, 0, head)

    def high(ref):
        return by_rows_piece(ref, rows, head, tail)

    def shared(zz, xs):
        return bc_sum.at[zz * 2 + xs]

    def step(ref):
        return by_rows_piece(ref, rows)

    items = [
        (low(grads[0]), low(early[0]), lands[0:2], outs[0].at[first, :], "zx", BIG / 2, 0.0),
        (high(grads[0]), high(early[0]), lands[2:4], outs[0].at[second, :], "xz", BIG / 2, 0.0),
        (step(grads[1]), step(early[1]), lands[4:6], outs[1], "xz", BIG, 0.0),
        (low(grads[2]), low(grads[2]), lands[6:8], outs[2].at[first, :], "xz", BIG / 2, late),
        (high(grads[2]), high(grads[2]), lands[8:10], outs[2].at[second, :], "xz", BIG / 2, late),
        (step(grads[3]), step(grads[3]), lands[10:12], outs[3], "xz", SMALL, late),
        (shared, shared, lands[12:14], outs[4], "xz", SMALL / 2, bc_ready + 0.1),
    ]
    scatter_weights(place, timeline, items, sems)


def scatter_outputs(width, inner, dp):
    shape = jax.ShapeDtypeStruct
    rows = width // dp
    return [shape((rows, inner), F32)] * 3 + [
        shape((rows, LANES), F32),
        shape((rows // TENSOR, 2 * N), F32),
    ]


def scatter_scratch(line, width, inner):
    dp = 2 * line
    rows = width // dp
    head, tail = halves(rows)
    fine = rows // TENSOR
    scratch = [
        pltpu.VMEM((1, head, inner), BF16),
        pltpu.VMEM((line + 1, 2, head, inner), BF16),
    ]
    for count, cols in ((tail, inner), (rows, inner), (head, inner), (tail, inner), (rows, LANES), (fine, 2 * N)):
        scratch += [pltpu.VMEM((line, count, cols), BF16), pltpu.VMEM((line + 1, count, cols), BF16)]
    scratch += [
        pltpu.VMEM((3, dp, fine, 2 * N), BF16),
        pltpu.VMEM((dp, fine, 2 * N), BF16),
    ]
    return scratch + scatter_semaphores(7, line) + share_semaphores()


def input_gradient(state, gain, before, sums):
    scale = row_norm(state)
    gained = sums * gain
    mean = jnp.mean(gained * state, axis=1, keepdims=True)
    grad = before + scale * gained - state * (scale * scale * scale * mean)
    return grad, jnp.sum(sums * state * scale, axis=0, keepdims=True)


def late_dots(rows_all, ginner, gstep, gshared, dinner, dstep, dshared):
    dp, tensor, fine, _ = dshared.shape
    tile = rows_all.shape[1] // 2
    per_tile = tile // (tensor * fine)

    def body(n, carry):
        part = pl.ds(pl.multiple_of(n * tile, tile), tile)
        left = rows_all[:, part]
        dinner[part, :] = contract(left, ginner[...])
        dstep[part, :] = contract(left, gstep[...])
        shared = contract_wide(left, gshared[...])
        for m in range(per_tile * tensor):
            block = shared[m * fine : (m + 1) * fine, :].astype(BF16)
            dshared[n * per_tile + m // tensor, m % tensor] = block
        return carry

    lax.fori_loop(0, 2, body, 0)


def pull_kernel(line, inner_all, final, *refs):
    work, refs = refs[:21], refs[21:]
    far_side, gain, refs = refs[:5], refs[5], refs[6:]
    if final:
        gnorm_top, small_more, small_top, small_top_more, bc_top, refs = *refs[:5], refs[5:]
        grad_out, norm_sum, small_sum, bc_sums, refs = *refs[:4], refs[4:]
    else:
        raw, scale_row, refs = *refs[:2], refs[2:]
        grad_out, gnorm, per_row, top_all, small, small_bc, refs = *refs[:6], refs[6:]
    outs, refs = refs[:5], refs[5:]
    scratch, refs = refs[:7], refs[7:]
    near_side, load_sems, refs = refs[:5], refs[5], refs[6:]
    rows_all, dout, dgate, before, state = near_side
    loads = [
        pltpu.make_async_copy(source, target, load_sems.at[n])
        for n, (source, target) in enumerate(zip(far_side, near_side))
    ]
    part, ginner, gstep, gshared, dinner, dstep, dshared = refs[:7]
    far, near, mate, refs = *refs[7:10], refs[10:]
    lands, bc_land, bc_sum, sems, share_sems = refs[:14], refs[14], refs[15], refs[16:22], refs[22:24]
    reduce_sems, refs = refs[24:30], refs[30:]
    if final:
        small, small_bc, small_land, bc_land_sums, norm_land = refs[:5]
        small_send, small_recv = refs[5:]
    else:
        row_land, cross_col, stage, low = refs[:4]
        row_sems, top_sems, local = refs[4:6], refs[6:12], refs[12]
    dp = 2 * line
    bits = [1 << n for n in range(dp.bit_length() - 1)]
    chunk = pl.program_id(0)
    chunks = part.shape[0] // CHUNK
    place = Place(line)
    far_bits = [bit for bit in bits if bit >= 4] if final else []
    pl.when(chunk == 0)(lambda: place.greet(far_bits=far_bits))
    timeline = Timeline()
    done = BACKWARD_US * chunks + 0.5
    late = done + 2.2 + DOTS_US
    rows = state.shape[0]
    step = rows // PIECES

    if not final:
        begin, forward, finish = spread_rows(place, low, top_all, top_sems)

    def clear():
        if final:
            norm_sum[...] = jnp.zeros_like(norm_sum)
            norm_sum[1:2, :] = gnorm_top[0:1, :]
        else:
            gnorm[...] = jnp.zeros_like(gnorm)

    def load():
        for n in (1, 2, 3, 4, 0):
            loads[n].start()

    timeline.add(-2.0, load)
    timeline.add(-2.0, clear)
    for n in (1, 2, 3, 4, 0):
        timeline.add(2.5 if n in (1, 2) else BACKWARD_US / 2, loads[n].wait)

    def owner(p, sums):
        part_rows = slice(p * step, (p + 1) * step)
        grad, column = input_gradient(
            state[part_rows, :].astype(F32), gain[...], before[part_rows, :], sums
        )
        grad_out[part_rows, :] = grad
        if final:
            norm_sum[0:1, :] += column
            return
        gnorm[0:1, :] += column
        low[part_rows, :] = grad.astype(BF16)
        cross = jnp.sum(low[part_rows, :].astype(F32) * raw[part_rows, :], axis=1, keepdims=True)
        cross_col[part_rows, :] = jnp.broadcast_to(cross, (step, LANES))
        begin(p)

    roll_rows(
        place, timeline, part, (far, near, mate), reduce_sems, owner, None if final else forward
    )
    timeline.add(
        done + 2.2, lambda: late_dots(rows_all, ginner, gstep, gshared, dinner, dstep, dshared)
    )
    if not final:
        block = pl.ds(pl.multiple_of(place.t * rows, rows), rows)
        keep = pltpu.make_async_copy(low, top_all.at[block, :], local.at[0])
        timeline.follow(5 + 3 * (PIECES - 1), lambda chunk: pl.when(place.t == chunk)(keep.start))
        timeline.add(LATE, keep.wait)
        timeline.add(LATE, finish)
        per_row_steps(
            place, timeline, scale_row, cross_col, stage, row_land, per_row, row_sems, inner_all, None
        )
    grads = (dout, dgate, dinner, dstep, dshared)
    weight_scatter(
        place, timeline, grads, far_side[1:3], outs, lands, sems, bc_land, bc_sum, share_sems, late
    )
    if final:

        def pack():
            small_sum[0:8, :] = small[...] + small_more[...]
            small_sum[8:16, :] = small_top[...] + small_top_more[...]
            bc_sums[0:8, :] = small_bc[...]
            bc_sums[8:16, :] = bc_top[...]

        timeline.add(done + 0.05, pack)
        along = [place.partner(bit) for bit in bits]
        across = [(place.dp, place.sibling), (place.dp, place.mate)]

        def exchange(n, partner, group, start, end):
            copies = [
                remote(own, land.at[n], small_send.at[n, m], small_recv.at[n, m], partner)
                for m, own, land in group
            ]

            def send():
                for copy in copies:
                    copy.start()

            def take():
                for copy, (_, own, land) in zip(copies, group):
                    copy.wait()
                    own[...] += land[n]

            timeline.add(start, send)
            timeline.add(end, take)

        when = done + 17.0 + LAG
        steps = [(len(bits), across[0], 3.0), (len(bits) + 1, across[1], 5.0)]
        steps += [(n, along[n], 7.0) for n in range(len(bits))][::-1]
        for n, partner, wait in steps:
            group = [(0, bc_sums, bc_land_sums), (1, norm_sum, norm_land)]
            if n < len(bits):
                group.append((2, small_sum, small_land))
            exchange(n, partner, group, when, when + wait)
            when += wait + 0.01
    hook, end = timeline.spread(chunks, SLOTS, BACKWARD_US, lambda n: chunks - 1 - n)
    at = pl.ds(pl.multiple_of((chunks - 1 - chunk) * CHUNK, CHUNK), CHUNK)
    mix_back_kernel(
        *work,
        part.at[at, :],
        ginner.at[at, :],
        gstep.at[at, :],
        gshared.at[at, :],
        small,
        small_bc,
        *scratch,
        hook=hook,
    )
    end()


def pull_layer(
    line, inner_all, saved, gates, weights, layer_args, spread, aux, segrow, rows_all, dout, dgate,
    before, state, gain, more, final,
):
    length, width = rows_all.shape
    rows = state.shape[0]
    inner = dout.shape[1]
    dp = 2 * line
    fine = width // (dp * TENSOR)
    steps = dp.bit_length() - 1
    shape = jax.ShapeDtypeStruct
    _, iraw, iconv, sraw, sconv, step, mixed, sin = saved
    far_side = (rows_all, dout, dgate, before, state)
    whole = (gain, *more)
    if final:
        outs = [
            shape((rows, width), F32),
            shape((8, width), F32),
            shape((16, inner), F32),
            shape((16, 2 * N), F32),
        ]
        out_specs = [whole_spec(out.shape) for out in outs]
    else:
        outs = [
            shape((rows, width), F32),
            shape((8, width), F32),
            shape((8, rows * TENSOR), F32),
            shape((length, width), BF16),
            shape((8, inner), F32),
            shape((8, 2 * N), F32),
        ]
        out_specs = [whole_spec(out.shape) for out in outs]
        out_specs[3] = ANY
    tail_outs = scatter_outputs(width, inner, dp)
    scratch = mix_back_scratch(inner)
    scratch += [pltpu.VMEM(array.shape, array.dtype) for array in far_side]
    scratch += [pltpu.SemaphoreType.DMA((5,))]
    scratch += [
        pltpu.VMEM((length, width), BF16),
        pltpu.VMEM((length, inner), BF16),
        pltpu.VMEM((length, LANES), BF16),
        pltpu.VMEM((length, 2 * N), BF16),
        pltpu.VMEM((width, inner), BF16),
        pltpu.VMEM((width, LANES), BF16),
        pltpu.VMEM((dp, TENSOR, fine, 2 * N), BF16),
    ]
    scratch += [pltpu.VMEM((rows, width), BF16)] * 3
    scratch += scatter_scratch(line, width, inner) + reduce_semaphores()
    if final:
        scratch += [
            pltpu.VMEM((8, inner), F32),
            pltpu.VMEM((8, 2 * N), F32),
            pltpu.VMEM((steps, 16, inner), F32),
            pltpu.VMEM((steps + 2, 16, 2 * N), F32),
            pltpu.VMEM((steps + 2, 8, width), F32),
            pltpu.SemaphoreType.DMA((steps + 2, 3)),
            pltpu.SemaphoreType.DMA((steps + 2, 3)),
        ]
    else:
        scratch += [
            pltpu.VMEM((3, 8, rows), F32),
            pltpu.VMEM((rows, LANES), F32),
            pltpu.VMEM((8, rows), F32),
            pltpu.VMEM((rows, width), BF16),
        ]
        scratch += share_semaphores() + spread_semaphores() + [pltpu.SemaphoreType.DMA((1,))]
    weights = weights[:4]
    return call_kernel(
        functools.partial(pull_kernel, line, inner_all, final),
        outs + tail_outs,
        mix_back_specs(length // CHUNK, inner, weights, layer_args, spread)
        + [ANY] * 5
        + [whole_spec(array.shape) for array in whole],
        out_specs + [whole_spec(out.shape) for out in tail_outs],
        scratch,
        4 if final else 3,
        (
            iraw, iconv, sraw, sconv, step, mixed, sin, sin, *gates,
            *weights, *layer_args, spread, aux, segrow, *far_side, *whole,
        ),
        (length // CHUNK,),
    )


def contract_wide(left, right):
    return lax.dot_general(
        left, right, (((0,), (0,)), ((), ())), preferred_element_type=F32
    )


def contract(left, right):
    return contract_wide(left, right).astype(BF16)


def on_device(
    resid,
    segment_ids,
    cotangent,
    w_z,
    w_x,
    w_bc,
    w_dt,
    w_out,
    norm_gain,
    conv_x,
    conv_bc,
    a_log,
    dt_bias,
    d_skip,
    gated_gain,
):
    dp = lax.axis_size("dp")
    assert lax.axis_size("tensor") == TENSOR and segment_ids.shape[0] == LEN and a_log.shape[0] == 2
    line = dp // 2
    heads = a_log.shape[1]
    inner = heads * P_SIZE
    inner_all = inner * TENSOR
    width = resid.shape[1]
    aux, segrow = row_masks(segment_ids)
    spread = head_spread(inner)
    args = [
        layer_parameters(layer, conv_x, conv_bc, a_log, dt_bias, d_skip, gated_gain)
        for layer in range(2)
    ]
    own = [
        (
            w_z[layer],
            w_x[layer],
            jnp.transpose(w_out[layer]),
            jnp.pad(w_dt[layer], ((0, 0), (0, LANES - heads))),
            w_bc[layer],
        )
        for layer in range(2)
    ]
    gains = [norm_gain[layer : layer + 1] for layer in range(2)]

    def arranged(gathered):
        gate, inner_w, out_w, step_w, shared_w = gathered
        return gate, inner_w, shared_w.reshape(width, 2 * N), step_w, out_w

    *gathered, rows_low, top_high = start_layer(line, resid, cotangent, gains[0], own[0])
    weights_low = arranged(gathered)
    results = middle_layer(
        line, inner_all, rows_low, weights_low, args[0], aux, segrow, resid, gains[1], own[1]
    )
    saved_low = results[:8]
    state, raw, scale_row, rows_high, *gathered = results[8:]
    weights_high = arranged(gathered)
    part, sq, *saved_high = forward_layer(rows_high, weights_high, args[1], aux, segrow)
    hidden, per_row = top_layer(line, inner_all, part, sq, state, cotangent)

    def early_grads(rows_all, top_all, per_row, saved, weights, wide):
        ggate, gout, outlow, small = gate_back(top_all, per_row, saved, weights[4], wide)
        return (ggate, gout), contract(top_all, outlow), contract(rows_all, ggate), small

    gates, dout, dgate, small_high_more = early_grads(
        rows_high, top_high, per_row, saved_high, weights_high, args[1][3]
    )
    results = pull_layer(
        line, inner_all, saved_high, gates, weights_high, args[1], spread, aux, segrow, rows_high,
        dout, dgate, cotangent, state, gains[1], (raw, scale_row), False,
    )
    grad_state, gnorm_high, per_row, top_low, small_high, bc_high, *grads_high = results
    gates, dout, dgate, small_low_more = early_grads(
        rows_low, top_low, per_row, saved_low, weights_low, args[0][3]
    )
    more = (gnorm_high, small_low_more, small_high, small_high_more, bc_high)
    grad_resid, norm_sum, small, small_bc, *grads_low = pull_layer(
        line, inner_all, saved_low, gates, weights_low, args[0], spread, aux, segrow, rows_low,
        dout, dgate, grad_state, resid, gains[0], more, True,
    )
    gout, gz, gx, gdt, gbc = [
        jnp.stack([low, high]) for low, high in zip(grads_low, grads_high)
    ]
    small = small.reshape(2, 8, inner)
    return (
        hidden,
        grad_resid,
        gz,
        gx,
        gbc,
        gdt[:, :, :heads],
        jnp.swapaxes(gout, 1, 2),
        norm_sum[:2],
        small[:, :TAPS],
        small_bc.reshape(2, 8, 2 * N)[:, :TAPS],
        small[:, 6, :heads],
        small[:, 7, :heads],
        jnp.sum(small[:, 5].reshape(2, heads, P_SIZE), axis=2),
        small[:, 4],
    )


def solution(mesh):
    rows = P(("dp", "tensor"), None)
    matrix = P(None, "dp", "tensor")
    shared = P(None, ("dp", "tensor"), None)
    wide = P(None, None, "tensor")
    head = P(None, "tensor")
    out = P(None, "tensor", "dp")
    return jax.shard_map(
        on_device,
        mesh=mesh,
        in_specs=(
            rows, P("dp"), rows, matrix, matrix, shared, matrix, out, P(), wide, P(), head, head, head, head,
        ),
        out_specs=(
            rows, rows, matrix, matrix, shared, matrix, out, P(), wide, P(), head, head, head, head,
        ),
        check_vma=False,
    )
```

```python
import functools
import heapq
import itertools

import jax
import jax.numpy as jnp
import numpy as np
from jax import lax
from jax.experimental import pallas as pl
from jax.experimental.pallas import tpu as pltpu
from jax.sharding import PartitionSpec as P

P_SIZE = 64
N = 128
LEN = 1024
CHUNK = 256
LANES = 128
TAPS = 4
STEPS = 16

highest = lax.Precision.HIGHEST
epsilon = 1e-05
F32 = jnp.float32
BF16 = jnp.bfloat16


def mm(left, right):
    return jnp.dot(left, right, preferred_element_type=F32)


def mm_nt(left, right):
    return lax.dot_general(left, right, (((1,), (1,)), ((), ())), preferred_element_type=F32)


def sigmoid(values):
    return 1.0 / (1.0 + jnp.exp(-values))


def softplus(values):
    return jnp.maximum(values, 0.0) + jnp.log1p(jnp.exp(-jnp.abs(values)))


def iota2(shape, dim):
    return lax.broadcasted_iota(jnp.int32, shape, dim)


def pair_of(columns, head):
    shape = (columns.shape[0], LANES)
    first = jnp.broadcast_to(columns[:, head : head + 1], shape)
    second = jnp.broadcast_to(columns[:, head + 1 : head + 2], shape)
    return jnp.where(iota2(shape, 1) < P_SIZE, first, second)


def head_sums(values, spread):
    high = values.astype(BF16)
    low = (values - high.astype(F32)).astype(BF16)
    return mm(high, spread) + mm(low, spread)


def decays(step_pre, rate, aux):
    step = softplus(step_pre)
    order = (iota2((CHUNK, CHUNK), 0) >= iota2((CHUNK, CHUNK), 1)).astype(F32)
    cum = jnp.dot(order, step * rate, precision=highest, preferred_element_type=F32)
    last = cum[CHUNK - 1 : CHUNK, :]
    decay_in = jnp.exp(cum) * aux[:, 4:5]
    decay_out = jnp.exp(last - cum) * aux[:, 5:6]
    decay_pass = jnp.exp(last) * aux[0:1, 6:7]
    return step, cum, decay_in, decay_out, decay_pass


def step_weights(blocks):
    joined = jnp.concatenate([blocks[n] for n in range(blocks.shape[0])], axis=1)
    return jnp.concatenate([joined, jnp.zeros((LANES - STEPS, joined.shape[1]), BF16)], axis=0)


def forward_kernel(
    rows_ref,
    wz_ref,
    wx_ref,
    wbc_ref,
    wdt_ref,
    wout_ref,
    convx_ref,
    convbc_ref,
    heads_ref,
    wide_ref,
    aux_ref,
    segrow_ref,
    part_ref,
    sq_ref,
    gate_ref,
    iraw_ref,
    iconv_ref,
    sraw_ref,
    sconv_ref,
    step_ref,
    mixed_ref,
    sin_ref,
    full_ref,
    ext_x,
    ext_bc,
    state,
    gg_ref,
    gate_raw,
    hook,
):
    inner = wx_ref.shape[1]

    @pl.when(pl.program_id(0) == 0)
    def _():
        state[...] = jnp.zeros_like(state)
        ext_x[0:8, :] = jnp.zeros((8, inner), F32)
        ext_bc[0:8, :] = jnp.zeros((8, 2 * N), F32)

    hook(0)
    rows = rows_ref[...]
    aux = aux_ref[...]
    rate = heads_ref[1:2, :]
    shared = mm(rows, wbc_ref[...])
    sraw_ref[...] = shared
    ext_bc[8 : 8 + CHUNK, :] = shared
    shared_conv = convbc_ref[TAPS - 1 : TAPS, :] * shared
    for j in range(1, TAPS):
        shared_conv = shared_conv + convbc_ref[TAPS - 1 - j : TAPS - j, :] * (
            ext_bc[8 - j : 8 - j + CHUNK, :] * aux[:, j : j + 1]
        )
    sconv_ref[...] = shared_conv
    ext_bc[0:8, :] = ext_bc[CHUNK : CHUNK + 8, :]
    shared_act = shared_conv * sigmoid(shared_conv)
    keys = shared_act[:, :N].astype(BF16)
    keys_t = jnp.transpose(shared_act[:, :N]).astype(BF16)
    query = shared_act[:, N:].astype(BF16)
    visible = (aux[:, 15:16] == segrow_ref[0:1, :]) & (
        iota2((CHUNK, CHUNK), 0) >= iota2((CHUNK, CHUNK), 1)
    )
    coupling = jnp.where(visible, mm_nt(query, keys), 0.0)
    step_raw = mm_nt(rows, step_weights(wdt_ref))
    step_ref[...] = step_raw
    step, cum, decay_in, decay_out, decay_pass = decays(
        step_raw + heads_ref[0:1, :], rate, aux
    )
    cum_t = jnp.transpose(cum)
    ext_x[8 : 8 + CHUNK, :] = mm(rows, wx_ref[...])
    gate_raw[...] = mm(rows, wz_ref[...])
    hook(1)
    squares = jnp.zeros((CHUNK, LANES), F32)
    half = iota2((CHUNK, LANES), 1) < P_SIZE
    for pair in range(inner // LANES):
        cols = slice(pair * LANES, (pair + 1) * LANES)
        head = 2 * pair
        raw = ext_x[8 : 8 + CHUNK, cols]
        iraw_ref[:, cols] = raw.astype(BF16)
        conv = convx_ref[TAPS - 1 : TAPS, cols] * raw
        for j in range(1, TAPS):
            conv = conv + convx_ref[TAPS - 1 - j : TAPS - j, cols] * (
                ext_x[8 - j : 8 - j + CHUNK, cols] * aux[:, j : j + 1]
            )
        iconv_ref[:, cols] = conv
        ext_x[0:8, cols] = ext_x[CHUNK : CHUNK + 8, cols]
        act = conv * sigmoid(conv)
        scaled = (act * pair_of(step, head)).astype(BF16)
        parts = []
        for one in (head, head + 1):
            gap = cum[:, one : one + 1] - cum_t[one : one + 1, :]
            weights = (coupling * jnp.exp(jnp.minimum(gap, 0.0))).astype(BF16)
            parts.append(mm(weights, scaled))
        before = state[:, cols]
        sin_ref[0, :, cols] = before
        mixed = jnp.where(half, parts[0], parts[1])
        mixed = mixed + pair_of(decay_in, head) * mm(query, before.astype(BF16))
        mixed_ref[:, cols] = mixed
        leaving = (scaled.astype(F32) * pair_of(decay_out, head)).astype(BF16)
        state[:, cols] = pair_of(decay_pass, head) * before + mm(keys_t, leaving)
        gate = gate_raw[:, cols]
        gate_ref[:, cols] = gate.astype(BF16)
        full = mixed + wide_ref[0:1, cols] * act
        full_ref[:, cols] = full.astype(BF16)
        gated = full * (gate * sigmoid(gate))
        squares = squares + gated * gated
        gg_ref[:, cols] = (gated * wide_ref[1:2, cols]).astype(BF16)
        hook(2 + pair)
    total = jnp.sum(squares, axis=1, keepdims=True)
    sq_ref[...] = jnp.transpose(jnp.broadcast_to(total, (CHUNK, LANES)))[0:8, :]
    part_ref[...] = mm_nt(gg_ref[...], wout_ref[...]).astype(BF16)


def gate_back_kernel(
    top_ref,
    sc_ref,
    gate_ref,
    full_ref,
    wout_ref,
    wide_ref,
    ggate_ref,
    gout_ref,
    outlow_ref,
    small_ref,
    gno_ref,
):
    inner = wout_ref.shape[1]

    @pl.when(pl.program_id(0) == 0)
    def _():
        small_ref[...] = jnp.zeros_like(small_ref)

    gno_ref[...] = mm(top_ref[...], wout_ref[...])
    per_row = jnp.transpose(sc_ref[...])
    scale = per_row[:, 0:1]
    coef = per_row[:, 1:2]
    for pair in range(inner // LANES):
        cols = slice(pair * LANES, (pair + 1) * LANES)
        gain = wide_ref[1:2, cols]
        gate = gate_ref[:, cols].astype(F32)
        gate_sig = sigmoid(gate)
        gate_act = gate * gate_sig
        full = full_ref[:, cols].astype(F32)
        gated = full * gate_act
        gno = gno_ref[:, cols]
        gated_scaled = gated * scale
        small_ref[4:5, cols] += jnp.sum(gno * gated_scaled, axis=0, keepdims=True)
        outlow_ref[:, cols] = (gated_scaled * gain).astype(BF16)
        ggated = scale * (gno * gain) - gated * coef
        gout_ref[:, cols] = (ggated * gate_act).astype(BF16)
        ggate_ref[:, cols] = (
            ggated * full * (gate_sig * (1.0 + gate * (1.0 - gate_sig)))
        ).astype(BF16)


def gate_back(layer, top_all, per_row, saved, weight_out, wide):
    length, width = top_all.shape
    inner = weight_out.shape[1]
    gate, full = saved[0], saved[8]
    shape = jax.ShapeDtypeStruct
    return pl.pallas_call(
        gate_back_kernel,
        grid=(length // CHUNK,),
        in_specs=[block_rows(width), pl.BlockSpec((8, CHUNK), lambda i: (0, i))]
        + [block_rows(inner)] * 2
        + [whole_spec(weight_out.shape), layer_spec(layer, wide.shape)],
        out_specs=[block_rows(inner)] * 3 + [pl.BlockSpec((8, inner), lambda i: (0, 0))],
        out_shape=[shape((length, inner), BF16)] * 3 + [shape((8, inner), F32)],
        scratch_shapes=[pltpu.VMEM((CHUNK, inner), F32)],
        compiler_params=pltpu.CompilerParams(
            dimension_semantics=("arbitrary",), vmem_limit_bytes=VMEM_LIMIT
        ),
    )(top_all, per_row, gate, full, weight_out, wide)


def mix_back_kernel(
    iraw_ref,
    iconv_ref,
    sraw_ref,
    sconv_ref,
    step_ref,
    mixed_ref,
    sin_ref,
    sout_ref,
    ggate_ref,
    gout_ref,
    wz_ref,
    wx_ref,
    wbc_ref,
    wdt_ref,
    convx_ref,
    convbc_ref,
    heads_ref,
    wide_ref,
    spread_ref,
    aux_ref,
    segrow_ref,
    part_ref,
    ginner_ref,
    gstep_ref,
    gshared_ref,
    small_ref,
    smallbc_ref,
    gext_x,
    gext_bc,
    dstate,
    balance,
    direct,
    edge,
    dcoup,
    hook,
):
    inner = wx_ref.shape[1]

    @pl.when(pl.program_id(0) == 0)
    def _():
        dstate[...] = jnp.zeros_like(dstate)
        gext_x[CHUNK : CHUNK + 8, :] = jnp.zeros((8, inner), F32)
        gext_bc[CHUNK : CHUNK + 8, :] = jnp.zeros((8, 2 * N), F32)
        small_ref[...] = jnp.zeros_like(small_ref)
        smallbc_ref[...] = jnp.zeros_like(smallbc_ref)
        edge[...] = jnp.zeros_like(edge)

    hook(0)
    aux = aux_ref[...]
    rate = heads_ref[1:2, :]
    step_pre = step_ref[...] + heads_ref[0:1, :]
    step, cum, decay_in, decay_out, decay_pass = decays(step_pre, rate, aux)
    cum_t = jnp.transpose(cum)
    shared_conv = sconv_ref[...]
    shared_sig = sigmoid(shared_conv)
    shared_act = shared_conv * shared_sig
    keys = shared_act[:, :N].astype(BF16)
    query = shared_act[:, N:].astype(BF16)
    query_t = jnp.transpose(shared_act[:, N:]).astype(BF16)
    visible = (aux[:, 15:16] == segrow_ref[0:1, :]) & (
        iota2((CHUNK, CHUNK), 0) <= iota2((CHUNK, CHUNK), 1)
    )
    coupling = jnp.where(visible, mm_nt(keys, query), 0.0)
    half = iota2((CHUNK, LANES), 1) < P_SIZE
    dcoup[...] = jnp.zeros_like(dcoup)
    dkeys = jnp.zeros((CHUNK, N), F32)
    dquery = jnp.zeros((CHUNK, N), F32)
    for pair in range(inner // LANES):
        cols = slice(pair * LANES, (pair + 1) * LANES)
        head = 2 * pair
        skip = wide_ref[0:1, cols]
        conv = iconv_ref[:, cols]
        conv_sig = sigmoid(conv)
        act = conv * conv_sig
        step_pair = pair_of(step, head)
        scaled = (act * step_pair).astype(BF16)
        gout_low = gout_ref[:, cols]
        gout = gout_low.astype(F32)
        small_ref[5:6, cols] += jnp.sum(gout * act, axis=0, keepdims=True)
        zero = jnp.zeros_like(gout)
        parts = []
        for one, own in (
            (head, jnp.where(half, gout, zero).astype(BF16)),
            (head + 1, jnp.where(half, zero, gout).astype(BF16)),
        ):
            gap = cum_t[one : one + 1, :] - cum[:, one : one + 1]
            decay = jnp.exp(jnp.minimum(gap, 0.0))
            weights = (coupling * decay).astype(BF16)
            parts.append(mm(weights, gout_low))
            dcoup[...] += mm_nt(scaled, own) * decay
        after = dstate[:, cols]
        after_low = after.astype(BF16)
        out_pair = pair_of(decay_out, head)
        gscaled = jnp.where(half, parts[0], parts[1]) + out_pair * mm(keys, after_low)
        scaled_wide = scaled.astype(F32)
        dkeys = dkeys + mm_nt((scaled_wide * out_pair).astype(BF16), after_low)
        entering = (gout * pair_of(decay_in, head)).astype(BF16)
        dquery = dquery + mm_nt(entering, sin_ref[0, :, cols].astype(BF16))
        edge[0:1, cols] = jnp.sum(sout_ref[0, :, cols] * after, axis=0, keepdims=True)
        dstate[:, cols] = pair_of(decay_pass, head) * after + mm(query_t, entering)
        balance[:, cols] = gout * mixed_ref[:, cols] - scaled_wide * gscaled
        direct[:, cols] = act * gscaled
        gact = step_pair * gscaled + skip * gout
        gext_x[0:CHUNK, cols] = gact * (conv_sig * (1.0 + conv * (1.0 - conv_sig)))
        raw = iraw_ref[:, cols].astype(F32)
        gconv = gext_x[0:CHUNK, cols]
        graw = convx_ref[TAPS - 1 : TAPS, cols] * gconv
        small_ref[TAPS - 1 : TAPS, cols] += jnp.sum(raw * gconv, axis=0, keepdims=True)
        for j in range(1, TAPS):
            moved = gext_x[j : j + CHUNK, cols] * aux[:, 8 + j : 9 + j]
            graw = graw + convx_ref[TAPS - 1 - j : TAPS - j, cols] * moved
            small_ref[TAPS - 1 - j : TAPS - j, cols] += jnp.sum(
                raw * moved, axis=0, keepdims=True
            )
        ginner_ref[:, cols] = graw.astype(BF16)
        gext_x[CHUNK : CHUNK + 8, cols] = gext_x[0:8, cols]
        hook(1 + pair)
    spread = spread_ref[...]
    order = (iota2((CHUNK, CHUNK), 0) <= iota2((CHUNK, CHUNK), 1)).astype(F32)
    running = jnp.dot(
        order, head_sums(balance[...], spread), precision=highest, preferred_element_type=F32
    )
    running = running + head_sums(edge[...], spread)[0:1, :]
    gstep = (head_sums(direct[...], spread) + running * rate) * sigmoid(step_pre)
    small_ref[6:7, 0:LANES] += rate * jnp.sum(running * step, axis=0, keepdims=True)
    small_ref[7:8, 0:LANES] += jnp.sum(gstep, axis=0, keepdims=True)
    gstep_ref[...] = gstep.astype(BF16)
    dcoupling = jnp.where(visible, dcoup[...], 0.0)
    dkeys = dkeys + mm(dcoupling.astype(BF16), query)
    dquery = dquery + mm(jnp.transpose(dcoupling).astype(BF16), keys)
    slope = shared_sig * (1.0 + shared_conv * (1.0 - shared_sig))
    gext_bc[0:CHUNK, 0:N] = dkeys * slope[:, :N]
    gext_bc[0:CHUNK, N : 2 * N] = dquery * slope[:, N:]
    raw = sraw_ref[...]
    gconv = gext_bc[0:CHUNK, :]
    graw = convbc_ref[TAPS - 1 : TAPS, :] * gconv
    smallbc_ref[TAPS - 1 : TAPS, :] += jnp.sum(raw * gconv, axis=0, keepdims=True)
    for j in range(1, TAPS):
        moved = gext_bc[j : j + CHUNK, :] * aux[:, 8 + j : 9 + j]
        graw = graw + convbc_ref[TAPS - 1 - j : TAPS - j, :] * moved
        smallbc_ref[TAPS - 1 - j : TAPS - j, :] += jnp.sum(raw * moved, axis=0, keepdims=True)
    gshared_ref[...] = graw.astype(BF16)
    gext_bc[CHUNK : CHUNK + 8, :] = gext_bc[0:8, :]
    hook(7)
    total = mm_nt(ggate_ref[...], wz_ref[...]) + mm_nt(ginner_ref[...], wx_ref[...])
    total = total + mm(gstep_ref[...], step_weights(wdt_ref))
    part_ref[...] = (total + mm_nt(gshared_ref[...], wbc_ref[...])).astype(BF16)


def whole_spec(shape):
    zeros = (0,) * len(shape)
    return pl.BlockSpec(shape, lambda i: zeros, pipeline_mode=pl.Buffered(1))


def layer_spec(layer, shape):
    return pl.BlockSpec(
        (None, *shape[1:]),
        lambda i: (layer,) + (0,) * (len(shape) - 1),
        pipeline_mode=pl.Buffered(1),
    )


VMEM_LIMIT = 62 * 1024 * 1024


def block_rows(cols):
    return pl.BlockSpec((CHUNK, cols), lambda i: (i, 0))


def forward_in_specs(layer, rows_all, weights, layer_args):
    return (
        [block_rows(rows_all.shape[1])]
        + [whole_spec(w.shape) for w in weights]
        + [layer_spec(layer, w.shape) for w in layer_args]
        + [block_rows(LANES), pl.BlockSpec((8, CHUNK), lambda i: (0, i))]
    )


def saved_specs(inner):
    return [
        block_rows(inner),
        block_rows(inner),
        block_rows(inner),
        block_rows(2 * N),
        block_rows(2 * N),
        block_rows(LANES),
        block_rows(inner),
        pl.BlockSpec((1, N, inner), lambda i: (i, 0, 0)),
        block_rows(inner),
    ]


def saved_shapes(length, inner):
    shape = jax.ShapeDtypeStruct
    return [
        shape((length, inner), BF16),
        shape((length, inner), BF16),
        shape((length, inner), F32),
        shape((length, 2 * N), F32),
        shape((length, 2 * N), F32),
        shape((length, LANES), F32),
        shape((length, inner), F32),
        shape((length // CHUNK, N, inner), F32),
        shape((length, inner), BF16),
    ]


def forward_scratch(inner):
    return [
        pltpu.VMEM((CHUNK + 8, inner), F32),
        pltpu.VMEM((CHUNK + 8, 2 * N), F32),
        pltpu.VMEM((N, inner), F32),
        pltpu.VMEM((CHUNK, inner), BF16),
        pltpu.VMEM((CHUNK, inner), F32),
    ]


def mix_back_specs(layer, chunks, inner, weights, layer_args, spread):
    last = chunks - 1

    def turned(cols):
        return pl.BlockSpec((CHUNK, cols), lambda i: (last - i, 0))

    return (
        [
            turned(inner),
            turned(inner),
            turned(2 * N),
            turned(2 * N),
            turned(LANES),
            turned(inner),
            pl.BlockSpec((1, N, inner), lambda i: (last - i, 0, 0)),
            pl.BlockSpec((1, N, inner), lambda i: (jnp.minimum(chunks - i, last), 0, 0)),
            turned(inner),
            turned(inner),
        ]
        + [whole_spec(w.shape) for w in weights]
        + [layer_spec(layer, w.shape) for w in layer_args]
        + [
            whole_spec(spread.shape),
            turned(LANES),
            pl.BlockSpec((8, CHUNK), lambda i: (0, last - i)),
        ]
    )


def mix_back_scratch(inner):
    return [
        pltpu.VMEM((CHUNK + 8, inner), F32),
        pltpu.VMEM((CHUNK + 8, 2 * N), F32),
        pltpu.VMEM((N, inner), F32),
        pltpu.VMEM((CHUNK, inner), F32),
        pltpu.VMEM((CHUNK, inner), F32),
        pltpu.VMEM((8, inner), F32),
        pltpu.VMEM((CHUNK, CHUNK), F32),
    ]


def row_masks(segment_ids):
    length = segment_ids.shape[0]
    seg = segment_ids.astype(F32)

    def shifted(j):
        return jnp.concatenate([jnp.full((j,), -1.0, F32), seg[: length - j]])

    def ahead(j):
        return jnp.concatenate([seg[j:], jnp.full((j,), -1.0, F32)])

    ends = seg[CHUNK - 1 :: CHUNK]
    own_end = jnp.repeat(ends, CHUNK)
    old_end = jnp.repeat(jnp.concatenate([jnp.full((1,), -1.0, F32), ends[:-1]]), CHUNK)
    lanes = [jnp.zeros_like(seg)] * 16
    for j in range(1, TAPS):
        lanes[j] = (shifted(j) == seg).astype(F32)
        lanes[8 + j] = (ahead(j) == seg).astype(F32)
    lanes[4] = (old_end == seg).astype(F32)
    lanes[5] = (own_end == seg).astype(F32)
    lanes[6] = (own_end == old_end).astype(F32)
    lanes[15] = seg
    aux = jnp.pad(jnp.stack(lanes, axis=1), ((0, 0), (0, LANES - 16)))
    return aux, jnp.broadcast_to(seg[None, :], (8, length))


def layer_parameters(conv_x, conv_bc, a_log, dt_bias, d_skip, gated_gain):
    heads = a_log.shape[1]
    pad = ((0, 0), (0, 0), (0, LANES - heads))
    head_rows = jnp.pad(jnp.stack([dt_bias, -jnp.exp(a_log)], axis=1), pad)
    wide = jnp.stack([jnp.repeat(d_skip, P_SIZE, axis=1), gated_gain], axis=1)
    return (conv_x, conv_bc, head_rows, wide)


def head_spread(inner):
    return jnp.asarray(
        np.arange(inner)[:, None] // P_SIZE == np.arange(LANES)[None, :], dtype=BF16
    )


MESH = pl.DeviceIdType.MESH
ANY = pl.BlockSpec(memory_space=pl.ANY)
IN_VMEM = pl.BlockSpec(memory_space=pltpu.VMEM)
PIECES = 4
TENSOR = 4
LATE = 1e9
LAG = 14.0
EIGHTHS = 8
BIG = 6.5
SMALL = 1.1
TINY = 0.2


class Place:
    def __init__(self, line):
        self.line = line
        dp, t = lax.axis_index("dp"), lax.axis_index("tensor")
        self.dp, self.t = dp, t
        self.z, self.x = lax.div(dp, 2), lax.rem(dp, 2)
        self.other = 1 - self.x
        self.sibling = t + 1 - 2 * lax.rem(t, 2)
        self.mate = lax.rem(t + 2, TENSOR)
        self.diagonal = TENSOR - 1 - t
        self.right = (lax.rem(self.z + 1, line) * 2 + self.x, t)
        self.left = (lax.rem(self.z + line - 1, line) * 2 + self.x, t)
        self.across = (self.z * 2 + self.other, t)

    def tensor_peers(self):
        return [(self.dp, self.sibling), (self.dp, self.mate), (self.dp, self.diagonal)]

    def partner(self, bit):
        return (self.dp + bit - 2 * bit * lax.rem(lax.div(self.dp, bit), 2), self.t)

    def greet(self, across=True, far_bits=()):
        barrier = pltpu.get_barrier_semaphore()
        peers = self.tensor_peers()
        if across:
            peers = peers + [self.across]
        peers = peers + [self.partner(bit) for bit in far_bits]
        for peer in peers:
            pl.semaphore_signal(barrier, inc=1, device_id=peer, device_id_type=MESH)
        count = len(peers)
        if across and self.line > 1:
            has_right = self.z < self.line - 1
            has_left = self.z > 0

            @pl.when(has_right)
            def _():
                pl.semaphore_signal(barrier, inc=1, device_id=self.right, device_id_type=MESH)

            @pl.when(has_left)
            def _():
                pl.semaphore_signal(barrier, inc=1, device_id=self.left, device_id_type=MESH)

            count = count + has_right.astype(jnp.int32) + has_left.astype(jnp.int32)
        pl.semaphore_wait(barrier, count)


class Timeline:
    def __init__(self):
        self.steps = []
        self.rolling = []

    def follow(self, eighths, step):
        self.rolling.append((eighths, step))

    def add(self, when, step):
        self.steps.append((when, len(self.steps), step))

    def ordered(self):
        return sorted(self.steps, key=lambda entry: entry[:2])

    def run(self):
        for _, _, step in self.ordered():
            step()

    def spread(self, chunks, slots, chunk_us, order=lambda k: k, lag=LAG):
        places = {}
        rolling = [(-(-offset * slots // EIGHTHS), step) for offset, step in self.rolling]
        for slot, step in rolling:
            for k in range(chunks):
                if (k + 1) * slots + slot >= chunks * slots:
                    when = ((k + 1) * slots + slot) * chunk_us / slots + (lag if 2 * slot > slots else 0.0)
                    self.add(when, functools.partial(step, order(k)))
        after = []
        for when, _, step in self.ordered():
            spot = max(0, int(when / chunk_us * slots))
            if spot < chunks * slots:
                places.setdefault((spot % slots, spot // slots), []).append(step)
            else:
                after.append(step)
        now = pl.program_id(0)

        def hook(place):
            if place * slots % EIGHTHS:
                return
            slot = place * slots // EIGHTHS
            for chunk in range(chunks):
                steps = places.get((slot, chunk))
                if steps:

                    @pl.when(now == chunk)
                    def _(steps=steps):
                        for step in steps:
                            step()

            for offset, step in rolling:
                if offset % slots == slot:
                    behind = 1 + offset // slots
                    step(jnp.where(now >= behind, order(now - behind), -1))

        def end():
            @pl.when(now == chunks - 1)
            def _():
                for step in after:
                    step()

        return hook, end


def remote(src, dst, send, recv, device):
    return pltpu.make_async_remote_copy(
        src_ref=src, dst_ref=dst, send_sem=send, recv_sem=recv, device_id=device, device_id_type=MESH
    )


def gather_semaphores(count, line):
    return [pltpu.SemaphoreType.DMA((count, 2, line))] * 5


HOP_US = 0.8
ADD_US = 0.5


def plan_gather(items, line):
    free, plan = {}, {}
    queue, count = [], itertools.count()

    def push(when, *action):
        heapq.heappush(queue, (when, next(count), action))

    def transfer(link, when, cost):
        begin = max(when, free.get(link, 0.0))
        free[link] = begin + cost
        return begin + cost + HOP_US

    def note(step, when):
        plan[step] = max(plan.get(step, 0.0), when)

    def along(when, way, z, i, source, xs):
        stop = z + 1 if way == 0 else z - 1
        if 0 <= stop < line:
            push(transfer((way, z), when, items[i][1]), "hop", way, stop, i, source, xs)

    def cross(when, z, i, source):
        push(transfer(("x", z), when, items[i][1]), "side", z, i, source)

    for i, (_, _, ready) in enumerate(items):
        push(ready, "own", i)
    while queue:
        when, _, (kind, *rest) = heapq.heappop(queue)
        if kind == "own":
            (i,) = rest
            for z in range(line):
                along(when, 0, z, i, z, 0)
                along(when, 1, z, i, z, 0)
                cross(when, z, i, z)
        elif kind == "hop":
            way, z, i, source, xs = rest
            note(("hop", i, way, abs(z - source), xs), when)
            along(when, way, z, i, source, xs)
            if items[i][0] == "zx":
                cross(when, z, i, source)
        else:
            z, i, source = rest
            note(("side", i), when)
            if items[i][0] == "xz":
                along(when, 0, z, i, source, 1)
                along(when, 1, z, i, source, 1)
    return plan


def gather_weights(place, timeline, items, sems):
    send_r, send_l, send_x, recv_z, recv_x = sems
    line = place.line
    z = place.z

    def copy(i, way, zz, xs, src=None):
        dst = items[i][1](zz, xs)
        return remote(
            dst if src is None else src,
            dst,
            (send_r, send_l, send_x)[way].at[i, xs, zz],
            (recv_x if way == 2 else recv_z).at[i, xs, zz],
            (place.right, place.left, place.across)[way],
        )

    def begin(i):
        own = items[i][0]

        def step():
            @pl.when(z < line - 1)
            def _():
                copy(i, 0, z, place.x, own).start()

            @pl.when(z > 0)
            def _():
                copy(i, 1, z, place.x, own).start()

            copy(i, 2, z, place.x, own).start()

        return step

    def hop(i, way, k, xs, to_x):
        source = z - k if way == 0 else z + k
        here = source >= 0 if way == 0 else source < line
        more = z < line - 1 if way == 0 else z > 0

        def arrive():
            @pl.when(here)
            def _():
                copy(i, way, source, xs).wait_recv()
                if to_x:
                    copy(i, 2, source, xs).start()

            @pl.when(here & more)
            def _():
                copy(i, way, source, xs).start()

        def finish():
            @pl.when(here & more)
            def _():
                copy(i, way, source, xs).wait_send()

            if to_x:

                @pl.when(here)
                def _():
                    copy(i, 2, source, xs).wait_send()

        return arrive, finish

    def side(i):
        def step():
            copy(i, 2, z, place.other).wait_recv()

            @pl.when(z < line - 1)
            def _():
                copy(i, 0, z, place.other).start()

            @pl.when(z > 0)
            def _():
                copy(i, 1, z, place.other).start()

        return step

    def end(i):
        route = items[i][2]

        def step():
            for xs in (place.x,) if route == "zx" else (place.x, place.other):

                @pl.when(z < line - 1)
                def _(xs=xs):
                    copy(i, 0, z, xs).wait_send()

                @pl.when(z > 0)
                def _(xs=xs):
                    copy(i, 1, z, xs).wait_send()

            copy(i, 2, z, place.x).wait_send()

        return step

    def settle(i):
        def step():
            for zz in range(line):
                copy(i, 2, zz, place.other).wait_recv()

        return step

    plan = plan_gather([(item[2], item[3], 0.0) for item in items], line)
    for i, (_, _, route, _, early) in enumerate(items):
        timeline.add(0.0, begin(i))
        if route == "xz":
            timeline.add(plan["side", i], side(i))
        for way in (0, 1):
            for column, xs in enumerate((place.x,) if route == "zx" else (place.x, place.other)):
                when = plan["side", i] if column else 0.0
                for k in range(1, line):
                    when = max(plan["hop", i, way, k, column], when + 0.01)
                    arrive, finish = hop(i, way, k, xs, route == "zx")
                    timeline.add(when, arrive)
                    timeline.add(LATE, finish)
        if route == "zx":
            timeline.add(plan["side", i] + 1.0 if early else LATE, settle(i))
        timeline.add(LATE, end(i))
    return plan


def scatter_semaphores(count, line):
    return [pltpu.SemaphoreType.DMA((count, 2, line))] * 6


def add_into(target, other, rows):
    step = 48 if rows % 48 == 0 else rows

    def body(n, carry):
        part = pl.ds(pl.multiple_of(n * step, step), step)
        target[part, :] = (target[part, :].astype(F32) + other[part, :].astype(F32)).astype(BF16)
        return carry

    lax.fori_loop(0, rows // step, body, 0)


def scatter_order(line):
    order = []
    for n in range((line + 1) // 2):
        order += [n] if n == line - 1 - n else [n, line - 1 - n]
    return order


def plan_scatter(items, line):
    free, arrived, joined, plan = {}, {}, {}, {}
    queue, count = [], itertools.count()

    def push(when, *action):
        heapq.heappush(queue, (when, next(count), action))

    def transfer(link, when, cost):
        begin = max(when, free.get(link, 0.0))
        free[link] = begin + cost
        return begin + cost + HOP_US

    def note(step, when):
        plan[step] = max(plan.get(step, 0.0), when)

    def go(when, z, i, zz, xs):
        first = {"r": z == 0, "l": z == line - 1}
        if z == zz:
            need = [way for way, there in (("r", z > 0), ("l", z < line - 1)) if there]
            times = [arrived.get((way, z, i, zz, xs)) for way in need] + [joined.get((z, i, zz, xs))]
            if None in times:
                return
            when = max(times)
            if items[i][0] == "xz":
                note(("last", i), when)
                return
            note(("line", i, xs), when)
            done = joined.setdefault(("line", z, i), [])
            done.append(when)
            if len(done) == 2:
                note(("swap", i), max(done))
                note(("last", i), transfer(("x", z), max(done) + 2 * ADD_US, items[i][1]))
            return
        way = "r" if z < zz else "l"
        times = [joined.get((z, i, zz, xs))]
        if not first[way]:
            times.append(arrived.get((way, z, i, zz, xs)))
        if None in times:
            return
        when = max(times)
        h = z if way == "r" else line - 1 - z
        note(("send", i, zz, way, xs, h), when)
        stop = z + 1 if way == "r" else z - 1
        push(transfer((way, z), when + ADD_US, items[i][1]), "arrive", way, stop, i, zz, xs)

    for i, (route, cost, ready) in enumerate(items):
        for zz in scatter_order(line):
            for xs in (0,) if route == "xz" else (0, 1):
                push(ready, "start", i, zz, xs)
    while queue:
        when, _, (kind, *rest) = heapq.heappop(queue)
        if kind == "start":
            i, zz, xs = rest
            for z in range(line):
                if items[i][0] == "xz":
                    push(transfer(("x", z), when, items[i][1]), "join", z, i, zz, xs)
                else:
                    push(when, "join", z, i, zz, xs)
        elif kind == "join":
            z, i, zz, xs = rest
            if items[i][0] == "xz":
                note(("join", i, zz), when)
                when += ADD_US
            joined[z, i, zz, xs] = when
            go(when, z, i, zz, xs)
        else:
            way, z, i, zz, xs = rest
            arrived[way, z, i, zz, xs] = when
            go(when, z, i, zz, xs)
    return plan


def scatter_weights(place, timeline, items, sems):
    send_x, recv_x, send_r, recv_r, send_l, recv_l = sems
    line = place.line
    z = place.z

    def rows_of(i):
        return items[i][2][0].shape[1]

    def side(i, zz):
        _, source, (land_x, _), *_ = items[i]
        return remote(
            source(zz, place.other), land_x.at[zz], send_x.at[i, 0, zz], recv_x.at[i, 0, zz], place.across
        )

    def land_along(i, zz, way, xs, stop):
        slot = zz if way == 0 else jnp.where(stop == zz, line, zz)
        land = items[i][2][1]
        return land.at[slot, xs] if items[i][4] == "zx" else land.at[slot]

    def along(i, zz, way, xs, source=None):
        here = land_along(i, zz, way, xs, z)
        return remote(
            here if source is None else source,
            land_along(i, zz, way, xs, z + 1 if way == 0 else z - 1),
            (send_r, send_l)[way].at[i, xs, zz],
            (recv_r, recv_l)[way].at[i, xs, zz],
            (place.right, place.left)[way],
        )

    def own(i, zz, xs):
        return items[i][0](zz, xs) if items[i][4] == "zx" else items[i][2][0].at[zz]

    def outgoing(i, zz, xs):
        return items[i][1](zz, xs) if items[i][4] == "zx" else items[i][2][0].at[zz]

    def join(i, zz):
        def step():
            side(i, zz).wait_recv()
            add_into(items[i][2][0].at[zz], items[i][0](zz, place.x), rows_of(i))

        return step

    def send(i, zz, way, xs, h):
        if way == 0:
            mine = (z == h) & (z < zz)
        else:
            mine = (z == line - 1 - h) & (z > zz)

        def step():
            @pl.when(mine)
            def _():
                if h == 0:
                    along(i, zz, way, xs, outgoing(i, zz, xs)).start()
                else:
                    along(i, zz, way, xs).wait_recv()
                    add_into(land_along(i, zz, way, xs, z), own(i, zz, xs), rows_of(i))
                    along(i, zz, way, xs).start()

        return step

    def last(i):
        out = items[i][3]

        def step():
            out[...] = items[i][2][0][z].astype(F32)
            for way, there in ((0, z > 0), (1, z < line - 1)):

                @pl.when(there)
                def _(way=way):
                    along(i, z, way, 0).wait_recv()
                    out[...] += items[i][2][1][z if way == 0 else line].astype(F32)

        return step

    def swap(i):
        land_x, land = items[i][2]
        stage = land.at[z, place.other]
        return remote(stage, land_x.at[0], send_x.at[i, 0, 0], recv_x.at[i, 0, 0], place.across)

    def gather_line(i, xs):
        piece = items[i][0]

        def step():
            right, left = land_along(i, z, 0, xs, z), land_along(i, z, 1, xs, z)

            @pl.when(z > 0)
            def _():
                along(i, z, 0, xs).wait_recv()
                add_into(right, piece(z, xs), rows_of(i))

            @pl.when(z == 0)
            def _():
                right[...] = piece(z, xs)[...]

            @pl.when(z < line - 1)
            def _():
                along(i, z, 1, xs).wait_recv()
                add_into(right, left, rows_of(i))

        return step

    def swap_end(i):
        (land_x, land), out = items[i][2:4]

        def step():
            swap(i).wait()
            out[...] = land[z, place.x].astype(F32) + land_x[0].astype(F32)

        return step

    def end(i, zz, xs):
        def step():
            if items[i][4] == "xz":
                side(i, zz).wait_send()
            for way, there in ((0, z < zz), (1, z > zz)):

                @pl.when(there)
                def _(way=way):
                    along(i, zz, way, xs).wait_send()

        return step

    plan = plan_scatter([item[4:] for item in items], line)
    for i, (_, _, _, _, route, _, ready) in enumerate(items):
        columns = (0,) if route == "xz" else (0, 1)
        latest = ready
        for zz in scatter_order(line):
            if route == "xz":
                timeline.add(ready, lambda i=i, zz=zz: side(i, zz).start())
                timeline.add(plan["join", i, zz], join(i, zz))
                latest = max(latest, plan["join", i, zz])
            for xs in columns:
                for way, name in enumerate("rl"):
                    when = plan.get(("join", i, zz), ready)
                    for h in range(zz if way == 0 else line - 1 - zz):
                        when = max(plan["send", i, zz, name, xs, h], when + 0.01)
                        timeline.add(when, send(i, zz, way, xs, h))
                    latest = max(latest, when)
                timeline.add(LATE, end(i, zz, xs))
        latest += 0.01
        if route == "xz":
            timeline.add(max(plan["last", i], latest), last(i))
            continue
        swaps = max(plan["swap", i], latest) + ADD_US
        for xs in columns:
            timeline.add(max(plan["line", i, xs], latest), gather_line(i, xs))
        timeline.add(swaps, lambda i=i: swap(i).start())
        timeline.add(max(plan["last", i], swaps + 0.01), swap_end(i))


def spread_semaphores():
    return [pltpu.SemaphoreType.DMA((PIECES,))] * 6


def spread_rows(place, own, whole, sems):
    send_y, recv_y, send_s, recv_s, send_f, recv_f = sems
    rows = own.shape[0]
    step = rows // PIECES

    def at(owner, p):
        return whole.at[pl.ds(pl.multiple_of(owner * rows, rows) + p * step, step), :]

    def source(p):
        return own.at[pl.ds(p * step, step), :]

    def to_mate(p):
        return remote(
            source(p), at(place.t, p), send_y.at[p], recv_y.at[p], (place.dp, place.mate)
        )

    def to_sibling(p):
        return remote(
            source(p), at(place.t, p), send_s.at[p], recv_s.at[p], (place.dp, place.sibling)
        )

    def passed_on(p):
        return remote(
            at(place.mate, p), at(place.mate, p), send_f.at[p], recv_f.at[p], (place.dp, place.sibling)
        )

    def begin(p):
        to_mate(p).start()
        to_sibling(p).start()

    def forward(p):
        to_mate(p).wait_recv()
        passed_on(p).start()

    def finish():
        for p in range(PIECES):
            to_mate(p).wait_send()
            to_sibling(p).wait()
            passed_on(p).wait()

    return begin, forward, finish


def reduce_semaphores():
    return [pltpu.SemaphoreType.DMA((PIECES,))] * 6


def roll_rows(place, timeline, part, lands, sems, owner, forward, slot=4):
    land_far, land_near, land_mate = lands
    send_a, recv_a, send_b, recv_b, send_z, recv_z = sems
    rows = land_far.shape[0]
    step = rows // PIECES

    def at(block, p):
        return part.at[pl.ds(pl.multiple_of(block * rows, rows) + p * step, step), :]

    def own(ref, p):
        return ref.at[pl.ds(p * step, step), :]

    def far(p):
        return remote(
            at(place.diagonal, p), own(land_far, p), send_a.at[p], recv_a.at[p], (place.dp, place.sibling)
        )

    def near(p):
        return remote(
            at(place.sibling, p), own(land_near, p), send_b.at[p], recv_b.at[p], (place.dp, place.sibling)
        )

    def over(p):
        return remote(
            own(land_far, p), own(land_mate, p), send_z.at[p], recv_z.at[p], (place.dp, place.mate)
        )

    def begin(chunk):
        @pl.when(place.diagonal == chunk)
        def _():
            for p in range(PIECES):
                far(p).start()

        @pl.when(place.sibling == chunk)
        def _():
            for p in range(PIECES):
                near(p).start()

    def middle(p, chunk):
        @pl.when(place.mate == chunk)
        def _():
            far(p).wait_recv()
            mine = own(land_far, p)
            mine[...] = (mine[...].astype(F32) + at(place.mate, p)[...].astype(F32)).astype(BF16)
            over(p).start()

    def final(p, chunk):
        @pl.when(place.t == chunk)
        def _():
            near(p).wait_recv()
            over(p).wait_recv()
            sums = at(place.t, p)[...].astype(F32) + own(land_near, p)[...].astype(F32)
            owner(p, sums + own(land_mate, p)[...].astype(F32))

    def pass_on(p, chunk):
        @pl.when(place.mate == chunk)
        def _():
            forward(p)

    def finish():
        for p in range(PIECES):
            far(p).wait_send()
            near(p).wait_send()
            over(p).wait_send()

    timeline.follow(0, begin)
    for p in range(PIECES):
        timeline.follow(1 + p // 2, functools.partial(middle, p))
        timeline.follow(slot + 3 * p, functools.partial(final, p))
        if forward:
            timeline.follow(slot + 4 + 3 * p, functools.partial(pass_on, p))
    timeline.add(LATE, finish)


def share_semaphores():
    return [pltpu.SemaphoreType.DMA((3,))] * 2


def share_blocks(place, source_of, target_of, sems):
    send, recv = sems
    peers = (place.sibling, place.mate, place.diagonal)
    return [
        remote(source_of(peer), target_of(n), send.at[n], recv.at[n], (place.dp, peer))
        for n, peer in enumerate(peers)
    ]


def row_norm(state):
    return lax.rsqrt(jnp.mean(state * state, axis=1, keepdims=True) + epsilon)


def by_rows_piece(whole, rows, start=0, count=None):
    count = rows if count is None else count

    def piece(zz, xs):
        return whole.at[pl.ds(pl.multiple_of((zz * 2 + xs) * rows, rows) + start, count), :]

    return piece


def own_copies(place, blocks, sems):
    return [
        pltpu.make_async_copy(own, piece(place.z, place.x), sems.at[n])
        for n, (own, piece) in enumerate(blocks)
    ]


def weight_gather(place, timeline, refs, wholes, sems, share_sems, own_sems):
    bc_own, bc_all = refs[4], wholes[4]
    rows = refs[0].shape[0]
    head, tail = halves(rows)
    pieces = [by_rows_piece(whole, rows) for whole in wholes[:3]]
    step_all = wholes[3]

    def bc_piece(zz, xs):
        return bc_all.at[zz * 2 + xs, place.t]

    items = [
        (bc_own, bc_piece, "zx", SMALL / 2, True),
        (refs[3], lambda zz, xs: step_all.at[zz * 2 + xs], "zx", TINY, False),
        (refs[1], pieces[1], "zx", BIG, False),
        (refs[0], pieces[0], "zx", BIG, False),
        (refs[2].at[pl.ds(0, head), :], by_rows_piece(wholes[2], rows, 0, head), "xz", BIG / 2, False),
        (refs[2].at[pl.ds(head, tail), :], by_rows_piece(wholes[2], rows, head, tail), "zx", BIG / 2, False),
    ]
    copies = own_copies(place, [(item[0], item[1]) for item in items], own_sems)
    shares = share_blocks(
        place, lambda peer: bc_all.at[:, place.t], lambda n: bc_all.at[:, place.t], share_sems
    )
    timeline.add(-1.0, lambda: [copy.start() for copy in copies] and None)
    timeline.add(1.0, lambda: copies[0].wait())
    plan = gather_weights(place, timeline, items, sems)
    timeline.add(plan["side", 0] + 1.1, lambda: [copy.start() for copy in shares] and None)
    timeline.add(LATE + 1, lambda: [copy.wait() for copy in shares] and None)
    timeline.add(LATE + 1, lambda: [copy.wait() for copy in copies[1:]] and None)


def gather_outputs(line, width, inner, dp):
    shape = jax.ShapeDtypeStruct
    return [
        shape((width, inner), BF16),
        shape((width, inner), BF16),
        shape((width, inner), BF16),
        shape((dp, STEPS, width // dp), BF16),
        shape((dp, TENSOR, width // (dp * TENSOR), 2 * N), BF16),
    ]


def gather_scratch(line):
    return gather_semaphores(6, line) + share_semaphores() + [pltpu.SemaphoreType.DMA((6,))]


def start_kernel(line, resid, cotangent, gain, *refs):
    own, wholes, refs = refs[:5], refs[5:10], refs[10:]
    rows_all, top_all, normed, low = refs[:4]
    sems, share_sems, own_sems = refs[4:9], refs[9:11], refs[11]
    rows_sems, top_sems, local = refs[12:18], refs[18:24], refs[24]
    place = Place(line)
    place.greet()
    timeline = Timeline()
    own = [ref.at[0] for ref in own]
    weight_gather(place, timeline, own, wholes, sems, share_sems, own_sems)
    rows = normed.shape[0]
    block = pl.ds(pl.multiple_of(place.t * rows, rows), rows)
    local_copies = [
        pltpu.make_async_copy(normed, rows_all.at[block, :], local.at[0]),
        pltpu.make_async_copy(low, top_all.at[block, :], local.at[1]),
    ]

    def prepare():
        state = resid[...].astype(F32)
        normed[...] = (state * row_norm(state) * gain[0:1, :]).astype(BF16)
        low[...] = cotangent[...].astype(BF16)
        for copy in local_copies:
            copy.start()

    timeline.add(0.5, prepare)
    for n, (source, whole, group) in enumerate(((normed, rows_all, rows_sems), (low, top_all, top_sems))):
        begin, forward, finish = spread_rows(place, source, whole, group)
        for p in range(PIECES):
            timeline.add(0.6, functools.partial(begin, p))
            timeline.add(1.0 + (4 * n + p + 1) * 4.4, functools.partial(forward, p))
        timeline.add(LATE, finish)
    timeline.add(LATE, lambda: [copy.wait() for copy in local_copies] and None)
    timeline.run()


def call_kernel(kernel, outs, in_specs, out_specs, scratch, number, args, grid=()):
    return pl.pallas_call(
        kernel,
        grid=grid,
        out_shape=outs,
        in_specs=in_specs,
        out_specs=out_specs,
        scratch_shapes=scratch,
        compiler_params=pltpu.CompilerParams(
            collective_id=number, has_side_effects=True, vmem_limit_bytes=VMEM_LIMIT
        ),
    )(*args)


def start_layer(line, resid, cotangent, gain, own):
    rows, width = resid.shape
    inner = own[0].shape[2]
    shape = jax.ShapeDtypeStruct
    outs = gather_outputs(line, width, inner, 2 * line) + [
        shape((rows * TENSOR, width), BF16),
        shape((rows * TENSOR, width), BF16),
    ]
    scratch = [pltpu.VMEM((rows, width), BF16)] * 2 + gather_scratch(line)
    scratch += spread_semaphores() * 2 + [pltpu.SemaphoreType.DMA((2,))]
    return call_kernel(
        functools.partial(start_kernel, line),
        outs,
        [IN_VMEM] * 3 + [ANY] * 5,
        [ANY] * 7,
        scratch,
        0,
        (resid, cotangent, gain, *own),
    )


def scale_steps(place, timeline, sq, land, scale_row, scale_col, sems, inner_all):
    rows = scale_col.shape[0]

    def at(owner):
        return sq.at[:, pl.ds(pl.multiple_of(owner * rows, rows), rows)]

    peers = (place.sibling, place.mate, place.diagonal)
    copies = share_blocks(place, at, lambda n: land.at[n], sems)

    def begin(chunk):
        for peer, copy in zip(peers, copies):
            pl.when(peer == chunk)(copy.start)

    def arrive(chunk):
        @pl.when(place.t == chunk)
        def _():
            for copy in copies:
                copy.wait_recv()
            squares = at(place.t)[...] + land[0] + land[1] + land[2]
            scale = lax.rsqrt(squares / inner_all + epsilon)
            scale_row[...] = scale
            scale_col[...] = jnp.transpose(scale)

    def finish():
        for copy in copies:
            copy.wait_send()

    timeline.follow(0, begin)
    timeline.follow(FORWARD_SLOT - 1, arrive)
    timeline.add(LATE, finish)


FORWARD_SLOTS = 8
BACKWARD_SLOTS = 8
FORWARD_US = 6.7
FORWARD_SLOT = 8


def middle_kernel(line, inner_all, *refs):
    work, refs = refs[:12], refs[12:]
    (resid, gain), own, refs = refs[:2], refs[2:7], refs[7:]
    saved, refs = refs[:9], refs[9:]
    state_out, raw_out, scale_row, rows_all, refs = *refs[:4], refs[4:]
    wholes, refs = refs[:5], refs[5:]
    scratch, refs = refs[:5], refs[5:]
    part, sq, far, near, mate, land, scale_col, normed = refs[:8]
    refs = refs[8:]
    sems, share_sems, own_sems = refs[:5], refs[5:7], refs[7]
    reduce_sems, sq_sems, rows_sems, local = refs[8:14], refs[14:16], refs[16:22], refs[22]
    chunk = pl.program_id(0)
    chunks = part.shape[0] // CHUNK
    place = Place(line)
    pl.when(chunk == 0)(place.greet)
    timeline = Timeline()
    scale_steps(place, timeline, sq, land, scale_row, scale_col, sq_sems, inner_all)
    rows = normed.shape[0]
    step = rows // PIECES
    begin, forward, finish = spread_rows(place, normed, rows_all, rows_sems)

    def owner(p, sums):
        part_rows = slice(p * step, (p + 1) * step)
        raw_out[part_rows, :] = sums
        state = resid[part_rows, :].astype(F32) + sums * scale_col[part_rows, 0:1]
        state_out[part_rows, :] = state
        normed[part_rows, :] = (state * row_norm(state) * gain[1:2, :]).astype(BF16)
        begin(p)

    roll_rows(
        place, timeline, part, (far, near, mate), reduce_sems, owner, forward, FORWARD_SLOT
    )
    own = [ref.at[1] for ref in own]
    weight_gather(place, timeline, own, wholes, sems, share_sems, own_sems)
    block = pl.ds(pl.multiple_of(place.t * rows, rows), rows)
    keep = pltpu.make_async_copy(normed, rows_all.at[block, :], local.at[0])
    timeline.add(LATE, keep.start)
    timeline.add(LATE, finish)
    timeline.add(LATE, keep.wait)
    hook, end = timeline.spread(chunks, FORWARD_SLOTS, FORWARD_US)
    at = pl.multiple_of(chunk * CHUNK, CHUNK)
    forward_kernel(
        *work, part.at[pl.ds(at, CHUNK), :], sq.at[:, pl.ds(at, CHUNK)], *saved, *scratch, hook=hook
    )
    end()


def row_scratch(length, rows, width):
    return [
        pltpu.VMEM((length, width), BF16),
        pltpu.VMEM((8, length), F32),
        pltpu.VMEM((rows, width), BF16),
        pltpu.VMEM((rows, width), BF16),
        pltpu.VMEM((rows, width), BF16),
        pltpu.VMEM((3, 8, rows), F32),
        pltpu.VMEM((rows, 8), F32),
    ]


def middle_layer(line, inner_all, rows_all, weights, layer_args, aux, segrow, resid, gain, own):
    rows, width = resid.shape
    length = rows_all.shape[0]
    inner = own[0].shape[2]
    shape = jax.ShapeDtypeStruct
    outs = (
        saved_shapes(length, inner)
        + [
            shape((rows, width), F32),
            shape((rows, width), F32),
            shape((8, rows), F32),
            shape((length, width), BF16),
        ]
        + gather_outputs(line, width, inner, 2 * line)
    )
    scratch = forward_scratch(inner) + row_scratch(length, rows, width)
    scratch += [pltpu.VMEM((rows, width), BF16)]
    scratch += gather_scratch(line) + reduce_semaphores() + share_semaphores() + spread_semaphores()
    scratch += [pltpu.SemaphoreType.DMA((1,))]
    return call_kernel(
        functools.partial(middle_kernel, line, inner_all),
        outs,
        forward_in_specs(0, rows_all, weights, layer_args)
        + [whole_spec(resid.shape), whole_spec(gain.shape)]
        + [ANY] * 5,
        saved_specs(inner)
        + [whole_spec((rows, width)), whole_spec((rows, width)), whole_spec((8, rows))]
        + [ANY] * 6,
        scratch,
        1,
        (rows_all, *weights, *layer_args, aux, segrow, resid, gain, *own),
        (length // CHUNK,),
    )


def per_row_steps(place, timeline, scale_row, cross_col, stage, land, out, sems, inner_all, slot):
    rows = cross_col.shape[0]
    copies = share_blocks(place, lambda peer: stage, lambda n: land.at[n], sems)
    peers = (place.sibling, place.mate, place.diagonal)

    def send():
        cross = jnp.transpose(jnp.broadcast_to(cross_col[:, 0:1], (rows, LANES)))[0:8, :]
        scale = scale_row[...]
        coef = scale * scale * scale * cross / inner_all
        stage[...] = jnp.where(iota2((8, rows), 0) == 0, scale, coef)
        for copy in copies:
            copy.start()
        out[:, pl.ds(pl.multiple_of(place.t * rows, rows), rows)] = stage[...]

    def follow(chunk):
        pl.when(place.t == chunk)(send)

    def arrive():
        for n, (copy, peer) in enumerate(zip(copies, peers)):
            copy.wait()
            out[:, pl.ds(pl.multiple_of(peer * rows, rows), rows)] = land[n]

    timeline.follow(slot + 1 + 3 * (PIECES - 1), follow)
    timeline.add(LATE, arrive)


def top_kernel(line, inner_all, *refs):
    work, (state, cotangent), refs = refs[:12], refs[12:14], refs[14:]
    saved, (hidden, per_row), refs = refs[:9], refs[9:11], refs[11:]
    scratch, refs = refs[:5], refs[5:]
    part, sq, far, near, mate, sq_land, scale_col = refs[:7]
    row_land, scale_row, cross_col, stage = refs[7:11]
    reduce_sems, sq_sems, row_sems = refs[11:17], refs[17:19], refs[19:21]
    chunk = pl.program_id(0)
    chunks = part.shape[0] // CHUNK
    place = Place(line)
    pl.when(chunk == 0)(lambda: place.greet(across=False))
    timeline = Timeline()
    scale_steps(place, timeline, sq, sq_land, scale_row, scale_col, sq_sems, inner_all)
    step = cross_col.shape[0] // PIECES

    def owner(p, sums):
        part_rows = slice(p * step, (p + 1) * step)
        hidden[part_rows, :] = state[part_rows, :] + sums * scale_col[part_rows, 0:1]
        low = cotangent[part_rows, :].astype(BF16).astype(F32)
        cross = jnp.sum(low * sums, axis=1, keepdims=True)
        cross_col[part_rows, :] = jnp.broadcast_to(cross, (step, LANES))

    roll_rows(place, timeline, part, (far, near, mate), reduce_sems, owner, None, FORWARD_SLOT)
    per_row_steps(
        place, timeline, scale_row, cross_col, stage, row_land, per_row, row_sems, inner_all,
        FORWARD_SLOT,
    )
    hook, end = timeline.spread(chunks, FORWARD_SLOTS, FORWARD_US)
    at = pl.multiple_of(chunk * CHUNK, CHUNK)
    forward_kernel(
        *work, part.at[pl.ds(at, CHUNK), :], sq.at[:, pl.ds(at, CHUNK)], *saved, *scratch, hook=hook
    )
    end()


def top_layer(line, inner_all, rows_all, weights, layer_args, aux, segrow, state, cotangent):
    rows, width = state.shape
    length = rows_all.shape[0]
    inner = weights[0].shape[1]
    shape = jax.ShapeDtypeStruct
    scratch = forward_scratch(inner) + row_scratch(length, rows, width)
    scratch += [
        pltpu.VMEM((3, 8, rows), F32),
        pltpu.VMEM((8, rows), F32),
        pltpu.VMEM((rows, LANES), F32),
        pltpu.VMEM((8, rows), F32),
    ]
    scratch += reduce_semaphores() + share_semaphores() * 2
    return call_kernel(
        functools.partial(top_kernel, line, inner_all),
        saved_shapes(length, inner) + [shape((rows, width), F32), shape((8, length), F32)],
        forward_in_specs(1, rows_all, weights, layer_args)
        + [whole_spec(state.shape), whole_spec(cotangent.shape)],
        saved_specs(inner) + [whole_spec((rows, width)), whole_spec((8, length))],
        scratch,
        2,
        (rows_all, *weights, *layer_args, aux, segrow, state, cotangent),
        (length // CHUNK,),
    )


def halves(rows):
    first = max(rows // 32 * 16, 16)
    return first, rows - first


def thirds(rows):
    first = max(rows // 64 * 16, 16)
    return (first, *halves(rows - first))


BACKWARD_US = 10.0
END_LAG = 7.0
DOTS_US = 6.0


def weight_scatter(
    place, timeline, grads, early, outs, lands, sems, bc_land, bc_sum, share_sems, late
):
    bc = grads[4]
    shares = share_blocks(
        place, lambda peer: bc.at[:, peer], lambda n: bc_land.at[n], share_sems
    )
    bc_ready = late + 12.0

    def bc_add():
        for copy in shares:
            copy.wait()

        def body(n, carry):
            total = bc[n, place.t].astype(F32) + bc_land[0, n].astype(F32)
            total = total + bc_land[1, n].astype(F32) + bc_land[2, n].astype(F32)
            bc_sum[n] = total.astype(BF16)
            return carry

        lax.fori_loop(0, bc.shape[0], body, 0)

    timeline.add(late, lambda: [copy.start() for copy in shares] and None)
    timeline.add(bc_ready, bc_add)
    rows = outs[0].shape[0]
    head, tail = halves(rows)
    first, second = pl.ds(0, head), pl.ds(head, tail)

    def low(ref):
        return by_rows_piece(ref, rows, 0, head)

    def high(ref):
        return by_rows_piece(ref, rows, head, tail)

    def shared(zz, xs):
        return bc_sum.at[zz * 2 + xs]

    def steps(zz, xs):
        return grads[3].at[zz * 2 + xs]

    count = thirds(rows)
    starts = (0, count[0], count[0] + count[1])

    def third(n):
        return by_rows_piece(grads[2], rows, starts[n], count[n])

    def inner_item(n, route):
        out = outs[2].at[pl.ds(starts[n], count[n]), :]
        return (third(n), third(n), lands[6 + 2 * n : 8 + 2 * n], out, route, BIG * count[n] / rows, late)

    items = [
        (low(grads[0]), low(early[0]), lands[0:2], outs[0].at[first, :], "zx", BIG / 2, 0.0),
        (high(grads[0]), high(early[0]), lands[2:4], outs[0].at[second, :], "xz", BIG / 2, 0.0),
        (by_rows_piece(grads[1], rows), by_rows_piece(early[1], rows), lands[4:6], outs[1], "xz", BIG, 0.0),
        inner_item(0, "zx"),
        inner_item(1, "xz"),
        inner_item(2, "xz"),
        (steps, steps, lands[12:14], outs[3], "xz", TINY, late),
        (shared, shared, lands[14:16], outs[4], "xz", SMALL / 2, bc_ready + 0.1),
    ]
    scatter_weights(place, timeline, items, sems)


def scatter_outputs(width, inner, dp):
    shape = jax.ShapeDtypeStruct
    rows = width // dp
    return [shape((rows, inner), F32)] * 3 + [
        shape((STEPS, rows), F32),
        shape((rows // TENSOR, 2 * N), F32),
    ]


def scatter_scratch(line, width, inner):
    dp = 2 * line
    rows = width // dp
    head, tail = halves(rows)
    fine = rows // TENSOR
    scratch = [
        pltpu.VMEM((1, head, inner), BF16),
        pltpu.VMEM((line + 1, 2, head, inner), BF16),
    ]
    few, some, more = thirds(rows)
    for count, cols in ((tail, inner), (rows, inner)):
        scratch += [pltpu.VMEM((line, count, cols), BF16), pltpu.VMEM((line + 1, count, cols), BF16)]
    scratch += [
        pltpu.VMEM((1, few, inner), BF16),
        pltpu.VMEM((line + 1, 2, few, inner), BF16),
    ]
    for count, cols in ((some, inner), (more, inner), (STEPS, rows), (fine, 2 * N)):
        scratch += [pltpu.VMEM((line, count, cols), BF16), pltpu.VMEM((line + 1, count, cols), BF16)]
    scratch += [
        pltpu.VMEM((3, dp, fine, 2 * N), BF16),
        pltpu.VMEM((dp, fine, 2 * N), BF16),
    ]
    return scratch + scatter_semaphores(8, line) + share_semaphores()


def input_gradient(state, gain, before, sums):
    scale = row_norm(state)
    gained = sums * gain
    mean = jnp.mean(gained * state, axis=1, keepdims=True)
    grad = before + scale * gained - state * (scale * scale * scale * mean)
    return grad, jnp.sum(sums * state * scale, axis=0, keepdims=True)


def late_dots(rows_all, ginner, gstep, gshared, dinner, dstep, dshared):
    dp, tensor, fine, _ = dshared.shape
    tile = rows_all.shape[1] // 2
    per_tile = tile // (tensor * fine)
    rows = tensor * fine

    def body(n, carry):
        part = pl.ds(pl.multiple_of(n * tile, tile), tile)
        left = rows_all[:, part]
        dinner[part, :] = contract(left, ginner[...])
        steps = contract_wide(gstep[...], left)[0:STEPS, :].astype(BF16)
        for m in range(per_tile):
            dstep[n * per_tile + m] = steps[:, m * rows : (m + 1) * rows]
        shared = contract_wide(left, gshared[...])
        for m in range(per_tile * tensor):
            block = shared[m * fine : (m + 1) * fine, :].astype(BF16)
            dshared[n * per_tile + m // tensor, m % tensor] = block
        return carry

    lax.fori_loop(0, 2, body, 0)


def pull_kernel(line, inner_all, final, *refs):
    work, refs = refs[:21], refs[21:]
    far_side, gain, refs = refs[:5], refs[5], refs[6:]
    if final:
        gnorm_top, small_more, small_top, small_top_more, bc_top, refs = *refs[:5], refs[5:]
        grad_out, norm_sum, small_sum, bc_sums, refs = *refs[:4], refs[4:]
    else:
        raw, scale_row, refs = *refs[:2], refs[2:]
        grad_out, gnorm, per_row, top_all, small, small_bc, refs = *refs[:6], refs[6:]
    outs, refs = refs[:5], refs[5:]
    scratch, refs = refs[:7], refs[7:]
    near_side, load_sems, refs = refs[:5], refs[5], refs[6:]
    rows_all, dout, dgate, before, state = near_side
    loads = [
        pltpu.make_async_copy(source, target, load_sems.at[n])
        for n, (source, target) in enumerate(zip(far_side, near_side))
    ]
    part, ginner, gstep, gshared, dinner, dstep, dshared = refs[:7]
    far, near, mate, refs = *refs[7:10], refs[10:]
    lands, bc_land, bc_sum, sems, share_sems = refs[:16], refs[16], refs[17], refs[18:24], refs[24:26]
    reduce_sems, refs = refs[26:32], refs[32:]
    if final:
        small, small_bc, small_land, bc_land_sums, norm_land = refs[:5]
        small_send, small_recv = refs[5:]
    else:
        row_land, cross_col, stage, low = refs[:4]
        row_sems, top_sems, local = refs[4:6], refs[6:12], refs[12]
    dp = 2 * line
    bits = [1 << n for n in range(dp.bit_length() - 1)]
    chunk = pl.program_id(0)
    chunks = part.shape[0] // CHUNK
    place = Place(line)
    far_bits = [bit for bit in bits if bit >= 4] if final else []
    pl.when(chunk == 0)(lambda: place.greet(far_bits=far_bits))
    timeline = Timeline()
    done = BACKWARD_US * chunks + 0.5
    late = done + 2.2 + DOTS_US
    rows = state.shape[0]
    step = rows // PIECES

    if not final:
        begin, forward, finish = spread_rows(place, low, top_all, top_sems)

    def clear():
        if final:
            norm_sum[...] = jnp.zeros_like(norm_sum)
            norm_sum[1:2, :] = gnorm_top[0:1, :]
        else:
            gnorm[...] = jnp.zeros_like(gnorm)

    def load():
        for n in (1, 2, 3, 4, 0):
            loads[n].start()

    timeline.add(-2.0, load)
    timeline.add(-2.0, clear)
    for n in (1, 2, 3, 4, 0):
        timeline.add(2.5 if n in (1, 2) else BACKWARD_US / 2, loads[n].wait)

    def own_gain():
        return gain[0:1, :] if final else gain[1:2, :]

    def owner(p, sums):
        part_rows = slice(p * step, (p + 1) * step)
        grad, column = input_gradient(
            state[part_rows, :].astype(F32), own_gain(), before[part_rows, :], sums
        )
        grad_out[part_rows, :] = grad
        if final:
            norm_sum[0:1, :] += column
            return
        gnorm[0:1, :] += column
        low[part_rows, :] = grad.astype(BF16)
        cross = jnp.sum(low[part_rows, :].astype(F32) * raw[part_rows, :], axis=1, keepdims=True)
        cross_col[part_rows, :] = jnp.broadcast_to(cross, (step, LANES))
        begin(p)

    roll_rows(
        place, timeline, part, (far, near, mate), reduce_sems, owner, None if final else forward
    )
    timeline.add(
        done + 2.2, lambda: late_dots(rows_all, ginner, gstep, gshared, dinner, dstep, dshared)
    )
    if not final:
        block = pl.ds(pl.multiple_of(place.t * rows, rows), rows)
        keep = pltpu.make_async_copy(low, top_all.at[block, :], local.at[0])
        timeline.follow(5 + 3 * (PIECES - 1), lambda chunk: pl.when(place.t == chunk)(keep.start))
        timeline.add(LATE, keep.wait)
        timeline.add(LATE, finish)
        per_row_steps(
            place, timeline, scale_row, cross_col, stage, row_land, per_row, row_sems, inner_all, 4
        )
    grads = (dout, dgate, dinner, dstep, dshared)
    weight_scatter(
        place, timeline, grads, far_side[1:3], outs, lands, sems, bc_land, bc_sum, share_sems, late
    )
    if final:

        def pack():
            small_sum[0:8, :] = small[...] + small_more[...]
            small_sum[8:16, :] = small_top[...] + small_top_more[...]
            bc_sums[0:8, :] = small_bc[...]
            bc_sums[8:16, :] = bc_top[...]

        timeline.add(done + 0.05, pack)
        along = [place.partner(bit) for bit in bits]
        across = [(place.dp, place.sibling), (place.dp, place.mate)]

        def exchange(n, partner, group, start, end):
            copies = [
                remote(own, land.at[n], small_send.at[n, m], small_recv.at[n, m], partner)
                for m, own, land in group
            ]

            def send():
                for copy in copies:
                    copy.start()

            def take():
                for copy, (_, own, land) in zip(copies, group):
                    copy.wait()
                    own[...] += land[n]

            timeline.add(start, send)
            timeline.add(end, take)

        when = BACKWARD_US * (chunks + (4 + 3 * (PIECES - 1)) / EIGHTHS) + END_LAG + 0.5
        steps = [(len(bits), across[0], 3.0), (len(bits) + 1, across[1], 5.0)]
        steps += [(n, along[n], 7.0) for n in range(len(bits))][::-1]
        for n, partner, wait in steps:
            group = [(0, bc_sums, bc_land_sums), (1, norm_sum, norm_land)]
            if n < len(bits):
                group.append((2, small_sum, small_land))
            exchange(n, partner, group, when, when + wait)
            when += wait + 0.01
    hook, end = timeline.spread(
        chunks, BACKWARD_SLOTS, BACKWARD_US, lambda n: chunks - 1 - n, END_LAG if final else LAG
    )
    at = pl.ds(pl.multiple_of((chunks - 1 - chunk) * CHUNK, CHUNK), CHUNK)
    mix_back_kernel(
        *work,
        part.at[at, :],
        ginner.at[at, :],
        gstep.at[at, :],
        gshared.at[at, :],
        small,
        small_bc,
        *scratch,
        hook=hook,
    )
    end()


def pull_layer(
    line, inner_all, saved, gates, weights, layer_args, spread, aux, segrow, rows_all, dout, dgate,
    before, state, gain, more, final,
):
    length, width = rows_all.shape
    rows = state.shape[0]
    inner = dout.shape[1]
    dp = 2 * line
    fine = width // (dp * TENSOR)
    steps = dp.bit_length() - 1
    shape = jax.ShapeDtypeStruct
    _, iraw, iconv, sraw, sconv, step, mixed, sin, _ = saved
    layer = 0 if final else 1
    far_side = (rows_all, dout, dgate, before, state)
    if final:
        outs = [
            shape((rows, width), F32),
            shape((8, width), F32),
            shape((16, inner), F32),
            shape((16, 2 * N), F32),
        ]
        out_specs = [whole_spec(out.shape) for out in outs]
    else:
        outs = [
            shape((rows, width), F32),
            shape((8, width), F32),
            shape((8, rows * TENSOR), F32),
            shape((length, width), BF16),
            shape((8, inner), F32),
            shape((8, 2 * N), F32),
        ]
        out_specs = [whole_spec(out.shape) for out in outs]
        out_specs[3] = ANY
    tail_outs = scatter_outputs(width, inner, dp)
    scratch = mix_back_scratch(inner)
    scratch += [pltpu.VMEM(array.shape, array.dtype) for array in far_side]
    scratch += [pltpu.SemaphoreType.DMA((5,))]
    scratch += [
        pltpu.VMEM((length, width), BF16),
        pltpu.VMEM((length, inner), BF16),
        pltpu.VMEM((length, LANES), BF16),
        pltpu.VMEM((length, 2 * N), BF16),
        pltpu.VMEM((width, inner), BF16),
        pltpu.VMEM((dp, STEPS, width // dp), BF16),
        pltpu.VMEM((dp, TENSOR, fine, 2 * N), BF16),
    ]
    scratch += [pltpu.VMEM((rows, width), BF16)] * 3
    scratch += scatter_scratch(line, width, inner) + reduce_semaphores()
    if final:
        scratch += [
            pltpu.VMEM((8, inner), F32),
            pltpu.VMEM((8, 2 * N), F32),
            pltpu.VMEM((steps, 16, inner), F32),
            pltpu.VMEM((steps + 2, 16, 2 * N), F32),
            pltpu.VMEM((steps + 2, 8, width), F32),
            pltpu.SemaphoreType.DMA((steps + 2, 3)),
            pltpu.SemaphoreType.DMA((steps + 2, 3)),
        ]
    else:
        scratch += [
            pltpu.VMEM((3, 8, rows), F32),
            pltpu.VMEM((rows, LANES), F32),
            pltpu.VMEM((8, rows), F32),
            pltpu.VMEM((rows, width), BF16),
        ]
        scratch += share_semaphores() + spread_semaphores() + [pltpu.SemaphoreType.DMA((1,))]
    weights = weights[:4]
    return call_kernel(
        functools.partial(pull_kernel, line, inner_all, final),
        outs + tail_outs,
        mix_back_specs(layer, length // CHUNK, inner, weights, layer_args, spread)
        + [ANY] * 5
        + [whole_spec(gain.shape)]
        + [whole_spec(array.shape) for array in more],
        out_specs + [whole_spec(out.shape) for out in tail_outs],
        scratch,
        4 if final else 3,
        (
            iraw, iconv, sraw, sconv, step, mixed, sin, sin, *gates,
            *weights, *layer_args, spread, aux, segrow, *far_side, gain, *more,
        ),
        (length // CHUNK,),
    )


def contract_wide(left, right):
    return lax.dot_general(
        left, right, (((0,), (0,)), ((), ())), preferred_element_type=F32
    )


def contract(left, right):
    return contract_wide(left, right).astype(BF16)


def on_device(
    resid,
    segment_ids,
    cotangent,
    w_z,
    w_x,
    w_bc,
    w_dt,
    w_out,
    norm_gain,
    conv_x,
    conv_bc,
    a_log,
    dt_bias,
    d_skip,
    gated_gain,
):
    dp = lax.axis_size("dp")
    assert lax.axis_size("tensor") == TENSOR and segment_ids.shape[0] == LEN
    assert a_log.shape[0] == 2 and a_log.shape[1] <= STEPS
    line = dp // 2
    heads = a_log.shape[1]
    inner = heads * P_SIZE
    inner_all = inner * TENSOR
    width = resid.shape[1]
    aux, segrow = row_masks(segment_ids)
    spread = head_spread(inner)
    args = layer_parameters(conv_x, conv_bc, a_log, dt_bias, d_skip, gated_gain)
    own = (
        w_z,
        w_x,
        jnp.swapaxes(w_out, 1, 2),
        jnp.pad(jnp.swapaxes(w_dt, 1, 2), ((0, 0), (0, STEPS - heads), (0, 0))),
        w_bc,
    )
    gains = norm_gain

    def arranged(gathered):
        gate, inner_w, out_w, step_w, shared_w = gathered
        return gate, inner_w, shared_w.reshape(width, 2 * N), step_w, out_w

    *gathered, rows_low, top_high = start_layer(line, resid, cotangent, gains, own)
    weights_low = arranged(gathered)
    results = middle_layer(
        line, inner_all, rows_low, weights_low, args, aux, segrow, resid, gains, own
    )
    saved_low = results[:9]
    state, raw, scale_row, rows_high, *gathered = results[9:]
    weights_high = arranged(gathered)
    *saved_high, hidden, per_row = top_layer(
        line, inner_all, rows_high, weights_high, args, aux, segrow, state, cotangent
    )

    def early_grads(layer, rows_all, top_all, per_row, saved, weights):
        ggate, gout, outlow, small = gate_back(layer, top_all, per_row, saved, weights[4], args[3])
        return (ggate, gout), contract(top_all, outlow), contract(rows_all, ggate), small

    gates, dout, dgate, small_high_more = early_grads(
        1, rows_high, top_high, per_row, saved_high, weights_high
    )
    results = pull_layer(
        line, inner_all, saved_high, gates, weights_high, args, spread, aux, segrow, rows_high,
        dout, dgate, cotangent, state, gains, (raw, scale_row), False,
    )
    grad_state, gnorm_high, per_row, top_low, small_high, bc_high, *grads_high = results
    gates, dout, dgate, small_low_more = early_grads(
        0, rows_low, top_low, per_row, saved_low, weights_low
    )
    more = (gnorm_high, small_low_more, small_high, small_high_more, bc_high)
    grad_resid, norm_sum, small, small_bc, *grads_low = pull_layer(
        line, inner_all, saved_low, gates, weights_low, args, spread, aux, segrow, rows_low,
        dout, dgate, grad_state, resid, gains, more, True,
    )
    gout, gz, gx, gdt, gbc = [
        jnp.stack([low, high]) for low, high in zip(grads_low, grads_high)
    ]
    small = small.reshape(2, 8, inner)
    return (
        hidden,
        grad_resid,
        gz,
        gx,
        gbc,
        jnp.swapaxes(gdt[:, :heads], 1, 2),
        jnp.swapaxes(gout, 1, 2),
        norm_sum[:2],
        small[:, :TAPS],
        small_bc.reshape(2, 8, 2 * N)[:, :TAPS],
        small[:, 6, :heads],
        small[:, 7, :heads],
        jnp.sum(small[:, 5].reshape(2, heads, P_SIZE), axis=2),
        small[:, 4],
    )


def solution(mesh):
    rows = P(("dp", "tensor"), None)
    matrix = P(None, "dp", "tensor")
    shared = P(None, ("dp", "tensor"), None)
    wide = P(None, None, "tensor")
    head = P(None, "tensor")
    out = P(None, "tensor", "dp")
    return jax.shard_map(
        on_device,
        mesh=mesh,
        in_specs=(
            rows, P("dp"), rows, matrix, matrix, shared, matrix, out, P(), wide, P(), head, head, head, head,
        ),
        out_specs=(
            rows, rows, matrix, matrix, shared, matrix, out, P(), wide, P(), head, head, head, head,
        ),
        check_vma=False,
    )
```

```python
import functools
import heapq
import itertools

import jax
import jax.numpy as jnp
import numpy as np
from jax import lax
from jax.experimental import pallas as pl
from jax.experimental.pallas import tpu as pltpu
from jax.sharding import PartitionSpec as P

P_SIZE = 64
N = 128
LEN = 1024
CHUNK = 256
LANES = 128
TAPS = 4
STEPS = 16

highest = lax.Precision.HIGHEST
epsilon = 1e-05
F32 = jnp.float32
BF16 = jnp.bfloat16


def mm(left, right):
    return jnp.dot(left, right, preferred_element_type=F32)


def mm_nt(left, right):
    return lax.dot_general(left, right, (((1,), (1,)), ((), ())), preferred_element_type=F32)


def sigmoid(values):
    return 1.0 / (1.0 + jnp.exp(-values))


def softplus(values):
    return jnp.maximum(values, 0.0) + jnp.log1p(jnp.exp(-jnp.abs(values)))


def iota2(shape, dim):
    return lax.broadcasted_iota(jnp.int32, shape, dim)


def pair_of(columns, head):
    shape = (columns.shape[0], LANES)
    first = jnp.broadcast_to(columns[:, head : head + 1], shape)
    second = jnp.broadcast_to(columns[:, head + 1 : head + 2], shape)
    return jnp.where(iota2(shape, 1) < P_SIZE, first, second)


def head_sums(values, spread):
    high = values.astype(BF16)
    low = (values - high.astype(F32)).astype(BF16)
    return mm(high, spread) + mm(low, spread)


def decays(step_pre, rate, aux):
    step = softplus(step_pre)
    order = (iota2((CHUNK, CHUNK), 0) >= iota2((CHUNK, CHUNK), 1)).astype(F32)
    cum = jnp.dot(order, step * rate, precision=highest, preferred_element_type=F32)
    last = cum[CHUNK - 1 : CHUNK, :]
    decay_in = jnp.exp(cum) * aux[:, 4:5]
    decay_out = jnp.exp(last - cum) * aux[:, 5:6]
    decay_pass = jnp.exp(last) * aux[0:1, 6:7]
    return step, cum, decay_in, decay_out, decay_pass


def step_weights(blocks):
    joined = jnp.concatenate([blocks[n] for n in range(blocks.shape[0])], axis=1)
    return jnp.concatenate([joined, jnp.zeros((LANES - STEPS, joined.shape[1]), BF16)], axis=0)


def forward_kernel(
    rows_ref,
    wz_ref,
    wx_ref,
    wbc_ref,
    wdt_ref,
    wout_ref,
    convx_ref,
    convbc_ref,
    heads_ref,
    wide_ref,
    aux_ref,
    segrow_ref,
    part_ref,
    sq_ref,
    gate_ref,
    iraw_ref,
    iconv_ref,
    sraw_ref,
    sconv_ref,
    step_ref,
    mixed_ref,
    sin_ref,
    full_ref,
    ext_x,
    ext_bc,
    state,
    gg_ref,
    gate_raw,
    hook,
):
    inner = wx_ref.shape[1]

    @pl.when(pl.program_id(0) == 0)
    def _():
        state[...] = jnp.zeros_like(state)
        ext_x[0:8, :] = jnp.zeros((8, inner), F32)
        ext_bc[0:8, :] = jnp.zeros((8, 2 * N), F32)

    hook(0)
    rows = rows_ref[...]
    aux = aux_ref[...]
    rate = heads_ref[1:2, :]
    shared = mm(rows, wbc_ref[...])
    sraw_ref[...] = shared
    ext_bc[8 : 8 + CHUNK, :] = shared
    shared_conv = convbc_ref[TAPS - 1 : TAPS, :] * shared
    for j in range(1, TAPS):
        shared_conv = shared_conv + convbc_ref[TAPS - 1 - j : TAPS - j, :] * (
            ext_bc[8 - j : 8 - j + CHUNK, :] * aux[:, j : j + 1]
        )
    sconv_ref[...] = shared_conv
    ext_bc[0:8, :] = ext_bc[CHUNK : CHUNK + 8, :]
    shared_act = shared_conv * sigmoid(shared_conv)
    keys = shared_act[:, :N].astype(BF16)
    keys_t = jnp.transpose(shared_act[:, :N]).astype(BF16)
    query = shared_act[:, N:].astype(BF16)
    visible = (aux[:, 15:16] == segrow_ref[0:1, :]) & (
        iota2((CHUNK, CHUNK), 0) >= iota2((CHUNK, CHUNK), 1)
    )
    coupling = jnp.where(visible, mm_nt(query, keys), 0.0)
    step_raw = mm_nt(rows, step_weights(wdt_ref))
    step_ref[...] = step_raw
    step, cum, decay_in, decay_out, decay_pass = decays(
        step_raw + heads_ref[0:1, :], rate, aux
    )
    cum_t = jnp.transpose(cum)
    ext_x[8 : 8 + CHUNK, :] = mm(rows, wx_ref[...])
    gate_raw[...] = mm(rows, wz_ref[...])
    hook(1)
    squares = jnp.zeros((CHUNK, LANES), F32)
    half = iota2((CHUNK, LANES), 1) < P_SIZE
    for pair in range(inner // LANES):
        cols = slice(pair * LANES, (pair + 1) * LANES)
        head = 2 * pair
        raw = ext_x[8 : 8 + CHUNK, cols]
        iraw_ref[:, cols] = raw.astype(BF16)
        conv = convx_ref[TAPS - 1 : TAPS, cols] * raw
        for j in range(1, TAPS):
            conv = conv + convx_ref[TAPS - 1 - j : TAPS - j, cols] * (
                ext_x[8 - j : 8 - j + CHUNK, cols] * aux[:, j : j + 1]
            )
        iconv_ref[:, cols] = conv
        ext_x[0:8, cols] = ext_x[CHUNK : CHUNK + 8, cols]
        act = conv * sigmoid(conv)
        scaled = (act * pair_of(step, head)).astype(BF16)
        parts = []
        for one in (head, head + 1):
            gap = cum[:, one : one + 1] - cum_t[one : one + 1, :]
            weights = (coupling * jnp.exp(jnp.minimum(gap, 0.0))).astype(BF16)
            parts.append(mm(weights, scaled))
        before = state[:, cols]
        sin_ref[0, :, cols] = before
        mixed = jnp.where(half, parts[0], parts[1])
        mixed = mixed + pair_of(decay_in, head) * mm(query, before.astype(BF16))
        mixed_ref[:, cols] = mixed
        leaving = (scaled.astype(F32) * pair_of(decay_out, head)).astype(BF16)
        state[:, cols] = pair_of(decay_pass, head) * before + mm(keys_t, leaving)
        gate = gate_raw[:, cols]
        gate_ref[:, cols] = gate.astype(BF16)
        full = mixed + wide_ref[0:1, cols] * act
        full_ref[:, cols] = full.astype(BF16)
        gated = full * (gate * sigmoid(gate))
        squares = squares + gated * gated
        gg_ref[:, cols] = (gated * wide_ref[1:2, cols]).astype(BF16)
        hook(2 + pair)
    total = jnp.sum(squares, axis=1, keepdims=True)
    sq_ref[...] = jnp.transpose(jnp.broadcast_to(total, (CHUNK, LANES)))[0:8, :]
    part_ref[...] = mm_nt(gg_ref[...], wout_ref[...]).astype(BF16)


def gate_back_kernel(
    top_ref,
    sc_ref,
    gate_ref,
    full_ref,
    wout_ref,
    wide_ref,
    ggate_ref,
    gout_ref,
    outlow_ref,
    small_ref,
    gno_ref,
):
    inner = wout_ref.shape[1]

    @pl.when(pl.program_id(0) == 0)
    def _():
        small_ref[...] = jnp.zeros_like(small_ref)

    gno_ref[...] = mm(top_ref[...], wout_ref[...])
    per_row = jnp.transpose(sc_ref[...])
    scale = per_row[:, 0:1]
    coef = per_row[:, 1:2]
    for pair in range(inner // LANES):
        cols = slice(pair * LANES, (pair + 1) * LANES)
        gain = wide_ref[1:2, cols]
        gate = gate_ref[:, cols].astype(F32)
        gate_sig = sigmoid(gate)
        gate_act = gate * gate_sig
        full = full_ref[:, cols].astype(F32)
        gated = full * gate_act
        gno = gno_ref[:, cols]
        gated_scaled = gated * scale
        small_ref[4:5, cols] += jnp.sum(gno * gated_scaled, axis=0, keepdims=True)
        outlow_ref[:, cols] = (gated_scaled * gain).astype(BF16)
        ggated = scale * (gno * gain) - gated * coef
        gout_ref[:, cols] = (ggated * gate_act).astype(BF16)
        ggate_ref[:, cols] = (
            ggated * full * (gate_sig * (1.0 + gate * (1.0 - gate_sig)))
        ).astype(BF16)


def gate_back(layer, top_all, per_row, saved, weight_out, wide):
    length, width = top_all.shape
    inner = weight_out.shape[1]
    gate, full = saved[0], saved[8]
    shape = jax.ShapeDtypeStruct
    return pl.pallas_call(
        gate_back_kernel,
        grid=(length // CHUNK,),
        in_specs=[block_rows(width), pl.BlockSpec((8, CHUNK), lambda i: (0, i))]
        + [block_rows(inner)] * 2
        + [whole_spec(weight_out.shape), layer_spec(layer, wide.shape)],
        out_specs=[block_rows(inner)] * 3 + [pl.BlockSpec((8, inner), lambda i: (0, 0))],
        out_shape=[shape((length, inner), BF16)] * 3 + [shape((8, inner), F32)],
        scratch_shapes=[pltpu.VMEM((CHUNK, inner), F32)],
        compiler_params=pltpu.CompilerParams(
            dimension_semantics=("arbitrary",), vmem_limit_bytes=VMEM_LIMIT
        ),
    )(top_all, per_row, gate, full, weight_out, wide)


def mix_back_kernel(
    iraw_ref,
    iconv_ref,
    sraw_ref,
    sconv_ref,
    step_ref,
    mixed_ref,
    sin_ref,
    sout_ref,
    ggate_ref,
    gout_ref,
    wz_ref,
    wx_ref,
    wbc_ref,
    wdt_ref,
    convx_ref,
    convbc_ref,
    heads_ref,
    wide_ref,
    spread_ref,
    aux_ref,
    segrow_ref,
    part_ref,
    ginner_ref,
    gstep_ref,
    gshared_ref,
    small_ref,
    smallbc_ref,
    gext_x,
    gext_bc,
    dstate,
    balance,
    direct,
    edge,
    dcoup,
    hook,
):
    inner = wx_ref.shape[1]

    @pl.when(pl.program_id(0) == 0)
    def _():
        dstate[...] = jnp.zeros_like(dstate)
        gext_x[CHUNK : CHUNK + 8, :] = jnp.zeros((8, inner), F32)
        gext_bc[CHUNK : CHUNK + 8, :] = jnp.zeros((8, 2 * N), F32)
        small_ref[...] = jnp.zeros_like(small_ref)
        smallbc_ref[...] = jnp.zeros_like(smallbc_ref)
        edge[...] = jnp.zeros_like(edge)

    hook(0)
    aux = aux_ref[...]
    rate = heads_ref[1:2, :]
    step_pre = step_ref[...] + heads_ref[0:1, :]
    step, cum, decay_in, decay_out, decay_pass = decays(step_pre, rate, aux)
    cum_t = jnp.transpose(cum)
    shared_conv = sconv_ref[...]
    shared_sig = sigmoid(shared_conv)
    shared_act = shared_conv * shared_sig
    keys = shared_act[:, :N].astype(BF16)
    query = shared_act[:, N:].astype(BF16)
    query_t = jnp.transpose(shared_act[:, N:]).astype(BF16)
    visible = (aux[:, 15:16] == segrow_ref[0:1, :]) & (
        iota2((CHUNK, CHUNK), 0) <= iota2((CHUNK, CHUNK), 1)
    )
    coupling = jnp.where(visible, mm_nt(keys, query), 0.0)
    half = iota2((CHUNK, LANES), 1) < P_SIZE
    dcoup[...] = jnp.zeros_like(dcoup)
    dkeys = jnp.zeros((CHUNK, N), F32)
    dquery = jnp.zeros((CHUNK, N), F32)
    for pair in range(inner // LANES):
        cols = slice(pair * LANES, (pair + 1) * LANES)
        head = 2 * pair
        skip = wide_ref[0:1, cols]
        conv = iconv_ref[:, cols]
        conv_sig = sigmoid(conv)
        act = conv * conv_sig
        step_pair = pair_of(step, head)
        scaled = (act * step_pair).astype(BF16)
        gout_low = gout_ref[:, cols]
        gout = gout_low.astype(F32)
        small_ref[5:6, cols] += jnp.sum(gout * act, axis=0, keepdims=True)
        zero = jnp.zeros_like(gout)
        parts = []
        for one, own in (
            (head, jnp.where(half, gout, zero).astype(BF16)),
            (head + 1, jnp.where(half, zero, gout).astype(BF16)),
        ):
            gap = cum_t[one : one + 1, :] - cum[:, one : one + 1]
            decay = jnp.exp(jnp.minimum(gap, 0.0))
            weights = (coupling * decay).astype(BF16)
            parts.append(mm(weights, gout_low))
            dcoup[...] += mm_nt(scaled, own) * decay
        after = dstate[:, cols]
        after_low = after.astype(BF16)
        out_pair = pair_of(decay_out, head)
        gscaled = jnp.where(half, parts[0], parts[1]) + out_pair * mm(keys, after_low)
        scaled_wide = scaled.astype(F32)
        dkeys = dkeys + mm_nt((scaled_wide * out_pair).astype(BF16), after_low)
        entering = (gout * pair_of(decay_in, head)).astype(BF16)
        dquery = dquery + mm_nt(entering, sin_ref[0, :, cols].astype(BF16))
        edge[0:1, cols] = jnp.sum(sout_ref[0, :, cols] * after, axis=0, keepdims=True)
        dstate[:, cols] = pair_of(decay_pass, head) * after + mm(query_t, entering)
        balance[:, cols] = gout * mixed_ref[:, cols] - scaled_wide * gscaled
        direct[:, cols] = act * gscaled
        gact = step_pair * gscaled + skip * gout
        gext_x[0:CHUNK, cols] = gact * (conv_sig * (1.0 + conv * (1.0 - conv_sig)))
        raw = iraw_ref[:, cols].astype(F32)
        gconv = gext_x[0:CHUNK, cols]
        graw = convx_ref[TAPS - 1 : TAPS, cols] * gconv
        small_ref[TAPS - 1 : TAPS, cols] += jnp.sum(raw * gconv, axis=0, keepdims=True)
        for j in range(1, TAPS):
            moved = gext_x[j : j + CHUNK, cols] * aux[:, 8 + j : 9 + j]
            graw = graw + convx_ref[TAPS - 1 - j : TAPS - j, cols] * moved
            small_ref[TAPS - 1 - j : TAPS - j, cols] += jnp.sum(
                raw * moved, axis=0, keepdims=True
            )
        ginner_ref[:, cols] = graw.astype(BF16)
        gext_x[CHUNK : CHUNK + 8, cols] = gext_x[0:8, cols]
        hook(1 + pair)
    spread = spread_ref[...]
    order = (iota2((CHUNK, CHUNK), 0) <= iota2((CHUNK, CHUNK), 1)).astype(F32)
    running = jnp.dot(
        order, head_sums(balance[...], spread), precision=highest, preferred_element_type=F32
    )
    running = running + head_sums(edge[...], spread)[0:1, :]
    gstep = (head_sums(direct[...], spread) + running * rate) * sigmoid(step_pre)
    small_ref[6:7, 0:LANES] += rate * jnp.sum(running * step, axis=0, keepdims=True)
    small_ref[7:8, 0:LANES] += jnp.sum(gstep, axis=0, keepdims=True)
    gstep_ref[...] = gstep.astype(BF16)
    dcoupling = jnp.where(visible, dcoup[...], 0.0)
    dkeys = dkeys + mm(dcoupling.astype(BF16), query)
    dquery = dquery + mm(jnp.transpose(dcoupling).astype(BF16), keys)
    slope = shared_sig * (1.0 + shared_conv * (1.0 - shared_sig))
    gext_bc[0:CHUNK, 0:N] = dkeys * slope[:, :N]
    gext_bc[0:CHUNK, N : 2 * N] = dquery * slope[:, N:]
    raw = sraw_ref[...]
    gconv = gext_bc[0:CHUNK, :]
    graw = convbc_ref[TAPS - 1 : TAPS, :] * gconv
    smallbc_ref[TAPS - 1 : TAPS, :] += jnp.sum(raw * gconv, axis=0, keepdims=True)
    for j in range(1, TAPS):
        moved = gext_bc[j : j + CHUNK, :] * aux[:, 8 + j : 9 + j]
        graw = graw + convbc_ref[TAPS - 1 - j : TAPS - j, :] * moved
        smallbc_ref[TAPS - 1 - j : TAPS - j, :] += jnp.sum(raw * moved, axis=0, keepdims=True)
    gshared_ref[...] = graw.astype(BF16)
    gext_bc[CHUNK : CHUNK + 8, :] = gext_bc[0:8, :]
    hook(7)
    total = mm_nt(ggate_ref[...], wz_ref[...]) + mm_nt(ginner_ref[...], wx_ref[...])
    total = total + mm(gstep_ref[...], step_weights(wdt_ref))
    part_ref[...] = (total + mm_nt(gshared_ref[...], wbc_ref[...])).astype(BF16)


def whole_spec(shape):
    zeros = (0,) * len(shape)
    return pl.BlockSpec(shape, lambda i: zeros, pipeline_mode=pl.Buffered(1))


def layer_spec(layer, shape):
    return pl.BlockSpec(
        (None, *shape[1:]),
        lambda i: (layer,) + (0,) * (len(shape) - 1),
        pipeline_mode=pl.Buffered(1),
    )


VMEM_LIMIT = 62 * 1024 * 1024


def block_rows(cols):
    return pl.BlockSpec((CHUNK, cols), lambda i: (i, 0))


def forward_in_specs(layer, rows_all, weight_specs, layer_args):
    return (
        [block_rows(rows_all.shape[1])]
        + weight_specs
        + [layer_spec(layer, w.shape) for w in layer_args]
        + [block_rows(LANES), pl.BlockSpec((8, CHUNK), lambda i: (0, i))]
    )


def saved_specs(inner):
    return [
        block_rows(inner),
        block_rows(inner),
        block_rows(inner),
        block_rows(2 * N),
        block_rows(2 * N),
        block_rows(LANES),
        block_rows(inner),
        pl.BlockSpec((1, N, inner), lambda i: (i, 0, 0)),
        block_rows(inner),
    ]


def saved_shapes(length, inner):
    shape = jax.ShapeDtypeStruct
    return [
        shape((length, inner), BF16),
        shape((length, inner), BF16),
        shape((length, inner), F32),
        shape((length, 2 * N), F32),
        shape((length, 2 * N), F32),
        shape((length, LANES), F32),
        shape((length, inner), F32),
        shape((length // CHUNK, N, inner), F32),
        shape((length, inner), BF16),
    ]


def forward_scratch(inner):
    return [
        pltpu.VMEM((CHUNK + 8, inner), F32),
        pltpu.VMEM((CHUNK + 8, 2 * N), F32),
        pltpu.VMEM((N, inner), F32),
        pltpu.VMEM((CHUNK, inner), BF16),
        pltpu.VMEM((CHUNK, inner), F32),
    ]


def mix_back_specs(layer, chunks, inner, weight_specs, layer_args, spread):
    last = chunks - 1

    def turned(cols):
        return pl.BlockSpec((CHUNK, cols), lambda i: (last - i, 0))

    return (
        [
            turned(inner),
            turned(inner),
            turned(2 * N),
            turned(2 * N),
            turned(LANES),
            turned(inner),
            pl.BlockSpec((1, N, inner), lambda i: (last - i, 0, 0)),
            pl.BlockSpec((1, N, inner), lambda i: (jnp.minimum(chunks - i, last), 0, 0)),
            turned(inner),
            turned(inner),
        ]
        + weight_specs
        + [layer_spec(layer, w.shape) for w in layer_args]
        + [
            whole_spec(spread.shape),
            turned(LANES),
            pl.BlockSpec((8, CHUNK), lambda i: (0, last - i)),
        ]
    )


def mix_back_scratch(inner):
    return [
        pltpu.VMEM((CHUNK + 8, inner), F32),
        pltpu.VMEM((CHUNK + 8, 2 * N), F32),
        pltpu.VMEM((N, inner), F32),
        pltpu.VMEM((CHUNK, inner), F32),
        pltpu.VMEM((CHUNK, inner), F32),
        pltpu.VMEM((8, inner), F32),
        pltpu.VMEM((CHUNK, CHUNK), F32),
    ]


def row_masks(segment_ids):
    length = segment_ids.shape[0]
    seg = segment_ids.astype(F32)

    def shifted(j):
        return jnp.concatenate([jnp.full((j,), -1.0, F32), seg[: length - j]])

    def ahead(j):
        return jnp.concatenate([seg[j:], jnp.full((j,), -1.0, F32)])

    ends = seg[CHUNK - 1 :: CHUNK]
    own_end = jnp.repeat(ends, CHUNK)
    old_end = jnp.repeat(jnp.concatenate([jnp.full((1,), -1.0, F32), ends[:-1]]), CHUNK)
    lanes = [jnp.zeros_like(seg)] * 16
    for j in range(1, TAPS):
        lanes[j] = (shifted(j) == seg).astype(F32)
        lanes[8 + j] = (ahead(j) == seg).astype(F32)
    lanes[4] = (old_end == seg).astype(F32)
    lanes[5] = (own_end == seg).astype(F32)
    lanes[6] = (own_end == old_end).astype(F32)
    lanes[15] = seg
    aux = jnp.pad(jnp.stack(lanes, axis=1), ((0, 0), (0, LANES - 16)))
    return aux, jnp.broadcast_to(seg[None, :], (8, length))


def layer_parameters(conv_x, conv_bc, a_log, dt_bias, d_skip, gated_gain):
    heads = a_log.shape[1]
    pad = ((0, 0), (0, 0), (0, LANES - heads))
    head_rows = jnp.pad(jnp.stack([dt_bias, -jnp.exp(a_log)], axis=1), pad)
    wide = jnp.stack([jnp.repeat(d_skip, P_SIZE, axis=1), gated_gain], axis=1)
    return (conv_x, conv_bc, head_rows, wide)


def head_spread(inner):
    return jnp.asarray(
        np.arange(inner)[:, None] // P_SIZE == np.arange(LANES)[None, :], dtype=BF16
    )


MESH = pl.DeviceIdType.MESH
ANY = pl.BlockSpec(memory_space=pl.ANY)
IN_VMEM = pl.BlockSpec(memory_space=pltpu.VMEM)
PIECES = 4
TENSOR = 4
LATE = 1e9
LAG = 14.0
EIGHTHS = 8
BIG = 6.5
SMALL = 1.1
TINY = 0.2


class Place:
    def __init__(self, line):
        self.line = line
        dp, t = lax.axis_index("dp"), lax.axis_index("tensor")
        self.dp, self.t = dp, t
        self.z, self.x = lax.div(dp, 2), lax.rem(dp, 2)
        self.other = 1 - self.x
        self.sibling = t + 1 - 2 * lax.rem(t, 2)
        self.mate = lax.rem(t + 2, TENSOR)
        self.diagonal = TENSOR - 1 - t
        self.right = (lax.rem(self.z + 1, line) * 2 + self.x, t)
        self.left = (lax.rem(self.z + line - 1, line) * 2 + self.x, t)
        self.across = (self.z * 2 + self.other, t)

    def tensor_peers(self):
        return [(self.dp, self.sibling), (self.dp, self.mate), (self.dp, self.diagonal)]

    def partner(self, bit):
        return (self.dp + bit - 2 * bit * lax.rem(lax.div(self.dp, bit), 2), self.t)

    def greet(self, across=True, far_bits=()):
        barrier = pltpu.get_barrier_semaphore()
        peers = self.tensor_peers()
        if across:
            peers = peers + [self.across]
        peers = peers + [self.partner(bit) for bit in far_bits]
        for peer in peers:
            pl.semaphore_signal(barrier, inc=1, device_id=peer, device_id_type=MESH)
        count = len(peers)
        if across and self.line > 1:
            has_right = self.z < self.line - 1
            has_left = self.z > 0

            @pl.when(has_right)
            def _():
                pl.semaphore_signal(barrier, inc=1, device_id=self.right, device_id_type=MESH)

            @pl.when(has_left)
            def _():
                pl.semaphore_signal(barrier, inc=1, device_id=self.left, device_id_type=MESH)

            count = count + has_right.astype(jnp.int32) + has_left.astype(jnp.int32)
        pl.semaphore_wait(barrier, count)


class Timeline:
    def __init__(self):
        self.steps = []
        self.rolling = []

    def follow(self, eighths, step):
        self.rolling.append((eighths, step))

    def add(self, when, step):
        self.steps.append((when, len(self.steps), step))

    def ordered(self):
        return sorted(self.steps, key=lambda entry: entry[:2])

    def run(self):
        for _, _, step in self.ordered():
            step()

    def spread(self, chunks, slots, chunk_us, order=lambda k: k, lag=LAG):
        places = {}
        rolling = [(-(-offset * slots // EIGHTHS), step) for offset, step in self.rolling]
        for slot, step in rolling:
            for k in range(chunks):
                if (k + 1) * slots + slot >= chunks * slots:
                    when = ((k + 1) * slots + slot) * chunk_us / slots + (lag if 2 * slot > slots else 0.0)
                    self.add(when, functools.partial(step, order(k)))
        after = []
        for when, _, step in self.ordered():
            spot = max(0, int(when / chunk_us * slots))
            if spot < chunks * slots:
                places.setdefault((spot % slots, spot // slots), []).append(step)
            else:
                after.append(step)
        now = pl.program_id(0)

        def hook(place):
            if place * slots % EIGHTHS:
                return
            slot = place * slots // EIGHTHS
            for chunk in range(chunks):
                steps = places.get((slot, chunk))
                if steps:

                    @pl.when(now == chunk)
                    def _(steps=steps):
                        for step in steps:
                            step()

            for offset, step in rolling:
                if offset % slots == slot:
                    behind = 1 + offset // slots
                    step(jnp.where(now >= behind, order(now - behind), -1))

        def end():
            @pl.when(now == chunks - 1)
            def _():
                for step in after:
                    step()

        return hook, end


def remote(src, dst, send, recv, device):
    return pltpu.make_async_remote_copy(
        src_ref=src, dst_ref=dst, send_sem=send, recv_sem=recv, device_id=device, device_id_type=MESH
    )


def gather_semaphores(count, line):
    return [pltpu.SemaphoreType.DMA((count, 2, line))] * 5


HOP_US = 0.8
ADD_US = 0.5


def plan_gather(items, line):
    free, plan = {}, {}
    queue, count = [], itertools.count()

    def push(when, *action):
        heapq.heappush(queue, (when, next(count), action))

    def transfer(link, when, cost):
        begin = max(when, free.get(link, 0.0))
        free[link] = begin + cost
        return begin + cost + HOP_US

    def note(step, when):
        plan[step] = max(plan.get(step, 0.0), when)

    def along(when, way, z, i, source, xs):
        stop = z + 1 if way == 0 else z - 1
        if 0 <= stop < line:
            push(transfer((way, z), when, items[i][1]), "hop", way, stop, i, source, xs)

    def cross(when, z, i, source):
        push(transfer(("x", z), when, items[i][1]), "side", z, i, source)

    for i, (_, _, ready) in enumerate(items):
        push(ready, "own", i)
    while queue:
        when, _, (kind, *rest) = heapq.heappop(queue)
        if kind == "own":
            (i,) = rest
            for z in range(line):
                along(when, 0, z, i, z, 0)
                along(when, 1, z, i, z, 0)
                cross(when, z, i, z)
        elif kind == "hop":
            way, z, i, source, xs = rest
            note(("hop", i, way, abs(z - source), xs), when)
            along(when, way, z, i, source, xs)
            if items[i][0] == "zx":
                cross(when, z, i, source)
        else:
            z, i, source = rest
            note(("side", i), when)
            if items[i][0] == "xz":
                along(when, 0, z, i, source, 1)
                along(when, 1, z, i, source, 1)
    return plan


def gather_weights(place, timeline, items, sems):
    send_r, send_l, send_x, recv_z, recv_x = sems
    line = place.line
    z = place.z

    def copy(i, way, zz, xs, src=None):
        dst = items[i][1](zz, xs)
        return remote(
            dst if src is None else src,
            dst,
            (send_r, send_l, send_x)[way].at[i, xs, zz],
            (recv_x if way == 2 else recv_z).at[i, xs, zz],
            (place.right, place.left, place.across)[way],
        )

    def begin(i):
        own = items[i][0]

        def step():
            @pl.when(z < line - 1)
            def _():
                copy(i, 0, z, place.x, own).start()

            @pl.when(z > 0)
            def _():
                copy(i, 1, z, place.x, own).start()

            copy(i, 2, z, place.x, own).start()

        return step

    def hop(i, way, k, xs, to_x):
        source = z - k if way == 0 else z + k
        here = source >= 0 if way == 0 else source < line
        more = z < line - 1 if way == 0 else z > 0

        def arrive():
            @pl.when(here)
            def _():
                copy(i, way, source, xs).wait_recv()
                if to_x:
                    copy(i, 2, source, xs).start()

            @pl.when(here & more)
            def _():
                copy(i, way, source, xs).start()

        def finish():
            @pl.when(here & more)
            def _():
                copy(i, way, source, xs).wait_send()

            if to_x:

                @pl.when(here)
                def _():
                    copy(i, 2, source, xs).wait_send()

        return arrive, finish

    def side(i):
        def step():
            copy(i, 2, z, place.other).wait_recv()

            @pl.when(z < line - 1)
            def _():
                copy(i, 0, z, place.other).start()

            @pl.when(z > 0)
            def _():
                copy(i, 1, z, place.other).start()

        return step

    def end(i):
        route = items[i][2]

        def step():
            for xs in (place.x,) if route == "zx" else (place.x, place.other):

                @pl.when(z < line - 1)
                def _(xs=xs):
                    copy(i, 0, z, xs).wait_send()

                @pl.when(z > 0)
                def _(xs=xs):
                    copy(i, 1, z, xs).wait_send()

            copy(i, 2, z, place.x).wait_send()

        return step

    def settle(i):
        def step():
            for zz in range(line):
                copy(i, 2, zz, place.other).wait_recv()

        return step

    plan = plan_gather([(item[2], item[3], 0.0) for item in items], line)
    for i, (_, _, route, _, early) in enumerate(items):
        timeline.add(0.0, begin(i))
        if route == "xz":
            timeline.add(plan["side", i], side(i))
        for way in (0, 1):
            for column, xs in enumerate((place.x,) if route == "zx" else (place.x, place.other)):
                when = plan["side", i] if column else 0.0
                for k in range(1, line):
                    when = max(plan["hop", i, way, k, column], when + 0.01)
                    arrive, finish = hop(i, way, k, xs, route == "zx")
                    timeline.add(when, arrive)
                    timeline.add(LATE, finish)
        if route == "zx":
            timeline.add(plan["side", i] + 1.0 if early else LATE, settle(i))
        timeline.add(LATE, end(i))
    return plan


def scatter_semaphores(count, line):
    return [pltpu.SemaphoreType.DMA((count, 2, line))] * 6


def add_into(target, other, rows):
    step = 48 if rows % 48 == 0 else rows

    def body(n, carry):
        part = pl.ds(pl.multiple_of(n * step, step), step)
        target[part, :] = (target[part, :].astype(F32) + other[part, :].astype(F32)).astype(BF16)
        return carry

    lax.fori_loop(0, rows // step, body, 0)


def scatter_order(line):
    order = []
    for n in range((line + 1) // 2):
        order += [n] if n == line - 1 - n else [n, line - 1 - n]
    return order


def plan_scatter(items, line):
    free, arrived, joined, plan = {}, {}, {}, {}
    queue, count = [], itertools.count()

    def push(when, *action):
        heapq.heappush(queue, (when, next(count), action))

    def transfer(link, when, cost):
        begin = max(when, free.get(link, 0.0))
        free[link] = begin + cost
        return begin + cost + HOP_US

    def note(step, when):
        plan[step] = max(plan.get(step, 0.0), when)

    def go(when, z, i, zz, xs):
        first = {"r": z == 0, "l": z == line - 1}
        if z == zz:
            need = [way for way, there in (("r", z > 0), ("l", z < line - 1)) if there]
            times = [arrived.get((way, z, i, zz, xs)) for way in need] + [joined.get((z, i, zz, xs))]
            if None in times:
                return
            when = max(times)
            if items[i][0] == "xz":
                note(("last", i), when)
                return
            note(("line", i, xs), when)
            done = joined.setdefault(("line", z, i), [])
            done.append(when)
            if len(done) == 2:
                note(("swap", i), max(done))
                note(("last", i), transfer(("x", z), max(done) + 2 * ADD_US, items[i][1]))
            return
        way = "r" if z < zz else "l"
        times = [joined.get((z, i, zz, xs))]
        if not first[way]:
            times.append(arrived.get((way, z, i, zz, xs)))
        if None in times:
            return
        when = max(times)
        h = z if way == "r" else line - 1 - z
        note(("send", i, zz, way, xs, h), when)
        stop = z + 1 if way == "r" else z - 1
        push(transfer((way, z), when + ADD_US, items[i][1]), "arrive", way, stop, i, zz, xs)

    for i, (route, cost, ready) in enumerate(items):
        for zz in scatter_order(line):
            for xs in (0,) if route == "xz" else (0, 1):
                push(ready, "start", i, zz, xs)
    while queue:
        when, _, (kind, *rest) = heapq.heappop(queue)
        if kind == "start":
            i, zz, xs = rest
            for z in range(line):
                if items[i][0] == "xz":
                    push(transfer(("x", z), when, items[i][1]), "join", z, i, zz, xs)
                else:
                    push(when, "join", z, i, zz, xs)
        elif kind == "join":
            z, i, zz, xs = rest
            if items[i][0] == "xz":
                note(("join", i, zz), when)
                when += ADD_US
            joined[z, i, zz, xs] = when
            go(when, z, i, zz, xs)
        else:
            way, z, i, zz, xs = rest
            arrived[way, z, i, zz, xs] = when
            go(when, z, i, zz, xs)
    return plan


def scatter_weights(place, timeline, items, sems):
    send_x, recv_x, send_r, recv_r, send_l, recv_l = sems
    line = place.line
    z = place.z

    def rows_of(i):
        return items[i][2][0].shape[1]

    def side(i, zz):
        _, source, (land_x, _), *_ = items[i]
        return remote(
            source(zz, place.other), land_x.at[zz], send_x.at[i, 0, zz], recv_x.at[i, 0, zz], place.across
        )

    def land_along(i, zz, way, xs, stop):
        slot = zz if way == 0 else jnp.where(stop == zz, line, zz)
        land = items[i][2][1]
        return land.at[slot, xs] if items[i][4] == "zx" else land.at[slot]

    def along(i, zz, way, xs, source=None):
        here = land_along(i, zz, way, xs, z)
        return remote(
            here if source is None else source,
            land_along(i, zz, way, xs, z + 1 if way == 0 else z - 1),
            (send_r, send_l)[way].at[i, xs, zz],
            (recv_r, recv_l)[way].at[i, xs, zz],
            (place.right, place.left)[way],
        )

    def own(i, zz, xs):
        return items[i][0](zz, xs) if items[i][4] == "zx" else items[i][2][0].at[zz]

    def outgoing(i, zz, xs):
        return items[i][1](zz, xs) if items[i][4] == "zx" else items[i][2][0].at[zz]

    def join(i, zz):
        def step():
            side(i, zz).wait_recv()
            add_into(items[i][2][0].at[zz], items[i][0](zz, place.x), rows_of(i))

        return step

    def send(i, zz, way, xs, h):
        if way == 0:
            mine = (z == h) & (z < zz)
        else:
            mine = (z == line - 1 - h) & (z > zz)

        def step():
            @pl.when(mine)
            def _():
                if h == 0:
                    along(i, zz, way, xs, outgoing(i, zz, xs)).start()
                else:
                    along(i, zz, way, xs).wait_recv()
                    add_into(land_along(i, zz, way, xs, z), own(i, zz, xs), rows_of(i))
                    along(i, zz, way, xs).start()

        return step

    def last(i):
        out = items[i][3]

        def step():
            out[...] = items[i][2][0][z].astype(F32)
            for way, there in ((0, z > 0), (1, z < line - 1)):

                @pl.when(there)
                def _(way=way):
                    along(i, z, way, 0).wait_recv()
                    out[...] += items[i][2][1][z if way == 0 else line].astype(F32)

        return step

    def swap(i):
        land_x, land = items[i][2]
        stage = land.at[z, place.other]
        return remote(stage, land_x.at[0], send_x.at[i, 0, 0], recv_x.at[i, 0, 0], place.across)

    def gather_line(i, xs):
        piece = items[i][0]

        def step():
            right, left = land_along(i, z, 0, xs, z), land_along(i, z, 1, xs, z)

            @pl.when(z > 0)
            def _():
                along(i, z, 0, xs).wait_recv()
                add_into(right, piece(z, xs), rows_of(i))

            @pl.when(z == 0)
            def _():
                right[...] = piece(z, xs)[...]

            @pl.when(z < line - 1)
            def _():
                along(i, z, 1, xs).wait_recv()
                add_into(right, left, rows_of(i))

        return step

    def swap_end(i):
        (land_x, land), out = items[i][2:4]

        def step():
            swap(i).wait()
            out[...] = land[z, place.x].astype(F32) + land_x[0].astype(F32)

        return step

    def end(i, zz, xs):
        def step():
            if items[i][4] == "xz":
                side(i, zz).wait_send()
            for way, there in ((0, z < zz), (1, z > zz)):

                @pl.when(there)
                def _(way=way):
                    along(i, zz, way, xs).wait_send()

        return step

    plan = plan_scatter([item[4:] for item in items], line)
    for i, (_, _, _, _, route, _, ready) in enumerate(items):
        columns = (0,) if route == "xz" else (0, 1)
        latest = ready
        for zz in scatter_order(line):
            if route == "xz":
                timeline.add(ready, lambda i=i, zz=zz: side(i, zz).start())
                timeline.add(plan["join", i, zz], join(i, zz))
                latest = max(latest, plan["join", i, zz])
            for xs in columns:
                for way, name in enumerate("rl"):
                    when = plan.get(("join", i, zz), ready)
                    for h in range(zz if way == 0 else line - 1 - zz):
                        when = max(plan["send", i, zz, name, xs, h], when + 0.01)
                        timeline.add(when, send(i, zz, way, xs, h))
                    latest = max(latest, when)
                timeline.add(LATE, end(i, zz, xs))
        latest += 0.01
        if route == "xz":
            timeline.add(max(plan["last", i], latest), last(i))
            continue
        swaps = max(plan["swap", i], latest) + ADD_US
        for xs in columns:
            timeline.add(max(plan["line", i, xs], latest), gather_line(i, xs))
        timeline.add(swaps, lambda i=i: swap(i).start())
        timeline.add(max(plan["last", i], swaps + 0.01), swap_end(i))


def spread_semaphores():
    return [pltpu.SemaphoreType.DMA((PIECES,))] * 6


def spread_rows(place, own, whole, sems):
    send_y, recv_y, send_s, recv_s, send_f, recv_f = sems
    rows = own.shape[0]
    step = rows // PIECES

    def at(owner, p):
        return whole.at[pl.ds(pl.multiple_of(owner * rows, rows) + p * step, step), :]

    def source(p):
        return own.at[pl.ds(p * step, step), :]

    def to_mate(p):
        return remote(
            source(p), at(place.t, p), send_y.at[p], recv_y.at[p], (place.dp, place.mate)
        )

    def to_sibling(p):
        return remote(
            source(p), at(place.t, p), send_s.at[p], recv_s.at[p], (place.dp, place.sibling)
        )

    def passed_on(p):
        return remote(
            at(place.mate, p), at(place.mate, p), send_f.at[p], recv_f.at[p], (place.dp, place.sibling)
        )

    def begin(p):
        to_mate(p).start()
        to_sibling(p).start()

    def forward(p):
        to_mate(p).wait_recv()
        passed_on(p).start()

    def finish():
        for p in range(PIECES):
            to_mate(p).wait_send()
            to_sibling(p).wait()
            passed_on(p).wait()

    return begin, forward, finish


def reduce_semaphores():
    return [pltpu.SemaphoreType.DMA((PIECES,))] * 6


def roll_rows(place, timeline, part, lands, sems, owner, forward, slot=4):
    land_far, land_near, land_mate = lands
    send_a, recv_a, send_b, recv_b, send_z, recv_z = sems
    rows = land_far.shape[0]
    step = rows // PIECES

    def at(block, p):
        return part.at[pl.ds(pl.multiple_of(block * rows, rows) + p * step, step), :]

    def own(ref, p):
        return ref.at[pl.ds(p * step, step), :]

    def far(p):
        return remote(
            at(place.diagonal, p), own(land_far, p), send_a.at[p], recv_a.at[p], (place.dp, place.sibling)
        )

    def near(p):
        return remote(
            at(place.sibling, p), own(land_near, p), send_b.at[p], recv_b.at[p], (place.dp, place.sibling)
        )

    def over(p):
        return remote(
            own(land_far, p), own(land_mate, p), send_z.at[p], recv_z.at[p], (place.dp, place.mate)
        )

    def begin(chunk):
        @pl.when(place.diagonal == chunk)
        def _():
            for p in range(PIECES):
                far(p).start()

        @pl.when(place.sibling == chunk)
        def _():
            for p in range(PIECES):
                near(p).start()

    def middle(p, chunk):
        @pl.when(place.mate == chunk)
        def _():
            far(p).wait_recv()
            mine = own(land_far, p)
            mine[...] = (mine[...].astype(F32) + at(place.mate, p)[...].astype(F32)).astype(BF16)
            over(p).start()

    def final(p, chunk):
        @pl.when(place.t == chunk)
        def _():
            near(p).wait_recv()
            over(p).wait_recv()
            sums = at(place.t, p)[...].astype(F32) + own(land_near, p)[...].astype(F32)
            owner(p, sums + own(land_mate, p)[...].astype(F32))

    def pass_on(p, chunk):
        @pl.when(place.mate == chunk)
        def _():
            forward(p)

    def finish():
        for p in range(PIECES):
            far(p).wait_send()
            near(p).wait_send()
            over(p).wait_send()

    timeline.follow(0, begin)
    for p in range(PIECES):
        timeline.follow(1 + p // 2, functools.partial(middle, p))
        timeline.follow(slot + 3 * p, functools.partial(final, p))
        if forward:
            timeline.follow(slot + 4 + 3 * p, functools.partial(pass_on, p))
    timeline.add(LATE, finish)


def share_semaphores():
    return [pltpu.SemaphoreType.DMA((3,))] * 2


def share_blocks(place, source_of, target_of, sems):
    send, recv = sems
    peers = (place.sibling, place.mate, place.diagonal)
    return [
        remote(source_of(peer), target_of(n), send.at[n], recv.at[n], (place.dp, peer))
        for n, peer in enumerate(peers)
    ]


def row_norm(state):
    return lax.rsqrt(jnp.mean(state * state, axis=1, keepdims=True) + epsilon)


def by_rows_piece(whole, rows, start=0, count=None):
    count = rows if count is None else count

    def piece(zz, xs):
        return whole.at[pl.ds(pl.multiple_of((zz * 2 + xs) * rows, rows) + start, count), :]

    return piece


def own_copies(place, blocks, sems):
    return [
        pltpu.make_async_copy(own, piece(place.z, place.x), sems.at[n])
        for n, (own, piece) in enumerate(blocks)
    ]


def weight_gather(place, timeline, refs, wholes, sems, share_sems, own_sems):
    bc_own, bc_all = refs[4], wholes[4]
    rows = refs[0].shape[0]
    head, tail = halves(rows)
    pieces = [by_rows_piece(whole, rows) for whole in wholes[:3]]
    step_all = wholes[3]

    def bc_piece(zz, xs):
        return bc_all.at[zz * 2 + xs, place.t]

    items = [
        (bc_own, bc_piece, "zx", SMALL / 2, True),
        (refs[3], lambda zz, xs: step_all.at[zz * 2 + xs], "zx", TINY, False),
        (refs[1], pieces[1], "zx", BIG, False),
        (refs[0], pieces[0], "zx", BIG, False),
        (refs[2].at[pl.ds(0, head), :], by_rows_piece(wholes[2], rows, 0, head), "xz", BIG / 2, False),
        (refs[2].at[pl.ds(head, tail), :], by_rows_piece(wholes[2], rows, head, tail), "zx", BIG / 2, False),
    ]
    copies = own_copies(place, [(item[0], item[1]) for item in items], own_sems)
    shares = share_blocks(
        place, lambda peer: bc_all.at[:, place.t], lambda n: bc_all.at[:, place.t], share_sems
    )
    timeline.add(-1.0, lambda: [copy.start() for copy in copies] and None)
    timeline.add(1.0, lambda: copies[0].wait())
    plan = gather_weights(place, timeline, items, sems)
    timeline.add(plan["side", 0] + 1.1, lambda: [copy.start() for copy in shares] and None)
    timeline.add(LATE + 1, lambda: [copy.wait() for copy in shares] and None)
    timeline.add(LATE + 1, lambda: [copy.wait() for copy in copies[1:]] and None)


def gather_outputs(line, width, inner, dp):
    shape = jax.ShapeDtypeStruct
    return [
        shape((width, inner), BF16),
        shape((width, inner), BF16),
        shape((width, inner), BF16),
        shape((dp, STEPS, width // dp), BF16),
        shape((dp, TENSOR, width // (dp * TENSOR), 2 * N), BF16),
    ]


def gather_scratch(line):
    return gather_semaphores(6, line) + share_semaphores() + [pltpu.SemaphoreType.DMA((6,))]


def start_kernel(line, resid, cotangent, gain, *refs):
    own, wholes, refs = refs[:5], refs[5:10], refs[10:]
    rows_all, top_all, normed, low = refs[:4]
    sems, share_sems, own_sems = refs[4:9], refs[9:11], refs[11]
    rows_sems, top_sems, local = refs[12:18], refs[18:24], refs[24]
    place = Place(line)
    place.greet()
    timeline = Timeline()
    own = [ref.at[0] for ref in own]
    weight_gather(place, timeline, own, wholes, sems, share_sems, own_sems)
    rows = normed.shape[0]
    block = pl.ds(pl.multiple_of(place.t * rows, rows), rows)
    local_copies = [
        pltpu.make_async_copy(normed, rows_all.at[block, :], local.at[0]),
        pltpu.make_async_copy(low, top_all.at[block, :], local.at[1]),
    ]

    def prepare():
        state = resid[...].astype(F32)
        normed[...] = (state * row_norm(state) * gain[0:1, :]).astype(BF16)
        low[...] = cotangent[...].astype(BF16)
        for copy in local_copies:
            copy.start()

    timeline.add(0.5, prepare)
    for n, (source, whole, group) in enumerate(((normed, rows_all, rows_sems), (low, top_all, top_sems))):
        begin, forward, finish = spread_rows(place, source, whole, group)
        for p in range(PIECES):
            timeline.add(0.6, functools.partial(begin, p))
            timeline.add(1.0 + (4 * n + p + 1) * 4.4, functools.partial(forward, p))
        timeline.add(LATE, finish)
    timeline.add(LATE, lambda: [copy.wait() for copy in local_copies] and None)
    timeline.run()


def call_kernel(kernel, outs, in_specs, out_specs, scratch, number, args, grid=()):
    return pl.pallas_call(
        kernel,
        grid=grid,
        out_shape=outs,
        in_specs=in_specs,
        out_specs=out_specs,
        scratch_shapes=scratch,
        compiler_params=pltpu.CompilerParams(
            collective_id=number, has_side_effects=True, vmem_limit_bytes=VMEM_LIMIT
        ),
    )(*args)


def start_layer(line, resid, cotangent, gain, own):
    rows, width = resid.shape
    inner = own[0].shape[2]
    shape = jax.ShapeDtypeStruct
    outs = gather_outputs(line, width, inner, 2 * line) + [
        shape((rows * TENSOR, width), BF16),
        shape((rows * TENSOR, width), BF16),
    ]
    scratch = [pltpu.VMEM((rows, width), BF16)] * 2 + gather_scratch(line)
    scratch += spread_semaphores() * 2 + [pltpu.SemaphoreType.DMA((2,))]
    return call_kernel(
        functools.partial(start_kernel, line),
        outs,
        [IN_VMEM] * 3 + [ANY] * 5,
        [ANY] * 7,
        scratch,
        0,
        (resid, cotangent, gain, *own),
    )


def scale_steps(place, timeline, sq, land, scale_row, scale_col, sems, inner_all):
    rows = scale_col.shape[0]

    def at(owner):
        return sq.at[:, pl.ds(pl.multiple_of(owner * rows, rows), rows)]

    peers = (place.sibling, place.mate, place.diagonal)
    copies = share_blocks(place, at, lambda n: land.at[n], sems)

    def begin(chunk):
        for peer, copy in zip(peers, copies):
            pl.when(peer == chunk)(copy.start)

    def arrive(chunk):
        @pl.when(place.t == chunk)
        def _():
            for copy in copies:
                copy.wait_recv()
            squares = at(place.t)[...] + land[0] + land[1] + land[2]
            scale = lax.rsqrt(squares / inner_all + epsilon)
            scale_row[...] = scale
            scale_col[...] = jnp.transpose(scale)

    def finish():
        for copy in copies:
            copy.wait_send()

    timeline.follow(0, begin)
    timeline.follow(FORWARD_SLOT - 1, arrive)
    timeline.add(LATE, finish)


FORWARD_SLOTS = 8
BACKWARD_SLOTS = 8
FORWARD_US = 6.7
FORWARD_SLOT = 8


def middle_kernel(line, inner_all, *refs):
    work, refs = refs[:12], refs[12:]
    (resid, gain), own, refs = refs[:2], refs[2:7], refs[7:]
    saved, refs = refs[:9], refs[9:]
    state_out, raw_out, scale_row, rows_all, refs = *refs[:4], refs[4:]
    wholes, refs = refs[:5], refs[5:]
    scratch, refs = refs[:5], refs[5:]
    near_weights, load_sems, refs = refs[:5], refs[5], refs[6:]
    loads = [
        pltpu.make_async_copy(source, target, load_sems.at[n])
        for n, (source, target) in enumerate(zip(work[1:6], near_weights))
    ]
    work = (work[0], *near_weights, *work[6:])
    part, sq, far, near, mate, land, scale_col, normed = refs[:8]
    refs = refs[8:]
    sems, share_sems, own_sems = refs[:5], refs[5:7], refs[7]
    reduce_sems, sq_sems, rows_sems, local = refs[8:14], refs[14:16], refs[16:22], refs[22]
    chunk = pl.program_id(0)
    chunks = part.shape[0] // CHUNK
    place = Place(line)
    pl.when(chunk == 0)(place.greet)
    timeline = Timeline()
    scale_steps(place, timeline, sq, land, scale_row, scale_col, sq_sems, inner_all)
    rows = normed.shape[0]
    step = rows // PIECES
    begin, forward, finish = spread_rows(place, normed, rows_all, rows_sems)

    def owner(p, sums):
        part_rows = slice(p * step, (p + 1) * step)
        raw_out[part_rows, :] = sums
        state = resid[part_rows, :].astype(F32) + sums * scale_col[part_rows, 0:1]
        state_out[part_rows, :] = state
        normed[part_rows, :] = (state * row_norm(state) * gain[1:2, :]).astype(BF16)
        begin(p)

    roll_rows(
        place, timeline, part, (far, near, mate), reduce_sems, owner, forward, FORWARD_SLOT
    )
    own = [ref.at[1] for ref in own]
    for copy in loads:
        timeline.add(-2.0, copy.start)
        timeline.add(0.6, copy.wait)
    weight_gather(place, timeline, own, wholes, sems, share_sems, own_sems)
    block = pl.ds(pl.multiple_of(place.t * rows, rows), rows)
    keep = pltpu.make_async_copy(normed, rows_all.at[block, :], local.at[0])
    timeline.add(LATE, keep.start)
    timeline.add(LATE, finish)
    timeline.add(LATE, keep.wait)
    hook, end = timeline.spread(chunks, FORWARD_SLOTS, FORWARD_US)
    at = pl.multiple_of(chunk * CHUNK, CHUNK)
    forward_kernel(
        *work, part.at[pl.ds(at, CHUNK), :], sq.at[:, pl.ds(at, CHUNK)], *saved, *scratch, hook=hook
    )
    end()


def row_scratch(length, rows, width):
    return [
        pltpu.VMEM((length, width), BF16),
        pltpu.VMEM((8, length), F32),
        pltpu.VMEM((rows, width), BF16),
        pltpu.VMEM((rows, width), BF16),
        pltpu.VMEM((rows, width), BF16),
        pltpu.VMEM((3, 8, rows), F32),
        pltpu.VMEM((rows, 8), F32),
    ]


def middle_layer(line, inner_all, rows_all, weights, layer_args, aux, segrow, resid, gain, own):
    rows, width = resid.shape
    length = rows_all.shape[0]
    inner = own[0].shape[2]
    shape = jax.ShapeDtypeStruct
    outs = (
        saved_shapes(length, inner)
        + [
            shape((rows, width), F32),
            shape((rows, width), F32),
            shape((8, rows), F32),
            shape((length, width), BF16),
        ]
        + gather_outputs(line, width, inner, 2 * line)
    )
    scratch = forward_scratch(inner)
    scratch += [pltpu.VMEM(array.shape, array.dtype) for array in weights]
    scratch += [pltpu.SemaphoreType.DMA((5,))] + row_scratch(length, rows, width)
    scratch += [pltpu.VMEM((rows, width), BF16)]
    scratch += gather_scratch(line) + reduce_semaphores() + share_semaphores() + spread_semaphores()
    scratch += [pltpu.SemaphoreType.DMA((1,))]
    return call_kernel(
        functools.partial(middle_kernel, line, inner_all),
        outs,
        forward_in_specs(0, rows_all, [ANY] * 5, layer_args)
        + [whole_spec(resid.shape), whole_spec(gain.shape)]
        + [ANY] * 5,
        saved_specs(inner)
        + [whole_spec((rows, width)), whole_spec((rows, width)), whole_spec((8, rows))]
        + [ANY] * 6,
        scratch,
        1,
        (rows_all, *weights, *layer_args, aux, segrow, resid, gain, *own),
        (length // CHUNK,),
    )


def per_row_steps(place, timeline, scale_row, cross_col, stage, land, out, sems, inner_all, slot):
    rows = cross_col.shape[0]
    copies = share_blocks(place, lambda peer: stage, lambda n: land.at[n], sems)
    peers = (place.sibling, place.mate, place.diagonal)

    def send():
        cross = jnp.transpose(jnp.broadcast_to(cross_col[:, 0:1], (rows, LANES)))[0:8, :]
        scale = scale_row[...]
        coef = scale * scale * scale * cross / inner_all
        stage[...] = jnp.where(iota2((8, rows), 0) == 0, scale, coef)
        for copy in copies:
            copy.start()
        out[:, pl.ds(pl.multiple_of(place.t * rows, rows), rows)] = stage[...]

    def follow(chunk):
        pl.when(place.t == chunk)(send)

    def arrive():
        for n, (copy, peer) in enumerate(zip(copies, peers)):
            copy.wait()
            out[:, pl.ds(pl.multiple_of(peer * rows, rows), rows)] = land[n]

    timeline.follow(slot + 1 + 3 * (PIECES - 1), follow)
    timeline.add(LATE, arrive)


def top_kernel(line, inner_all, *refs):
    work, (state, cotangent), refs = refs[:12], refs[12:14], refs[14:]
    saved, (hidden, per_row), refs = refs[:9], refs[9:11], refs[11:]
    scratch, refs = refs[:5], refs[5:]
    part, sq, far, near, mate, sq_land, scale_col = refs[:7]
    row_land, scale_row, cross_col, stage = refs[7:11]
    reduce_sems, sq_sems, row_sems = refs[11:17], refs[17:19], refs[19:21]
    chunk = pl.program_id(0)
    chunks = part.shape[0] // CHUNK
    place = Place(line)
    pl.when(chunk == 0)(lambda: place.greet(across=False))
    timeline = Timeline()
    scale_steps(place, timeline, sq, sq_land, scale_row, scale_col, sq_sems, inner_all)
    step = cross_col.shape[0] // PIECES

    def owner(p, sums):
        part_rows = slice(p * step, (p + 1) * step)
        hidden[part_rows, :] = state[part_rows, :] + sums * scale_col[part_rows, 0:1]
        low = cotangent[part_rows, :].astype(BF16).astype(F32)
        cross = jnp.sum(low * sums, axis=1, keepdims=True)
        cross_col[part_rows, :] = jnp.broadcast_to(cross, (step, LANES))

    roll_rows(place, timeline, part, (far, near, mate), reduce_sems, owner, None, FORWARD_SLOT)
    per_row_steps(
        place, timeline, scale_row, cross_col, stage, row_land, per_row, row_sems, inner_all,
        FORWARD_SLOT,
    )
    hook, end = timeline.spread(chunks, FORWARD_SLOTS, FORWARD_US)
    at = pl.multiple_of(chunk * CHUNK, CHUNK)
    forward_kernel(
        *work, part.at[pl.ds(at, CHUNK), :], sq.at[:, pl.ds(at, CHUNK)], *saved, *scratch, hook=hook
    )
    end()


def top_layer(line, inner_all, rows_all, weights, layer_args, aux, segrow, state, cotangent):
    rows, width = state.shape
    length = rows_all.shape[0]
    inner = weights[0].shape[1]
    shape = jax.ShapeDtypeStruct
    scratch = forward_scratch(inner) + row_scratch(length, rows, width)
    scratch += [
        pltpu.VMEM((3, 8, rows), F32),
        pltpu.VMEM((8, rows), F32),
        pltpu.VMEM((rows, LANES), F32),
        pltpu.VMEM((8, rows), F32),
    ]
    scratch += reduce_semaphores() + share_semaphores() * 2
    return call_kernel(
        functools.partial(top_kernel, line, inner_all),
        saved_shapes(length, inner) + [shape((rows, width), F32), shape((8, length), F32)],
        forward_in_specs(1, rows_all, [whole_spec(w.shape) for w in weights], layer_args)
        + [whole_spec(state.shape), whole_spec(cotangent.shape)],
        saved_specs(inner) + [whole_spec((rows, width)), whole_spec((8, length))],
        scratch,
        2,
        (rows_all, *weights, *layer_args, aux, segrow, state, cotangent),
        (length // CHUNK,),
    )


def halves(rows):
    first = max(rows // 32 * 16, 16)
    return first, rows - first


def thirds(rows):
    first = max(rows // 64 * 16, 16)
    return (first, *halves(rows - first))


BACKWARD_US = 10.0
END_LAG = 7.0
DOTS_US = 6.0


def weight_scatter(
    place, timeline, grads, early, outs, lands, sems, bc_land, bc_sum, share_sems, late
):
    bc = grads[4]
    shares = share_blocks(
        place, lambda peer: bc.at[:, peer], lambda n: bc_land.at[n], share_sems
    )
    bc_ready = late + 12.0

    def bc_add():
        for copy in shares:
            copy.wait()

        def body(n, carry):
            total = bc[n, place.t].astype(F32) + bc_land[0, n].astype(F32)
            total = total + bc_land[1, n].astype(F32) + bc_land[2, n].astype(F32)
            bc_sum[n] = total.astype(BF16)
            return carry

        lax.fori_loop(0, bc.shape[0], body, 0)

    timeline.add(late, lambda: [copy.start() for copy in shares] and None)
    timeline.add(bc_ready, bc_add)
    rows = outs[0].shape[0]
    head, tail = halves(rows)
    first, second = pl.ds(0, head), pl.ds(head, tail)

    def low(ref):
        return by_rows_piece(ref, rows, 0, head)

    def high(ref):
        return by_rows_piece(ref, rows, head, tail)

    def shared(zz, xs):
        return bc_sum.at[zz * 2 + xs]

    def steps(zz, xs):
        return grads[3].at[zz * 2 + xs]

    count = thirds(rows)
    starts = (0, count[0], count[0] + count[1])

    def third(n):
        return by_rows_piece(grads[2], rows, starts[n], count[n])

    def inner_item(n, route):
        out = outs[2].at[pl.ds(starts[n], count[n]), :]
        return (third(n), third(n), lands[6 + 2 * n : 8 + 2 * n], out, route, BIG * count[n] / rows, late)

    items = [
        (low(grads[0]), low(early[0]), lands[0:2], outs[0].at[first, :], "zx", BIG / 2, 0.0),
        (high(grads[0]), high(early[0]), lands[2:4], outs[0].at[second, :], "xz", BIG / 2, 0.0),
        (by_rows_piece(grads[1], rows), by_rows_piece(early[1], rows), lands[4:6], outs[1], "xz", BIG, 0.0),
        inner_item(0, "zx"),
        inner_item(1, "xz"),
        inner_item(2, "xz"),
        (steps, steps, lands[12:14], outs[3], "xz", TINY, late),
        (shared, shared, lands[14:16], outs[4], "xz", SMALL / 2, bc_ready + 0.1),
    ]
    scatter_weights(place, timeline, items, sems)


def scatter_outputs(width, inner, dp):
    shape = jax.ShapeDtypeStruct
    rows = width // dp
    return [shape((rows, inner), F32)] * 3 + [
        shape((STEPS, rows), F32),
        shape((rows // TENSOR, 2 * N), F32),
    ]


def scatter_scratch(line, width, inner):
    dp = 2 * line
    rows = width // dp
    head, tail = halves(rows)
    fine = rows // TENSOR
    scratch = [
        pltpu.VMEM((1, head, inner), BF16),
        pltpu.VMEM((line + 1, 2, head, inner), BF16),
    ]
    few, some, more = thirds(rows)
    for count, cols in ((tail, inner), (rows, inner)):
        scratch += [pltpu.VMEM((line, count, cols), BF16), pltpu.VMEM((line + 1, count, cols), BF16)]
    scratch += [
        pltpu.VMEM((1, few, inner), BF16),
        pltpu.VMEM((line + 1, 2, few, inner), BF16),
    ]
    for count, cols in ((some, inner), (more, inner), (STEPS, rows), (fine, 2 * N)):
        scratch += [pltpu.VMEM((line, count, cols), BF16), pltpu.VMEM((line + 1, count, cols), BF16)]
    scratch += [
        pltpu.VMEM((3, dp, fine, 2 * N), BF16),
        pltpu.VMEM((dp, fine, 2 * N), BF16),
    ]
    return scratch + scatter_semaphores(8, line) + share_semaphores()


def input_gradient(state, gain, before, sums):
    scale = row_norm(state)
    gained = sums * gain
    mean = jnp.mean(gained * state, axis=1, keepdims=True)
    grad = before + scale * gained - state * (scale * scale * scale * mean)
    return grad, jnp.sum(sums * state * scale, axis=0, keepdims=True)


def late_dots(rows_all, ginner, gstep, gshared, dinner, dstep, dshared):
    dp, tensor, fine, _ = dshared.shape
    tile = rows_all.shape[1] // 2
    per_tile = tile // (tensor * fine)
    rows = tensor * fine

    def body(n, carry):
        part = pl.ds(pl.multiple_of(n * tile, tile), tile)
        left = rows_all[:, part]
        dinner[part, :] = contract(left, ginner[...])
        steps = contract_wide(gstep[...], left)[0:STEPS, :].astype(BF16)
        for m in range(per_tile):
            dstep[n * per_tile + m] = steps[:, m * rows : (m + 1) * rows]
        shared = contract_wide(left, gshared[...])
        for m in range(per_tile * tensor):
            block = shared[m * fine : (m + 1) * fine, :].astype(BF16)
            dshared[n * per_tile + m // tensor, m % tensor] = block
        return carry

    lax.fori_loop(0, 2, body, 0)


def pull_kernel(line, inner_all, final, *refs):
    work, refs = refs[:21], refs[21:]
    far_side, gain, refs = refs[:5], refs[5], refs[6:]
    if final:
        gnorm_top, small_more, small_top, small_top_more, bc_top, refs = *refs[:5], refs[5:]
        grad_out, norm_sum, small_sum, bc_sums, refs = *refs[:4], refs[4:]
    else:
        raw, scale_row, refs = *refs[:2], refs[2:]
        grad_out, gnorm, per_row, top_all, small, small_bc, refs = *refs[:6], refs[6:]
    outs, refs = refs[:5], refs[5:]
    scratch, refs = refs[:7], refs[7:]
    near_side, load_sems, refs = refs[:9], refs[9], refs[10:]
    rows_all, dout, dgate, before, state = near_side[:5]
    far_side = (*far_side, *work[10:14])
    work = (*work[:10], *near_side[5:], *work[14:])
    loads = [
        pltpu.make_async_copy(source, target, load_sems.at[n])
        for n, (source, target) in enumerate(zip(far_side, near_side))
    ]
    part, ginner, gstep, gshared, dinner, dstep, dshared = refs[:7]
    far, near, mate, refs = *refs[7:10], refs[10:]
    lands, bc_land, bc_sum, sems, share_sems = refs[:16], refs[16], refs[17], refs[18:24], refs[24:26]
    reduce_sems, refs = refs[26:32], refs[32:]
    if final:
        small, small_bc, small_land, bc_land_sums, norm_land = refs[:5]
        small_send, small_recv = refs[5:]
    else:
        row_land, cross_col, stage, low = refs[:4]
        row_sems, top_sems, local = refs[4:6], refs[6:12], refs[12]
    dp = 2 * line
    bits = [1 << n for n in range(dp.bit_length() - 1)]
    chunk = pl.program_id(0)
    chunks = part.shape[0] // CHUNK
    place = Place(line)
    far_bits = [bit for bit in bits if bit >= 4] if final else []
    pl.when(chunk == 0)(lambda: place.greet(far_bits=far_bits))
    timeline = Timeline()
    done = BACKWARD_US * chunks + 0.5
    late = done + 2.2 + DOTS_US
    rows = state.shape[0]
    step = rows // PIECES

    if not final:
        begin, forward, finish = spread_rows(place, low, top_all, top_sems)

    def clear():
        if final:
            norm_sum[...] = jnp.zeros_like(norm_sum)
            norm_sum[1:2, :] = gnorm_top[0:1, :]
        else:
            gnorm[...] = jnp.zeros_like(gnorm)

    def load():
        for n in (1, 2, 3, 4, 0, 5, 6, 7, 8):
            loads[n].start()

    timeline.add(-2.0, load)
    timeline.add(-2.0, clear)
    for n in (1, 2, 3, 4, 0):
        timeline.add(2.5 if n in (1, 2) else BACKWARD_US / 2, loads[n].wait)
    for n in (5, 6, 7, 8):
        timeline.add(BACKWARD_US * 0.8, loads[n].wait)

    def own_gain():
        return gain[0:1, :] if final else gain[1:2, :]

    def owner(p, sums):
        part_rows = slice(p * step, (p + 1) * step)
        grad, column = input_gradient(
            state[part_rows, :].astype(F32), own_gain(), before[part_rows, :], sums
        )
        grad_out[part_rows, :] = grad
        if final:
            norm_sum[0:1, :] += column
            return
        gnorm[0:1, :] += column
        low[part_rows, :] = grad.astype(BF16)
        cross = jnp.sum(low[part_rows, :].astype(F32) * raw[part_rows, :], axis=1, keepdims=True)
        cross_col[part_rows, :] = jnp.broadcast_to(cross, (step, LANES))
        begin(p)

    roll_rows(
        place, timeline, part, (far, near, mate), reduce_sems, owner, None if final else forward
    )
    timeline.add(
        done + 2.2, lambda: late_dots(rows_all, ginner, gstep, gshared, dinner, dstep, dshared)
    )
    if not final:
        block = pl.ds(pl.multiple_of(place.t * rows, rows), rows)
        keep = pltpu.make_async_copy(low, top_all.at[block, :], local.at[0])
        timeline.follow(5 + 3 * (PIECES - 1), lambda chunk: pl.when(place.t == chunk)(keep.start))
        timeline.add(LATE, keep.wait)
        timeline.add(LATE, finish)
        per_row_steps(
            place, timeline, scale_row, cross_col, stage, row_land, per_row, row_sems, inner_all, 4
        )
    grads = (dout, dgate, dinner, dstep, dshared)
    weight_scatter(
        place, timeline, grads, far_side[1:3], outs, lands, sems, bc_land, bc_sum, share_sems, late
    )
    if final:

        def pack():
            small_sum[0:8, :] = small[...] + small_more[...]
            small_sum[8:16, :] = small_top[...] + small_top_more[...]
            bc_sums[0:8, :] = small_bc[...]
            bc_sums[8:16, :] = bc_top[...]

        timeline.add(done + 0.05, pack)
        along = [place.partner(bit) for bit in bits]
        across = [(place.dp, place.sibling), (place.dp, place.mate)]

        def exchange(n, partner, group, start, end):
            copies = [
                remote(own, land.at[n], small_send.at[n, m], small_recv.at[n, m], partner)
                for m, own, land in group
            ]

            def send():
                for copy in copies:
                    copy.start()

            def take():
                for copy, (_, own, land) in zip(copies, group):
                    copy.wait()
                    own[...] += land[n]

            timeline.add(start, send)
            timeline.add(end, take)

        when = BACKWARD_US * (chunks + (4 + 3 * (PIECES - 1)) / EIGHTHS) + END_LAG + 0.5
        steps = [(len(bits), across[0], 3.0), (len(bits) + 1, across[1], 5.0)]
        steps += [(n, along[n], 7.0) for n in range(len(bits))][::-1]
        for n, partner, wait in steps:
            group = [(0, bc_sums, bc_land_sums), (1, norm_sum, norm_land)]
            if n < len(bits):
                group.append((2, small_sum, small_land))
            exchange(n, partner, group, when, when + wait)
            when += wait + 0.01
    hook, end = timeline.spread(
        chunks, BACKWARD_SLOTS, BACKWARD_US, lambda n: chunks - 1 - n, END_LAG if final else LAG
    )
    at = pl.ds(pl.multiple_of((chunks - 1 - chunk) * CHUNK, CHUNK), CHUNK)
    mix_back_kernel(
        *work,
        part.at[at, :],
        ginner.at[at, :],
        gstep.at[at, :],
        gshared.at[at, :],
        small,
        small_bc,
        *scratch,
        hook=hook,
    )
    end()


def pull_layer(
    line, inner_all, saved, gates, weights, layer_args, spread, aux, segrow, rows_all, dout, dgate,
    before, state, gain, more, final,
):
    length, width = rows_all.shape
    rows = state.shape[0]
    inner = dout.shape[1]
    dp = 2 * line
    fine = width // (dp * TENSOR)
    steps = dp.bit_length() - 1
    shape = jax.ShapeDtypeStruct
    _, iraw, iconv, sraw, sconv, step, mixed, sin, _ = saved
    layer = 0 if final else 1
    far_side = (rows_all, dout, dgate, before, state)
    if final:
        outs = [
            shape((rows, width), F32),
            shape((8, width), F32),
            shape((16, inner), F32),
            shape((16, 2 * N), F32),
        ]
        out_specs = [whole_spec(out.shape) for out in outs]
    else:
        outs = [
            shape((rows, width), F32),
            shape((8, width), F32),
            shape((8, rows * TENSOR), F32),
            shape((length, width), BF16),
            shape((8, inner), F32),
            shape((8, 2 * N), F32),
        ]
        out_specs = [whole_spec(out.shape) for out in outs]
        out_specs[3] = ANY
    tail_outs = scatter_outputs(width, inner, dp)
    scratch = mix_back_scratch(inner)
    weights = weights[:4]
    scratch += [pltpu.VMEM(array.shape, array.dtype) for array in (*far_side, *weights)]
    scratch += [pltpu.SemaphoreType.DMA((9,))]
    scratch += [
        pltpu.VMEM((length, width), BF16),
        pltpu.VMEM((length, inner), BF16),
        pltpu.VMEM((length, LANES), BF16),
        pltpu.VMEM((length, 2 * N), BF16),
        pltpu.VMEM((width, inner), BF16),
        pltpu.VMEM((dp, STEPS, width // dp), BF16),
        pltpu.VMEM((dp, TENSOR, fine, 2 * N), BF16),
    ]
    scratch += [pltpu.VMEM((rows, width), BF16)] * 3
    scratch += scatter_scratch(line, width, inner) + reduce_semaphores()
    if final:
        scratch += [
            pltpu.VMEM((8, inner), F32),
            pltpu.VMEM((8, 2 * N), F32),
            pltpu.VMEM((steps, 16, inner), F32),
            pltpu.VMEM((steps + 2, 16, 2 * N), F32),
            pltpu.VMEM((steps + 2, 8, width), F32),
            pltpu.SemaphoreType.DMA((steps + 2, 3)),
            pltpu.SemaphoreType.DMA((steps + 2, 3)),
        ]
    else:
        scratch += [
            pltpu.VMEM((3, 8, rows), F32),
            pltpu.VMEM((rows, LANES), F32),
            pltpu.VMEM((8, rows), F32),
            pltpu.VMEM((rows, width), BF16),
        ]
        scratch += share_semaphores() + spread_semaphores() + [pltpu.SemaphoreType.DMA((1,))]
    return call_kernel(
        functools.partial(pull_kernel, line, inner_all, final),
        outs + tail_outs,
        mix_back_specs(layer, length // CHUNK, inner, [ANY] * 4, layer_args, spread)
        + [ANY] * 5
        + [whole_spec(gain.shape)]
        + [whole_spec(array.shape) for array in more],
        out_specs + [whole_spec(out.shape) for out in tail_outs],
        scratch,
        4 if final else 3,
        (
            iraw, iconv, sraw, sconv, step, mixed, sin, sin, *gates,
            *weights, *layer_args, spread, aux, segrow, *far_side, gain, *more,
        ),
        (length // CHUNK,),
    )


def contract_wide(left, right):
    return lax.dot_general(
        left, right, (((0,), (0,)), ((), ())), preferred_element_type=F32
    )


def contract(left, right):
    return contract_wide(left, right).astype(BF16)


def on_device(
    resid,
    segment_ids,
    cotangent,
    w_z,
    w_x,
    w_bc,
    w_dt,
    w_out,
    norm_gain,
    conv_x,
    conv_bc,
    a_log,
    dt_bias,
    d_skip,
    gated_gain,
):
    dp = lax.axis_size("dp")
    assert lax.axis_size("tensor") == TENSOR and segment_ids.shape[0] == LEN
    assert a_log.shape[0] == 2 and a_log.shape[1] <= STEPS
    line = dp // 2
    heads = a_log.shape[1]
    inner = heads * P_SIZE
    inner_all = inner * TENSOR
    width = resid.shape[1]
    aux, segrow = row_masks(segment_ids)
    spread = head_spread(inner)
    args = layer_parameters(conv_x, conv_bc, a_log, dt_bias, d_skip, gated_gain)
    own = (
        w_z,
        w_x,
        jnp.swapaxes(w_out, 1, 2),
        jnp.pad(jnp.swapaxes(w_dt, 1, 2), ((0, 0), (0, STEPS - heads), (0, 0))),
        w_bc,
    )
    gains = norm_gain

    def arranged(gathered):
        gate, inner_w, out_w, step_w, shared_w = gathered
        return gate, inner_w, shared_w.reshape(width, 2 * N), step_w, out_w

    *gathered, rows_low, top_high = start_layer(line, resid, cotangent, gains, own)
    weights_low = arranged(gathered)
    results = middle_layer(
        line, inner_all, rows_low, weights_low, args, aux, segrow, resid, gains, own
    )
    saved_low = results[:9]
    state, raw, scale_row, rows_high, *gathered = results[9:]
    weights_high = arranged(gathered)
    *saved_high, hidden, per_row = top_layer(
        line, inner_all, rows_high, weights_high, args, aux, segrow, state, cotangent
    )

    def early_grads(layer, rows_all, top_all, per_row, saved, weights):
        ggate, gout, outlow, small = gate_back(layer, top_all, per_row, saved, weights[4], args[3])
        return (ggate, gout), contract(top_all, outlow), contract(rows_all, ggate), small

    gates, dout, dgate, small_high_more = early_grads(
        1, rows_high, top_high, per_row, saved_high, weights_high
    )
    results = pull_layer(
        line, inner_all, saved_high, gates, weights_high, args, spread, aux, segrow, rows_high,
        dout, dgate, cotangent, state, gains, (raw, scale_row), False,
    )
    grad_state, gnorm_high, per_row, top_low, small_high, bc_high, *grads_high = results
    gates, dout, dgate, small_low_more = early_grads(
        0, rows_low, top_low, per_row, saved_low, weights_low
    )
    more = (gnorm_high, small_low_more, small_high, small_high_more, bc_high)
    grad_resid, norm_sum, small, small_bc, *grads_low = pull_layer(
        line, inner_all, saved_low, gates, weights_low, args, spread, aux, segrow, rows_low,
        dout, dgate, grad_state, resid, gains, more, True,
    )
    gout, gz, gx, gdt, gbc = [
        jnp.stack([low, high]) for low, high in zip(grads_low, grads_high)
    ]
    small = small.reshape(2, 8, inner)
    return (
        hidden,
        grad_resid,
        gz,
        gx,
        gbc,
        jnp.swapaxes(gdt[:, :heads], 1, 2),
        jnp.swapaxes(gout, 1, 2),
        norm_sum[:2],
        small[:, :TAPS],
        small_bc.reshape(2, 8, 2 * N)[:, :TAPS],
        small[:, 6, :heads],
        small[:, 7, :heads],
        jnp.sum(small[:, 5].reshape(2, heads, P_SIZE), axis=2),
        small[:, 4],
    )


def solution(mesh):
    rows = P(("dp", "tensor"), None)
    matrix = P(None, "dp", "tensor")
    shared = P(None, ("dp", "tensor"), None)
    wide = P(None, None, "tensor")
    head = P(None, "tensor")
    out = P(None, "tensor", "dp")
    return jax.shard_map(
        on_device,
        mesh=mesh,
        in_specs=(
            rows, P("dp"), rows, matrix, matrix, shared, matrix, out, P(), wide, P(), head, head, head, head,
        ),
        out_specs=(
            rows, rows, matrix, matrix, shared, matrix, out, P(), wide, P(), head, head, head, head,
        ),
        check_vma=False,
    )
```

```python
import functools
import heapq
import itertools

import jax
import jax.numpy as jnp
import numpy as np
from jax import lax
from jax.experimental import pallas as pl
from jax.experimental.pallas import tpu as pltpu
from jax.sharding import PartitionSpec as P

P_SIZE = 64
N = 128
LEN = 1024
CHUNK = 256
LANES = 128
TAPS = 4
STEPS = 16

highest = lax.Precision.HIGHEST
epsilon = 1e-05
F32 = jnp.float32
BF16 = jnp.bfloat16


def mm(left, right):
    return jnp.dot(left, right, preferred_element_type=F32)


def mm_nt(left, right):
    return lax.dot_general(left, right, (((1,), (1,)), ((), ())), preferred_element_type=F32)


def sigmoid(values):
    return 1.0 / (1.0 + jnp.exp(-values))


def softplus(values):
    return jnp.maximum(values, 0.0) + jnp.log1p(jnp.exp(-jnp.abs(values)))


def iota2(shape, dim):
    return lax.broadcasted_iota(jnp.int32, shape, dim)


def pair_of(columns, head):
    shape = (columns.shape[0], LANES)
    first = jnp.broadcast_to(columns[:, head : head + 1], shape)
    second = jnp.broadcast_to(columns[:, head + 1 : head + 2], shape)
    return jnp.where(iota2(shape, 1) < P_SIZE, first, second)


def head_sums(values, spread):
    high = values.astype(BF16)
    low = (values - high.astype(F32)).astype(BF16)
    return mm(high, spread) + mm(low, spread)


def decays(step_pre, rate, aux):
    step = softplus(step_pre)
    order = (iota2((CHUNK, CHUNK), 0) >= iota2((CHUNK, CHUNK), 1)).astype(F32)
    cum = jnp.dot(order, step * rate, precision=highest, preferred_element_type=F32)
    last = cum[CHUNK - 1 : CHUNK, :]
    decay_in = jnp.exp(cum) * aux[:, 4:5]
    decay_out = jnp.exp(last - cum) * aux[:, 5:6]
    decay_pass = jnp.exp(last) * aux[0:1, 6:7]
    return step, cum, decay_in, decay_out, decay_pass


def step_weights(blocks):
    joined = jnp.concatenate([blocks[n] for n in range(blocks.shape[0])], axis=1)
    return jnp.concatenate([joined, jnp.zeros((LANES - STEPS, joined.shape[1]), BF16)], axis=0)


def forward_kernel(
    rows_ref,
    wz_ref,
    wx_ref,
    wbc_ref,
    wdt_ref,
    wout_ref,
    convx_ref,
    convbc_ref,
    heads_ref,
    wide_ref,
    aux_ref,
    segrow_ref,
    part_ref,
    sq_ref,
    gate_ref,
    iraw_ref,
    iconv_ref,
    sraw_ref,
    sconv_ref,
    step_ref,
    mixed_ref,
    sin_ref,
    full_ref,
    ext_x,
    ext_bc,
    state,
    gg_ref,
    gate_raw,
    hook,
):
    inner = wx_ref.shape[1]

    @pl.when(pl.program_id(0) == 0)
    def _():
        state[...] = jnp.zeros_like(state)
        ext_x[0:8, :] = jnp.zeros((8, inner), F32)
        ext_bc[0:8, :] = jnp.zeros((8, 2 * N), F32)

    hook(0)
    rows = rows_ref[...]
    aux = aux_ref[...]
    rate = heads_ref[1:2, :]
    shared = mm(rows, wbc_ref[...])
    sraw_ref[...] = shared
    ext_bc[8 : 8 + CHUNK, :] = shared
    shared_conv = convbc_ref[TAPS - 1 : TAPS, :] * shared
    for j in range(1, TAPS):
        shared_conv = shared_conv + convbc_ref[TAPS - 1 - j : TAPS - j, :] * (
            ext_bc[8 - j : 8 - j + CHUNK, :] * aux[:, j : j + 1]
        )
    sconv_ref[...] = shared_conv
    ext_bc[0:8, :] = ext_bc[CHUNK : CHUNK + 8, :]
    shared_act = shared_conv * sigmoid(shared_conv)
    keys = shared_act[:, :N].astype(BF16)
    keys_t = jnp.transpose(shared_act[:, :N]).astype(BF16)
    query = shared_act[:, N:].astype(BF16)
    visible = (aux[:, 15:16] == segrow_ref[0:1, :]) & (
        iota2((CHUNK, CHUNK), 0) >= iota2((CHUNK, CHUNK), 1)
    )
    coupling = jnp.where(visible, mm_nt(query, keys), 0.0)
    step_raw = mm_nt(rows, step_weights(wdt_ref))
    step_ref[...] = step_raw
    step, cum, decay_in, decay_out, decay_pass = decays(
        step_raw + heads_ref[0:1, :], rate, aux
    )
    cum_t = jnp.transpose(cum)
    ext_x[8 : 8 + CHUNK, :] = mm(rows, wx_ref[...])
    gate_raw[...] = mm(rows, wz_ref[...])
    hook(1)
    squares = jnp.zeros((CHUNK, LANES), F32)
    half = iota2((CHUNK, LANES), 1) < P_SIZE
    for pair in range(inner // LANES):
        cols = slice(pair * LANES, (pair + 1) * LANES)
        head = 2 * pair
        raw = ext_x[8 : 8 + CHUNK, cols]
        iraw_ref[:, cols] = raw.astype(BF16)
        conv = convx_ref[TAPS - 1 : TAPS, cols] * raw
        for j in range(1, TAPS):
            conv = conv + convx_ref[TAPS - 1 - j : TAPS - j, cols] * (
                ext_x[8 - j : 8 - j + CHUNK, cols] * aux[:, j : j + 1]
            )
        iconv_ref[:, cols] = conv
        ext_x[0:8, cols] = ext_x[CHUNK : CHUNK + 8, cols]
        act = conv * sigmoid(conv)
        scaled = (act * pair_of(step, head)).astype(BF16)
        parts = []
        for one in (head, head + 1):
            gap = cum[:, one : one + 1] - cum_t[one : one + 1, :]
            weights = (coupling * jnp.exp(jnp.minimum(gap, 0.0))).astype(BF16)
            parts.append(mm(weights, scaled))
        before = state[:, cols]
        sin_ref[0, :, cols] = before
        mixed = jnp.where(half, parts[0], parts[1])
        mixed = mixed + pair_of(decay_in, head) * mm(query, before.astype(BF16))
        mixed_ref[:, cols] = mixed
        leaving = (scaled.astype(F32) * pair_of(decay_out, head)).astype(BF16)
        state[:, cols] = pair_of(decay_pass, head) * before + mm(keys_t, leaving)
        gate = gate_raw[:, cols]
        gate_ref[:, cols] = gate.astype(BF16)
        full = mixed + wide_ref[0:1, cols] * act
        full_ref[:, cols] = full.astype(BF16)
        gated = full * (gate * sigmoid(gate))
        squares = squares + gated * gated
        gg_ref[:, cols] = (gated * wide_ref[1:2, cols]).astype(BF16)
        hook(2 + pair)
    total = jnp.sum(squares, axis=1, keepdims=True)
    sq_ref[...] = jnp.transpose(jnp.broadcast_to(total, (CHUNK, LANES)))[0:8, :]
    part_ref[...] = mm_nt(gg_ref[...], wout_ref[...]).astype(BF16)


def gate_back_kernel(
    top_ref,
    sc_ref,
    gate_ref,
    full_ref,
    wout_ref,
    wide_ref,
    ggate_ref,
    gout_ref,
    outlow_ref,
    small_ref,
    gno_ref,
):
    inner = wout_ref.shape[1]

    @pl.when(pl.program_id(0) == 0)
    def _():
        small_ref[...] = jnp.zeros_like(small_ref)

    gno_ref[...] = mm(top_ref[...], wout_ref[...])
    per_row = jnp.transpose(sc_ref[...])
    scale = per_row[:, 0:1]
    coef = per_row[:, 1:2]
    for pair in range(inner // LANES):
        cols = slice(pair * LANES, (pair + 1) * LANES)
        gain = wide_ref[1:2, cols]
        gate = gate_ref[:, cols].astype(F32)
        gate_sig = sigmoid(gate)
        gate_act = gate * gate_sig
        full = full_ref[:, cols].astype(F32)
        gated = full * gate_act
        gno = gno_ref[:, cols]
        gated_scaled = gated * scale
        small_ref[4:5, cols] += jnp.sum(gno * gated_scaled, axis=0, keepdims=True)
        outlow_ref[:, cols] = (gated_scaled * gain).astype(BF16)
        ggated = scale * (gno * gain) - gated * coef
        gout_ref[:, cols] = (ggated * gate_act).astype(BF16)
        ggate_ref[:, cols] = (
            ggated * full * (gate_sig * (1.0 + gate * (1.0 - gate_sig)))
        ).astype(BF16)


def gate_back(layer, top_all, per_row, saved, weight_out, wide):
    length, width = top_all.shape
    inner = weight_out.shape[1]
    gate, full = saved[0], saved[8]
    shape = jax.ShapeDtypeStruct
    return pl.pallas_call(
        gate_back_kernel,
        grid=(length // CHUNK,),
        in_specs=[block_rows(width), pl.BlockSpec((8, CHUNK), lambda i: (0, i))]
        + [block_rows(inner)] * 2
        + [whole_spec(weight_out.shape), layer_spec(layer, wide.shape)],
        out_specs=[block_rows(inner)] * 3 + [pl.BlockSpec((8, inner), lambda i: (0, 0))],
        out_shape=[shape((length, inner), BF16)] * 3 + [shape((8, inner), F32)],
        scratch_shapes=[pltpu.VMEM((CHUNK, inner), F32)],
        compiler_params=pltpu.CompilerParams(
            dimension_semantics=("arbitrary",), vmem_limit_bytes=VMEM_LIMIT
        ),
    )(top_all, per_row, gate, full, weight_out, wide)


def mix_back_kernel(
    iraw_ref,
    iconv_ref,
    sraw_ref,
    sconv_ref,
    step_ref,
    mixed_ref,
    sin_ref,
    sout_ref,
    ggate_ref,
    gout_ref,
    wz_ref,
    wx_ref,
    wbc_ref,
    wdt_ref,
    convx_ref,
    convbc_ref,
    heads_ref,
    wide_ref,
    spread_ref,
    aux_ref,
    segrow_ref,
    part_ref,
    ginner_ref,
    gstep_ref,
    gshared_ref,
    small_ref,
    smallbc_ref,
    gext_x,
    gext_bc,
    dstate,
    balance,
    direct,
    edge,
    dcoup,
    hook,
):
    inner = wx_ref.shape[1]

    @pl.when(pl.program_id(0) == 0)
    def _():
        dstate[...] = jnp.zeros_like(dstate)
        gext_x[CHUNK : CHUNK + 8, :] = jnp.zeros((8, inner), F32)
        gext_bc[CHUNK : CHUNK + 8, :] = jnp.zeros((8, 2 * N), F32)
        small_ref[...] = jnp.zeros_like(small_ref)
        smallbc_ref[...] = jnp.zeros_like(smallbc_ref)
        edge[...] = jnp.zeros_like(edge)

    hook(0)
    aux = aux_ref[...]
    rate = heads_ref[1:2, :]
    step_pre = step_ref[...] + heads_ref[0:1, :]
    step, cum, decay_in, decay_out, decay_pass = decays(step_pre, rate, aux)
    cum_t = jnp.transpose(cum)
    shared_conv = sconv_ref[...]
    shared_sig = sigmoid(shared_conv)
    shared_act = shared_conv * shared_sig
    keys = shared_act[:, :N].astype(BF16)
    query = shared_act[:, N:].astype(BF16)
    query_t = jnp.transpose(shared_act[:, N:]).astype(BF16)
    visible = (aux[:, 15:16] == segrow_ref[0:1, :]) & (
        iota2((CHUNK, CHUNK), 0) <= iota2((CHUNK, CHUNK), 1)
    )
    coupling = jnp.where(visible, mm_nt(keys, query), 0.0)
    half = iota2((CHUNK, LANES), 1) < P_SIZE
    dcoup[...] = jnp.zeros_like(dcoup)
    dkeys = jnp.zeros((CHUNK, N), F32)
    dquery = jnp.zeros((CHUNK, N), F32)
    for pair in range(inner // LANES):
        cols = slice(pair * LANES, (pair + 1) * LANES)
        head = 2 * pair
        skip = wide_ref[0:1, cols]
        conv = iconv_ref[:, cols]
        conv_sig = sigmoid(conv)
        act = conv * conv_sig
        step_pair = pair_of(step, head)
        scaled = (act * step_pair).astype(BF16)
        gout_low = gout_ref[:, cols]
        gout = gout_low.astype(F32)
        small_ref[5:6, cols] += jnp.sum(gout * act, axis=0, keepdims=True)
        zero = jnp.zeros_like(gout)
        parts = []
        for one, own in (
            (head, jnp.where(half, gout, zero).astype(BF16)),
            (head + 1, jnp.where(half, zero, gout).astype(BF16)),
        ):
            gap = cum_t[one : one + 1, :] - cum[:, one : one + 1]
            decay = jnp.exp(jnp.minimum(gap, 0.0))
            weights = (coupling * decay).astype(BF16)
            parts.append(mm(weights, gout_low))
            dcoup[...] += mm_nt(scaled, own) * decay
        after = dstate[:, cols]
        after_low = after.astype(BF16)
        out_pair = pair_of(decay_out, head)
        gscaled = jnp.where(half, parts[0], parts[1]) + out_pair * mm(keys, after_low)
        scaled_wide = scaled.astype(F32)
        dkeys = dkeys + mm_nt((scaled_wide * out_pair).astype(BF16), after_low)
        entering = (gout * pair_of(decay_in, head)).astype(BF16)
        dquery = dquery + mm_nt(entering, sin_ref[0, :, cols].astype(BF16))
        edge[0:1, cols] = jnp.sum(sout_ref[0, :, cols] * after, axis=0, keepdims=True)
        dstate[:, cols] = pair_of(decay_pass, head) * after + mm(query_t, entering)
        balance[:, cols] = gout * mixed_ref[:, cols] - scaled_wide * gscaled
        direct[:, cols] = act * gscaled
        gact = step_pair * gscaled + skip * gout
        gext_x[0:CHUNK, cols] = gact * (conv_sig * (1.0 + conv * (1.0 - conv_sig)))
        raw = iraw_ref[:, cols].astype(F32)
        gconv = gext_x[0:CHUNK, cols]
        graw = convx_ref[TAPS - 1 : TAPS, cols] * gconv
        small_ref[TAPS - 1 : TAPS, cols] += jnp.sum(raw * gconv, axis=0, keepdims=True)
        for j in range(1, TAPS):
            moved = gext_x[j : j + CHUNK, cols] * aux[:, 8 + j : 9 + j]
            graw = graw + convx_ref[TAPS - 1 - j : TAPS - j, cols] * moved
            small_ref[TAPS - 1 - j : TAPS - j, cols] += jnp.sum(
                raw * moved, axis=0, keepdims=True
            )
        ginner_ref[:, cols] = graw.astype(BF16)
        gext_x[CHUNK : CHUNK + 8, cols] = gext_x[0:8, cols]
        hook(1 + pair)
    spread = spread_ref[...]
    order = (iota2((CHUNK, CHUNK), 0) <= iota2((CHUNK, CHUNK), 1)).astype(F32)
    running = jnp.dot(
        order, head_sums(balance[...], spread), precision=highest, preferred_element_type=F32
    )
    running = running + head_sums(edge[...], spread)[0:1, :]
    gstep = (head_sums(direct[...], spread) + running * rate) * sigmoid(step_pre)
    small_ref[6:7, 0:LANES] += rate * jnp.sum(running * step, axis=0, keepdims=True)
    small_ref[7:8, 0:LANES] += jnp.sum(gstep, axis=0, keepdims=True)
    gstep_ref[...] = gstep.astype(BF16)
    dcoupling = jnp.where(visible, dcoup[...], 0.0)
    dkeys = dkeys + mm(dcoupling.astype(BF16), query)
    dquery = dquery + mm(jnp.transpose(dcoupling).astype(BF16), keys)
    slope = shared_sig * (1.0 + shared_conv * (1.0 - shared_sig))
    gext_bc[0:CHUNK, 0:N] = dkeys * slope[:, :N]
    gext_bc[0:CHUNK, N : 2 * N] = dquery * slope[:, N:]
    raw = sraw_ref[...]
    gconv = gext_bc[0:CHUNK, :]
    graw = convbc_ref[TAPS - 1 : TAPS, :] * gconv
    smallbc_ref[TAPS - 1 : TAPS, :] += jnp.sum(raw * gconv, axis=0, keepdims=True)
    for j in range(1, TAPS):
        moved = gext_bc[j : j + CHUNK, :] * aux[:, 8 + j : 9 + j]
        graw = graw + convbc_ref[TAPS - 1 - j : TAPS - j, :] * moved
        smallbc_ref[TAPS - 1 - j : TAPS - j, :] += jnp.sum(raw * moved, axis=0, keepdims=True)
    gshared_ref[...] = graw.astype(BF16)
    gext_bc[CHUNK : CHUNK + 8, :] = gext_bc[0:8, :]
    hook(7)
    total = mm_nt(ggate_ref[...], wz_ref[...]) + mm_nt(ginner_ref[...], wx_ref[...])
    total = total + mm(gstep_ref[...], step_weights(wdt_ref))
    part_ref[...] = (total + mm_nt(gshared_ref[...], wbc_ref[...])).astype(BF16)


def whole_spec(shape):
    zeros = (0,) * len(shape)
    return pl.BlockSpec(shape, lambda i: zeros, pipeline_mode=pl.Buffered(1))


def layer_spec(layer, shape):
    return pl.BlockSpec(
        (None, *shape[1:]),
        lambda i: (layer,) + (0,) * (len(shape) - 1),
        pipeline_mode=pl.Buffered(1),
    )


VMEM_LIMIT = 62 * 1024 * 1024


def block_rows(cols):
    return pl.BlockSpec((CHUNK, cols), lambda i: (i, 0))


def forward_in_specs(layer, rows_all, weight_specs, layer_args):
    return (
        [block_rows(rows_all.shape[1])]
        + weight_specs
        + [layer_spec(layer, w.shape) for w in layer_args]
        + [block_rows(LANES), pl.BlockSpec((8, CHUNK), lambda i: (0, i))]
    )


def saved_specs(inner):
    return [
        block_rows(inner),
        block_rows(inner),
        block_rows(inner),
        block_rows(2 * N),
        block_rows(2 * N),
        block_rows(LANES),
        block_rows(inner),
        pl.BlockSpec((1, N, inner), lambda i: (i, 0, 0)),
        block_rows(inner),
    ]


def saved_shapes(length, inner):
    shape = jax.ShapeDtypeStruct
    return [
        shape((length, inner), BF16),
        shape((length, inner), BF16),
        shape((length, inner), F32),
        shape((length, 2 * N), F32),
        shape((length, 2 * N), F32),
        shape((length, LANES), F32),
        shape((length, inner), F32),
        shape((length // CHUNK, N, inner), F32),
        shape((length, inner), BF16),
    ]


def forward_scratch(inner):
    return [
        pltpu.VMEM((CHUNK + 8, inner), F32),
        pltpu.VMEM((CHUNK + 8, 2 * N), F32),
        pltpu.VMEM((N, inner), F32),
        pltpu.VMEM((CHUNK, inner), BF16),
        pltpu.VMEM((CHUNK, inner), F32),
    ]


def mix_back_specs(layer, chunks, inner, weight_specs, layer_args, spread):
    last = chunks - 1

    def turned(cols):
        return pl.BlockSpec((CHUNK, cols), lambda i: (last - i, 0))

    return (
        [
            turned(inner),
            turned(inner),
            turned(2 * N),
            turned(2 * N),
            turned(LANES),
            turned(inner),
            pl.BlockSpec((1, N, inner), lambda i: (last - i, 0, 0)),
            pl.BlockSpec((1, N, inner), lambda i: (jnp.minimum(chunks - i, last), 0, 0)),
            turned(inner),
            turned(inner),
        ]
        + weight_specs
        + [layer_spec(layer, w.shape) for w in layer_args]
        + [
            whole_spec(spread.shape),
            turned(LANES),
            pl.BlockSpec((8, CHUNK), lambda i: (0, last - i)),
        ]
    )


def mix_back_scratch(inner):
    return [
        pltpu.VMEM((CHUNK + 8, inner), F32),
        pltpu.VMEM((CHUNK + 8, 2 * N), F32),
        pltpu.VMEM((N, inner), F32),
        pltpu.VMEM((CHUNK, inner), F32),
        pltpu.VMEM((CHUNK, inner), F32),
        pltpu.VMEM((8, inner), F32),
        pltpu.VMEM((CHUNK, CHUNK), F32),
    ]


def row_masks(segment_ids):
    length = segment_ids.shape[0]
    seg = segment_ids.astype(F32)

    def shifted(j):
        return jnp.concatenate([jnp.full((j,), -1.0, F32), seg[: length - j]])

    def ahead(j):
        return jnp.concatenate([seg[j:], jnp.full((j,), -1.0, F32)])

    ends = seg[CHUNK - 1 :: CHUNK]
    own_end = jnp.repeat(ends, CHUNK)
    old_end = jnp.repeat(jnp.concatenate([jnp.full((1,), -1.0, F32), ends[:-1]]), CHUNK)
    lanes = [jnp.zeros_like(seg)] * 16
    for j in range(1, TAPS):
        lanes[j] = (shifted(j) == seg).astype(F32)
        lanes[8 + j] = (ahead(j) == seg).astype(F32)
    lanes[4] = (old_end == seg).astype(F32)
    lanes[5] = (own_end == seg).astype(F32)
    lanes[6] = (own_end == old_end).astype(F32)
    lanes[15] = seg
    aux = jnp.pad(jnp.stack(lanes, axis=1), ((0, 0), (0, LANES - 16)))
    return aux, jnp.broadcast_to(seg[None, :], (8, length))


def layer_parameters(conv_x, conv_bc, a_log, dt_bias, d_skip, gated_gain):
    heads = a_log.shape[1]
    pad = ((0, 0), (0, 0), (0, LANES - heads))
    head_rows = jnp.pad(jnp.stack([dt_bias, -jnp.exp(a_log)], axis=1), pad)
    wide = jnp.stack([jnp.repeat(d_skip, P_SIZE, axis=1), gated_gain], axis=1)
    return (conv_x, conv_bc, head_rows, wide)


def head_spread(inner):
    return jnp.asarray(
        np.arange(inner)[:, None] // P_SIZE == np.arange(LANES)[None, :], dtype=BF16
    )


MESH = pl.DeviceIdType.MESH
ANY = pl.BlockSpec(memory_space=pl.ANY)
IN_VMEM = pl.BlockSpec(memory_space=pltpu.VMEM)
PIECES = 4
TENSOR = 4
LATE = 1e9
LAG = 14.0
EIGHTHS = 8
BIG = 6.5
SMALL = 1.1
TINY = 0.2


class Place:
    def __init__(self, line):
        self.line = line
        dp, t = lax.axis_index("dp"), lax.axis_index("tensor")
        self.dp, self.t = dp, t
        self.z, self.x = lax.div(dp, 2), lax.rem(dp, 2)
        self.other = 1 - self.x
        self.sibling = t + 1 - 2 * lax.rem(t, 2)
        self.mate = lax.rem(t + 2, TENSOR)
        self.diagonal = TENSOR - 1 - t
        self.right = (lax.rem(self.z + 1, line) * 2 + self.x, t)
        self.left = (lax.rem(self.z + line - 1, line) * 2 + self.x, t)
        self.across = (self.z * 2 + self.other, t)

    def tensor_peers(self):
        return [(self.dp, self.sibling), (self.dp, self.mate), (self.dp, self.diagonal)]

    def partner(self, bit):
        return (self.dp + bit - 2 * bit * lax.rem(lax.div(self.dp, bit), 2), self.t)

    def greet(self, across=True, far_bits=()):
        barrier = pltpu.get_barrier_semaphore()
        peers = self.tensor_peers()
        if across:
            peers = peers + [self.across]
        peers = peers + [self.partner(bit) for bit in far_bits]
        for peer in peers:
            pl.semaphore_signal(barrier, inc=1, device_id=peer, device_id_type=MESH)
        count = len(peers)
        if across and self.line > 1:
            has_right = self.z < self.line - 1
            has_left = self.z > 0

            @pl.when(has_right)
            def _():
                pl.semaphore_signal(barrier, inc=1, device_id=self.right, device_id_type=MESH)

            @pl.when(has_left)
            def _():
                pl.semaphore_signal(barrier, inc=1, device_id=self.left, device_id_type=MESH)

            count = count + has_right.astype(jnp.int32) + has_left.astype(jnp.int32)
        pl.semaphore_wait(barrier, count)


class Timeline:
    def __init__(self):
        self.steps = []
        self.rolling = []

    def follow(self, eighths, step):
        self.rolling.append((eighths, step))

    def add(self, when, step):
        self.steps.append((when, len(self.steps), step))

    def ordered(self):
        return sorted(self.steps, key=lambda entry: entry[:2])

    def run(self):
        for _, _, step in self.ordered():
            step()

    def spread(self, chunks, slots, chunk_us, order=lambda k: k, lag=LAG):
        places = {}
        rolling = [(-(-offset * slots // EIGHTHS), step) for offset, step in self.rolling]
        for slot, step in rolling:
            for k in range(chunks):
                if (k + 1) * slots + slot >= chunks * slots:
                    when = ((k + 1) * slots + slot) * chunk_us / slots + (lag if 2 * slot > slots else 0.0)
                    self.add(when, functools.partial(step, order(k)))
        after = []
        for when, _, step in self.ordered():
            spot = max(0, int(when / chunk_us * slots))
            if spot < chunks * slots:
                places.setdefault((spot % slots, spot // slots), []).append(step)
            else:
                after.append(step)
        now = pl.program_id(0)

        def hook(place):
            if place * slots % EIGHTHS:
                return
            slot = place * slots // EIGHTHS
            for chunk in range(chunks):
                steps = places.get((slot, chunk))
                if steps:

                    @pl.when(now == chunk)
                    def _(steps=steps):
                        for step in steps:
                            step()

            for offset, step in rolling:
                if offset % slots == slot:
                    behind = 1 + offset // slots
                    step(jnp.where(now >= behind, order(now - behind), -1))

        def end():
            @pl.when(now == chunks - 1)
            def _():
                for step in after:
                    step()

        return hook, end


def remote(src, dst, send, recv, device):
    return pltpu.make_async_remote_copy(
        src_ref=src, dst_ref=dst, send_sem=send, recv_sem=recv, device_id=device, device_id_type=MESH
    )


def gather_semaphores(count, line):
    return [pltpu.SemaphoreType.DMA((count, 2, line))] * 5


HOP_US = 0.8
ADD_US = 0.5


def plan_gather(items, line):
    free, plan = {}, {}
    queue, count = [], itertools.count()

    def push(when, *action):
        heapq.heappush(queue, (when, next(count), action))

    def transfer(link, when, cost):
        begin = max(when, free.get(link, 0.0))
        free[link] = begin + cost
        return begin + cost + HOP_US

    def note(step, when):
        plan[step] = max(plan.get(step, 0.0), when)

    def along(when, way, z, i, source, xs):
        stop = z + 1 if way == 0 else z - 1
        if 0 <= stop < line:
            push(transfer((way, z), when, items[i][1]), "hop", way, stop, i, source, xs)

    def cross(when, z, i, source):
        push(transfer(("x", z), when, items[i][1]), "side", z, i, source)

    for i, (_, _, ready) in enumerate(items):
        push(ready, "own", i)
    while queue:
        when, _, (kind, *rest) = heapq.heappop(queue)
        if kind == "own":
            (i,) = rest
            for z in range(line):
                along(when, 0, z, i, z, 0)
                along(when, 1, z, i, z, 0)
                cross(when, z, i, z)
        elif kind == "hop":
            way, z, i, source, xs = rest
            note(("hop", i, way, abs(z - source), xs), when)
            along(when, way, z, i, source, xs)
            if items[i][0] == "zx":
                cross(when, z, i, source)
        else:
            z, i, source = rest
            note(("side", i), when)
            if items[i][0] == "xz":
                along(when, 0, z, i, source, 1)
                along(when, 1, z, i, source, 1)
    return plan


def gather_weights(place, timeline, items, sems):
    send_r, send_l, send_x, recv_z, recv_x = sems
    line = place.line
    z = place.z

    def copy(i, way, zz, xs, src=None):
        dst = items[i][1](zz, xs)
        return remote(
            dst if src is None else src,
            dst,
            (send_r, send_l, send_x)[way].at[i, xs, zz],
            (recv_x if way == 2 else recv_z).at[i, xs, zz],
            (place.right, place.left, place.across)[way],
        )

    def begin(i):
        own = items[i][0]

        def step():
            @pl.when(z < line - 1)
            def _():
                copy(i, 0, z, place.x, own).start()

            @pl.when(z > 0)
            def _():
                copy(i, 1, z, place.x, own).start()

            copy(i, 2, z, place.x, own).start()

        return step

    def hop(i, way, k, xs, to_x):
        source = z - k if way == 0 else z + k
        here = source >= 0 if way == 0 else source < line
        more = z < line - 1 if way == 0 else z > 0

        def arrive():
            @pl.when(here)
            def _():
                copy(i, way, source, xs).wait_recv()
                if to_x:
                    copy(i, 2, source, xs).start()

            @pl.when(here & more)
            def _():
                copy(i, way, source, xs).start()

        def finish():
            @pl.when(here & more)
            def _():
                copy(i, way, source, xs).wait_send()

            if to_x:

                @pl.when(here)
                def _():
                    copy(i, 2, source, xs).wait_send()

        return arrive, finish

    def side(i):
        def step():
            copy(i, 2, z, place.other).wait_recv()

            @pl.when(z < line - 1)
            def _():
                copy(i, 0, z, place.other).start()

            @pl.when(z > 0)
            def _():
                copy(i, 1, z, place.other).start()

        return step

    def end(i):
        route = items[i][2]

        def step():
            for xs in (place.x,) if route == "zx" else (place.x, place.other):

                @pl.when(z < line - 1)
                def _(xs=xs):
                    copy(i, 0, z, xs).wait_send()

                @pl.when(z > 0)
                def _(xs=xs):
                    copy(i, 1, z, xs).wait_send()

            copy(i, 2, z, place.x).wait_send()

        return step

    def settle(i):
        def step():
            for zz in range(line):
                copy(i, 2, zz, place.other).wait_recv()

        return step

    plan = plan_gather([(item[2], item[3], 0.0) for item in items], line)
    for i, (_, _, route, _, early) in enumerate(items):
        timeline.add(0.0, begin(i))
        if route == "xz":
            timeline.add(plan["side", i], side(i))
        for way in (0, 1):
            for column, xs in enumerate((place.x,) if route == "zx" else (place.x, place.other)):
                when = plan["side", i] if column else 0.0
                for k in range(1, line):
                    when = max(plan["hop", i, way, k, column], when + 0.01)
                    arrive, finish = hop(i, way, k, xs, route == "zx")
                    timeline.add(when, arrive)
                    timeline.add(LATE, finish)
        if route == "zx":
            timeline.add(plan["side", i] + 1.0 if early else LATE, settle(i))
        timeline.add(LATE, end(i))
    return plan


def scatter_semaphores(count, line):
    return [pltpu.SemaphoreType.DMA((count, 2, line))] * 6


def add_into(target, other, rows):
    step = 48 if rows % 48 == 0 else rows

    def body(n, carry):
        part = pl.ds(pl.multiple_of(n * step, step), step)
        target[part, :] = (target[part, :].astype(F32) + other[part, :].astype(F32)).astype(BF16)
        return carry

    lax.fori_loop(0, rows // step, body, 0)


def scatter_order(line):
    order = []
    for n in range((line + 1) // 2):
        order += [n] if n == line - 1 - n else [n, line - 1 - n]
    return order


def plan_scatter(items, line):
    free, arrived, joined, plan = {}, {}, {}, {}
    queue, count = [], itertools.count()

    def push(when, *action):
        heapq.heappush(queue, (when, next(count), action))

    def transfer(link, when, cost):
        begin = max(when, free.get(link, 0.0))
        free[link] = begin + cost
        return begin + cost + HOP_US

    def note(step, when):
        plan[step] = max(plan.get(step, 0.0), when)

    def go(when, z, i, zz, xs):
        first = {"r": z == 0, "l": z == line - 1}
        if z == zz:
            need = [way for way, there in (("r", z > 0), ("l", z < line - 1)) if there]
            times = [arrived.get((way, z, i, zz, xs)) for way in need] + [joined.get((z, i, zz, xs))]
            if None in times:
                return
            when = max(times)
            if items[i][0] == "xz":
                note(("last", i), when)
                return
            note(("line", i, xs), when)
            done = joined.setdefault(("line", z, i), [])
            done.append(when)
            if len(done) == 2:
                note(("swap", i), max(done))
                note(("last", i), transfer(("x", z), max(done) + 2 * ADD_US, items[i][1]))
            return
        way = "r" if z < zz else "l"
        times = [joined.get((z, i, zz, xs))]
        if not first[way]:
            times.append(arrived.get((way, z, i, zz, xs)))
        if None in times:
            return
        when = max(times)
        h = z if way == "r" else line - 1 - z
        note(("send", i, zz, way, xs, h), when)
        stop = z + 1 if way == "r" else z - 1
        push(transfer((way, z), when + ADD_US, items[i][1]), "arrive", way, stop, i, zz, xs)

    for i, (route, cost, ready) in enumerate(items):
        for zz in scatter_order(line):
            for xs in (0,) if route == "xz" else (0, 1):
                push(ready, "start", i, zz, xs)
    while queue:
        when, _, (kind, *rest) = heapq.heappop(queue)
        if kind == "start":
            i, zz, xs = rest
            for z in range(line):
                if items[i][0] == "xz":
                    push(transfer(("x", z), when, items[i][1]), "join", z, i, zz, xs)
                else:
                    push(when, "join", z, i, zz, xs)
        elif kind == "join":
            z, i, zz, xs = rest
            if items[i][0] == "xz":
                note(("join", i, zz), when)
                when += ADD_US
            joined[z, i, zz, xs] = when
            go(when, z, i, zz, xs)
        else:
            way, z, i, zz, xs = rest
            arrived[way, z, i, zz, xs] = when
            go(when, z, i, zz, xs)
    return plan


def scatter_weights(place, timeline, items, sems):
    send_x, recv_x, send_r, recv_r, send_l, recv_l = sems
    line = place.line
    z = place.z

    def rows_of(i):
        return items[i][2][0].shape[1]

    def side(i, zz):
        _, source, (land_x, _), *_ = items[i]
        return remote(
            source(zz, place.other), land_x.at[zz], send_x.at[i, 0, zz], recv_x.at[i, 0, zz], place.across
        )

    def land_along(i, zz, way, xs, stop):
        slot = zz if way == 0 else jnp.where(stop == zz, line, zz)
        land = items[i][2][1]
        return land.at[slot, xs] if items[i][4] == "zx" else land.at[slot]

    def along(i, zz, way, xs, source=None):
        here = land_along(i, zz, way, xs, z)
        return remote(
            here if source is None else source,
            land_along(i, zz, way, xs, z + 1 if way == 0 else z - 1),
            (send_r, send_l)[way].at[i, xs, zz],
            (recv_r, recv_l)[way].at[i, xs, zz],
            (place.right, place.left)[way],
        )

    def own(i, zz, xs):
        return items[i][0](zz, xs) if items[i][4] == "zx" else items[i][2][0].at[zz]

    def outgoing(i, zz, xs):
        return items[i][1](zz, xs) if items[i][4] == "zx" else items[i][2][0].at[zz]

    def join(i, zz):
        def step():
            side(i, zz).wait_recv()
            add_into(items[i][2][0].at[zz], items[i][0](zz, place.x), rows_of(i))

        return step

    def send(i, zz, way, xs, h):
        if way == 0:
            mine = (z == h) & (z < zz)
        else:
            mine = (z == line - 1 - h) & (z > zz)

        def step():
            @pl.when(mine)
            def _():
                if h == 0:
                    along(i, zz, way, xs, outgoing(i, zz, xs)).start()
                else:
                    along(i, zz, way, xs).wait_recv()
                    add_into(land_along(i, zz, way, xs, z), own(i, zz, xs), rows_of(i))
                    along(i, zz, way, xs).start()

        return step

    def last(i):
        out = items[i][3]

        def step():
            out[...] = items[i][2][0][z].astype(F32)
            for way, there in ((0, z > 0), (1, z < line - 1)):

                @pl.when(there)
                def _(way=way):
                    along(i, z, way, 0).wait_recv()
                    out[...] += items[i][2][1][z if way == 0 else line].astype(F32)

        return step

    def swap(i):
        land_x, land = items[i][2]
        stage = land.at[z, place.other]
        return remote(stage, land_x.at[0], send_x.at[i, 0, 0], recv_x.at[i, 0, 0], place.across)

    def gather_line(i, xs):
        piece = items[i][0]

        def step():
            right, left = land_along(i, z, 0, xs, z), land_along(i, z, 1, xs, z)

            @pl.when(z > 0)
            def _():
                along(i, z, 0, xs).wait_recv()
                add_into(right, piece(z, xs), rows_of(i))

            @pl.when(z == 0)
            def _():
                right[...] = piece(z, xs)[...]

            @pl.when(z < line - 1)
            def _():
                along(i, z, 1, xs).wait_recv()
                add_into(right, left, rows_of(i))

        return step

    def swap_end(i):
        (land_x, land), out = items[i][2:4]

        def step():
            swap(i).wait()
            out[...] = land[z, place.x].astype(F32) + land_x[0].astype(F32)

        return step

    def end(i, zz, xs):
        def step():
            if items[i][4] == "xz":
                side(i, zz).wait_send()
            for way, there in ((0, z < zz), (1, z > zz)):

                @pl.when(there)
                def _(way=way):
                    along(i, zz, way, xs).wait_send()

        return step

    plan = plan_scatter([item[4:] for item in items], line)
    for i, (_, _, _, _, route, _, ready) in enumerate(items):
        columns = (0,) if route == "xz" else (0, 1)
        latest = ready
        for zz in scatter_order(line):
            if route == "xz":
                timeline.add(ready, lambda i=i, zz=zz: side(i, zz).start())
                timeline.add(plan["join", i, zz], join(i, zz))
                latest = max(latest, plan["join", i, zz])
            for xs in columns:
                for way, name in enumerate("rl"):
                    when = plan.get(("join", i, zz), ready)
                    for h in range(zz if way == 0 else line - 1 - zz):
                        when = max(plan["send", i, zz, name, xs, h], when + 0.01)
                        timeline.add(when, send(i, zz, way, xs, h))
                    latest = max(latest, when)
                timeline.add(LATE, end(i, zz, xs))
        latest += 0.01
        if route == "xz":
            timeline.add(max(plan["last", i], latest), last(i))
            continue
        swaps = max(plan["swap", i], latest) + ADD_US
        for xs in columns:
            timeline.add(max(plan["line", i, xs], latest), gather_line(i, xs))
        timeline.add(swaps, lambda i=i: swap(i).start())
        timeline.add(max(plan["last", i], swaps + 0.01), swap_end(i))


def spread_semaphores():
    return [pltpu.SemaphoreType.DMA((PIECES,))] * 6


def spread_rows(place, own, whole, sems):
    send_y, recv_y, send_s, recv_s, send_f, recv_f = sems
    rows = own.shape[0]
    step = rows // PIECES

    def at(owner, p):
        return whole.at[pl.ds(pl.multiple_of(owner * rows, rows) + p * step, step), :]

    def source(p):
        return own.at[pl.ds(p * step, step), :]

    def to_mate(p):
        return remote(
            source(p), at(place.t, p), send_y.at[p], recv_y.at[p], (place.dp, place.mate)
        )

    def to_sibling(p):
        return remote(
            source(p), at(place.t, p), send_s.at[p], recv_s.at[p], (place.dp, place.sibling)
        )

    def passed_on(p):
        return remote(
            at(place.mate, p), at(place.mate, p), send_f.at[p], recv_f.at[p], (place.dp, place.sibling)
        )

    def begin(p):
        to_mate(p).start()
        to_sibling(p).start()

    def forward(p):
        to_mate(p).wait_recv()
        passed_on(p).start()

    def finish():
        for p in range(PIECES):
            to_mate(p).wait_send()
            to_sibling(p).wait()
            passed_on(p).wait()

    return begin, forward, finish


def reduce_semaphores():
    return [pltpu.SemaphoreType.DMA((PIECES,))] * 6


def roll_rows(place, timeline, part, lands, sems, owner, forward, slot=4):
    land_far, land_near, land_mate = lands
    send_a, recv_a, send_b, recv_b, send_z, recv_z = sems
    rows = land_far.shape[0]
    step = rows // PIECES

    def at(block, p):
        return part.at[pl.ds(pl.multiple_of(block * rows, rows) + p * step, step), :]

    def own(ref, p):
        return ref.at[pl.ds(p * step, step), :]

    def far(p):
        return remote(
            at(place.diagonal, p), own(land_far, p), send_a.at[p], recv_a.at[p], (place.dp, place.sibling)
        )

    def near(p):
        return remote(
            at(place.sibling, p), own(land_near, p), send_b.at[p], recv_b.at[p], (place.dp, place.sibling)
        )

    def over(p):
        return remote(
            own(land_far, p), own(land_mate, p), send_z.at[p], recv_z.at[p], (place.dp, place.mate)
        )

    def begin(chunk):
        @pl.when(place.diagonal == chunk)
        def _():
            for p in range(PIECES):
                far(p).start()

        @pl.when(place.sibling == chunk)
        def _():
            for p in range(PIECES):
                near(p).start()

    def middle(p, chunk):
        @pl.when(place.mate == chunk)
        def _():
            far(p).wait_recv()
            mine = own(land_far, p)
            mine[...] = (mine[...].astype(F32) + at(place.mate, p)[...].astype(F32)).astype(BF16)
            over(p).start()

    def final(p, chunk):
        @pl.when(place.t == chunk)
        def _():
            near(p).wait_recv()
            over(p).wait_recv()
            sums = at(place.t, p)[...].astype(F32) + own(land_near, p)[...].astype(F32)
            owner(p, sums + own(land_mate, p)[...].astype(F32))

    def pass_on(p, chunk):
        @pl.when(place.mate == chunk)
        def _():
            forward(p)

    def finish():
        for p in range(PIECES):
            far(p).wait_send()
            near(p).wait_send()
            over(p).wait_send()

    timeline.follow(0, begin)
    for p in range(PIECES):
        timeline.follow(1 + p // 2, functools.partial(middle, p))
        timeline.follow(slot + 3 * p, functools.partial(final, p))
        if forward:
            timeline.follow(slot + 4 + 3 * p, functools.partial(pass_on, p))
    timeline.add(LATE, finish)


def share_semaphores():
    return [pltpu.SemaphoreType.DMA((3,))] * 2


def share_blocks(place, source_of, target_of, sems):
    send, recv = sems
    peers = (place.sibling, place.mate, place.diagonal)
    return [
        remote(source_of(peer), target_of(n), send.at[n], recv.at[n], (place.dp, peer))
        for n, peer in enumerate(peers)
    ]


def row_norm(state):
    return lax.rsqrt(jnp.mean(state * state, axis=1, keepdims=True) + epsilon)


def by_rows_piece(whole, rows, start=0, count=None):
    count = rows if count is None else count

    def piece(zz, xs):
        return whole.at[pl.ds(pl.multiple_of((zz * 2 + xs) * rows, rows) + start, count), :]

    return piece


def own_copies(place, blocks, sems):
    return [
        pltpu.make_async_copy(own, piece(place.z, place.x), sems.at[n])
        for n, (own, piece) in enumerate(blocks)
    ]


def weight_gather(place, timeline, refs, wholes, sems, share_sems, own_sems):
    bc_own, bc_all = refs[4], wholes[4]
    rows = refs[0].shape[0]
    head, tail = halves(rows)
    pieces = [by_rows_piece(whole, rows) for whole in wholes[:3]]
    step_all = wholes[3]

    def bc_piece(zz, xs):
        return bc_all.at[zz * 2 + xs, place.t]

    items = [
        (bc_own, bc_piece, "zx", SMALL / 2, True),
        (refs[3], lambda zz, xs: step_all.at[zz * 2 + xs], "zx", TINY, False),
        (refs[1], pieces[1], "zx", BIG, False),
        (refs[0], pieces[0], "zx", BIG, False),
        (refs[2].at[pl.ds(0, head), :], by_rows_piece(wholes[2], rows, 0, head), "xz", BIG / 2, False),
        (refs[2].at[pl.ds(head, tail), :], by_rows_piece(wholes[2], rows, head, tail), "zx", BIG / 2, False),
    ]
    copies = own_copies(place, [(item[0], item[1]) for item in items], own_sems)
    shares = share_blocks(
        place, lambda peer: bc_all.at[:, place.t], lambda n: bc_all.at[:, place.t], share_sems
    )
    timeline.add(-1.0, lambda: [copy.start() for copy in copies] and None)
    timeline.add(1.0, lambda: copies[0].wait())
    plan = gather_weights(place, timeline, items, sems)
    timeline.add(plan["side", 0] + 1.1, lambda: [copy.start() for copy in shares] and None)
    timeline.add(LATE + 1, lambda: [copy.wait() for copy in shares] and None)
    timeline.add(LATE + 1, lambda: [copy.wait() for copy in copies[1:]] and None)


def gather_outputs(line, width, inner, dp):
    shape = jax.ShapeDtypeStruct
    return [
        shape((width, inner), BF16),
        shape((width, inner), BF16),
        shape((width, inner), BF16),
        shape((dp, STEPS, width // dp), BF16),
        shape((dp, TENSOR, width // (dp * TENSOR), 2 * N), BF16),
    ]


def gather_scratch(line):
    return gather_semaphores(6, line) + share_semaphores() + [pltpu.SemaphoreType.DMA((6,))]


def start_kernel(line, resid, cotangent, gain, *refs):
    own, wholes, refs = refs[:5], refs[5:10], refs[10:]
    rows_all, top_all, normed, low = refs[:4]
    sems, share_sems, own_sems = refs[4:9], refs[9:11], refs[11]
    rows_sems, top_sems, local = refs[12:18], refs[18:24], refs[24]
    place = Place(line)
    place.greet()
    timeline = Timeline()
    own = [ref.at[0] for ref in own]
    weight_gather(place, timeline, own, wholes, sems, share_sems, own_sems)
    rows = normed.shape[0]
    block = pl.ds(pl.multiple_of(place.t * rows, rows), rows)
    local_copies = [
        pltpu.make_async_copy(normed, rows_all.at[block, :], local.at[0]),
        pltpu.make_async_copy(low, top_all.at[block, :], local.at[1]),
    ]

    def prepare():
        state = resid[...].astype(F32)
        normed[...] = (state * row_norm(state) * gain[0:1, :]).astype(BF16)
        low[...] = cotangent[...].astype(BF16)
        for copy in local_copies:
            copy.start()

    timeline.add(0.5, prepare)
    for n, (source, whole, group) in enumerate(((normed, rows_all, rows_sems), (low, top_all, top_sems))):
        begin, forward, finish = spread_rows(place, source, whole, group)
        for p in range(PIECES):
            timeline.add(0.6, functools.partial(begin, p))
            timeline.add(1.0 + (4 * n + p + 1) * 4.4, functools.partial(forward, p))
        timeline.add(LATE, finish)
    timeline.add(LATE, lambda: [copy.wait() for copy in local_copies] and None)
    timeline.run()


def call_kernel(kernel, outs, in_specs, out_specs, scratch, number, args, grid=()):
    return pl.pallas_call(
        kernel,
        grid=grid,
        out_shape=outs,
        in_specs=in_specs,
        out_specs=out_specs,
        scratch_shapes=scratch,
        compiler_params=pltpu.CompilerParams(
            collective_id=number, has_side_effects=True, vmem_limit_bytes=VMEM_LIMIT
        ),
    )(*args)


def start_layer(line, resid, cotangent, gain, own):
    rows, width = resid.shape
    inner = own[0].shape[2]
    shape = jax.ShapeDtypeStruct
    outs = gather_outputs(line, width, inner, 2 * line) + [
        shape((rows * TENSOR, width), BF16),
        shape((rows * TENSOR, width), BF16),
    ]
    scratch = [pltpu.VMEM((rows, width), BF16)] * 2 + gather_scratch(line)
    scratch += spread_semaphores() * 2 + [pltpu.SemaphoreType.DMA((2,))]
    return call_kernel(
        functools.partial(start_kernel, line),
        outs,
        [IN_VMEM] * 3 + [ANY] * 5,
        [ANY] * 7,
        scratch,
        0,
        (resid, cotangent, gain, *own),
    )


def scale_steps(place, timeline, sq, land, scale_row, scale_col, sems, inner_all):
    rows = scale_col.shape[0]

    def at(owner):
        return sq.at[:, pl.ds(pl.multiple_of(owner * rows, rows), rows)]

    peers = (place.sibling, place.mate, place.diagonal)
    copies = share_blocks(place, at, lambda n: land.at[n], sems)

    def begin(chunk):
        for peer, copy in zip(peers, copies):
            pl.when(peer == chunk)(copy.start)

    def arrive(chunk):
        @pl.when(place.t == chunk)
        def _():
            for copy in copies:
                copy.wait_recv()
            squares = at(place.t)[...] + land[0] + land[1] + land[2]
            scale = lax.rsqrt(squares / inner_all + epsilon)
            scale_row[...] = scale
            scale_col[...] = jnp.transpose(scale)

    def finish():
        for copy in copies:
            copy.wait_send()

    timeline.follow(0, begin)
    timeline.follow(FORWARD_SLOT - 1, arrive)
    timeline.add(LATE, finish)


FORWARD_SLOTS = 8
BACKWARD_SLOTS = 8
FORWARD_US = 6.7
FORWARD_SLOT = 8


def middle_kernel(line, inner_all, *refs):
    work, refs = refs[:12], refs[12:]
    (resid, gain), own, refs = refs[:2], refs[2:7], refs[7:]
    saved, refs = refs[:9], refs[9:]
    state_out, raw_out, scale_row, rows_all, refs = *refs[:4], refs[4:]
    wholes, refs = refs[:5], refs[5:]
    scratch, refs = refs[:5], refs[5:]
    near_weights, load_sems, refs = refs[:5], refs[5], refs[6:]
    loads = [
        pltpu.make_async_copy(source, target, load_sems.at[n])
        for n, (source, target) in enumerate(zip(work[1:6], near_weights))
    ]
    work = (work[0], *near_weights, *work[6:])
    part, sq, far, near, mate, land, scale_col, normed = refs[:8]
    refs = refs[8:]
    sems, share_sems, own_sems = refs[:5], refs[5:7], refs[7]
    reduce_sems, sq_sems, rows_sems, local = refs[8:14], refs[14:16], refs[16:22], refs[22]
    chunk = pl.program_id(0)
    chunks = part.shape[0] // CHUNK
    place = Place(line)
    pl.when(chunk == 0)(place.greet)
    timeline = Timeline()
    scale_steps(place, timeline, sq, land, scale_row, scale_col, sq_sems, inner_all)
    rows = normed.shape[0]
    step = rows // PIECES
    begin, forward, finish = spread_rows(place, normed, rows_all, rows_sems)

    def owner(p, sums):
        part_rows = slice(p * step, (p + 1) * step)
        raw_out[part_rows, :] = sums
        state = resid[part_rows, :].astype(F32) + sums * scale_col[part_rows, 0:1]
        state_out[part_rows, :] = state
        normed[part_rows, :] = (state * row_norm(state) * gain[1:2, :]).astype(BF16)
        begin(p)

    roll_rows(
        place, timeline, part, (far, near, mate), reduce_sems, owner, forward, FORWARD_SLOT
    )
    own = [ref.at[1] for ref in own]
    for copy in loads:
        timeline.add(-2.0, copy.start)
        timeline.add(0.6, copy.wait)
    weight_gather(place, timeline, own, wholes, sems, share_sems, own_sems)
    block = pl.ds(pl.multiple_of(place.t * rows, rows), rows)
    keep = pltpu.make_async_copy(normed, rows_all.at[block, :], local.at[0])
    timeline.add(LATE, keep.start)
    timeline.add(LATE, finish)
    timeline.add(LATE, keep.wait)
    hook, end = timeline.spread(chunks, FORWARD_SLOTS, FORWARD_US)
    at = pl.multiple_of(chunk * CHUNK, CHUNK)
    forward_kernel(
        *work, part.at[pl.ds(at, CHUNK), :], sq.at[:, pl.ds(at, CHUNK)], *saved, *scratch, hook=hook
    )
    end()


def row_scratch(length, rows, width):
    return [
        pltpu.VMEM((length, width), BF16),
        pltpu.VMEM((8, length), F32),
        pltpu.VMEM((rows, width), BF16),
        pltpu.VMEM((rows, width), BF16),
        pltpu.VMEM((rows, width), BF16),
        pltpu.VMEM((3, 8, rows), F32),
        pltpu.VMEM((rows, 8), F32),
    ]


def middle_layer(line, inner_all, rows_all, weights, layer_args, aux, segrow, resid, gain, own):
    rows, width = resid.shape
    length = rows_all.shape[0]
    inner = own[0].shape[2]
    shape = jax.ShapeDtypeStruct
    outs = (
        saved_shapes(length, inner)
        + [
            shape((rows, width), F32),
            shape((rows, width), F32),
            shape((8, rows), F32),
            shape((length, width), BF16),
        ]
        + gather_outputs(line, width, inner, 2 * line)
    )
    scratch = forward_scratch(inner)
    scratch += [pltpu.VMEM(array.shape, array.dtype) for array in weights]
    scratch += [pltpu.SemaphoreType.DMA((5,))] + row_scratch(length, rows, width)
    scratch += [pltpu.VMEM((rows, width), BF16)]
    scratch += gather_scratch(line) + reduce_semaphores() + share_semaphores() + spread_semaphores()
    scratch += [pltpu.SemaphoreType.DMA((1,))]
    return call_kernel(
        functools.partial(middle_kernel, line, inner_all),
        outs,
        forward_in_specs(0, rows_all, [ANY] * 5, layer_args)
        + [whole_spec(resid.shape), whole_spec(gain.shape)]
        + [ANY] * 5,
        saved_specs(inner)
        + [whole_spec((rows, width)), whole_spec((rows, width)), whole_spec((8, rows))]
        + [ANY] * 6,
        scratch,
        1,
        (rows_all, *weights, *layer_args, aux, segrow, resid, gain, *own),
        (length // CHUNK,),
    )


def per_row_steps(place, timeline, scale_row, cross_col, stage, land, out, sems, inner_all, slot):
    rows = cross_col.shape[0]
    copies = share_blocks(place, lambda peer: stage, lambda n: land.at[n], sems)
    peers = (place.sibling, place.mate, place.diagonal)

    def send():
        cross = jnp.transpose(jnp.broadcast_to(cross_col[:, 0:1], (rows, LANES)))[0:8, :]
        scale = scale_row[...]
        coef = scale * scale * scale * cross / inner_all
        stage[...] = jnp.where(iota2((8, rows), 0) == 0, scale, coef)
        for copy in copies:
            copy.start()
        out[:, pl.ds(pl.multiple_of(place.t * rows, rows), rows)] = stage[...]

    def follow(chunk):
        pl.when(place.t == chunk)(send)

    def arrive():
        for n, (copy, peer) in enumerate(zip(copies, peers)):
            copy.wait()
            out[:, pl.ds(pl.multiple_of(peer * rows, rows), rows)] = land[n]

    timeline.follow(slot + 1 + 3 * (PIECES - 1), follow)
    timeline.add(LATE, arrive)


def top_kernel(line, inner_all, *refs):
    work, (state, cotangent), refs = refs[:12], refs[12:14], refs[14:]
    saved, (hidden, per_row), refs = refs[:9], refs[9:11], refs[11:]
    scratch, refs = refs[:5], refs[5:]
    part, sq, far, near, mate, sq_land, scale_col = refs[:7]
    row_land, scale_row, cross_col, stage = refs[7:11]
    reduce_sems, sq_sems, row_sems = refs[11:17], refs[17:19], refs[19:21]
    chunk = pl.program_id(0)
    chunks = part.shape[0] // CHUNK
    place = Place(line)
    pl.when(chunk == 0)(lambda: place.greet(across=False))
    timeline = Timeline()
    scale_steps(place, timeline, sq, sq_land, scale_row, scale_col, sq_sems, inner_all)
    step = cross_col.shape[0] // PIECES

    def owner(p, sums):
        part_rows = slice(p * step, (p + 1) * step)
        hidden[part_rows, :] = state[part_rows, :] + sums * scale_col[part_rows, 0:1]
        low = cotangent[part_rows, :].astype(BF16).astype(F32)
        cross = jnp.sum(low * sums, axis=1, keepdims=True)
        cross_col[part_rows, :] = jnp.broadcast_to(cross, (step, LANES))

    roll_rows(place, timeline, part, (far, near, mate), reduce_sems, owner, None, FORWARD_SLOT)
    per_row_steps(
        place, timeline, scale_row, cross_col, stage, row_land, per_row, row_sems, inner_all,
        FORWARD_SLOT,
    )
    hook, end = timeline.spread(chunks, FORWARD_SLOTS, FORWARD_US)
    at = pl.multiple_of(chunk * CHUNK, CHUNK)
    forward_kernel(
        *work, part.at[pl.ds(at, CHUNK), :], sq.at[:, pl.ds(at, CHUNK)], *saved, *scratch, hook=hook
    )
    end()


def top_layer(line, inner_all, rows_all, weights, layer_args, aux, segrow, state, cotangent):
    rows, width = state.shape
    length = rows_all.shape[0]
    inner = weights[0].shape[1]
    shape = jax.ShapeDtypeStruct
    scratch = forward_scratch(inner) + row_scratch(length, rows, width)
    scratch += [
        pltpu.VMEM((3, 8, rows), F32),
        pltpu.VMEM((8, rows), F32),
        pltpu.VMEM((rows, LANES), F32),
        pltpu.VMEM((8, rows), F32),
    ]
    scratch += reduce_semaphores() + share_semaphores() * 2
    return call_kernel(
        functools.partial(top_kernel, line, inner_all),
        saved_shapes(length, inner) + [shape((rows, width), F32), shape((8, length), F32)],
        forward_in_specs(1, rows_all, [whole_spec(w.shape) for w in weights], layer_args)
        + [whole_spec(state.shape), whole_spec(cotangent.shape)],
        saved_specs(inner) + [whole_spec((rows, width)), whole_spec((8, length))],
        scratch,
        2,
        (rows_all, *weights, *layer_args, aux, segrow, state, cotangent),
        (length // CHUNK,),
    )


def halves(rows):
    first = max(rows // 32 * 16, 16)
    return first, rows - first


def thirds(rows):
    first = max(rows // 64 * 16, 16)
    return (first, *halves(rows - first))


BACKWARD_US = 10.0
END_LAG = 7.0
DOTS_US = 6.0


def weight_scatter(
    place, timeline, grads, early, outs, lands, sems, bc_land, bc_sum, share_sems, late
):
    bc = grads[4]
    shares = share_blocks(
        place, lambda peer: bc.at[:, peer], lambda n: bc_land.at[n], share_sems
    )
    bc_ready = late + 12.0

    def bc_add():
        for copy in shares:
            copy.wait()

        def body(n, carry):
            total = bc[n, place.t].astype(F32) + bc_land[0, n].astype(F32)
            total = total + bc_land[1, n].astype(F32) + bc_land[2, n].astype(F32)
            bc_sum[n] = total.astype(BF16)
            return carry

        lax.fori_loop(0, bc.shape[0], body, 0)

    timeline.add(late, lambda: [copy.start() for copy in shares] and None)
    timeline.add(bc_ready, bc_add)
    rows = outs[0].shape[0]
    head, tail = halves(rows)
    first, second = pl.ds(0, head), pl.ds(head, tail)

    def low(ref):
        return by_rows_piece(ref, rows, 0, head)

    def high(ref):
        return by_rows_piece(ref, rows, head, tail)

    def shared(zz, xs):
        return bc_sum.at[zz * 2 + xs]

    def steps(zz, xs):
        return grads[3].at[zz * 2 + xs]

    count = thirds(rows)
    starts = (0, count[0], count[0] + count[1])

    def third(n):
        return by_rows_piece(grads[2], rows, starts[n], count[n])

    def inner_item(n, route):
        out = outs[2].at[pl.ds(starts[n], count[n]), :]
        return (third(n), third(n), lands[6 + 2 * n : 8 + 2 * n], out, route, BIG * count[n] / rows, late)

    items = [
        (low(grads[0]), low(early[0]), lands[0:2], outs[0].at[first, :], "zx", BIG / 2, 0.0),
        (high(grads[0]), high(early[0]), lands[2:4], outs[0].at[second, :], "xz", BIG / 2, 0.0),
        (by_rows_piece(grads[1], rows), by_rows_piece(early[1], rows), lands[4:6], outs[1], "xz", BIG, 0.0),
        inner_item(0, "zx"),
        inner_item(1, "xz"),
        inner_item(2, "xz"),
        (steps, steps, lands[12:14], outs[3], "xz", TINY, late),
        (shared, shared, lands[14:16], outs[4], "xz", SMALL / 2, bc_ready + 0.1),
    ]
    scatter_weights(place, timeline, items, sems)


def scatter_outputs(width, inner, dp):
    shape = jax.ShapeDtypeStruct
    rows = width // dp
    return [shape((rows, inner), F32)] * 3 + [
        shape((STEPS, rows), F32),
        shape((rows // TENSOR, 2 * N), F32),
    ]


def scatter_scratch(line, width, inner):
    dp = 2 * line
    rows = width // dp
    head, tail = halves(rows)
    fine = rows // TENSOR
    scratch = [
        pltpu.VMEM((1, head, inner), BF16),
        pltpu.VMEM((line + 1, 2, head, inner), BF16),
    ]
    few, some, more = thirds(rows)
    for count, cols in ((tail, inner), (rows, inner)):
        scratch += [pltpu.VMEM((line, count, cols), BF16), pltpu.VMEM((line + 1, count, cols), BF16)]
    scratch += [
        pltpu.VMEM((1, few, inner), BF16),
        pltpu.VMEM((line + 1, 2, few, inner), BF16),
    ]
    for count, cols in ((some, inner), (more, inner), (STEPS, rows), (fine, 2 * N)):
        scratch += [pltpu.VMEM((line, count, cols), BF16), pltpu.VMEM((line + 1, count, cols), BF16)]
    scratch += [
        pltpu.VMEM((3, dp, fine, 2 * N), BF16),
        pltpu.VMEM((dp, fine, 2 * N), BF16),
    ]
    return scratch + scatter_semaphores(8, line) + share_semaphores()


def input_gradient(state, gain, before, sums):
    scale = row_norm(state)
    gained = sums * gain
    mean = jnp.mean(gained * state, axis=1, keepdims=True)
    grad = before + scale * gained - state * (scale * scale * scale * mean)
    return grad, jnp.sum(sums * state * scale, axis=0, keepdims=True)


def late_dots(rows_all, ginner, gstep, gshared, dinner, dstep, dshared):
    dp, tensor, fine, _ = dshared.shape
    tile = rows_all.shape[1] // 2
    per_tile = tile // (tensor * fine)
    rows = tensor * fine

    def body(n, carry):
        part = pl.ds(pl.multiple_of(n * tile, tile), tile)
        left = rows_all[:, part]
        dinner[part, :] = contract(left, ginner[...])
        steps = contract_wide(gstep[...], left)[0:STEPS, :].astype(BF16)
        for m in range(per_tile):
            dstep[n * per_tile + m] = steps[:, m * rows : (m + 1) * rows]
        shared = contract_wide(left, gshared[...])
        for m in range(per_tile * tensor):
            block = shared[m * fine : (m + 1) * fine, :].astype(BF16)
            dshared[n * per_tile + m // tensor, m % tensor] = block
        return carry

    lax.fori_loop(0, 2, body, 0)


def pull_kernel(line, inner_all, final, *refs):
    work, refs = refs[:21], refs[21:]
    far_side, gain, refs = refs[:5], refs[5], refs[6:]
    if final:
        gnorm_top, small_more, small_top, small_top_more, bc_top, refs = *refs[:5], refs[5:]
        grad_out, norm_sum, small_sum, bc_sums, refs = *refs[:4], refs[4:]
    else:
        raw, scale_row, refs = *refs[:2], refs[2:]
        grad_out, gnorm, per_row, top_all, small, small_bc, refs = *refs[:6], refs[6:]
    outs, refs = refs[:5], refs[5:]
    scratch, refs = refs[:7], refs[7:]
    near_side, load_sems, refs = refs[:9], refs[9], refs[10:]
    rows_all, dout, dgate, before, state = near_side[:5]
    far_side = (*far_side, *work[10:14])
    work = (*work[:10], *near_side[5:], *work[14:])
    loads = [
        pltpu.make_async_copy(source, target, load_sems.at[n])
        for n, (source, target) in enumerate(zip(far_side, near_side))
    ]
    part, ginner, gstep, gshared, dinner, dstep, dshared = refs[:7]
    far, near, mate, refs = *refs[7:10], refs[10:]
    lands, bc_land, bc_sum, sems, share_sems = refs[:16], refs[16], refs[17], refs[18:24], refs[24:26]
    reduce_sems, refs = refs[26:32], refs[32:]
    if final:
        small, small_bc, small_land, bc_land_sums, norm_land = refs[:5]
        small_send, small_recv = refs[5:]
    else:
        row_land, cross_col, stage, low = refs[:4]
        row_sems, top_sems, local = refs[4:6], refs[6:12], refs[12]
    dp = 2 * line
    bits = [1 << n for n in range(dp.bit_length() - 1)]
    chunk = pl.program_id(0)
    chunks = part.shape[0] // CHUNK
    place = Place(line)
    far_bits = [bit for bit in bits if bit >= 4] if final else []
    pl.when(chunk == 0)(lambda: place.greet(far_bits=far_bits))
    timeline = Timeline()
    done = BACKWARD_US * chunks + 0.5
    late = done + 2.2 + DOTS_US
    rows = state.shape[0]
    step = rows // PIECES

    if not final:
        begin, forward, finish = spread_rows(place, low, top_all, top_sems)

    def clear():
        if final:
            norm_sum[...] = jnp.zeros_like(norm_sum)
            norm_sum[1:2, :] = gnorm_top[0:1, :]
        else:
            gnorm[...] = jnp.zeros_like(gnorm)

    def load():
        for n in (1, 2, 3, 4, 0, 5, 6, 7, 8):
            loads[n].start()

    timeline.add(-2.0, load)
    timeline.add(-2.0, clear)
    for n in (1, 2, 3, 4, 0):
        timeline.add(2.5 if n in (1, 2) else BACKWARD_US / 2, loads[n].wait)
    for n in (5, 6, 7, 8):
        timeline.add(BACKWARD_US * 0.8, loads[n].wait)

    def own_gain():
        return gain[0:1, :] if final else gain[1:2, :]

    def owner(p, sums):
        part_rows = slice(p * step, (p + 1) * step)
        grad, column = input_gradient(
            state[part_rows, :].astype(F32), own_gain(), before[part_rows, :], sums
        )
        grad_out[part_rows, :] = grad
        if final:
            norm_sum[0:1, :] += column
            return
        gnorm[0:1, :] += column
        low[part_rows, :] = grad.astype(BF16)
        cross = jnp.sum(low[part_rows, :].astype(F32) * raw[part_rows, :], axis=1, keepdims=True)
        cross_col[part_rows, :] = jnp.broadcast_to(cross, (step, LANES))
        begin(p)

    roll_rows(
        place, timeline, part, (far, near, mate), reduce_sems, owner, None if final else forward
    )
    timeline.add(
        done + 2.2, lambda: late_dots(rows_all, ginner, gstep, gshared, dinner, dstep, dshared)
    )
    if not final:
        block = pl.ds(pl.multiple_of(place.t * rows, rows), rows)
        keep = pltpu.make_async_copy(low, top_all.at[block, :], local.at[0])
        timeline.follow(5 + 3 * (PIECES - 1), lambda chunk: pl.when(place.t == chunk)(keep.start))
        timeline.add(LATE, keep.wait)
        timeline.add(LATE, finish)
        per_row_steps(
            place, timeline, scale_row, cross_col, stage, row_land, per_row, row_sems, inner_all, 4
        )
    grads = (dout, dgate, dinner, dstep, dshared)
    weight_scatter(
        place, timeline, grads, far_side[1:3], outs, lands, sems, bc_land, bc_sum, share_sems, late
    )
    if final:

        def pack():
            small_sum[0:8, :] = small[...] + small_more[...]
            small_sum[8:16, :] = small_top[...] + small_top_more[...]
            bc_sums[0:8, :] = small_bc[...]
            bc_sums[8:16, :] = bc_top[...]

        timeline.add(done + 0.05, pack)
        along = [place.partner(bit) for bit in bits]
        across = [(place.dp, place.sibling), (place.dp, place.mate)]

        def exchange(n, partner, group, start, end):
            copies = [
                remote(own, land.at[n], small_send.at[n, m], small_recv.at[n, m], partner)
                for m, own, land in group
            ]

            def send():
                for copy in copies:
                    copy.start()

            def take():
                for copy, (_, own, land) in zip(copies, group):
                    copy.wait()
                    own[...] += land[n]

            timeline.add(start, send)
            timeline.add(end, take)

        when = BACKWARD_US * (chunks + (4 + 3 * (PIECES - 1)) / EIGHTHS) + END_LAG + 0.5
        steps = [(len(bits), across[0], 2.5), (len(bits) + 1, across[1], 4.0)]
        steps += [(n, along[n], 5.0) for n in range(len(bits))][::-1]
        for n, partner, wait in steps:
            group = [(0, bc_sums, bc_land_sums), (1, norm_sum, norm_land)]
            if n < len(bits):
                group.append((2, small_sum, small_land))
            exchange(n, partner, group, when, when + wait)
            when += wait + 0.01
    hook, end = timeline.spread(
        chunks, BACKWARD_SLOTS, BACKWARD_US, lambda n: chunks - 1 - n, END_LAG if final else LAG
    )
    at = pl.ds(pl.multiple_of((chunks - 1 - chunk) * CHUNK, CHUNK), CHUNK)
    mix_back_kernel(
        *work,
        part.at[at, :],
        ginner.at[at, :],
        gstep.at[at, :],
        gshared.at[at, :],
        small,
        small_bc,
        *scratch,
        hook=hook,
    )
    end()


def pull_layer(
    line, inner_all, saved, gates, weights, layer_args, spread, aux, segrow, rows_all, dout, dgate,
    before, state, gain, more, final,
):
    length, width = rows_all.shape
    rows = state.shape[0]
    inner = dout.shape[1]
    dp = 2 * line
    fine = width // (dp * TENSOR)
    steps = dp.bit_length() - 1
    shape = jax.ShapeDtypeStruct
    _, iraw, iconv, sraw, sconv, step, mixed, sin, _ = saved
    layer = 0 if final else 1
    far_side = (rows_all, dout, dgate, before, state)
    if final:
        outs = [
            shape((rows, width), F32),
            shape((8, width), F32),
            shape((16, inner), F32),
            shape((16, 2 * N), F32),
        ]
        out_specs = [whole_spec(out.shape) for out in outs]
    else:
        outs = [
            shape((rows, width), F32),
            shape((8, width), F32),
            shape((8, rows * TENSOR), F32),
            shape((length, width), BF16),
            shape((8, inner), F32),
            shape((8, 2 * N), F32),
        ]
        out_specs = [whole_spec(out.shape) for out in outs]
        out_specs[3] = ANY
    tail_outs = scatter_outputs(width, inner, dp)
    scratch = mix_back_scratch(inner)
    weights = weights[:4]
    scratch += [pltpu.VMEM(array.shape, array.dtype) for array in (*far_side, *weights)]
    scratch += [pltpu.SemaphoreType.DMA((9,))]
    scratch += [
        pltpu.VMEM((length, width), BF16),
        pltpu.VMEM((length, inner), BF16),
        pltpu.VMEM((length, LANES), BF16),
        pltpu.VMEM((length, 2 * N), BF16),
        pltpu.VMEM((width, inner), BF16),
        pltpu.VMEM((dp, STEPS, width // dp), BF16),
        pltpu.VMEM((dp, TENSOR, fine, 2 * N), BF16),
    ]
    scratch += [pltpu.VMEM((rows, width), BF16)] * 3
    scratch += scatter_scratch(line, width, inner) + reduce_semaphores()
    if final:
        scratch += [
            pltpu.VMEM((8, inner), F32),
            pltpu.VMEM((8, 2 * N), F32),
            pltpu.VMEM((steps, 16, inner), F32),
            pltpu.VMEM((steps + 2, 16, 2 * N), F32),
            pltpu.VMEM((steps + 2, 8, width), F32),
            pltpu.SemaphoreType.DMA((steps + 2, 3)),
            pltpu.SemaphoreType.DMA((steps + 2, 3)),
        ]
    else:
        scratch += [
            pltpu.VMEM((3, 8, rows), F32),
            pltpu.VMEM((rows, LANES), F32),
            pltpu.VMEM((8, rows), F32),
            pltpu.VMEM((rows, width), BF16),
        ]
        scratch += share_semaphores() + spread_semaphores() + [pltpu.SemaphoreType.DMA((1,))]
    return call_kernel(
        functools.partial(pull_kernel, line, inner_all, final),
        outs + tail_outs,
        mix_back_specs(layer, length // CHUNK, inner, [ANY] * 4, layer_args, spread)
        + [ANY] * 5
        + [whole_spec(gain.shape)]
        + [whole_spec(array.shape) for array in more],
        out_specs + [whole_spec(out.shape) for out in tail_outs],
        scratch,
        4 if final else 3,
        (
            iraw, iconv, sraw, sconv, step, mixed, sin, sin, *gates,
            *weights, *layer_args, spread, aux, segrow, *far_side, gain, *more,
        ),
        (length // CHUNK,),
    )


def contract_wide(left, right):
    return lax.dot_general(
        left, right, (((0,), (0,)), ((), ())), preferred_element_type=F32
    )


def contract(left, right):
    return contract_wide(left, right).astype(BF16)


def on_device(
    resid,
    segment_ids,
    cotangent,
    w_z,
    w_x,
    w_bc,
    w_dt,
    w_out,
    norm_gain,
    conv_x,
    conv_bc,
    a_log,
    dt_bias,
    d_skip,
    gated_gain,
):
    dp = lax.axis_size("dp")
    assert lax.axis_size("tensor") == TENSOR and segment_ids.shape[0] == LEN
    assert a_log.shape[0] == 2 and a_log.shape[1] <= STEPS
    line = dp // 2
    heads = a_log.shape[1]
    inner = heads * P_SIZE
    inner_all = inner * TENSOR
    width = resid.shape[1]
    aux, segrow = row_masks(segment_ids)
    spread = head_spread(inner)
    args = layer_parameters(conv_x, conv_bc, a_log, dt_bias, d_skip, gated_gain)
    own = (
        w_z,
        w_x,
        jnp.swapaxes(w_out, 1, 2),
        jnp.pad(jnp.swapaxes(w_dt, 1, 2), ((0, 0), (0, STEPS - heads), (0, 0))),
        w_bc,
    )
    gains = norm_gain

    def arranged(gathered):
        gate, inner_w, out_w, step_w, shared_w = gathered
        return gate, inner_w, shared_w.reshape(width, 2 * N), step_w, out_w

    *gathered, rows_low, top_high = start_layer(line, resid, cotangent, gains, own)
    weights_low = arranged(gathered)
    results = middle_layer(
        line, inner_all, rows_low, weights_low, args, aux, segrow, resid, gains, own
    )
    saved_low = results[:9]
    state, raw, scale_row, rows_high, *gathered = results[9:]
    weights_high = arranged(gathered)
    *saved_high, hidden, per_row = top_layer(
        line, inner_all, rows_high, weights_high, args, aux, segrow, state, cotangent
    )

    def early_grads(layer, rows_all, top_all, per_row, saved, weights):
        ggate, gout, outlow, small = gate_back(layer, top_all, per_row, saved, weights[4], args[3])
        return (ggate, gout), contract(top_all, outlow), contract(rows_all, ggate), small

    gates, dout, dgate, small_high_more = early_grads(
        1, rows_high, top_high, per_row, saved_high, weights_high
    )
    results = pull_layer(
        line, inner_all, saved_high, gates, weights_high, args, spread, aux, segrow, rows_high,
        dout, dgate, cotangent, state, gains, (raw, scale_row), False,
    )
    grad_state, gnorm_high, per_row, top_low, small_high, bc_high, *grads_high = results
    gates, dout, dgate, small_low_more = early_grads(
        0, rows_low, top_low, per_row, saved_low, weights_low
    )
    more = (gnorm_high, small_low_more, small_high, small_high_more, bc_high)
    grad_resid, norm_sum, small, small_bc, *grads_low = pull_layer(
        line, inner_all, saved_low, gates, weights_low, args, spread, aux, segrow, rows_low,
        dout, dgate, grad_state, resid, gains, more, True,
    )
    gout, gz, gx, gdt, gbc = [
        jnp.stack([low, high]) for low, high in zip(grads_low, grads_high)
    ]
    small = small.reshape(2, 8, inner)
    return (
        hidden,
        grad_resid,
        gz,
        gx,
        gbc,
        jnp.swapaxes(gdt[:, :heads], 1, 2),
        jnp.swapaxes(gout, 1, 2),
        norm_sum[:2],
        small[:, :TAPS],
        small_bc.reshape(2, 8, 2 * N)[:, :TAPS],
        small[:, 6, :heads],
        small[:, 7, :heads],
        jnp.sum(small[:, 5].reshape(2, heads, P_SIZE), axis=2),
        small[:, 4],
    )


def solution(mesh):
    rows = P(("dp", "tensor"), None)
    matrix = P(None, "dp", "tensor")
    shared = P(None, ("dp", "tensor"), None)
    wide = P(None, None, "tensor")
    head = P(None, "tensor")
    out = P(None, "tensor", "dp")
    return jax.shard_map(
        on_device,
        mesh=mesh,
        in_specs=(
            rows, P("dp"), rows, matrix, matrix, shared, matrix, out, P(), wide, P(), head, head, head, head,
        ),
        out_specs=(
            rows, rows, matrix, matrix, shared, matrix, out, P(), wide, P(), head, head, head, head,
        ),
        check_vma=False,
    )
```
